32 devices in a mesh: groups: 2 (over y), seq: 4 (over z), head: 2 (over x), sub: 2 (over core).
Axes of the slice: x: 2, y: 2, z: 4, core: 2. Of those that a mesh axis runs over, the one named last changes fastest.
Arguments:
- queries: bfloat16 [8192, 2560], P(('groups', 'seq'), 'head'), parts along dimension 0, may hold values from -8 to 8
- cur_keys: bfloat16 [8192, 2560], P(('groups', 'seq', 'sub'), 'head'), parts along dimension 0, may hold values from -8 to 8
- cur_values: bfloat16 [8192, 2560], P(('groups', 'seq', 'sub'), 'head'), parts along dimension 0, may hold values from -6 to 6
- mem_keys: bfloat16 [256, 64, 2560], P(('groups', 'seq', 'sub'), None, 'head'), parts along dimension 0, may hold values from -6.5 to 6.5
- mem_values: bfloat16 [256, 64, 2560], P(('groups', 'seq', 'sub'), None, 'head'), parts along dimension 0, may hold values from -6 to 6
- frame_ids: int32 [8, 8], P('groups'), parts along dimension 0, may hold values from 0 to 127, as said below
- frame_counts: int32 [256], P('groups'), parts along dimension 0, may hold values from 1 to 64, as said below
- out_weight: bfloat16 [2560, 5120], P('head', 'sub'), may hold values from -0.125 to 0.125
Outputs:
- projected: bfloat16 [8192, 5120], P(('groups', 'seq', 'head'), 'sub'), parts along dimension 0
The draws below stay inside these ranges and needn't reach their ends.
There are 2 independent parts, one for each index of `groups`. The reference program is written for one: setup_inputs(seed, part) draws one part's arguments, and reference() takes and returns one part's arrays. A program takes and returns all parts, laid end to end along the dimension named above; an argument that names none is the same for every part. Nothing has to cross between parts.
Inputs may be any that keep to these rules, and one draw needn't show every extreme that they name: `frame_ids`: row c lists the 8 memory frames retrieved for stretch c; frame f is held by owner f // 16, and the 8 frames of a row lie on 8 different owners, one on each. Frame f has its first frame_counts[f] token slots valid; the other slots are padding.
All inputs are finite; a program needn't handle non-finite values.
Results may differ from the reference program's by a relative error of at most 0.009.
Values may be sent and summed in bfloat16 or wider, within the bound.
No kernel may reach another device: no remote copies, remote signals or barrier semaphores. Data moves between devices by JAX's collectives and lax.ppermute only.
A program may use at most 192 MiB of HBM per device.

```python
import math
import jax
import jax.numpy as jnp
from jax import lax

D = 5120
HD = 128
HEADS = 20
FT = 64
CUR = 1024
FR_DEV = 16
STRETCHES = 4
TOKENS = 4096
RET = 8
FRAMES = 128
HEAD_GROUPS = 2


planted_levels = (8.0, 7.5, 7.0)


def drawn_rows(key):
    stretch_total = TOKENS // CUR
    key_query, key_key, key_sign = jax.random.split(key, 3)
    query_spots = jax.vmap(lambda subkey: jax.random.permutation(subkey, CUR)[:3])(jax.random.split(key_query, stretch_total))
    key_spots = jax.vmap(lambda subkey: jax.random.permutation(subkey, CUR)[:6])(jax.random.split(key_key, stretch_total))
    signs = jax.random.rademacher(key_sign, (stretch_total, 3, HEADS * HD), jnp.float32)
    return (query_spots, key_spots, signs)


def place_rows(base, spots, filling):
    within = jnp.arange(CUR)[None, :] == spots[:, None]
    return jnp.where(within[:, :, None], filling[:, None, :], base)


def draw_queries(key, part):
    own_key = jax.random.fold_in(key, 5)
    query_spots, key_spots, signs = drawn_rows(key)
    base = jnp.clip(1.7 * jax.random.normal(own_key, (TOKENS // CUR, CUR, HEADS * HD), jnp.float32), -6.5, 6.5)
    for index in range(3):
        base = place_rows(base, query_spots[:, index], planted_levels[index] * signs[:, index])
    return base.reshape(TOKENS, HEADS * HD).astype(jnp.bfloat16)


def draw_cur_keys(key, part):
    own_key = jax.random.fold_in(key, 7)
    query_spots, key_spots, signs = drawn_rows(key)
    base = jnp.clip(1.7 * jax.random.normal(own_key, (TOKENS // CUR, CUR, HEADS * HD), jnp.float32), -6.5, 6.5)
    for index in range(3):
        base = place_rows(base, key_spots[:, index], planted_levels[index] * signs[:, index])
        base = place_rows(base, key_spots[:, 3 + index], (planted_levels[index] - 0.03125) * signs[:, index])
    return base.reshape(TOKENS, HEADS * HD).astype(jnp.bfloat16)


def draw_frame_ids(key, part):
    key = jax.random.fold_in(key, 11)
    key_owner, key_local, key_stretch = jax.random.split(key, 3)
    owners = jax.vmap(lambda subkey: jax.random.permutation(subkey, RET))(jax.random.split(key_owner, STRETCHES))
    local = jax.random.randint(key_local, (STRETCHES, RET), 0, FR_DEV)
    picked = jax.random.randint(key_stretch, (), 0, STRETCHES)
    chosen_row = jnp.arange(STRETCHES)[:, None] == picked
    local = jnp.where(chosen_row & (owners == 0), 0, local)
    local = jnp.where(chosen_row & (owners == RET - 1), FR_DEV - 1, local)
    return (owners * FR_DEV + local).astype(jnp.int32)


def draw_frame_counts(key, part):
    key = jax.random.fold_in(key, 13)
    key_value, key_full, key_short = jax.random.split(key, 3)
    valid_slots = jax.random.randint(key_value, (FRAMES,), 1, FT + 1)
    full_frame = jax.random.randint(key_full, (), 0, FRAMES)
    short_frame = (full_frame + 1 + jax.random.randint(key_short, (), 0, FRAMES - 1)) % FRAMES
    frame_index = jnp.arange(FRAMES)
    valid_slots = jnp.where(frame_index == full_frame, FT, valid_slots)
    valid_slots = jnp.where(frame_index == short_frame, 1, valid_slots)
    return valid_slots.astype(jnp.int32)


def levels(key, shape, cuts, smallest, high):
    def one(dim, parts):
        steps = jax.random.uniform(jax.random.fold_in(jax.random.fold_in(key, 6), dim), (parts,), jnp.float32, smallest / len(cuts), high / len(cuts))
        return jnp.repeat(jnp.exp(steps), shape[dim] // parts).reshape((-1,) + (1,) * (len(shape) - dim - 1))

    level = one(*cuts[0])
    for cut in cuts[1:]:
        level = level * one(*cut)
    return level


def scatter_about(stream_key, dims, spread, limit, shards=(), kind=jnp.bfloat16):
    entries = spread * jax.random.normal(stream_key, dims, jnp.float32)
    if shards:
        entries = entries * levels(stream_key, dims, shards, -0.22, 0.18)
    return jnp.clip(entries, -limit, limit).astype(kind)


def setup_inputs(seed: int = 0, part: int = 0) -> dict:
    keys = jax.random.split(jax.random.key(seed), 9)
    part_splits = jax.random.split(jax.random.fold_in(keys[8], part), 9)
    return {
        "queries": draw_queries(jax.random.fold_in(jax.random.fold_in(keys[8], part), 71), part),
        "cur_keys": draw_cur_keys(jax.random.fold_in(jax.random.fold_in(keys[8], part), 71), part),
        "cur_values": scatter_about(part_splits[2], (TOKENS, HEADS * HD), 1.0, 6.0, ((0, 8), (1, 2))),
        "mem_keys": scatter_about(part_splits[3], (FRAMES, FT, HEADS * HD), 1.7, 6.5, ((0, 8), (2, 2))),
        "mem_values": scatter_about(part_splits[4], (FRAMES, FT, HEADS * HD), 1.0, 6.0, ((0, 8), (2, 2))),
        "frame_ids": draw_frame_ids(jax.random.fold_in(jax.random.fold_in(keys[8], part), 71), part),
        "frame_counts": draw_frame_counts(jax.random.fold_in(jax.random.fold_in(keys[8], part), 71), part),
        "out_weight": scatter_about(keys[7], (HEADS * HD, D), (HEADS * HD) ** -0.5, 0.125, ((0, 2), (1, 2))),
    }


def reference(queries, cur_keys, cur_values, mem_keys, mem_values, frame_ids, frame_counts, out_weight):
    col_count = HEADS * HD
    score_scale = 1.0 / math.sqrt(HD)
    group_cols = col_count // HEAD_GROUPS

    def one_stretch(stretch_index):
        row_start = (stretch_index * CUR).astype(jnp.int32)
        query_heads = lax.dynamic_slice_in_dim(queries, row_start, CUR, 0).reshape(CUR, HEADS, HD).astype(jnp.float32)
        own_keys = lax.dynamic_slice_in_dim(cur_keys, row_start, CUR, 0).reshape(CUR, HEADS, HD)
        own_values = lax.dynamic_slice_in_dim(cur_values, row_start, CUR, 0).reshape(CUR, HEADS, HD)
        frame_list = lax.dynamic_index_in_dim(frame_ids, stretch_index.astype(jnp.int32), 0, keepdims=False).astype(jnp.int32)
        far_keys = jnp.take(mem_keys, frame_list, axis=0).reshape(RET * FT, HEADS, HD)
        far_values = jnp.take(mem_values, frame_list, axis=0).reshape(RET * FT, HEADS, HD)
        valid_slots = jnp.take(frame_counts, frame_list)
        far_live = (jnp.arange(FT, dtype=jnp.int32)[None, :] < valid_slots[:, None]).reshape(RET * FT)
        key_live = jnp.concatenate([jnp.ones((CUR,), dtype=bool), far_live])
        all_keys = jnp.concatenate([own_keys, far_keys], axis=0).astype(jnp.float32)
        all_values = jnp.concatenate([own_values, far_values], axis=0).astype(jnp.float32)
        scores = jnp.einsum('qhd,khd->hqk', query_heads, all_keys) * score_scale
        scores = jnp.where(key_live[None, None, :], scores, -jnp.inf)
        row_max = lax.optimization_barrier(jnp.max(scores, axis=-1, keepdims=True))
        expo = jnp.exp(scores - row_max)
        row_total = lax.optimization_barrier(jnp.sum(expo, axis=-1))
        weights = lax.optimization_barrier(expo.astype(jnp.bfloat16)).astype(jnp.float32)
        weighted = jnp.einsum('hqk,khd->qhd', weights, all_values)
        attended = (weighted / row_total.T[:, :, None]).reshape(CUR, col_count).astype(jnp.bfloat16)
        summed = jnp.zeros((CUR, D), dtype=jnp.float32)
        for group_index in range(HEAD_GROUPS):
            low = group_index * group_cols
            partial_sum = jnp.dot(attended[:, low:low + group_cols], out_weight[low:low + group_cols], preferred_element_type=jnp.float32)
            summed = summed + lax.optimization_barrier(partial_sum.astype(jnp.bfloat16)).astype(jnp.float32)
        return summed.astype(jnp.bfloat16)
    stretch_outputs = lax.map(one_stretch, jnp.arange(STRETCHES, dtype=jnp.int32))
    return stretch_outputs.reshape(TOKENS, D)
```

```python
import functools
import math

import jax
import jax.numpy as jnp
from jax import lax
from jax.experimental import pallas as pl
from jax.experimental.pallas import tpu as pltpu
from jax.sharding import PartitionSpec as P

HD = 128
FT = 64
FR_DEV = 16
F32 = jnp.float32
BF16 = jnp.bfloat16
EXP2_SCALE = math.log2(math.e) / math.sqrt(HD)
MASKED = -1e30
VMEM_LIMIT = 48 * 1024 * 1024


def params(**kw):
    return pltpu.CompilerParams(vmem_limit_bytes=VMEM_LIMIT, **kw)


def pick_kernel(seq_count, sub_count, ids, keys, values, *rest):
    outs, sems = rest[:-1], rest[-1]
    seq_index = lax.axis_index("seq")
    sub_index = lax.axis_index("sub")
    owner = seq_index * sub_count + sub_index
    width = outs[0].shape[1]
    copies = []
    for shift in range(seq_count):
        target = lax.rem(seq_index + shift, seq_count)
        wanted = jnp.int32(0)
        for entry in range(seq_count * sub_count):
            frame = ids[target, entry]
            wanted = jnp.where(lax.div(frame, FR_DEV) == owner, frame - owner * FR_DEV, wanted)
        for turn in range(sub_count):
            target_sub = lax.rem(sub_index + turn, sub_count)
            columns = pl.ds(pl.multiple_of(target_sub * width, 128), width)
            place = shift * sub_count + turn
            for part, source in enumerate((keys, values)):
                copy = pltpu.make_async_copy(
                    source.at[wanted, :, columns],
                    outs[place].at[pl.ds(part * FT, FT), :],
                    sems.at[2 * place + part],
                )
                copy.start()
                copies.append(copy)
    for copy in copies:
        copy.wait()


def pick_frames(frame_ids, mem_keys, mem_values, seq_count, sub_count):
    count = seq_count * sub_count
    width = mem_keys.shape[2] // sub_count
    return pl.pallas_call(
        functools.partial(pick_kernel, seq_count, sub_count),
        out_shape=[jax.ShapeDtypeStruct((2 * FT, width), BF16)] * count,
        in_specs=[
            pl.BlockSpec(memory_space=pltpu.SMEM),
            pl.BlockSpec(memory_space=pl.ANY),
            pl.BlockSpec(memory_space=pl.ANY),
        ],
        out_specs=[pl.BlockSpec(memory_space=pl.ANY)] * count,
        scratch_shapes=[pltpu.SemaphoreType.DMA((2 * count,))],
        name="pick_frames",
        cost_estimate=pl.CostEstimate(flops=0, bytes_accessed=4 * count * FT * width * 2, transcendentals=0),
    )(frame_ids, mem_keys, mem_values)


def dot_t(left, right):
    return lax.dot_general(left, right, (((1,), (1,)), ((), ())), preferred_element_type=F32)


def current_kernel(step, place, q, own_k, own_v, sib_k, sib_v, acc, stat):
    keys = jnp.concatenate([own_k[...], sib_k[...]], axis=0)
    values = jnp.concatenate([own_v[...], sib_v[...]], axis=0)
    values = jnp.concatenate([values, jnp.ones_like(values)], axis=1)
    for low in range(0, q.shape[0], step):
        rows = pl.ds(low, step)
        scores = dot_t(q[rows, :], keys)
        row_max = jnp.max(scores, axis=1, keepdims=True)
        weights = jnp.exp2((scores - row_max) * EXP2_SCALE).astype(BF16)
        acc[0, rows, :] = jnp.dot(weights, values, preferred_element_type=F32)
        stat[0, rows, :] = jnp.broadcast_to(row_max, (step, HD))


def attend_current(place, queries, cur_keys, cur_values, sibling, heads):
    rows = queries.shape[0]
    keys = cur_keys.shape[0]
    own = lambda j, place: (0, place[0] * heads + j)
    return pl.pallas_call(
        functools.partial(current_kernel, 256),
        grid_spec=pltpu.PrefetchScalarGridSpec(
            num_scalar_prefetch=1,
            grid=(heads,),
            in_specs=[
                pl.BlockSpec((rows, HD), own),
                pl.BlockSpec((keys, HD), own),
                pl.BlockSpec((keys, HD), own),
                pl.BlockSpec((keys, HD), lambda j, place: (0, j)),
                pl.BlockSpec((keys, HD), lambda j, place: (0, heads + j)),
            ],
            out_specs=[
                pl.BlockSpec((1, rows, 2 * HD), lambda j, place: (j, 0, 0)),
                pl.BlockSpec((1, rows, HD), lambda j, place: (j, 0, 0)),
            ],
        ),
        out_shape=[
            jax.ShapeDtypeStruct((heads, rows, 2 * HD), F32),
            jax.ShapeDtypeStruct((heads, rows, HD), F32),
        ],
        compiler_params=params(),
        name="attend_current",
        cost_estimate=pl.CostEstimate(
            flops=6 * heads * rows * 2 * keys * HD, bytes_accessed=heads * rows * HD * 14, transcendentals=heads * rows * 2 * keys
        ),
    )(place, queries, cur_keys, cur_values, sibling, sibling)


def frames_kernel(step, count, place, counts, q, acc, stat, *rest):
    frames, out = rest[:count], rest[count]
    keys = jnp.concatenate([frame[:FT, :] for frame in frames], axis=0)
    values = jnp.concatenate([frame[FT:, :] for frame in frames], axis=0)
    values = jnp.concatenate([values, jnp.ones_like(values)], axis=1)
    slot = lax.broadcasted_iota(jnp.int32, (1, FT), 1)
    bias = jnp.concatenate(
        [jnp.where(slot < counts[index], 0.0, MASKED).astype(F32) for index in range(count)], axis=1
    )
    for low in range(0, q.shape[0], step):
        rows = pl.ds(low, step)
        scores = dot_t(q[rows, :], keys) + bias
        old_max = stat[0, rows, :]
        new_max = jnp.maximum(old_max, jnp.max(scores, axis=1, keepdims=True))
        weights = jnp.exp2((scores - new_max[:, :1]) * EXP2_SCALE).astype(BF16)
        product = jnp.dot(weights, values, preferred_element_type=F32)
        scale = jnp.exp2((old_max - new_max) * EXP2_SCALE)
        top = acc[0, rows, :HD] * scale + product[:, :HD]
        total = acc[0, rows, HD:] * scale + product[:, HD:]
        out[rows, :] = (top / total).astype(BF16)


def attend_frames(place, which, counts, queries, acc, stat, frames, heads, rows):
    count = len(frames)
    half = lambda place: place[which]
    return pl.pallas_call(
        functools.partial(frames_kernel, 256, count),
        grid_spec=pltpu.PrefetchScalarGridSpec(
            num_scalar_prefetch=2,
            grid=(heads,),
            in_specs=[
                pl.BlockSpec((rows, HD), lambda j, place, counts: (half(place), place[0] * heads + j)),
                pl.BlockSpec((1, rows, 2 * HD), lambda j, place, counts: (j, half(place), 0)),
                pl.BlockSpec((1, rows, HD), lambda j, place, counts: (j, half(place), 0)),
            ]
            + [pl.BlockSpec((2 * FT, HD), lambda j, place, counts: (0, j))] * count,
            out_specs=pl.BlockSpec((rows, HD), lambda j, place, counts: (0, j)),
        ),
        out_shape=jax.ShapeDtypeStruct((rows, heads * HD), BF16),
        compiler_params=params(),
        name="attend_frames",
        cost_estimate=pl.CostEstimate(
            flops=6 * heads * rows * count * FT * HD,
            bytes_accessed=heads * rows * HD * 16,
            transcendentals=heads * rows * count * FT,
        ),
    )(place, counts, queries, acc, stat, *frames)


def project_kernel(place, mine, other, w_mine, w_other, out):
    total = jnp.dot(mine[...], w_mine[...], preferred_element_type=F32)
    total += jnp.dot(other[...], w_other[...], preferred_element_type=F32)
    out[...] = total.astype(BF16)


def project(place, mine, other, weight, first, blocks, block):
    rows, depth = mine.shape
    return pl.pallas_call(
        project_kernel,
        grid_spec=pltpu.PrefetchScalarGridSpec(
            num_scalar_prefetch=1,
            grid=(blocks,),
            in_specs=[
                pl.BlockSpec((rows, depth), lambda j, place: (0, 0)),
                pl.BlockSpec((rows, depth), lambda j, place: (0, 0)),
                pl.BlockSpec((depth, block), lambda j, place: (place[0], first + j)),
                pl.BlockSpec((depth, block), lambda j, place: (1 - place[0], first + j)),
            ],
            out_specs=pl.BlockSpec((rows, block), lambda j, place: (0, j)),
        ),
        out_shape=jax.ShapeDtypeStruct((rows, blocks * block), BF16),
        compiler_params=params(),
        name="project",
        cost_estimate=pl.CostEstimate(
            flops=4 * rows * depth * blocks * block, bytes_accessed=4 * depth * blocks * block, transcendentals=0
        ),
    )(place, mine, other, weight, weight)


def add_kernel(held, came, out):
    out[...] = (held[...].astype(F32) + came[...].astype(F32)).astype(BF16)


def add_block(held, came, index):
    rows, block = came.shape
    return pl.pallas_call(
        add_kernel,
        grid=(1,),
        in_specs=[
            pl.BlockSpec((rows, block), lambda j: (0, index)),
            pl.BlockSpec((rows, block), lambda j: (0, 0)),
        ],
        out_specs=pl.BlockSpec((rows, block), lambda j: (0, index)),
        out_shape=jax.ShapeDtypeStruct(held.shape, BF16),
        input_output_aliases={0: 0},
        compiler_params=params(),
        name="add_block",
        cost_estimate=pl.CostEstimate(flops=rows * block, bytes_accessed=6 * rows * block, transcendentals=0),
    )(held, came)


def frame_counts_of(frame_ids, frame_counts, seq_count, sub_count):
    seq_index = lax.axis_index("seq")
    sub_index = lax.axis_index("sub")
    own_list = lax.dynamic_index_in_dim(frame_ids, seq_index, 0, keepdims=False)
    shift, turn = jnp.divmod(jnp.arange(seq_count * sub_count, dtype=jnp.int32), sub_count)
    owner = (seq_index - shift) % seq_count * sub_count + (sub_index - turn) % sub_count
    hit = (own_list // FR_DEV)[None, :] == owner[:, None]
    got_ids = jnp.sum(jnp.where(hit, own_list[None, :], 0), axis=1)
    every = jnp.arange(frame_counts.shape[0], dtype=jnp.int32)
    return jnp.sum(jnp.where(got_ids[:, None] == every[None, :], frame_counts[None, :], 0), axis=1)


def local(queries, cur_keys, cur_values, mem_keys, mem_values, frame_ids, frame_counts, out_weight):
    seq_count = lax.axis_size("seq")
    sub_count = lax.axis_size("sub")
    head_index = lax.axis_index("head")
    sub_index = lax.axis_index("sub")
    row_count, col_count = queries.shape
    heads = col_count // HD // sub_count
    width = heads * HD
    half = row_count // 2
    out_cols = out_weight.shape[1]

    sends = pick_frames(frame_ids, mem_keys, mem_values, seq_count, sub_count)
    frames = [sends[0]]
    for shift in range(seq_count):
        for turn in range(sub_count):
            if shift == turn == 0:
                continue
            pairs = []
            for seq_from in range(seq_count):
                for sub_from in range(sub_count):
                    seq_to, sub_to = (seq_from + shift) % seq_count, (sub_from + turn) % sub_count
                    pairs.append((seq_from * sub_count + sub_from, seq_to * sub_count + sub_to))
            frames.append(lax.ppermute(sends[shift * sub_count + turn], ("seq", "sub"), pairs))

    swap = [(0, 1), (1, 0)]
    sibling_start = (1 - sub_index) * width
    sibling = lax.ppermute(
        jnp.concatenate(
            [lax.dynamic_slice_in_dim(piece, sibling_start, width, 1) for piece in (cur_keys, cur_values)], axis=1
        ),
        "sub",
        swap,
    )
    place = jnp.stack([sub_index, 1 - head_index, head_index]).astype(jnp.int32)
    counts = frame_counts_of(frame_ids, frame_counts, seq_count, sub_count)
    acc, stat = attend_current(place, queries, cur_keys, cur_values, sibling, heads)

    far = attend_frames(place, 1, counts, queries, acc, stat, frames, heads, half)
    far_sibling = lax.ppermute(far, "sub", swap)
    near = attend_frames(place, 2, counts, queries, acc, stat, frames, heads, half)
    near_sibling = lax.ppermute(near, "sub", swap)

    block = 640
    came = []
    for index in range(out_cols // block):
        term = project(place, far, far_sibling, out_weight, index, 1, block)
        came.append(lax.ppermute(term, "head", swap))
    total = project(place, near, near_sibling, out_weight, 0, out_cols // block, block)
    for index, piece in enumerate(came):
        total = add_block(total, piece, index)
    return total


def local_any(queries, cur_keys, cur_values, mem_keys, mem_values, frame_ids, frame_counts, out_weight):
    seq_count = lax.axis_size("seq")
    sub_count = lax.axis_size("sub")
    seq_index = lax.axis_index("seq")
    owner_self = seq_index * sub_count + lax.axis_index("sub")
    row_count, col_count = queries.shape
    heads = col_count // HD
    mine = row_count // sub_count
    wanted = jnp.sum(jnp.where(frame_ids // FR_DEV == owner_self, frame_ids, 0), axis=1) - owner_self * FR_DEV
    own_list = lax.dynamic_index_in_dim(frame_ids, seq_index, 0, keepdims=False)
    owners = jnp.arange(seq_count * sub_count, dtype=jnp.int32)
    hit = (own_list // FR_DEV)[None, :] == owners[:, None]
    got_ids = jnp.sum(jnp.where(hit, own_list[None, :], 0), axis=1).reshape(seq_count, sub_count).T.reshape(-1)
    live = jnp.arange(FT, dtype=jnp.int32)[None, :] < jnp.take(frame_counts, got_ids)[:, None]

    def spread(cached, current):
        sent = lax.all_to_all(jnp.take(cached, wanted, axis=0), "seq", split_axis=0, concat_axis=0, tiled=True)
        far = lax.all_gather(sent, "sub").reshape(-1, heads, HD)
        return jnp.concatenate([lax.all_gather(current, "sub").reshape(-1, heads, HD), far], axis=0)

    keys, values = spread(mem_keys, cur_keys), spread(mem_values, cur_values)
    key_live = jnp.concatenate([jnp.ones((keys.shape[0] - live.size,), bool), live.reshape(-1)])
    start = lax.axis_index("sub") * mine
    query_heads = lax.dynamic_slice_in_dim(queries, start, mine, 0).reshape(mine, heads, HD)
    scores = jnp.einsum("qhd,khd->hqk", query_heads, keys, preferred_element_type=F32) / math.sqrt(HD)
    scores = jnp.where(key_live[None, None, :], scores, -jnp.inf)
    expo = jnp.exp(scores - jnp.max(scores, axis=-1, keepdims=True))
    total = jnp.sum(expo, axis=-1)
    weighted = jnp.einsum("hqk,khd->qhd", expo.astype(BF16), values, preferred_element_type=F32)
    attended = (weighted / total.T[:, :, None]).reshape(mine, col_count).astype(BF16)
    attended = lax.all_gather(attended, "sub", axis=0, tiled=True)
    term = jnp.dot(attended, out_weight, preferred_element_type=F32).astype(BF16)
    return lax.psum_scatter(term, "head", scatter_dimension=0, tiled=True)


def solution(mesh):
    in_specs = (
        P(("groups", "seq"), "head"),
        P(("groups", "seq", "sub"), "head"),
        P(("groups", "seq", "sub"), "head"),
        P(("groups", "seq", "sub"), None, "head"),
        P(("groups", "seq", "sub"), None, "head"),
        P("groups", None),
        P("groups"),
        P("head", "sub"),
    )
    out_specs = P(("groups", "seq", "head"), "sub")

    def apply(queries, *rest):
        heads = queries.shape[1] // mesh.shape["head"] // HD
        paired = mesh.shape["head"] == 2 and mesh.shape["sub"] == 2 and heads % 2 == 0
        body = local if paired else local_any
        return jax.shard_map(body, mesh=mesh, in_specs=in_specs, out_specs=out_specs, check_vma=False)(queries, *rest)

    return apply
```

```python
import functools
import math

import jax
import jax.numpy as jnp
from jax import lax
from jax.experimental import pallas as pl
from jax.experimental.pallas import tpu as pltpu
from jax.sharding import PartitionSpec as P

HD = 128
FT = 64
FR_DEV = 16
F32 = jnp.float32
BF16 = jnp.bfloat16
EXP2_SCALE = math.log2(math.e) / math.sqrt(HD)
MASKED = -1e30
VMEM_LIMIT = 24 * 1024 * 1024


def params(**kw):
    return pltpu.CompilerParams(vmem_limit_bytes=VMEM_LIMIT, **kw)


def pack_kernel(seq_count, sub_count, low, ids, mem_keys, mem_values, cur_keys, cur_values, weight, *rest):
    outs, sems = rest[:-1], rest[-1]
    crossing, sibling, columns_out = outs[:-2], outs[-2], outs[-1]
    seq_index = lax.axis_index("seq")
    sub_index = lax.axis_index("sub")
    owner = seq_index * sub_count + sub_index
    width = sibling.shape[1]
    keys = cur_keys.shape[0]
    block = columns_out.shape[1]
    copies = []

    def send(source, target):
        copy = pltpu.make_async_copy(source, target, sems.at[len(copies)])
        copy.start()
        copies.append(copy)

    for turn in range(sub_count):
        target_sub = lax.rem(sub_index + turn, sub_count)
        columns = pl.ds(pl.multiple_of(target_sub * width, 128), width)
        for shift in range(seq_count):
            target = lax.rem(seq_index + shift, seq_count)
            wanted = jnp.int32(0)
            for entry in range(seq_count * sub_count):
                frame = ids[target, entry]
                wanted = jnp.where(lax.div(frame, FR_DEV) == owner, frame - owner * FR_DEV, wanted)
            place = shift * sub_count + turn
            for part, source in enumerate((mem_keys, mem_values)):
                if place == 1:
                    target_ref = sibling.at[pl.ds(2 * keys + part * FT, FT), :]
                else:
                    target_ref = crossing[place - (place > 1)].at[pl.ds(part * FT, FT), :]
                send(source.at[wanted, :, columns], target_ref)
        if turn == 1:
            for part, source in enumerate((cur_keys, cur_values)):
                send(source.at[:, columns], sibling.at[pl.ds(part * keys, keys), :])
    group = lax.axis_index("groups")
    send(weight.at[:, pl.ds(pl.multiple_of(low + group * block, 128), block)], columns_out)
    for copy in copies:
        copy.wait()


def pack(frame_ids, mem_keys, mem_values, cur_keys, cur_values, weight, low, block, seq_count, sub_count):
    count = seq_count * sub_count - 1
    width = mem_keys.shape[2] // sub_count
    shapes = [(2 * FT, width)] * count + [(2 * cur_keys.shape[0] + 2 * FT, width), (weight.shape[0], block)]
    return pl.pallas_call(
        functools.partial(pack_kernel, seq_count, sub_count, low),
        out_shape=[jax.ShapeDtypeStruct(shape, BF16) for shape in shapes],
        in_specs=[pl.BlockSpec(memory_space=pltpu.SMEM)] + [pl.BlockSpec(memory_space=pltpu.HBM)] * 5,
        out_specs=[pl.BlockSpec(memory_space=pltpu.VMEM)] * len(shapes),
        scratch_shapes=[pltpu.SemaphoreType.DMA((2 * (count + 1) + 3,))],
        compiler_params=params(),
        name="pack",
        cost_estimate=pl.CostEstimate(
            flops=0, bytes_accessed=sum(4 * rows * cols for rows, cols in shapes), transcendentals=0
        ),
    )(frame_ids, mem_keys, mem_values, cur_keys, cur_values, weight)


def dot_t(left, right):
    return lax.dot_general(left, right, (((1,), (1,)), ((), ())), preferred_element_type=F32)


def wide(column, count):
    return jnp.concatenate([column] * count, axis=1)


def with_ones(values):
    return jnp.concatenate([values, jnp.ones_like(values)], axis=1)


def current_kernel(step, place, q, own_k, own_v, sib_k, sib_v, out, lse):
    keys = jnp.concatenate([own_k[...], sib_k[...]], axis=0)
    values = with_ones(jnp.concatenate([own_v[...], sib_v[...]], axis=0))
    for low in range(0, q.shape[0], step):
        rows = pl.ds(low, step)
        scores = dot_t(q[rows, :], keys)
        row_max = jnp.broadcast_to(jnp.max(scores, axis=1, keepdims=True), (step, HD))
        weights = jnp.exp2((scores - wide(row_max, keys.shape[0] // HD)) * EXP2_SCALE).astype(BF16)
        product = jnp.dot(weights, values, preferred_element_type=F32)
        total = product[:, HD:]
        out[0, rows, :] = product[:, :HD] / total
        lse[0, rows, :] = row_max * EXP2_SCALE + jnp.log2(total)


def attend_current(place, queries, cur_keys, cur_values, sibling, heads):
    rows = queries.shape[0]
    keys = cur_keys.shape[0]
    own = lambda j, place: (0, place[0] * heads + j)
    return pl.pallas_call(
        functools.partial(current_kernel, 512),
        grid_spec=pltpu.PrefetchScalarGridSpec(
            num_scalar_prefetch=1,
            grid=(heads,),
            in_specs=[
                pl.BlockSpec((rows, HD), own),
                pl.BlockSpec((keys, HD), own),
                pl.BlockSpec((keys, HD), own),
                pl.BlockSpec((keys, HD), lambda j, place: (0, j)),
                pl.BlockSpec((keys, HD), lambda j, place: (1, j)),
            ],
            out_specs=[pl.BlockSpec((1, rows, HD), lambda j, place: (j, 0, 0))] * 2,
        ),
        out_shape=[jax.ShapeDtypeStruct((heads, rows, HD), F32)] * 2,
        compiler_params=params(),
        name="attend_current",
        cost_estimate=pl.CostEstimate(
            flops=6 * heads * rows * 2 * keys * HD, bytes_accessed=heads * rows * HD * 12, transcendentals=heads * rows * 2 * keys
        ),
    )(place, queries, cur_keys, cur_values, sibling, sibling)


def frames_kernel(count, heads, place, counts, q, held, lse, *rest):
    frames, out = rest[:count], rest[count]
    slot = lax.broadcasted_iota(jnp.int32, (1, FT), 1)
    bias = jnp.concatenate(
        [jnp.where(slot < counts[index], 0.0, MASKED).astype(F32) for index in range(count)], axis=1
    )

    def scores_of(head):
        columns = pl.ds(head * HD, HD)
        keys = jnp.concatenate([frame[:FT, columns] for frame in frames], axis=0)
        return dot_t(q[:, columns], keys)

    def finish(head, scores):
        columns = pl.ds(head * HD, HD)
        scores = scores * EXP2_SCALE + bias
        old = lse[head]
        new_max = jnp.maximum(old, jnp.max(scores, axis=1, keepdims=True))
        weights = jnp.exp2(scores - wide(new_max, count * FT // HD)).astype(BF16)
        values = with_ones(jnp.concatenate([frame[FT:, columns] for frame in frames], axis=0))
        product = jnp.dot(weights, values, preferred_element_type=F32)
        scale = jnp.exp2(old - new_max)
        top = held[head] * scale + product[:, :HD]
        out[:, columns] = (top / (scale + product[:, HD:])).astype(BF16)

    scores = scores_of(0)
    for head in range(heads):
        following = scores_of(head + 1) if head + 1 < heads else None
        finish(head, scores)
        scores = following


def attend_frames(place, which, counts, queries, held, lse, frames, sibling, heads, rows):
    width = heads * HD
    count = len(frames) + 1
    half = lambda place: place[which]
    last = sibling.shape[0] // (2 * FT) - 1
    return pl.pallas_call(
        functools.partial(frames_kernel, count, heads),
        grid_spec=pltpu.PrefetchScalarGridSpec(
            num_scalar_prefetch=2,
            grid=(1,),
            in_specs=[
                pl.BlockSpec((rows, width), lambda j, place, counts: (half(place), place[0])),
                pl.BlockSpec((heads, rows, HD), lambda j, place, counts: (0, half(place), 0)),
                pl.BlockSpec((heads, rows, HD), lambda j, place, counts: (0, half(place), 0)),
                pl.BlockSpec((2 * FT, width), lambda j, place, counts: (0, 0)),
                pl.BlockSpec((2 * FT, width), lambda j, place, counts: (last, 0)),
            ]
            + [pl.BlockSpec((2 * FT, width), lambda j, place, counts: (0, 0))] * (count - 2),
            out_specs=pl.BlockSpec((rows, width), lambda j, place, counts: (0, 0)),
        ),
        out_shape=jax.ShapeDtypeStruct((rows, width), BF16),
        compiler_params=params(),
        name="attend_frames",
        cost_estimate=pl.CostEstimate(
            flops=6 * heads * rows * count * FT * HD,
            bytes_accessed=heads * rows * HD * 12,
            transcendentals=heads * rows * count * FT,
        ),
    )(place, counts, queries, held, lse, frames[0], sibling, *frames[1:])


def both(place, mine, other):
    first, second = mine[...], other[...]
    return jnp.where(
        place[0] == 0, jnp.concatenate([first, second], axis=1), jnp.concatenate([second, first], axis=1)
    )


def project_kernel(place, mine, other, weight, out):
    out[...] = jnp.dot(both(place, mine, other), weight[...], preferred_element_type=F32).astype(BF16)


def project(place, mine, other, weight, low, block, blocks):
    rows, depth = mine.shape
    first = low // block
    return pl.pallas_call(
        project_kernel,
        grid_spec=pltpu.PrefetchScalarGridSpec(
            num_scalar_prefetch=1,
            grid=(blocks,),
            in_specs=[
                pl.BlockSpec((rows, depth), lambda j, place: (0, 0)),
                pl.BlockSpec((rows, depth), lambda j, place: (0, 0)),
                pl.BlockSpec((2 * depth, block), lambda j, place: (0, first + j)),
            ],
            out_specs=pl.BlockSpec((rows, block), lambda j, place: (0, j)),
        ),
        out_shape=jax.ShapeDtypeStruct((rows, blocks * block), BF16),
        compiler_params=params(),
        name="project",
        cost_estimate=pl.CostEstimate(
            flops=4 * rows * depth * blocks * block, bytes_accessed=4 * depth * blocks * block, transcendentals=0
        ),
    )(place, mine, other, weight)


def remote_kernel(place, held, mine, other, weight, out):
    total = jnp.dot(both(place, mine, other), weight[...], preferred_element_type=F32)
    out[...] = (held[...].astype(F32) + total).astype(BF16)


def add_remote(place, held, mine, other, weight, where):
    rows, depth = mine.shape
    block = weight.shape[1]
    return pl.pallas_call(
        remote_kernel,
        grid_spec=pltpu.PrefetchScalarGridSpec(
            num_scalar_prefetch=1,
            grid=(1,),
            in_specs=[
                pl.BlockSpec((rows, block), lambda j, place: (0, where(place))),
                pl.BlockSpec((rows, depth), lambda j, place: (0, 0)),
                pl.BlockSpec((rows, depth), lambda j, place: (0, 0)),
                pl.BlockSpec((2 * depth, block), lambda j, place: (0, 0)),
            ],
            out_specs=pl.BlockSpec((rows, block), lambda j, place: (0, where(place))),
        ),
        out_shape=jax.ShapeDtypeStruct(held.shape, BF16),
        input_output_aliases={1: 0},
        compiler_params=params(),
        name="add_remote",
        cost_estimate=pl.CostEstimate(
            flops=4 * rows * depth * block, bytes_accessed=4 * depth * block, transcendentals=0
        ),
    )(place, held, mine, other, weight)


def add_kernel(held, came, out):
    out[...] = (held[...].astype(F32) + came[...].astype(F32)).astype(BF16)


def add_block(held, came, low):
    rows, block = came.shape
    index = low // block
    return pl.pallas_call(
        add_kernel,
        grid=(1,),
        in_specs=[
            pl.BlockSpec((rows, block), lambda j: (0, index)),
            pl.BlockSpec((rows, block), lambda j: (0, 0)),
        ],
        out_specs=pl.BlockSpec((rows, block), lambda j: (0, index)),
        out_shape=jax.ShapeDtypeStruct(held.shape, BF16),
        input_output_aliases={0: 0},
        compiler_params=params(),
        name="add_block",
        cost_estimate=pl.CostEstimate(flops=rows * block, bytes_accessed=6 * rows * block, transcendentals=0),
    )(held, came)


def frame_counts_of(frame_ids, frame_counts, seq_count, sub_count):
    seq_index = lax.axis_index("seq")
    sub_index = lax.axis_index("sub")
    own_list = lax.dynamic_index_in_dim(frame_ids, seq_index, 0, keepdims=False)
    shift, turn = jnp.divmod(jnp.arange(seq_count * sub_count, dtype=jnp.int32), sub_count)
    owner = (seq_index - shift) % seq_count * sub_count + (sub_index - turn) % sub_count
    hit = (own_list // FR_DEV)[None, :] == owner[:, None]
    got_ids = jnp.sum(jnp.where(hit, own_list[None, :], 0), axis=1)
    every = jnp.arange(frame_counts.shape[0], dtype=jnp.int32)
    return jnp.sum(jnp.where(got_ids[:, None] == every[None, :], frame_counts[None, :], 0), axis=1)


def local(queries, cur_keys, cur_values, mem_keys, mem_values, frame_ids, frame_counts, out_weight):
    seq_count = lax.axis_size("seq")
    sub_count = lax.axis_size("sub")
    head_index = lax.axis_index("head")
    sub_index = lax.axis_index("sub")
    row_count, col_count = queries.shape
    heads = col_count // HD // sub_count
    width = heads * HD
    half = row_count // 2
    out_cols = out_weight.shape[1]

    low = out_cols // 2
    share = (out_cols - low) // lax.axis_size("groups")
    swap = [(0, 1), (1, 0)]

    packed = pack(
        frame_ids, mem_keys, mem_values, cur_keys, cur_values, out_weight, low, share, seq_count, sub_count
    )
    sends, to_sibling, columns = packed[:-2], packed[-2], packed[-1]
    sibling = lax.ppermute(to_sibling, "sub", swap)
    columns = lax.ppermute(columns, "head", swap)
    frames = [sends[0]]
    for place in range(2, seq_count * sub_count):
        shift, turn = divmod(place, sub_count)
        pairs = []
        for seq_from in range(seq_count):
            for sub_from in range(sub_count):
                seq_to, sub_to = (seq_from + shift) % seq_count, (sub_from + turn) % sub_count
                pairs.append((seq_from * sub_count + sub_from, seq_to * sub_count + sub_to))
        frames.append(lax.ppermute(sends[place - 1], ("seq", "sub"), pairs))

    place = jnp.stack([sub_index, 1 - head_index, head_index, lax.axis_index("groups")]).astype(jnp.int32)
    counts = frame_counts_of(frame_ids, frame_counts, seq_count, sub_count)
    held, lse = attend_current(place, queries, cur_keys, cur_values, sibling, heads)

    far = attend_frames(place, 1, counts, queries, held, lse, frames, sibling, heads, half)
    came_mine = lax.ppermute(far, "head", swap)
    far_sibling = lax.ppermute(far, "sub", swap)
    near = attend_frames(place, 2, counts, queries, held, lse, frames, sibling, heads, half)
    near_sibling = lax.ppermute(near, "sub", swap)
    columns, near = lax.optimization_barrier((columns, near))
    other_columns = lax.ppermute(columns, "groups", swap)

    came = []
    for start, block in pieces(low):
        term = project(place, far, far_sibling, out_weight, start, block, 1)
        came.append((start, lax.ppermute(term, "head", swap)))
    total = project(place, near, near_sibling, out_weight, 0, 512, out_cols // 512)
    came_other = lax.ppermute(came_mine, "sub", swap)
    total = add_remote(place, total, came_mine, came_other, columns, lambda place: low // share + place[3])
    total = add_remote(place, total, came_mine, came_other, other_columns, lambda place: low // share + 1 - place[3])
    for start, piece in came:
        total = add_block(total, piece, start)
    return total


def pieces(width):
    found, start = [], 0
    while start < width:
        block = 512 if width - start >= 512 else 256 if width - start >= 256 else 128
        found.append((start, block))
        start += block
    return found


def local_any(queries, cur_keys, cur_values, mem_keys, mem_values, frame_ids, frame_counts, out_weight):
    seq_count = lax.axis_size("seq")
    sub_count = lax.axis_size("sub")
    seq_index = lax.axis_index("seq")
    owner_self = seq_index * sub_count + lax.axis_index("sub")
    row_count, col_count = queries.shape
    heads = col_count // HD
    mine = row_count // sub_count
    wanted = jnp.sum(jnp.where(frame_ids // FR_DEV == owner_self, frame_ids, 0), axis=1) - owner_self * FR_DEV
    own_list = lax.dynamic_index_in_dim(frame_ids, seq_index, 0, keepdims=False)
    owners = jnp.arange(seq_count * sub_count, dtype=jnp.int32)
    hit = (own_list // FR_DEV)[None, :] == owners[:, None]
    got_ids = jnp.sum(jnp.where(hit, own_list[None, :], 0), axis=1).reshape(seq_count, sub_count).T.reshape(-1)
    live = jnp.arange(FT, dtype=jnp.int32)[None, :] < jnp.take(frame_counts, got_ids)[:, None]

    def spread(cached, current):
        sent = lax.all_to_all(jnp.take(cached, wanted, axis=0), "seq", split_axis=0, concat_axis=0, tiled=True)
        far = lax.all_gather(sent, "sub").reshape(-1, heads, HD)
        return jnp.concatenate([lax.all_gather(current, "sub").reshape(-1, heads, HD), far], axis=0)

    keys, values = spread(mem_keys, cur_keys), spread(mem_values, cur_values)
    key_live = jnp.concatenate([jnp.ones((keys.shape[0] - live.size,), bool), live.reshape(-1)])
    start = lax.axis_index("sub") * mine
    query_heads = lax.dynamic_slice_in_dim(queries, start, mine, 0).reshape(mine, heads, HD)
    scores = jnp.einsum("qhd,khd->hqk", query_heads, keys, preferred_element_type=F32) / math.sqrt(HD)
    scores = jnp.where(key_live[None, None, :], scores, -jnp.inf)
    expo = jnp.exp(scores - jnp.max(scores, axis=-1, keepdims=True))
    total = jnp.sum(expo, axis=-1)
    weighted = jnp.einsum("hqk,khd->qhd", expo.astype(BF16), values, preferred_element_type=F32)
    attended = (weighted / total.T[:, :, None]).reshape(mine, col_count).astype(BF16)
    attended = lax.all_gather(attended, "sub", axis=0, tiled=True)
    term = jnp.dot(attended, out_weight, preferred_element_type=F32).astype(BF16)
    return lax.psum_scatter(term, "head", scatter_dimension=0, tiled=True)


def solution(mesh):
    in_specs = (
        P(("groups", "seq"), "head"),
        P(("groups", "seq", "sub"), "head"),
        P(("groups", "seq", "sub"), "head"),
        P(("groups", "seq", "sub"), None, "head"),
        P(("groups", "seq", "sub"), None, "head"),
        P("groups", None),
        P("groups"),
        P("head", "sub"),
    )
    out_specs = P(("groups", "seq", "head"), "sub")

    def apply(queries, *rest):
        heads = queries.shape[1] // mesh.shape["head"] // HD
        paired = mesh.shape["head"] == 2 and mesh.shape["sub"] == 2 and heads % 2 == 0
        body = local if paired else local_any
        return jax.shard_map(body, mesh=mesh, in_specs=in_specs, out_specs=out_specs, check_vma=False)(queries, *rest)

    return apply
```

```python
import functools
import math

import jax
import jax.numpy as jnp
from jax import lax
from jax.experimental import pallas as pl
from jax.experimental.pallas import tpu as pltpu
from jax.sharding import PartitionSpec as P

HD = 128
FT = 64
FR_DEV = 16
F32 = jnp.float32
BF16 = jnp.bfloat16
EXP2_SCALE = math.log2(math.e) / math.sqrt(HD)
MASKED = -1e30
VMEM_LIMIT = 24 * 1024 * 1024
SHORT = pl.CostEstimate(flops=0, bytes_accessed=0, transcendentals=0)


def params(limit=VMEM_LIMIT):
    return pltpu.CompilerParams(vmem_limit_bytes=limit)


def pack_kernel(seq_count, sub_count, low, ids, mem_keys, mem_values, cur_keys, cur_values, weight, *rest):
    outs, sems = rest[:-1], rest[-1]
    crossing, sibling, columns_out = outs[:-2], outs[-2], outs[-1]
    seq_index = lax.axis_index("seq")
    sub_index = lax.axis_index("sub")
    owner = seq_index * sub_count + sub_index
    width = sibling.shape[1]
    keys = cur_keys.shape[0]
    block = columns_out.shape[1]
    copies = []

    def send(source, target):
        copy = pltpu.make_async_copy(source, target, sems.at[len(copies)])
        copy.start()
        copies.append(copy)

    for turn in range(sub_count):
        target_sub = lax.rem(sub_index + turn, sub_count)
        columns = pl.ds(pl.multiple_of(target_sub * width, 128), width)
        for shift in range(seq_count):
            target = lax.rem(seq_index + shift, seq_count)
            wanted = jnp.int32(0)
            for entry in range(seq_count * sub_count):
                frame = ids[target, entry]
                wanted = jnp.where(lax.div(frame, FR_DEV) == owner, frame - owner * FR_DEV, wanted)
            place = shift * sub_count + turn
            for part, source in enumerate((mem_keys, mem_values)):
                if place == 1:
                    target_ref = sibling.at[pl.ds(2 * keys + part * FT, FT), :]
                else:
                    target_ref = crossing[place - (place > 1)].at[pl.ds(part * FT, FT), :]
                send(source.at[wanted, :, columns], target_ref)
        if turn == 1:
            for part, source in enumerate((cur_keys, cur_values)):
                send(source.at[:, columns], sibling.at[pl.ds(part * keys, keys), :])
    group = lax.axis_index("groups")
    send(weight.at[:, pl.ds(pl.multiple_of(low + group * block, 128), block)], columns_out)
    for copy in copies:
        copy.wait()


def pack(frame_ids, mem_keys, mem_values, cur_keys, cur_values, weight, low, block, seq_count, sub_count):
    count = seq_count * sub_count - 1
    width = mem_keys.shape[2] // sub_count
    shapes = [(2 * FT, width)] * count + [(2 * cur_keys.shape[0] + 2 * FT, width), (weight.shape[0], block)]
    return pl.pallas_call(
        functools.partial(pack_kernel, seq_count, sub_count, low),
        out_shape=[jax.ShapeDtypeStruct(shape, BF16) for shape in shapes],
        in_specs=[pl.BlockSpec(memory_space=pltpu.SMEM)] + [pl.BlockSpec(memory_space=pltpu.HBM)] * 5,
        out_specs=[pl.BlockSpec(memory_space=pltpu.VMEM)] * len(shapes),
        scratch_shapes=[pltpu.SemaphoreType.DMA((2 * (count + 1) + 3,))],
        compiler_params=params(60 * 1024 * 1024),
        name="pack",
        cost_estimate=pl.CostEstimate(
            flops=0, bytes_accessed=sum(4 * rows * cols for rows, cols in shapes), transcendentals=0
        ),
    )(frame_ids, mem_keys, mem_values, cur_keys, cur_values, weight)


def dot_t(left, right):
    return lax.dot_general(left, right, (((1,), (1,)), ((), ())), preferred_element_type=F32)


def wide(column, count):
    return jnp.concatenate([column] * count, axis=1)


def with_ones(values):
    return jnp.concatenate([values, jnp.ones_like(values)], axis=1)


def current_kernel(step, passed, place, q, own_k, own_v, sib_k, sib_v, *rest):
    out, lse = rest[passed : passed + 2]
    keys = jnp.concatenate([own_k[...], sib_k[...]], axis=0)
    values = with_ones(jnp.concatenate([own_v[...], sib_v[...]], axis=0))
    for low in range(0, q.shape[0], step):
        rows = pl.ds(low, step)
        scores = dot_t(q[rows, :], keys)
        row_max = jnp.broadcast_to(jnp.max(scores, axis=1, keepdims=True), (step, HD))
        weights = jnp.exp2((scores - wide(row_max, keys.shape[0] // HD)) * EXP2_SCALE).astype(BF16)
        product = jnp.dot(weights, values, preferred_element_type=F32)
        total = product[:, HD:]
        out[0, rows, :] = product[:, :HD] / total
        lse[0, rows, :] = row_max * EXP2_SCALE + jnp.log2(total)


def attend_current(place, queries, cur_keys, cur_values, sibling, heads, passed):
    rows = queries.shape[0]
    keys = cur_keys.shape[0]
    own = lambda j, place: (0, place[0] * heads + j)
    return pl.pallas_call(
        functools.partial(current_kernel, 512, len(passed)),
        grid_spec=pltpu.PrefetchScalarGridSpec(
            num_scalar_prefetch=1,
            grid=(heads,),
            in_specs=[
                pl.BlockSpec((rows, HD), own),
                pl.BlockSpec((keys, HD), own),
                pl.BlockSpec((keys, HD), own),
                pl.BlockSpec((keys, HD), lambda j, place: (0, j)),
                pl.BlockSpec((keys, HD), lambda j, place: (1, j)),
            ]
            + [pl.BlockSpec(memory_space=pl.ANY)] * len(passed),
            out_specs=[pl.BlockSpec((1, rows, HD), lambda j, place: (j, 0, 0))] * 2
            + [pl.BlockSpec(memory_space=pl.ANY)] * len(passed),
        ),
        out_shape=[jax.ShapeDtypeStruct((heads, rows, HD), F32)] * 2
        + [jax.ShapeDtypeStruct(array.shape, array.dtype) for array in passed],
        input_output_aliases={6 + index: 2 + index for index in range(len(passed))},
        compiler_params=params(),
        name="attend_current",
        cost_estimate=pl.CostEstimate(
            flops=6 * heads * rows * 2 * keys * HD, bytes_accessed=heads * rows * HD * 12, transcendentals=heads * rows * 2 * keys
        ),
    )(place, queries, cur_keys, cur_values, sibling, sibling, *passed)


def frames_kernel(count, heads, place, counts, q, held, lse, *rest):
    frames, out = rest[:count], rest[-1]
    slot = lax.broadcasted_iota(jnp.int32, (1, FT), 1)
    bias = jnp.concatenate(
        [jnp.where(slot < counts[index], 0.0, MASKED).astype(F32) for index in range(count)], axis=1
    )

    def scores_of(head):
        columns = pl.ds(head * HD, HD)
        keys = jnp.concatenate([frame[:FT, columns] for frame in frames], axis=0)
        return dot_t(q[:, columns], keys)

    def finish(head, scores):
        columns = pl.ds(head * HD, HD)
        scores = scores * EXP2_SCALE + bias
        old = lse[head]
        new_max = jnp.maximum(old, jnp.max(scores, axis=1, keepdims=True))
        weights = jnp.exp2(scores - wide(new_max, count * FT // HD)).astype(BF16)
        values = with_ones(jnp.concatenate([frame[FT:, columns] for frame in frames], axis=0))
        product = jnp.dot(weights, values, preferred_element_type=F32)
        scale = jnp.exp2(old - new_max)
        top = held[head] * scale + product[:, :HD]
        out[:, columns] = (top / (scale + product[:, HD:])).astype(BF16)

    scores = scores_of(0)
    for head in range(heads):
        following = scores_of(head + 1) if head + 1 < heads else None
        finish(head, scores)
        scores = following


def attend_frames(place, which, counts, queries, held, lse, frames, sibling, heads, rows, after=()):
    width = heads * HD
    count = len(frames) + 1
    half = lambda place: place[which]
    last = sibling.shape[0] // (2 * FT) - 1
    return pl.pallas_call(
        functools.partial(frames_kernel, count, heads),
        grid_spec=pltpu.PrefetchScalarGridSpec(
            num_scalar_prefetch=2,
            grid=(1,),
            in_specs=[
                pl.BlockSpec((rows, width), lambda j, place, counts: (half(place), place[0])),
                pl.BlockSpec((heads, rows, HD), lambda j, place, counts: (0, half(place), 0)),
                pl.BlockSpec((heads, rows, HD), lambda j, place, counts: (0, half(place), 0)),
                pl.BlockSpec((2 * FT, width), lambda j, place, counts: (0, 0)),
                pl.BlockSpec((2 * FT, width), lambda j, place, counts: (last, 0)),
            ]
            + [pl.BlockSpec((2 * FT, width), lambda j, place, counts: (0, 0))] * (count - 2)
            + [pl.BlockSpec(memory_space=pl.ANY)] * len(after),
            out_specs=pl.BlockSpec((rows, width), lambda j, place, counts: (0, 0)),
        ),
        out_shape=jax.ShapeDtypeStruct((rows, width), BF16),
        compiler_params=params(),
        name="attend_frames",
        cost_estimate=pl.CostEstimate(
            flops=6 * heads * rows * count * FT * HD,
            bytes_accessed=heads * rows * HD * 12,
            transcendentals=heads * rows * count * FT,
        ),
    )(place, counts, queries, held, lse, frames[0], sibling, *frames[1:], *after)


def both(place, mine, other):
    first, second = mine[...], other[...]
    return jnp.where(
        place[0] == 0, jnp.concatenate([first, second], axis=1), jnp.concatenate([second, first], axis=1)
    )


def project_kernel(passed, place, mine, other, weight, *rest):
    out = rest[-1 - passed]
    out[...] = jnp.dot(both(place, mine, other), weight[...], preferred_element_type=F32).astype(BF16)


def project(place, mine, other, weight, low, block, blocks, after=(), passed=()):
    rows, depth = mine.shape
    first = low // block
    outs = pl.pallas_call(
        functools.partial(project_kernel, len(passed)),
        grid_spec=pltpu.PrefetchScalarGridSpec(
            num_scalar_prefetch=1,
            grid=(blocks,),
            in_specs=[
                pl.BlockSpec((rows, depth), lambda j, place: (0, 0)),
                pl.BlockSpec((rows, depth), lambda j, place: (0, 0)),
                pl.BlockSpec((2 * depth, block), lambda j, place: (0, first + j)),
            ]
            + [pl.BlockSpec(memory_space=pl.ANY)] * (len(after) + len(passed)),
            out_specs=[pl.BlockSpec((rows, block), lambda j, place: (0, j))]
            + [pl.BlockSpec(memory_space=pl.ANY)] * len(passed),
        ),
        out_shape=[jax.ShapeDtypeStruct((rows, blocks * block), BF16)]
        + [jax.ShapeDtypeStruct(array.shape, array.dtype) for array in passed],
        input_output_aliases={4 + len(after) + index: 1 + index for index in range(len(passed))},
        compiler_params=params(),
        name="project",
        cost_estimate=SHORT,
    )(place, mine, other, weight, *after, *passed)
    return outs if passed else outs[0]


def remote_kernel(place, held, mine, other, weight, out):
    total = jnp.dot(both(place, mine, other), weight[...], preferred_element_type=F32)
    out[...] = (held[...].astype(F32) + total).astype(BF16)


def add_remote(place, held, mine, other, weight, where):
    rows, depth = mine.shape
    block = weight.shape[1]
    return pl.pallas_call(
        remote_kernel,
        grid_spec=pltpu.PrefetchScalarGridSpec(
            num_scalar_prefetch=1,
            grid=(1,),
            in_specs=[
                pl.BlockSpec((rows, block), lambda j, place: (0, where(place))),
                pl.BlockSpec((rows, depth), lambda j, place: (0, 0)),
                pl.BlockSpec((rows, depth), lambda j, place: (0, 0)),
                pl.BlockSpec((2 * depth, block), lambda j, place: (0, 0)),
            ],
            out_specs=pl.BlockSpec((rows, block), lambda j, place: (0, where(place))),
        ),
        out_shape=jax.ShapeDtypeStruct(held.shape, BF16),
        input_output_aliases={1: 0},
        compiler_params=params(),
        name="add_remote",
        cost_estimate=SHORT,
    )(place, held, mine, other, weight)


def gate(array, after):
    return pl.pallas_call(
        lambda *refs: None,
        in_specs=[pl.BlockSpec(memory_space=pl.ANY)] * 2,
        out_specs=pl.BlockSpec(memory_space=pl.ANY),
        out_shape=jax.ShapeDtypeStruct(array.shape, array.dtype),
        input_output_aliases={0: 0},
        name="gate",
        cost_estimate=SHORT,
    )(array, after)


def add_kernel(held, came, out):
    out[...] = (held[...].astype(F32) + came[...].astype(F32)).astype(BF16)


def add_block(held, came, low):
    rows, block = came.shape
    index = low // block
    return pl.pallas_call(
        add_kernel,
        grid=(1,),
        in_specs=[
            pl.BlockSpec((rows, block), lambda j: (0, index)),
            pl.BlockSpec((rows, block), lambda j: (0, 0)),
        ],
        out_specs=pl.BlockSpec((rows, block), lambda j: (0, index)),
        out_shape=jax.ShapeDtypeStruct(held.shape, BF16),
        input_output_aliases={0: 0},
        compiler_params=params(),
        name="add_block",
        cost_estimate=SHORT,
    )(held, came)


def frame_counts_of(frame_ids, frame_counts, seq_count, sub_count):
    seq_index = lax.axis_index("seq")
    sub_index = lax.axis_index("sub")
    own_list = lax.dynamic_index_in_dim(frame_ids, seq_index, 0, keepdims=False)
    shift, turn = jnp.divmod(jnp.arange(seq_count * sub_count, dtype=jnp.int32), sub_count)
    owner = (seq_index - shift) % seq_count * sub_count + (sub_index - turn) % sub_count
    hit = (own_list // FR_DEV)[None, :] == owner[:, None]
    got_ids = jnp.sum(jnp.where(hit, own_list[None, :], 0), axis=1)
    every = jnp.arange(frame_counts.shape[0], dtype=jnp.int32)
    return jnp.sum(jnp.where(got_ids[:, None] == every[None, :], frame_counts[None, :], 0), axis=1)


def local(queries, cur_keys, cur_values, mem_keys, mem_values, frame_ids, frame_counts, out_weight):
    seq_count = lax.axis_size("seq")
    sub_count = lax.axis_size("sub")
    head_index = lax.axis_index("head")
    sub_index = lax.axis_index("sub")
    row_count, col_count = queries.shape
    heads = col_count // HD // sub_count
    width = heads * HD
    half = row_count // 2
    out_cols = out_weight.shape[1]

    low = out_cols // 2
    share = (out_cols - low) // lax.axis_size("groups")
    swap = [(0, 1), (1, 0)]

    packed = pack(
        frame_ids, mem_keys, mem_values, cur_keys, cur_values, out_weight, low, share, seq_count, sub_count
    )
    sends, to_sibling, columns = packed[:-2], packed[-2], packed[-1]
    sibling = lax.ppermute(to_sibling, "sub", swap)
    columns = lax.ppermute(columns, "head", swap)
    place = jnp.stack([sub_index, 1 - head_index, head_index, lax.axis_index("groups")]).astype(jnp.int32)
    counts = frame_counts_of(frame_ids, frame_counts, seq_count, sub_count)

    def cross(index, sent):
        shift, turn = divmod(index, sub_count)
        pairs = []
        for seq_from in range(seq_count):
            for sub_from in range(sub_count):
                seq_to, sub_to = (seq_from + shift) % seq_count, (sub_from + turn) % sub_count
                pairs.append((seq_from * sub_count + sub_from, seq_to * sub_count + sub_to))
        return lax.ppermute(sent, ("seq", "sub"), pairs)

    order = sorted(range(2, seq_count * sub_count), key=lambda index: -min(index // 2, seq_count - index // 2))
    early, late = order[: len(order) // 2], order[len(order) // 2 :]
    got = {index: cross(index, sends[index - 1]) for index in early}
    held, lse, *late_sends = attend_current(
        place, queries, cur_keys, cur_values, sibling, heads, [sends[index - 1] for index in late]
    )
    got.update({index: cross(index, sent) for index, sent in zip(late, late_sends)})
    frames = [sends[0]] + [got[index] for index in sorted(got)]

    far = attend_frames(place, 1, counts, queries, held, lse, frames, sibling, heads, half)
    came_mine = lax.ppermute(far, "head", swap)
    far_sibling = lax.ppermute(far, "sub", swap)
    near = attend_frames(place, 2, counts, queries, held, lse, frames, sibling, heads, half, (far,))
    near_sibling = lax.ppermute(near, "sub", swap)
    columns = gate(columns, near)
    other_columns = lax.ppermute(columns, "groups", swap)

    came, term, blocks = [], near, pieces(low)
    for start, block in blocks:
        if start != blocks[-1][0]:
            term = project(place, far, far_sibling, out_weight, start, block, 1, (term,))
        else:
            term, came_mine = project(place, far, far_sibling, out_weight, start, block, 1, (term,), (came_mine,))
        came.append((start, lax.ppermute(term, "head", swap)))
    came_other = lax.ppermute(came_mine, "sub", swap)
    total = project(place, near, near_sibling, out_weight, 0, 512, out_cols // 512, (term,))
    for start, piece in came[:-1]:
        total = add_block(total, piece, start)
    total = add_remote(place, total, came_mine, came_other, columns, lambda place: low // share + place[3])
    total = add_remote(place, total, came_mine, came_other, other_columns, lambda place: low // share + 1 - place[3])
    start, piece = came[-1]
    return add_block(total, piece, start)


def pieces(width):
    found, start = [], 0
    while start < width:
        block = 512 if width - start >= 512 else 256 if width - start >= 256 else 128
        found.append((start, block))
        start += block
    return found


def local_any(queries, cur_keys, cur_values, mem_keys, mem_values, frame_ids, frame_counts, out_weight):
    seq_count = lax.axis_size("seq")
    sub_count = lax.axis_size("sub")
    seq_index = lax.axis_index("seq")
    owner_self = seq_index * sub_count + lax.axis_index("sub")
    row_count, col_count = queries.shape
    heads = col_count // HD
    mine = row_count // sub_count
    wanted = jnp.sum(jnp.where(frame_ids // FR_DEV == owner_self, frame_ids, 0), axis=1) - owner_self * FR_DEV
    own_list = lax.dynamic_index_in_dim(frame_ids, seq_index, 0, keepdims=False)
    owners = jnp.arange(seq_count * sub_count, dtype=jnp.int32)
    hit = (own_list // FR_DEV)[None, :] == owners[:, None]
    got_ids = jnp.sum(jnp.where(hit, own_list[None, :], 0), axis=1).reshape(seq_count, sub_count).T.reshape(-1)
    live = jnp.arange(FT, dtype=jnp.int32)[None, :] < jnp.take(frame_counts, got_ids)[:, None]

    def spread(cached, current):
        sent = lax.all_to_all(jnp.take(cached, wanted, axis=0), "seq", split_axis=0, concat_axis=0, tiled=True)
        far = lax.all_gather(sent, "sub").reshape(-1, heads, HD)
        return jnp.concatenate([lax.all_gather(current, "sub").reshape(-1, heads, HD), far], axis=0)

    keys, values = spread(mem_keys, cur_keys), spread(mem_values, cur_values)
    key_live = jnp.concatenate([jnp.ones((keys.shape[0] - live.size,), bool), live.reshape(-1)])
    start = lax.axis_index("sub") * mine
    query_heads = lax.dynamic_slice_in_dim(queries, start, mine, 0).reshape(mine, heads, HD)
    scores = jnp.einsum("qhd,khd->hqk", query_heads, keys, preferred_element_type=F32) / math.sqrt(HD)
    scores = jnp.where(key_live[None, None, :], scores, -jnp.inf)
    expo = jnp.exp(scores - jnp.max(scores, axis=-1, keepdims=True))
    total = jnp.sum(expo, axis=-1)
    weighted = jnp.einsum("hqk,khd->qhd", expo.astype(BF16), values, preferred_element_type=F32)
    attended = (weighted / total.T[:, :, None]).reshape(mine, col_count).astype(BF16)
    attended = lax.all_gather(attended, "sub", axis=0, tiled=True)
    term = jnp.dot(attended, out_weight, preferred_element_type=F32).astype(BF16)
    return lax.psum_scatter(term, "head", scatter_dimension=0, tiled=True)


def solution(mesh):
    in_specs = (
        P(("groups", "seq"), "head"),
        P(("groups", "seq", "sub"), "head"),
        P(("groups", "seq", "sub"), "head"),
        P(("groups", "seq", "sub"), None, "head"),
        P(("groups", "seq", "sub"), None, "head"),
        P("groups", None),
        P("groups"),
        P("head", "sub"),
    )
    out_specs = P(("groups", "seq", "head"), "sub")

    def apply(queries, *rest):
        heads = queries.shape[1] // mesh.shape["head"] // HD
        paired = mesh.shape["head"] == 2 and mesh.shape["sub"] == 2 and heads % 2 == 0
        body = local if paired else local_any
        return jax.shard_map(body, mesh=mesh, in_specs=in_specs, out_specs=out_specs, check_vma=False)(queries, *rest)

    return apply
```

```python
import functools
import math

import jax
import jax.numpy as jnp
from jax import lax
from jax.experimental import pallas as pl
from jax.experimental.pallas import tpu as pltpu
from jax.sharding import PartitionSpec as P

HD = 128
FT = 64
FR_DEV = 16
F32 = jnp.float32
BF16 = jnp.bfloat16
EXP2_SCALE = math.log2(math.e) / math.sqrt(HD)
MASKED = -1e30
VMEM_LIMIT = 24 * 1024 * 1024
SHORT = pl.CostEstimate(flops=0, bytes_accessed=0, transcendentals=0)


def params():
    return pltpu.CompilerParams(vmem_limit_bytes=VMEM_LIMIT)


def in_hbm(array):
    return pltpu.with_memory_space_constraint(array, pltpu.HBM)


def in_vmem(array):
    return pltpu.with_memory_space_constraint(array, pltpu.VMEM)


def copy_all(pairs, sems):
    copies = [pltpu.make_async_copy(*pair, sems.at[index]) for index, pair in enumerate(pairs)]
    for copy in copies:
        copy.start()
    for copy in copies:
        copy.wait()


def pack_kernel(seq_count, sub_count, low, ids, keys, values, weight, frames_out, columns_out, sems):
    owner = lax.axis_index("seq") * sub_count + lax.axis_index("sub")
    width = frames_out.shape[2]
    block = columns_out.shape[1]
    first = pl.multiple_of(low + lax.axis_index("groups") * block, 128)
    pairs = [(weight.at[:, pl.ds(first, block)], columns_out)]
    for target in range(seq_count):
        wanted = jnp.int32(0)
        for entry in range(seq_count * sub_count):
            frame = ids[target, entry]
            wanted = jnp.where(lax.div(frame, FR_DEV) == owner, frame - owner * FR_DEV, wanted)
        for target_sub in range(sub_count):
            columns = pl.ds(target_sub * width, width)
            for part, source in enumerate((keys, values)):
                target_ref = frames_out.at[target * sub_count + target_sub, pl.ds(part * FT, FT), :]
                pairs.append((source.at[wanted, :, columns], target_ref))
    copy_all(pairs, sems)


def pack(frame_ids, mem_keys, mem_values, weight, low, block, seq_count, sub_count):
    count = seq_count * sub_count
    shapes = [(count, 2 * FT, mem_keys.shape[2] // sub_count), (weight.shape[0], block)]
    return pl.pallas_call(
        functools.partial(pack_kernel, seq_count, sub_count, low),
        out_shape=[pltpu.VMEM(shape, BF16) for shape in shapes],
        in_specs=[pl.BlockSpec(memory_space=pltpu.SMEM)] + [pl.BlockSpec(memory_space=pltpu.HBM)] * 3,
        out_specs=[pl.BlockSpec(memory_space=pltpu.VMEM)] * 2,
        scratch_shapes=[pltpu.SemaphoreType.DMA((2 * count + 1,))],
        compiler_params=params(),
        name="pack",
        cost_estimate=pl.CostEstimate(flops=0, bytes_accessed=12 * 2**20, transcendentals=0),
    )(frame_ids, in_hbm(mem_keys), in_hbm(mem_values), in_hbm(weight))


def pack_sibling_kernel(keys, values, out, sems):
    count, width = keys.shape[0], out.shape[1]
    columns = pl.ds(pl.multiple_of((1 - lax.axis_index("sub")) * width, 128), width)
    copy_all([(source.at[:, columns], out.at[pl.ds(part * count, count), :]) for part, source in enumerate((keys, values))], sems)


def pack_sibling(cur_keys, cur_values, after):
    count, width = cur_keys.shape[0], cur_keys.shape[1] // 2
    return pl.pallas_call(
        lambda keys, values, after, *rest: pack_sibling_kernel(keys, values, *rest),
        out_shape=pltpu.VMEM((2 * count, width), BF16),
        in_specs=[pl.BlockSpec(memory_space=pltpu.HBM)] * 2 + [pl.BlockSpec(memory_space=pl.ANY)],
        out_specs=pl.BlockSpec(memory_space=pltpu.VMEM),
        scratch_shapes=[pltpu.SemaphoreType.DMA((2,))],
        compiler_params=params(),
        name="pack_sibling",
        cost_estimate=pl.CostEstimate(flops=0, bytes_accessed=8 * count * width, transcendentals=0),
    )(in_hbm(cur_keys), in_hbm(cur_values), in_vmem(after))


def dot_t(left, right):
    return lax.dot_general(left, right, (((1,), (1,)), ((), ())), preferred_element_type=F32)


def wide(column, count):
    return jnp.concatenate([column] * count, axis=1)


def with_ones(values):
    return jnp.concatenate([values, jnp.ones_like(values)], axis=1)


def current_kernel(step, place, q, own_k, own_v, sib_k, sib_v, out, lse):
    keys = jnp.concatenate([own_k[...], sib_k[...]], axis=0)
    values = with_ones(jnp.concatenate([own_v[...], sib_v[...]], axis=0))
    for low in range(0, q.shape[0], step):
        rows = pl.ds(low, step)
        scores = dot_t(q[rows, :], keys)
        row_max = jnp.broadcast_to(jnp.max(scores, axis=1, keepdims=True), (step, HD))
        weights = jnp.exp2((scores - wide(row_max, keys.shape[0] // HD)) * EXP2_SCALE).astype(BF16)
        product = jnp.dot(weights, values, preferred_element_type=F32)
        total = product[:, HD:]
        out[0, rows, :] = product[:, :HD] / total
        lse[0, rows, :] = row_max * EXP2_SCALE + jnp.log2(total)


def attend_current(place, queries, cur_keys, cur_values, sibling, heads):
    rows = queries.shape[0]
    keys = cur_keys.shape[0]
    own = lambda j, place: (0, place[0] * heads + j)
    return pl.pallas_call(
        functools.partial(current_kernel, 512),
        grid_spec=pltpu.PrefetchScalarGridSpec(
            num_scalar_prefetch=1,
            grid=(heads,),
            in_specs=[
                pl.BlockSpec((rows, HD), own),
                pl.BlockSpec((keys, HD), own),
                pl.BlockSpec((keys, HD), own),
                pl.BlockSpec((keys, HD), lambda j, place: (0, j)),
                pl.BlockSpec((keys, HD), lambda j, place: (1, j)),
            ],
            out_specs=[pl.BlockSpec((1, rows, HD), lambda j, place: (j, 0, 0))] * 2,
        ),
        out_shape=[pltpu.VMEM((heads, rows, HD), F32)] * 2,
        compiler_params=params(),
        name="attend_current",
        cost_estimate=pl.CostEstimate(
            flops=6 * heads * rows * 2 * keys * HD, bytes_accessed=heads * rows * HD * 12, transcendentals=heads * rows * 2 * keys
        ),
    )(place, in_hbm(queries), in_hbm(cur_keys), in_hbm(cur_values), in_vmem(sibling), in_vmem(sibling))


def frames_kernel(count, heads, place, counts, q, held, lse, frames, *rest):
    out = rest[-1]
    slot = lax.broadcasted_iota(jnp.int32, (1, FT), 1)
    bias = jnp.concatenate(
        [jnp.where(slot < counts[index], 0.0, MASKED).astype(F32) for index in range(count)], axis=1
    )

    def scores_of(head):
        columns = pl.ds(head * HD, HD)
        keys = jnp.concatenate([frames[index, :FT, columns] for index in range(count)], axis=0)
        return dot_t(q[:, columns], keys)

    def finish(head, scores):
        columns = pl.ds(head * HD, HD)
        scores = scores * EXP2_SCALE + bias
        old = lse[head]
        new_max = jnp.maximum(old, jnp.max(scores, axis=1, keepdims=True))
        weights = jnp.exp2(scores - wide(new_max, count * FT // HD)).astype(BF16)
        values = with_ones(jnp.concatenate([frames[index, FT:, columns] for index in range(count)], axis=0))
        product = jnp.dot(weights, values, preferred_element_type=F32)
        scale = jnp.exp2(old - new_max)
        top = held[head] * scale + product[:, :HD]
        out[:, columns] = (top / (scale + product[:, HD:])).astype(BF16)

    scores = scores_of(0)
    for head in range(heads):
        following = scores_of(head + 1) if head + 1 < heads else None
        finish(head, scores)
        scores = following


def attend_frames(place, which, counts, queries, held, lse, frames, heads, rows, after=()):
    width = heads * HD
    count = frames.shape[0]
    half = lambda place: place[which]
    return pl.pallas_call(
        functools.partial(frames_kernel, count, heads),
        grid_spec=pltpu.PrefetchScalarGridSpec(
            num_scalar_prefetch=2,
            grid=(1,),
            in_specs=[
                pl.BlockSpec((rows, width), lambda j, place, counts: (half(place), place[0])),
                pl.BlockSpec((heads, rows, HD), lambda j, place, counts: (0, half(place), 0)),
                pl.BlockSpec((heads, rows, HD), lambda j, place, counts: (0, half(place), 0)),
                pl.BlockSpec((count, 2 * FT, width), lambda j, place, counts: (0, 0, 0)),
            ]
            + [pl.BlockSpec(memory_space=pl.ANY)] * len(after),
            out_specs=pl.BlockSpec((rows, width), lambda j, place, counts: (0, 0)),
        ),
        out_shape=pltpu.VMEM((rows, width), BF16),
        compiler_params=params(),
        name="attend_frames",
        cost_estimate=SHORT,
    )(place, counts, in_hbm(queries), in_vmem(held), in_vmem(lse), in_vmem(frames), *map(in_vmem, after))


def both(place, mine, other):
    first, second = mine[...], other[...]
    return jnp.where(
        place[0] == 0, jnp.concatenate([first, second], axis=1), jnp.concatenate([second, first], axis=1)
    )


def project_kernel(passed, place, mine, other, weight, *rest):
    out = rest[-1 - passed]
    out[...] = jnp.dot(both(place, mine, other), weight[...], preferred_element_type=F32).astype(BF16)


def project(place, mine, other, weight, low, block, blocks, after=(), passed=()):
    rows, depth = mine.shape
    first = low // block
    outs = pl.pallas_call(
        functools.partial(project_kernel, len(passed)),
        grid_spec=pltpu.PrefetchScalarGridSpec(
            num_scalar_prefetch=1,
            grid=(blocks,),
            in_specs=[
                pl.BlockSpec((rows, depth), lambda j, place: (0, 0)),
                pl.BlockSpec((rows, depth), lambda j, place: (0, 0)),
                pl.BlockSpec((2 * depth, block), lambda j, place: (0, first + j)),
            ]
            + [pl.BlockSpec(memory_space=pl.ANY)] * (len(after) + len(passed)),
            out_specs=[pl.BlockSpec((rows, block), lambda j, place: (0, j))]
            + [pl.BlockSpec(memory_space=pl.ANY)] * len(passed),
        ),
        out_shape=[(pltpu.VMEM if blocks == 1 else pltpu.HBM)((rows, blocks * block), BF16)]
        + [jax.ShapeDtypeStruct(array.shape, array.dtype) for array in passed],
        input_output_aliases={4 + len(after) + index: 1 + index for index in range(len(passed))},
        compiler_params=params(),
        name="project",
        cost_estimate=SHORT,
    )(place, in_vmem(mine), in_vmem(other), in_hbm(weight), *map(in_vmem, after), *map(in_vmem, passed))
    return outs if passed else outs[0]


def remote_kernel(place, held, mine, other, weight, out):
    total = jnp.dot(both(place, mine, other), weight[...], preferred_element_type=F32)
    out[...] = (held[...].astype(F32) + total).astype(BF16)


def add_remote(place, held, mine, other, weight, where):
    rows, depth = mine.shape
    block = weight.shape[1]
    return pl.pallas_call(
        remote_kernel,
        grid_spec=pltpu.PrefetchScalarGridSpec(
            num_scalar_prefetch=1,
            grid=(1,),
            in_specs=[
                pl.BlockSpec((rows, block), lambda j, place: (0, where(place))),
                pl.BlockSpec((rows, depth), lambda j, place: (0, 0)),
                pl.BlockSpec((rows, depth), lambda j, place: (0, 0)),
                pl.BlockSpec((2 * depth, block), lambda j, place: (0, 0)),
            ],
            out_specs=pl.BlockSpec((rows, block), lambda j, place: (0, where(place))),
        ),
        out_shape=jax.ShapeDtypeStruct(held.shape, BF16),
        input_output_aliases={1: 0},
        compiler_params=params(),
        name="add_remote",
        cost_estimate=SHORT,
    )(place, in_hbm(held), in_vmem(mine), in_vmem(other), in_vmem(weight))


def gate(array, after):
    return pl.pallas_call(
        lambda *refs: None,
        in_specs=[pl.BlockSpec(memory_space=pl.ANY)] * 2,
        out_specs=pl.BlockSpec(memory_space=pl.ANY),
        out_shape=jax.ShapeDtypeStruct(array.shape, array.dtype),
        input_output_aliases={0: 0},
        name="gate",
        cost_estimate=SHORT,
    )(in_vmem(array), in_vmem(after))


def add_kernel(held, came, out):
    out[...] = (held[...].astype(F32) + came[...].astype(F32)).astype(BF16)


def add_block(held, came, low):
    rows, block = came.shape
    index = low // block
    return pl.pallas_call(
        add_kernel,
        grid=(1,),
        in_specs=[
            pl.BlockSpec((rows, block), lambda j: (0, index)),
            pl.BlockSpec((rows, block), lambda j: (0, 0)),
        ],
        out_specs=pl.BlockSpec((rows, block), lambda j: (0, index)),
        out_shape=jax.ShapeDtypeStruct(held.shape, BF16),
        input_output_aliases={0: 0},
        compiler_params=params(),
        name="add_block",
        cost_estimate=SHORT,
    )(in_hbm(held), in_vmem(came))


def frame_counts_of(frame_ids, frame_counts, owners):
    own_list = lax.dynamic_index_in_dim(frame_ids, lax.axis_index("seq"), 0, keepdims=False)
    hit = (own_list // FR_DEV)[None, :] == jnp.arange(owners, dtype=jnp.int32)[:, None]
    got_ids = jnp.sum(jnp.where(hit, own_list[None, :], 0), axis=1)
    every = jnp.arange(frame_counts.shape[0], dtype=jnp.int32)
    return jnp.sum(jnp.where(got_ids[:, None] == every[None, :], frame_counts[None, :], 0), axis=1)


def local(queries, cur_keys, cur_values, mem_keys, mem_values, frame_ids, frame_counts, out_weight):
    seq_count = lax.axis_size("seq")
    sub_count = lax.axis_size("sub")
    head_index = lax.axis_index("head")
    sub_index = lax.axis_index("sub")
    row_count, col_count = queries.shape
    heads = col_count // HD // sub_count
    width = heads * HD
    half = row_count // 2
    out_cols = out_weight.shape[1]

    low = out_cols // 2
    share = (out_cols - low) // lax.axis_size("groups")
    swap = [(0, 1), (1, 0)]

    frames, columns = pack(frame_ids, mem_keys, mem_values, out_weight, low, share, seq_count, sub_count)
    columns = lax.ppermute(columns, "head", swap)
    to_sibling = pack_sibling(cur_keys, cur_values, frames)
    frames = lax.all_to_all(frames, ("seq", "sub"), split_axis=0, concat_axis=0, tiled=True)
    sibling = lax.ppermute(to_sibling, "sub", swap)

    place = jnp.stack([sub_index, 1 - head_index, head_index, lax.axis_index("groups")]).astype(jnp.int32)
    counts = frame_counts_of(frame_ids, frame_counts, seq_count * sub_count)
    held, lse = attend_current(place, queries, cur_keys, cur_values, sibling, heads)

    far = attend_frames(place, 1, counts, queries, held, lse, frames, heads, half)
    came_mine = lax.ppermute(far, "head", swap)
    far_sibling = lax.ppermute(far, "sub", swap)
    columns = gate(columns, far)
    other_columns = lax.ppermute(columns, "groups", swap)

    came, after = [], ()
    blocks = pieces(low)
    for start, block in blocks[:-1]:
        term = project(place, far, far_sibling, out_weight, start, block, 1, after)
        came.append((start, lax.ppermute(term, "head", swap)))
        after = (term,)
    near = attend_frames(place, 2, counts, queries, held, lse, frames, heads, half, after)
    near_sibling = lax.ppermute(near, "sub", swap)
    start, block = blocks[-1]
    term, came_mine = project(place, far, far_sibling, out_weight, start, block, 1, (near,), (came_mine,))
    came.append((start, lax.ppermute(term, "head", swap)))
    came_other = lax.ppermute(came_mine, "sub", swap)
    total = project(place, near, near_sibling, out_weight, 0, 512, out_cols // 512, (term,))
    for start, piece in came[:-1]:
        total = add_block(total, piece, start)
    total = add_remote(place, total, came_mine, came_other, columns, lambda place: low // share + place[3])
    total = add_remote(place, total, came_mine, came_other, other_columns, lambda place: low // share + 1 - place[3])
    start, piece = came[-1]
    return add_block(total, piece, start)


def pieces(width):
    found, start = [], 0
    while start < width:
        block = 512 if width - start >= 512 else 256 if width - start >= 256 else 128
        found.append((start, block))
        start += block
    return found


def local_any(queries, cur_keys, cur_values, mem_keys, mem_values, frame_ids, frame_counts, out_weight):
    seq_count = lax.axis_size("seq")
    sub_count = lax.axis_size("sub")
    seq_index = lax.axis_index("seq")
    owner_self = seq_index * sub_count + lax.axis_index("sub")
    row_count, col_count = queries.shape
    heads = col_count // HD
    mine = row_count // sub_count
    wanted = jnp.sum(jnp.where(frame_ids // FR_DEV == owner_self, frame_ids, 0), axis=1) - owner_self * FR_DEV
    own_list = lax.dynamic_index_in_dim(frame_ids, seq_index, 0, keepdims=False)
    owners = jnp.arange(seq_count * sub_count, dtype=jnp.int32)
    hit = (own_list // FR_DEV)[None, :] == owners[:, None]
    got_ids = jnp.sum(jnp.where(hit, own_list[None, :], 0), axis=1).reshape(seq_count, sub_count).T.reshape(-1)
    live = jnp.arange(FT, dtype=jnp.int32)[None, :] < jnp.take(frame_counts, got_ids)[:, None]

    def spread(cached, current):
        sent = lax.all_to_all(jnp.take(cached, wanted, axis=0), "seq", split_axis=0, concat_axis=0, tiled=True)
        far = lax.all_gather(sent, "sub").reshape(-1, heads, HD)
        return jnp.concatenate([lax.all_gather(current, "sub").reshape(-1, heads, HD), far], axis=0)

    keys, values = spread(mem_keys, cur_keys), spread(mem_values, cur_values)
    key_live = jnp.concatenate([jnp.ones((keys.shape[0] - live.size,), bool), live.reshape(-1)])
    start = lax.axis_index("sub") * mine
    query_heads = lax.dynamic_slice_in_dim(queries, start, mine, 0).reshape(mine, heads, HD)
    scores = jnp.einsum("qhd,khd->hqk", query_heads, keys, preferred_element_type=F32) / math.sqrt(HD)
    scores = jnp.where(key_live[None, None, :], scores, -jnp.inf)
    expo = jnp.exp(scores - jnp.max(scores, axis=-1, keepdims=True))
    total = jnp.sum(expo, axis=-1)
    weighted = jnp.einsum("hqk,khd->qhd", expo.astype(BF16), values, preferred_element_type=F32)
    attended = (weighted / total.T[:, :, None]).reshape(mine, col_count).astype(BF16)
    attended = lax.all_gather(attended, "sub", axis=0, tiled=True)
    term = jnp.dot(attended, out_weight, preferred_element_type=F32).astype(BF16)
    return lax.psum_scatter(term, "head", scatter_dimension=0, tiled=True)


def solution(mesh):
    in_specs = (
        P(("groups", "seq"), "head"),
        P(("groups", "seq", "sub"), "head"),
        P(("groups", "seq", "sub"), "head"),
        P(("groups", "seq", "sub"), None, "head"),
        P(("groups", "seq", "sub"), None, "head"),
        P("groups", None),
        P("groups"),
        P("head", "sub"),
    )
    out_specs = P(("groups", "seq", "head"), "sub")

    def apply(queries, *rest):
        heads = queries.shape[1] // mesh.shape["head"] // HD
        paired = mesh.shape["head"] == 2 and mesh.shape["sub"] == 2 and heads % 2 == 0
        body = local if paired else local_any
        return jax.shard_map(body, mesh=mesh, in_specs=in_specs, out_specs=out_specs, check_vma=False)(queries, *rest)

    return apply
```

```python
import functools
import math

import jax
import jax.numpy as jnp
from jax import lax
from jax.experimental import pallas as pl
from jax.experimental.pallas import tpu as pltpu
from jax.sharding import PartitionSpec as P

HD = 128
FT = 64
FR_DEV = 16
F32 = jnp.float32
BF16 = jnp.bfloat16
EXP2_SCALE = math.log2(math.e) / math.sqrt(HD)
MASKED = -1e30
VMEM_LIMIT = 24 * 1024 * 1024
SWAP = [(0, 1), (1, 0)]
SHORT = pl.CostEstimate(flops=1024, bytes_accessed=1024, transcendentals=0)
ANY = pl.BlockSpec(memory_space=pl.ANY)
HBM = pl.BlockSpec(memory_space=pltpu.HBM)
VMEM = pl.BlockSpec(memory_space=pltpu.VMEM)


def params():
    return pltpu.CompilerParams(vmem_limit_bytes=VMEM_LIMIT)


def in_hbm(array):
    return pltpu.with_memory_space_constraint(array, pltpu.HBM)


def in_vmem(array):
    return pltpu.with_memory_space_constraint(array, pltpu.VMEM)


def copy_all(pairs, sems):
    copies = [pltpu.make_async_copy(*pair, sems.at[index]) for index, pair in enumerate(pairs)]
    for copy in copies:
        copy.start()
    for copy in copies:
        copy.wait()


def pack_kernel(seq_count, low, parts, ids, keys, values, weight, *rest):
    outs, columns_out, sems = rest[:-2], rest[-2], rest[-1]
    seq_index = lax.axis_index("seq")
    sub_index = lax.axis_index("sub")
    base = (seq_index * 2 + sub_index) * FR_DEV
    width = outs[0].shape[1]
    block = columns_out.shape[1]
    first = pl.multiple_of(low + lax.axis_index("groups") * block, 128)
    pairs = []
    for shift, out in enumerate(outs):
        target = lax.rem(seq_index + shift, seq_count)
        wanted = jnp.int32(0)
        for entry in range(2 * seq_count):
            slot = ids[target, entry] - base
            wanted = jnp.where((slot >= 0) & (slot < FR_DEV), slot, wanted)
        for turn in range(2):
            half = sub_index if turn == 0 else 1 - sub_index
            columns = pl.ds(pl.multiple_of(half * width, 128), width)
            for part, source in enumerate((keys, values)):
                pairs.append((source.at[wanted, :, columns], out.at[pl.ds((2 * turn + part) * FT, FT), :]))
    rows = weight.shape[0] // parts
    for part in range(parts):
        span = pl.ds(part * rows, rows)
        pairs.append((weight.at[span, pl.ds(first, block)], columns_out.at[span, :]))
    copy_all(pairs, sems)


def pack(frame_ids, mem_keys, mem_values, weight, low, block, seq_count):
    parts = 4
    width = mem_keys.shape[2] // 2
    shapes = [(4 * FT, width)] * seq_count + [(weight.shape[0], block)]
    return pl.pallas_call(
        functools.partial(pack_kernel, seq_count, low, parts),
        out_shape=[pltpu.VMEM(shape, BF16) for shape in shapes],
        in_specs=[pl.BlockSpec(memory_space=pltpu.SMEM)] + [HBM] * 3,
        out_specs=[VMEM] * len(shapes),
        scratch_shapes=[pltpu.SemaphoreType.DMA((4 * seq_count + parts,))],
        compiler_params=params(),
        name="pack",
        cost_estimate=pl.CostEstimate(flops=0, bytes_accessed=12 * 2**20, transcendentals=0),
    )(frame_ids, in_hbm(mem_keys), in_hbm(mem_values), in_hbm(weight))


def pack_sibling_kernel(keys, values, frame, out, sems):
    count, width = keys.shape[0], out.shape[1]
    columns = pl.ds(pl.multiple_of((1 - lax.axis_index("sub")) * width, 128), width)
    copy_all(
        [
            (keys.at[:, columns], out.at[pl.ds(0, count), :]),
            (values.at[:, columns], out.at[pl.ds(count, count), :]),
            (frame.at[pl.ds(2 * FT, 2 * FT), :], out.at[pl.ds(2 * count, 2 * FT), :]),
        ],
        sems,
    )


def pack_sibling(cur_keys, cur_values, frame):
    count, width = cur_keys.shape[0], cur_keys.shape[1] // 2
    return pl.pallas_call(
        pack_sibling_kernel,
        out_shape=pltpu.VMEM((2 * count + 2 * FT, width), BF16),
        in_specs=[HBM, HBM, VMEM],
        out_specs=VMEM,
        scratch_shapes=[pltpu.SemaphoreType.DMA((3,))],
        compiler_params=params(),
        name="pack_sibling",
        cost_estimate=pl.CostEstimate(flops=0, bytes_accessed=8 * count * width, transcendentals=0),
    )(in_hbm(cur_keys), in_hbm(cur_values), in_vmem(frame))


def pass_on_kernel(*refs):
    arrays, out, sems = refs[:-3], refs[-2], refs[-1]
    rows = out.shape[0] // len(arrays)
    copy_all(
        [(array.at[pl.ds(rows, rows), :], out.at[pl.ds(index * rows, rows), :]) for index, array in enumerate(arrays)],
        sems,
    )


def pass_on(arrays, after):
    rows, width = arrays[0].shape
    return pl.pallas_call(
        pass_on_kernel,
        out_shape=pltpu.VMEM((len(arrays) * rows // 2, width), BF16),
        in_specs=[VMEM] * len(arrays) + [ANY],
        out_specs=VMEM,
        scratch_shapes=[pltpu.SemaphoreType.DMA((len(arrays),))],
        compiler_params=params(),
        name="pass_on",
        cost_estimate=SHORT,
    )(*map(in_vmem, arrays), in_vmem(after))


def load_kernel(parts, weight, after, out, sems):
    rows = weight.shape[0] // parts
    spans = [pl.ds(part * rows, rows) for part in range(parts)]
    copy_all([(weight.at[span, :], out.at[span, :]) for span in spans], sems)


def load(weight, after):
    parts = 4
    return pl.pallas_call(
        functools.partial(load_kernel, parts),
        out_shape=pltpu.VMEM(weight.shape, BF16),
        in_specs=[HBM, ANY],
        out_specs=VMEM,
        scratch_shapes=[pltpu.SemaphoreType.DMA((parts,))],
        compiler_params=params(),
        name="load",
        cost_estimate=pl.CostEstimate(flops=0, bytes_accessed=2 * weight.size, transcendentals=0),
    )(in_hbm(weight), in_vmem(after))


def gate(array, after):
    return pl.pallas_call(
        lambda *refs: None,
        in_specs=[ANY, ANY],
        out_specs=ANY,
        out_shape=jax.ShapeDtypeStruct(array.shape, array.dtype),
        input_output_aliases={0: 0},
        compiler_params=params(),
        name="gate",
        cost_estimate=SHORT,
    )(in_vmem(array), in_vmem(after))


def dot_t(left, right):
    return lax.dot_general(left, right, (((1,), (1,)), ((), ())), preferred_element_type=F32)


def wide(column, count):
    return jnp.concatenate([column] * count, axis=1)


def with_ones(values):
    return jnp.concatenate([values, jnp.ones_like(values)], axis=1)


def current_kernel(step, place, q, own_k, own_v, sib_k, sib_v, out, lse, q_out):
    keys = jnp.concatenate([own_k[...], sib_k[...]], axis=0)
    values = with_ones(jnp.concatenate([own_v[...], sib_v[...]], axis=0))
    q_out[...] = q[...]
    for low in range(0, q.shape[0], step):
        rows = pl.ds(low, step)
        scores = dot_t(q[rows, :], keys)
        row_max = jnp.broadcast_to(jnp.max(scores, axis=1, keepdims=True), (step, HD))
        weights = jnp.exp2((scores - wide(row_max, keys.shape[0] // HD)) * EXP2_SCALE).astype(BF16)
        product = jnp.dot(weights, values, preferred_element_type=F32)
        total = product[:, HD:]
        out[0, rows, :] = product[:, :HD] / total
        lse[0, rows, :] = row_max * EXP2_SCALE + jnp.log2(total)


def attend_current(queries, cur_keys, cur_values, sibling, heads):
    rows = queries.shape[0]
    keys = cur_keys.shape[0]
    place = lax.axis_index("sub").astype(jnp.int32).reshape(1)
    own = lambda j, place: (0, place[0] * heads + j)
    return pl.pallas_call(
        functools.partial(current_kernel, 512),
        grid_spec=pltpu.PrefetchScalarGridSpec(
            num_scalar_prefetch=1,
            grid=(heads,),
            in_specs=[
                pl.BlockSpec((rows, HD), own),
                pl.BlockSpec((keys, HD), own),
                pl.BlockSpec((keys, HD), own),
                pl.BlockSpec((keys, HD), lambda j, place: (0, j)),
                pl.BlockSpec((keys, HD), lambda j, place: (1, j)),
            ],
            out_specs=[pl.BlockSpec((1, rows, HD), lambda j, place: (j, 0, 0))] * 2
            + [pl.BlockSpec((rows, HD), lambda j, place: (0, j))],
        ),
        out_shape=[pltpu.VMEM((heads, rows, HD), F32)] * 2 + [pltpu.VMEM((rows, heads * HD), BF16)],
        compiler_params=params(),
        name="attend_current",
        cost_estimate=pl.CostEstimate(
            flops=6 * heads * rows * 2 * keys * HD, bytes_accessed=heads * rows * HD * 12, transcendentals=heads * rows * 2 * keys
        ),
    )(place, in_hbm(queries), in_hbm(cur_keys), in_hbm(cur_values), in_vmem(sibling), in_vmem(sibling))


def frames_kernel(heads, far, starts, bias, q, held, lse, *rest):
    frames = rest[: len(starts)]
    out, *parts = rest[-3:] if far else rest[-1:]
    count, rows = len(starts), out.shape[0]
    head_index = lax.axis_index("head")
    half = 1 - head_index if far else head_index
    span = pl.ds(pl.multiple_of(half * rows, rows), rows)
    mask = bias[...]

    def gathered(head, part):
        columns = pl.ds(head * HD, HD)
        return jnp.concatenate(
            [frame[pl.ds(start + part * FT, FT), columns] for frame, start in zip(frames, starts)], axis=0
        )

    def scores_of(head):
        return dot_t(q[span, pl.ds(head * HD, HD)], gathered(head, 0))

    def finish(head, scores):
        scores = scores * EXP2_SCALE + mask
        old = lse[head, span, :]
        new_max = jnp.maximum(old, jnp.max(scores, axis=1, keepdims=True))
        weights = jnp.exp2(scores - wide(new_max, count * FT // HD)).astype(BF16)
        product = jnp.dot(weights, with_ones(gathered(head, 1)), preferred_element_type=F32)
        scale = jnp.exp2(old - new_max)
        top = held[head, span, :] * scale + product[:, :HD]
        done = (top / (scale + product[:, HD:])).astype(BF16)
        out[:, pl.ds(head * HD, HD)] = done
        column = head * HD
        for part in parts:
            if 0 <= column < part.shape[1]:
                part[:, pl.ds(column, HD)] = done
            column -= part.shape[1]

    scores = scores_of(0)
    for head in range(heads):
        following = scores_of(head + 1) if head + 1 < heads else None
        finish(head, scores)
        scores = following


def attend_frames(far, bias, q, held, lse, frames, starts, after=()):
    heads, rows, _ = held.shape
    operands = [bias, q, held, lse, *frames]
    counts = [heads, heads - heads // 2, heads // 2] if far else [heads]
    outs = pl.pallas_call(
        functools.partial(frames_kernel, heads, far, tuple(starts)),
        in_specs=[VMEM] * len(operands) + [ANY] * len(after),
        out_specs=[VMEM] * len(counts),
        out_shape=[pltpu.VMEM((rows // 2, count * HD), BF16) for count in counts],
        compiler_params=params(),
        name="attend_far" if far else "attend_near",
        cost_estimate=SHORT,
    )(*map(in_vmem, operands), *map(in_vmem, after))
    return outs if far else outs[0]


def join_kernel(first, second, after, out):
    out[:, pl.ds(0, first.shape[1])] = first[...]
    out[:, pl.ds(first.shape[1], second.shape[1])] = second[...]


def join(first, second, after):
    return pl.pallas_call(
        join_kernel,
        in_specs=[VMEM, VMEM, ANY],
        out_specs=VMEM,
        out_shape=pltpu.VMEM((first.shape[0], first.shape[1] + second.shape[1]), BF16),
        compiler_params=params(),
        name="join",
        cost_estimate=SHORT,
    )(*map(in_vmem, (first, second, after)))


def both(mine, other):
    first, second = mine[...], other[...]
    return jnp.where(
        lax.axis_index("sub") == 0,
        jnp.concatenate([first, second], axis=1),
        jnp.concatenate([second, first], axis=1),
    )


def project_kernel(passed, low, step, mine, other, weight, *rest):
    out = rest[-1 - passed]
    rows = both(mine, other)

    def block(start):
        columns = weight[:, pl.ds(low + start, step)]
        out[:, pl.ds(start, step)] = jnp.dot(rows, columns, preferred_element_type=F32).astype(BF16)

    if out.shape[1] == step:
        block(0)
    else:
        pl.loop(0, out.shape[1] // step)(lambda index: block(pl.multiple_of(index * step, step)))


def project(mine, other, weight, low, width, step, after=(), passed=()):
    outs = pl.pallas_call(
        functools.partial(project_kernel, len(passed), low, step),
        in_specs=[VMEM] * 3 + [ANY] * (len(after) + len(passed)),
        out_specs=[VMEM] + [ANY] * len(passed),
        out_shape=[pltpu.VMEM((mine.shape[0], width), BF16)]
        + [jax.ShapeDtypeStruct(array.shape, array.dtype) for array in passed],
        input_output_aliases={3 + len(after) + index: 1 + index for index in range(len(passed))},
        compiler_params=params(),
        name="project",
        cost_estimate=SHORT,
    )(*map(in_vmem, (mine, other, weight, *after, *passed)))
    return outs if passed else outs[0]


def write_block(block, out, low, scratch, sem):
    scratch[...] = block.astype(BF16)
    copy = pltpu.make_async_copy(scratch, out.at[:, pl.ds(low, scratch.shape[1])], sem)
    copy.start()
    copy.wait()


def remote_kernel(first, second, terms, mine, other, weight, total, out, scratch, sem):
    block = weight.shape[1]
    turn = lax.axis_index("groups")
    low = pl.multiple_of(first + (1 - turn if second else turn) * block, 128)
    product = jnp.dot(both(mine, other), weight[...], preferred_element_type=F32)
    write_block(terms[:, pl.ds(low, block)].astype(F32) + product, out, low, scratch, sem)


def add_kernel(low, terms, came, total, out, scratch, sem):
    block = terms[:, pl.ds(low, came.shape[1])].astype(F32) + came[...].astype(F32)
    write_block(block, out, low, scratch, sem)


def finish_block(kernel, name, operands, total, rows, width, block):
    count = len(operands)
    if total is None:
        body = lambda *refs: kernel(*refs[:count], None, *refs[count:])
        totals, aliases = [], {}
    else:
        body, totals, aliases = kernel, [in_hbm(total)], {count: 0}
    return pl.pallas_call(
        body,
        in_specs=[VMEM] * count + [HBM] * len(totals),
        out_specs=HBM,
        out_shape=pltpu.HBM((rows, width), BF16),
        input_output_aliases=aliases,
        scratch_shapes=[pltpu.VMEM((rows, block), BF16), pltpu.SemaphoreType.DMA],
        compiler_params=params(),
        name=name,
        cost_estimate=SHORT,
    )(*map(in_vmem, operands), *totals)


def add_remote(terms, mine, other, weight, first, second, total):
    kernel = functools.partial(remote_kernel, first, second)
    return finish_block(kernel, "add_remote", (terms, mine, other, weight), total, *terms.shape, weight.shape[1])


def add_block(terms, came, low, total):
    kernel = functools.partial(add_kernel, low)
    return finish_block(kernel, "add_block", (terms, came), total, *terms.shape, came.shape[1])


def frame_bias(frame_ids, frame_counts, owners):
    own_list = lax.dynamic_index_in_dim(frame_ids, lax.axis_index("seq"), 0, keepdims=False)
    hit = (own_list // FR_DEV)[None, :] == owners[:, None]
    got_ids = jnp.sum(jnp.where(hit, own_list[None, :], 0), axis=1)
    every = jnp.arange(frame_counts.shape[0], dtype=jnp.int32)
    counts = jnp.sum(jnp.where(got_ids[:, None] == every[None, :], frame_counts[None, :], 0), axis=1)
    live = jnp.arange(FT, dtype=jnp.int32)[None, :] < counts[:, None]
    return jnp.where(live, 0.0, MASKED).astype(F32).reshape(1, -1)


def pieces(width):
    found, start = [], 0
    while start < width:
        block = 512 if width - start >= 512 else 256 if width - start >= 256 else 128
        found.append((start, block))
        start += block
    return found


def local(queries, cur_keys, cur_values, mem_keys, mem_values, frame_ids, frame_counts, out_weight):
    seq_count = lax.axis_size("seq")
    seq_index = lax.axis_index("seq")
    sub_index = lax.axis_index("sub")
    heads = queries.shape[1] // HD // 2
    keys = cur_keys.shape[0]
    out_cols = out_weight.shape[1]
    low = out_cols // 2
    share = (out_cols - low) // lax.axis_size("groups")

    *sends, columns = pack(frame_ids, mem_keys, mem_values, out_weight, low, share, seq_count)
    columns = lax.ppermute(columns, "head", SWAP)
    mine = [sends[0]]
    for shift in range(1, seq_count):
        pairs = [(index, (index + shift) % seq_count) for index in range(seq_count)]
        mine.append(lax.ppermute(sends[shift], "seq", pairs))
    sibling = lax.ppermute(pack_sibling(cur_keys, cur_values, sends[0]), "sub", SWAP)

    sources = (seq_index - jnp.arange(seq_count, dtype=jnp.int32)) % seq_count * 2
    bias = frame_bias(frame_ids, frame_counts, jnp.concatenate([sources + sub_index, sources + 1 - sub_index]))

    held, lse, q = attend_current(queries, cur_keys, cur_values, sibling, heads)
    weight = load(out_weight, lse)
    theirs = lax.ppermute(pass_on(mine[1:], weight), "sub", SWAP)
    frames = [*mine, sibling] + [theirs] * (seq_count - 1)
    starts = [0] * seq_count + [2 * keys] + [2 * FT * index for index in range(seq_count - 1)]

    far, *parts = attend_frames(True, bias, q, held, lse, frames, starts)
    parts = [lax.ppermute(part, "head", SWAP) for part in parts]
    far_sibling = lax.ppermute(far, "sub", SWAP)
    columns = gate(columns, far)
    other_columns = lax.ppermute(columns, "groups", SWAP)
    near = attend_frames(False, bias, q, held, lse, frames, starts, (far,))
    near_sibling = lax.ppermute(near, "sub", SWAP)

    came, after, passed = [], (near,), (parts[0],)
    for start, block in pieces(low):
        term = project(far, far_sibling, weight, start, block, block, after, passed)
        if passed:
            term, first = term
        came.append((start, lax.ppermute(term, "head", SWAP)))
        after, passed = (term,), ()
    came_mine = join(first, parts[1], term)
    came_other = lax.ppermute(came_mine, "sub", SWAP)
    terms = project(near, near_sibling, weight, 0, out_cols, 512, (came_mine,))

    total = add_remote(terms, came_mine, came_other, columns, low, False, None)
    for start, piece in came[:-1]:
        total = add_block(terms, piece, start, total)
    total = add_remote(terms, came_mine, came_other, other_columns, low, True, total)
    start, piece = came[-1]
    return add_block(terms, piece, start, total)


def local_any(queries, cur_keys, cur_values, mem_keys, mem_values, frame_ids, frame_counts, out_weight):
    seq_count = lax.axis_size("seq")
    sub_count = lax.axis_size("sub")
    seq_index = lax.axis_index("seq")
    owner_self = seq_index * sub_count + lax.axis_index("sub")
    row_count, col_count = queries.shape
    heads = col_count // HD
    mine = row_count // sub_count
    wanted = jnp.sum(jnp.where(frame_ids // FR_DEV == owner_self, frame_ids, 0), axis=1) - owner_self * FR_DEV
    own_list = lax.dynamic_index_in_dim(frame_ids, seq_index, 0, keepdims=False)
    owners = jnp.arange(seq_count * sub_count, dtype=jnp.int32)
    hit = (own_list // FR_DEV)[None, :] == owners[:, None]
    got_ids = jnp.sum(jnp.where(hit, own_list[None, :], 0), axis=1).reshape(seq_count, sub_count).T.reshape(-1)
    live = jnp.arange(FT, dtype=jnp.int32)[None, :] < jnp.take(frame_counts, got_ids)[:, None]

    def spread(cached, current):
        sent = lax.all_to_all(jnp.take(cached, wanted, axis=0), "seq", split_axis=0, concat_axis=0, tiled=True)
        far = lax.all_gather(sent, "sub").reshape(-1, heads, HD)
        return jnp.concatenate([lax.all_gather(current, "sub").reshape(-1, heads, HD), far], axis=0)

    keys, values = spread(mem_keys, cur_keys), spread(mem_values, cur_values)
    key_live = jnp.concatenate([jnp.ones((keys.shape[0] - live.size,), bool), live.reshape(-1)])
    start = lax.axis_index("sub") * mine
    query_heads = lax.dynamic_slice_in_dim(queries, start, mine, 0).reshape(mine, heads, HD)
    scores = jnp.einsum("qhd,khd->hqk", query_heads, keys, preferred_element_type=F32) / math.sqrt(HD)
    scores = jnp.where(key_live[None, None, :], scores, -jnp.inf)
    expo = jnp.exp(scores - jnp.max(scores, axis=-1, keepdims=True))
    total = jnp.sum(expo, axis=-1)
    weighted = jnp.einsum("hqk,khd->qhd", expo.astype(BF16), values, preferred_element_type=F32)
    attended = (weighted / total.T[:, :, None]).reshape(mine, col_count).astype(BF16)
    attended = lax.all_gather(attended, "sub", axis=0, tiled=True)
    term = jnp.dot(attended, out_weight, preferred_element_type=F32).astype(BF16)
    return lax.psum_scatter(term, "head", scatter_dimension=0, tiled=True)


def solution(mesh):
    in_specs = (
        P(("groups", "seq"), "head"),
        P(("groups", "seq", "sub"), "head"),
        P(("groups", "seq", "sub"), "head"),
        P(("groups", "seq", "sub"), None, "head"),
        P(("groups", "seq", "sub"), None, "head"),
        P("groups", None),
        P("groups"),
        P("head", "sub"),
    )
    out_specs = P(("groups", "seq", "head"), "sub")

    def apply(queries, *rest):
        heads = queries.shape[1] // mesh.shape["head"] // HD
        paired = mesh.shape["head"] == 2 and mesh.shape["sub"] == 2 and heads % 2 == 0
        body = local if paired else local_any
        return jax.shard_map(body, mesh=mesh, in_specs=in_specs, out_specs=out_specs, check_vma=False)(queries, *rest)

    return apply
```

```python
import functools
import math

import jax
import jax.numpy as jnp
from jax import lax
from jax.experimental import pallas as pl
from jax.experimental.pallas import tpu as pltpu
from jax.sharding import PartitionSpec as P

HD = 128
FT = 64
FR_DEV = 16
F32 = jnp.float32
BF16 = jnp.bfloat16
EXP2_SCALE = math.log2(math.e) / math.sqrt(HD)
MASKED = -1e30
VMEM_LIMIT = 24 * 1024 * 1024
SWAP = [(0, 1), (1, 0)]
SHORT = pl.CostEstimate(flops=1024, bytes_accessed=1024, transcendentals=0)
ANY = pl.BlockSpec(memory_space=pl.ANY)
HBM = pl.BlockSpec(memory_space=pltpu.HBM)
VMEM = pl.BlockSpec(memory_space=pltpu.VMEM)


def params():
    return pltpu.CompilerParams(vmem_limit_bytes=VMEM_LIMIT)


def in_hbm(array):
    return pltpu.with_memory_space_constraint(array, pltpu.HBM)


def in_vmem(array):
    return pltpu.with_memory_space_constraint(array, pltpu.VMEM)


def copy_all(pairs, sems):
    copies = [pltpu.make_async_copy(*pair, sems.at[index]) for index, pair in enumerate(pairs)]
    for copy in copies:
        copy.start()
    for copy in copies:
        copy.wait()


def pack_kernel(seq_count, low, parts, ids, counts, keys, values, cur_keys, cur_values, weight, *rest):
    outs = rest[:seq_count]
    sibling, columns_out, mask, sems = rest[seq_count:]
    seq_index = lax.axis_index("seq")
    sub_index = lax.axis_index("sub")
    width = sibling.shape[1]
    block = columns_out.shape[1]
    count = cur_keys.shape[0]
    frame_count = 2 * seq_count

    def columns_of(half):
        return pl.ds(pl.multiple_of(half * width, 128), width)

    def held_by(stretch, owner):
        found = jnp.int32(0)
        for entry in range(frame_count):
            frame = ids[stretch, entry]
            slot = frame - owner * FR_DEV
            found = jnp.where((slot >= 0) & (slot < FR_DEV), frame, found)
        return found

    pairs = []
    for shift, out in enumerate(outs):
        owner = seq_index * 2 + sub_index
        wanted = held_by(lax.rem(seq_index + shift, seq_count), owner) - owner * FR_DEV
        for turn in range(2):
            half = sub_index if turn == 0 else 1 - sub_index
            for part, source in enumerate((keys, values)):
                if shift == 0 and turn == 1:
                    target = sibling.at[pl.ds(2 * count + part * FT, FT), :]
                else:
                    target = out.at[pl.ds((2 * turn + part) * FT, FT), :]
                pairs.append((source.at[wanted, :, columns_of(half)], target))
    for part, source in enumerate((cur_keys, cur_values)):
        pairs.append((source.at[:, columns_of(1 - sub_index)], sibling.at[pl.ds(part * count, count), :]))
    first = pl.multiple_of(low + lax.axis_index("groups") * block, 128)
    rows = weight.shape[0] // parts
    for part in range(parts):
        span = pl.ds(part * rows, rows)
        pairs.append((weight.at[span, pl.ds(first, block)], columns_out.at[span, :]))
    copies = [pltpu.make_async_copy(*pair, sems.at[index]) for index, pair in enumerate(pairs)]
    for copy in copies:
        copy.start()
    slot = lax.broadcasted_iota(jnp.int32, (1, FT), 1)
    for index in range(frame_count):
        turn, shift = divmod(index, seq_count)
        source = lax.rem(seq_index + seq_count - shift, seq_count) * 2
        owner = source + (sub_index if turn == 0 else 1 - sub_index)
        live = slot < counts[held_by(seq_index, owner)]
        mask[pl.ds(index, 1), :] = jnp.where(live, 0.0, MASKED).astype(F32)
    for copy in copies:
        copy.wait()


def pack(frame_ids, frame_counts, mem_keys, mem_values, cur_keys, cur_values, weight, low, block, seq_count):
    parts = 4
    width = mem_keys.shape[2] // 2
    rows = [2 * FT] + [4 * FT] * (seq_count - 1) + [2 * cur_keys.shape[0] + 2 * FT]
    shapes = [(count, width) for count in rows] + [(weight.shape[0], block)]
    return pl.pallas_call(
        functools.partial(pack_kernel, seq_count, low, parts),
        out_shape=[pltpu.VMEM(shape, BF16) for shape in shapes] + [pltpu.VMEM((2 * seq_count, FT), F32)],
        in_specs=[pl.BlockSpec(memory_space=pltpu.SMEM)] * 2 + [HBM] * 5,
        out_specs=[VMEM] * (len(shapes) + 1),
        scratch_shapes=[pltpu.SemaphoreType.DMA((4 * seq_count + 2 + parts,))],
        compiler_params=params(),
        name="pack",
        cost_estimate=pl.CostEstimate(flops=0, bytes_accessed=12 * 2**20, transcendentals=0),
    )(*map(in_hbm, (frame_ids, frame_counts, mem_keys, mem_values, cur_keys, cur_values, weight)))


def pass_on_kernel(*refs):
    arrays, out = refs[:-2], refs[-1]
    rows = out.shape[0] // len(arrays)
    for index, array in enumerate(arrays):
        out[pl.ds(index * rows, rows), :] = array[pl.ds(rows, rows), :]


def pass_on(arrays, after):
    rows, width = arrays[0].shape
    return pl.pallas_call(
        pass_on_kernel,
        out_shape=pltpu.VMEM((len(arrays) * rows // 2, width), BF16),
        in_specs=[VMEM] * len(arrays) + [ANY],
        out_specs=VMEM,
        compiler_params=params(),
        name="pass_on",
        cost_estimate=SHORT,
    )(*map(in_vmem, arrays), in_vmem(after))


def load_kernel(parts, weight, after, out, sems):
    rows = weight.shape[0] // parts
    spans = [pl.ds(part * rows, rows) for part in range(parts)]
    copy_all([(weight.at[span, :], out.at[span, :]) for span in spans], sems)


def load(weight, after):
    parts = 4
    return pl.pallas_call(
        functools.partial(load_kernel, parts),
        out_shape=pltpu.VMEM(weight.shape, BF16),
        in_specs=[HBM, ANY],
        out_specs=VMEM,
        scratch_shapes=[pltpu.SemaphoreType.DMA((parts,))],
        compiler_params=params(),
        name="load",
        cost_estimate=pl.CostEstimate(flops=0, bytes_accessed=2 * weight.size, transcendentals=0),
    )(in_hbm(weight), in_vmem(after))


def gate(array, after):
    return pl.pallas_call(
        lambda *refs: None,
        in_specs=[ANY, ANY],
        out_specs=ANY,
        out_shape=jax.ShapeDtypeStruct(array.shape, array.dtype),
        input_output_aliases={0: 0},
        compiler_params=params(),
        name="gate",
        cost_estimate=SHORT,
    )(in_vmem(array), in_vmem(after))


def dot_t(left, right):
    return lax.dot_general(left, right, (((1,), (1,)), ((), ())), preferred_element_type=F32)


def wide(column, count):
    return jnp.concatenate([column] * count, axis=1)


def with_ones(values):
    return jnp.concatenate([values, jnp.ones_like(values)], axis=1)


def current_kernel(step, queries, own_keys, own_values, sibling, out, lse, q, own_k, own_v, sems):
    heads, rows, _ = out.shape
    count = own_k.shape[0]
    half = pl.ds(pl.multiple_of(lax.axis_index("sub") * q.shape[1], 128), q.shape[1])
    copy_all(
        [(queries.at[:, half], q), (own_keys.at[:, half], own_k), (own_values.at[:, half], own_v)],
        sems,
    )

    @pl.loop(0, heads)
    def _(head):
        columns = pl.ds(pl.multiple_of(head * HD, HD), HD)
        keys = jnp.concatenate([own_k[:, columns], sibling[pl.ds(0, count), columns]], axis=0)
        values = with_ones(jnp.concatenate([own_v[:, columns], sibling[pl.ds(count, count), columns]], axis=0))
        for low in range(0, rows, step):
            span = pl.ds(low, step)
            scores = dot_t(q[span, columns], keys)
            row_max = jnp.broadcast_to(jnp.max(scores, axis=1, keepdims=True), (step, HD))
            weights = jnp.exp2((scores - wide(row_max, 2 * count // HD)) * EXP2_SCALE).astype(BF16)
            product = jnp.dot(weights, values, preferred_element_type=F32)
            total = product[:, HD:]
            out[head, span, :] = product[:, :HD] / total
            lse[head, span, :] = row_max * EXP2_SCALE + jnp.log2(total)


def attend_current(queries, cur_keys, cur_values, sibling, heads):
    rows = queries.shape[0]
    keys = cur_keys.shape[0]
    return pl.pallas_call(
        functools.partial(current_kernel, 512),
        in_specs=[HBM] * 3 + [VMEM],
        out_specs=[VMEM] * 3,
        out_shape=[pltpu.VMEM((heads, rows, HD), F32)] * 2 + [pltpu.VMEM((rows, heads * HD), BF16)],
        scratch_shapes=[pltpu.VMEM((keys, heads * HD), BF16)] * 2 + [pltpu.SemaphoreType.DMA((3,))],
        compiler_params=params(),
        name="attend_current",
        cost_estimate=pl.CostEstimate(
            flops=6 * heads * rows * 2 * keys * HD, bytes_accessed=heads * rows * HD * 12, transcendentals=heads * rows * 2 * keys
        ),
    )(in_hbm(queries), in_hbm(cur_keys), in_hbm(cur_values), in_vmem(sibling))


def frames_kernel(heads, far, starts, bias, q, held, lse, *rest):
    frames = rest[: len(starts)]
    out, *parts = rest[-3:] if far else rest[-1:]
    count, rows = len(starts), out.shape[0]
    head_index = lax.axis_index("head")
    half = 1 - head_index if far else head_index
    span = pl.ds(pl.multiple_of(half * rows, rows), rows)
    mask = jnp.concatenate([bias[pl.ds(index, 1), :] for index in range(count)], axis=1)

    def gathered(head, part):
        columns = pl.ds(head * HD, HD)
        return jnp.concatenate(
            [frame[pl.ds(start + part * FT, FT), columns] for frame, start in zip(frames, starts)], axis=0
        )

    def scores_of(head):
        return dot_t(q[span, pl.ds(head * HD, HD)], gathered(head, 0))

    def finish(head, scores):
        scores = scores * EXP2_SCALE + mask
        old = lse[head, span, :]
        new_max = jnp.maximum(old, jnp.max(scores, axis=1, keepdims=True))
        weights = jnp.exp2(scores - wide(new_max, count * FT // HD)).astype(BF16)
        product = jnp.dot(weights, with_ones(gathered(head, 1)), preferred_element_type=F32)
        scale = jnp.exp2(old - new_max)
        top = held[head, span, :] * scale + product[:, :HD]
        done = (top / (scale + product[:, HD:])).astype(BF16)
        out[:, pl.ds(head * HD, HD)] = done
        column = head * HD
        for part in parts:
            if 0 <= column < part.shape[1]:
                part[:, pl.ds(column, HD)] = done
            column -= part.shape[1]

    scores = scores_of(0)
    for head in range(heads):
        following = scores_of(head + 1) if head + 1 < heads else None
        finish(head, scores)
        scores = following


def attend_frames(far, bias, q, held, lse, frames, starts, after=()):
    heads, rows, _ = held.shape
    operands = [bias, q, held, lse, *frames]
    counts = [heads, heads - heads // 2, heads // 2] if far else [heads]
    outs = pl.pallas_call(
        functools.partial(frames_kernel, heads, far, tuple(starts)),
        in_specs=[VMEM] * len(operands) + [ANY] * len(after),
        out_specs=[VMEM] * len(counts),
        out_shape=[pltpu.VMEM((rows // 2, count * HD), BF16) for count in counts],
        compiler_params=params(),
        name="attend_far" if far else "attend_near",
        cost_estimate=SHORT,
    )(*map(in_vmem, operands), *map(in_vmem, after))
    return outs if far else outs[0]


def join_kernel(first, second, after, out):
    out[:, pl.ds(0, first.shape[1])] = first[...]
    out[:, pl.ds(first.shape[1], second.shape[1])] = second[...]


def join(first, second, after):
    return pl.pallas_call(
        join_kernel,
        in_specs=[VMEM, VMEM, ANY],
        out_specs=VMEM,
        out_shape=pltpu.VMEM((first.shape[0], first.shape[1] + second.shape[1]), BF16),
        compiler_params=params(),
        name="join",
        cost_estimate=SHORT,
    )(*map(in_vmem, (first, second, after)))


def both(mine, other):
    first, second = mine[...], other[...]
    return jnp.where(
        lax.axis_index("sub") == 0,
        jnp.concatenate([first, second], axis=1),
        jnp.concatenate([second, first], axis=1),
    )


def project_kernel(passed, low, step, mine, other, weight, *rest):
    out = rest[-1 - passed]
    rows = both(mine, other)

    def block(start):
        columns = weight[:, pl.ds(low + start, step)]
        out[:, pl.ds(start, step)] = jnp.dot(rows, columns, preferred_element_type=F32).astype(BF16)

    if out.shape[1] == step:
        block(0)
    else:
        pl.loop(0, out.shape[1] // step)(lambda index: block(pl.multiple_of(index * step, step)))


def project(mine, other, weight, low, width, step, after=(), passed=()):
    outs = pl.pallas_call(
        functools.partial(project_kernel, len(passed), low, step),
        in_specs=[VMEM] * 3 + [ANY] * (len(after) + len(passed)),
        out_specs=[VMEM] + [ANY] * len(passed),
        out_shape=[pltpu.VMEM((mine.shape[0], width), BF16)]
        + [jax.ShapeDtypeStruct(array.shape, array.dtype) for array in passed],
        input_output_aliases={3 + len(after) + index: 1 + index for index in range(len(passed))},
        compiler_params=params(),
        name="project",
        cost_estimate=SHORT,
    )(*map(in_vmem, (mine, other, weight, *after, *passed)))
    return outs if passed else outs[0]


def write_block(block, out, low, scratch, sem):
    scratch[...] = block.astype(BF16)
    copy = pltpu.make_async_copy(scratch, out.at[:, pl.ds(low, scratch.shape[1])], sem)
    copy.start()
    copy.wait()


def remote_kernel(first, second, terms, mine, other, weight, total, out, scratch, sem):
    block = weight.shape[1]
    turn = lax.axis_index("groups")
    low = pl.multiple_of(first + (1 - turn if second else turn) * block, 128)
    product = jnp.dot(both(mine, other), weight[...], preferred_element_type=F32)
    write_block(terms[:, pl.ds(low, block)].astype(F32) + product, out, low, scratch, sem)


def add_kernel(low, terms, came, total, out, scratch, sem):
    block = terms[:, pl.ds(low, came.shape[1])].astype(F32) + came[...].astype(F32)
    write_block(block, out, low, scratch, sem)


def finish_block(kernel, name, operands, total, rows, width, block):
    count = len(operands)
    if total is None:
        body = lambda *refs: kernel(*refs[:count], None, *refs[count:])
        totals, aliases = [], {}
    else:
        body, totals, aliases = kernel, [in_hbm(total)], {count: 0}
    return pl.pallas_call(
        body,
        in_specs=[VMEM] * count + [HBM] * len(totals),
        out_specs=HBM,
        out_shape=pltpu.HBM((rows, width), BF16),
        input_output_aliases=aliases,
        scratch_shapes=[pltpu.VMEM((rows, block), BF16), pltpu.SemaphoreType.DMA],
        compiler_params=params(),
        name=name,
        cost_estimate=SHORT,
    )(*map(in_vmem, operands), *totals)


def add_remote(terms, mine, other, weight, first, second, total):
    kernel = functools.partial(remote_kernel, first, second)
    return finish_block(kernel, "add_remote", (terms, mine, other, weight), total, *terms.shape, weight.shape[1])


def add_block(terms, came, low, total):
    kernel = functools.partial(add_kernel, low)
    return finish_block(kernel, "add_block", (terms, came), total, *terms.shape, came.shape[1])


def pieces(width):
    found, start = [], 0
    while start < width:
        block = 512 if width - start >= 512 else 256 if width - start >= 256 else 128
        found.append((start, block))
        start += block
    return found


def local(queries, cur_keys, cur_values, mem_keys, mem_values, frame_ids, frame_counts, out_weight):
    seq_count = lax.axis_size("seq")
    heads = queries.shape[1] // HD // 2
    keys = cur_keys.shape[0]
    out_cols = out_weight.shape[1]
    low = out_cols // 2
    share = (out_cols - low) // lax.axis_size("groups")

    *sends, to_sibling, columns, bias = pack(
        frame_ids, frame_counts, mem_keys, mem_values, cur_keys, cur_values, out_weight, low, share, seq_count
    )
    columns = lax.ppermute(columns, "head", SWAP)
    mine = [sends[0]]
    for shift in range(1, seq_count):
        pairs = [(index, (index + shift) % seq_count) for index in range(seq_count)]
        mine.append(lax.ppermute(sends[shift], "seq", pairs))
    sibling = lax.ppermute(to_sibling, "sub", SWAP)

    held, lse, q = attend_current(queries, cur_keys, cur_values, sibling, heads)
    weight = load(out_weight, lse)
    theirs = lax.ppermute(pass_on(mine[1:], weight), "sub", SWAP)
    frames = [*mine, sibling] + [theirs] * (seq_count - 1)
    starts = [0] * seq_count + [2 * keys] + [2 * FT * index for index in range(seq_count - 1)]

    far, *parts = attend_frames(True, bias, q, held, lse, frames, starts)
    parts = [lax.ppermute(part, "head", SWAP) for part in parts]
    far_sibling = lax.ppermute(far, "sub", SWAP)
    near = attend_frames(False, bias, q, held, lse, frames, starts, (far,))
    near_sibling = lax.ppermute(near, "sub", SWAP)
    columns = gate(columns, far)
    other_columns = lax.ppermute(columns, "groups", SWAP)

    came, after, passed = [], (near,), (parts[0],)
    for start, block in pieces(low):
        term = project(far, far_sibling, weight, start, block, block, after, passed)
        if passed:
            term, first = term
        came.append((start, lax.ppermute(term, "head", SWAP)))
        after, passed = (term,), ()
    came_mine = join(first, parts[1], term)
    came_other = lax.ppermute(came_mine, "sub", SWAP)
    terms = project(near, near_sibling, weight, 0, out_cols, 512, (came_mine,))

    total = add_remote(terms, came_mine, came_other, columns, low, False, None)
    for start, piece in came[:-1]:
        total = add_block(terms, piece, start, total)
    total = add_remote(terms, came_mine, came_other, other_columns, low, True, total)
    start, piece = came[-1]
    return add_block(terms, piece, start, total)


def local_any(queries, cur_keys, cur_values, mem_keys, mem_values, frame_ids, frame_counts, out_weight):
    seq_count = lax.axis_size("seq")
    sub_count = lax.axis_size("sub")
    seq_index = lax.axis_index("seq")
    owner_self = seq_index * sub_count + lax.axis_index("sub")
    row_count, col_count = queries.shape
    heads = col_count // HD
    mine = row_count // sub_count
    wanted = jnp.sum(jnp.where(frame_ids // FR_DEV == owner_self, frame_ids, 0), axis=1) - owner_self * FR_DEV
    own_list = lax.dynamic_index_in_dim(frame_ids, seq_index, 0, keepdims=False)
    owners = jnp.arange(seq_count * sub_count, dtype=jnp.int32)
    hit = (own_list // FR_DEV)[None, :] == owners[:, None]
    got_ids = jnp.sum(jnp.where(hit, own_list[None, :], 0), axis=1).reshape(seq_count, sub_count).T.reshape(-1)
    live = jnp.arange(FT, dtype=jnp.int32)[None, :] < jnp.take(frame_counts, got_ids)[:, None]

    def spread(cached, current):
        sent = lax.all_to_all(jnp.take(cached, wanted, axis=0), "seq", split_axis=0, concat_axis=0, tiled=True)
        far = lax.all_gather(sent, "sub").reshape(-1, heads, HD)
        return jnp.concatenate([lax.all_gather(current, "sub").reshape(-1, heads, HD), far], axis=0)

    keys, values = spread(mem_keys, cur_keys), spread(mem_values, cur_values)
    key_live = jnp.concatenate([jnp.ones((keys.shape[0] - live.size,), bool), live.reshape(-1)])
    start = lax.axis_index("sub") * mine
    query_heads = lax.dynamic_slice_in_dim(queries, start, mine, 0).reshape(mine, heads, HD)
    scores = jnp.einsum("qhd,khd->hqk", query_heads, keys, preferred_element_type=F32) / math.sqrt(HD)
    scores = jnp.where(key_live[None, None, :], scores, -jnp.inf)
    expo = jnp.exp(scores - jnp.max(scores, axis=-1, keepdims=True))
    total = jnp.sum(expo, axis=-1)
    weighted = jnp.einsum("hqk,khd->qhd", expo.astype(BF16), values, preferred_element_type=F32)
    attended = (weighted / total.T[:, :, None]).reshape(mine, col_count).astype(BF16)
    attended = lax.all_gather(attended, "sub", axis=0, tiled=True)
    term = jnp.dot(attended, out_weight, preferred_element_type=F32).astype(BF16)
    return lax.psum_scatter(term, "head", scatter_dimension=0, tiled=True)


def solution(mesh):
    in_specs = (
        P(("groups", "seq"), "head"),
        P(("groups", "seq", "sub"), "head"),
        P(("groups", "seq", "sub"), "head"),
        P(("groups", "seq", "sub"), None, "head"),
        P(("groups", "seq", "sub"), None, "head"),
        P("groups", None),
        P("groups"),
        P("head", "sub"),
    )
    out_specs = P(("groups", "seq", "head"), "sub")

    def apply(queries, *rest):
        heads = queries.shape[1] // mesh.shape["head"] // HD
        paired = mesh.shape["head"] == 2 and mesh.shape["sub"] == 2 and heads % 2 == 0
        body = local if paired else local_any
        return jax.shard_map(body, mesh=mesh, in_specs=in_specs, out_specs=out_specs, check_vma=False)(queries, *rest)

    return apply
```

```python
import functools
import math

import jax
import jax.numpy as jnp
from jax import lax
from jax.experimental import pallas as pl
from jax.experimental.pallas import tpu as pltpu
from jax.sharding import PartitionSpec as P

HD = 128
FT = 64
FR_DEV = 16
F32 = jnp.float32
BF16 = jnp.bfloat16
EXP2_SCALE = math.log2(math.e) / math.sqrt(HD)
MASKED = -1e30
VMEM_LIMIT = 24 * 1024 * 1024
SWAP = [(0, 1), (1, 0)]
SHORT = pl.CostEstimate(flops=1024, bytes_accessed=1024, transcendentals=0)
ANY = pl.BlockSpec(memory_space=pl.ANY)
HBM = pl.BlockSpec(memory_space=pltpu.HBM)
VMEM = pl.BlockSpec(memory_space=pltpu.VMEM)


def params():
    return pltpu.CompilerParams(vmem_limit_bytes=VMEM_LIMIT)


def in_hbm(array):
    return pltpu.with_memory_space_constraint(array, pltpu.HBM)


def in_vmem(array):
    return pltpu.with_memory_space_constraint(array, pltpu.VMEM)


def quarter(other_seq, other_group):
    seq_part = lax.rem(lax.axis_index("seq"), 2)
    group = lax.axis_index("groups")
    return 2 * (1 - seq_part if other_seq else seq_part) + (1 - group if other_group else group)


def copy_all(pairs, sems):
    copies = [pltpu.make_async_copy(*pair, sems.at[index]) for index, pair in enumerate(pairs)]
    for copy in copies:
        copy.start()
    for copy in copies:
        copy.wait()


def pack_kernel(seq_count, low, parts, ids, counts, keys, values, cur_keys, cur_values, weight, *rest):
    outs = rest[:seq_count]
    sibling, columns_out, mask, sems = rest[seq_count:]
    seq_index = lax.axis_index("seq")
    sub_index = lax.axis_index("sub")
    width = sibling.shape[1]
    block = columns_out.shape[1]
    count = cur_keys.shape[0]
    frame_count = 2 * seq_count

    def columns_of(half):
        return pl.ds(pl.multiple_of(half * width, 128), width)

    def held_by(stretch, owner):
        found = jnp.int32(0)
        for entry in range(frame_count):
            frame = ids[stretch, entry]
            slot = frame - owner * FR_DEV
            found = jnp.where((slot >= 0) & (slot < FR_DEV), frame, found)
        return found

    pairs = []
    for shift, out in enumerate(outs):
        owner = seq_index * 2 + sub_index
        wanted = held_by(lax.rem(seq_index + shift, seq_count), owner) - owner * FR_DEV
        for turn in range(2):
            half = sub_index if turn == 0 else 1 - sub_index
            for part, source in enumerate((keys, values)):
                if shift == 0 and turn == 1:
                    target = sibling.at[pl.ds(2 * count + part * FT, FT), :]
                else:
                    target = out.at[pl.ds((2 * turn + part) * FT, FT), :]
                pairs.append((source.at[wanted, :, columns_of(half)], target))
    for part, source in enumerate((cur_keys, cur_values)):
        pairs.append((source.at[:, columns_of(1 - sub_index)], sibling.at[pl.ds(part * count, count), :]))
    first = pl.multiple_of(low + quarter(False, False) * block, 128)
    rows = weight.shape[0] // parts
    for part in range(parts):
        span = pl.ds(part * rows, rows)
        pairs.append((weight.at[span, pl.ds(first, block)], columns_out.at[span, :]))
    copies = [pltpu.make_async_copy(*pair, sems.at[index]) for index, pair in enumerate(pairs)]
    for copy in copies:
        copy.start()
    slot = lax.broadcasted_iota(jnp.int32, (1, FT), 1)
    for index in range(frame_count):
        turn, shift = divmod(index, seq_count)
        source = lax.rem(seq_index + seq_count - shift, seq_count) * 2
        owner = source + (sub_index if turn == 0 else 1 - sub_index)
        live = slot < counts[held_by(seq_index, owner)]
        mask[pl.ds(index, 1), :] = jnp.where(live, 0.0, MASKED).astype(F32)
    for copy in copies:
        copy.wait()


def pack(frame_ids, frame_counts, mem_keys, mem_values, cur_keys, cur_values, weight, low, block, seq_count):
    parts = 4
    width = mem_keys.shape[2] // 2
    rows = [2 * FT] + [4 * FT] * (seq_count - 1) + [2 * cur_keys.shape[0] + 2 * FT]
    shapes = [(count, width) for count in rows] + [(weight.shape[0], block)]
    return pl.pallas_call(
        functools.partial(pack_kernel, seq_count, low, parts),
        out_shape=[pltpu.VMEM(shape, BF16) for shape in shapes] + [pltpu.VMEM((2 * seq_count, FT), F32)],
        in_specs=[pl.BlockSpec(memory_space=pltpu.SMEM)] * 2 + [HBM] * 5,
        out_specs=[VMEM] * (len(shapes) + 1),
        scratch_shapes=[pltpu.SemaphoreType.DMA((4 * seq_count + 2 + parts,))],
        compiler_params=params(),
        name="pack",
        cost_estimate=pl.CostEstimate(flops=0, bytes_accessed=12 * 2**20, transcendentals=0),
    )(*map(in_hbm, (frame_ids, frame_counts, mem_keys, mem_values, cur_keys, cur_values, weight)))


def pass_on_kernel(*refs):
    arrays, out = refs[:-2], refs[-1]
    rows = out.shape[0] // len(arrays)
    for index, array in enumerate(arrays):
        out[pl.ds(index * rows, rows), :] = array[pl.ds(rows, rows), :]


def pass_on(arrays, after):
    rows, width = arrays[0].shape
    return pl.pallas_call(
        pass_on_kernel,
        out_shape=pltpu.VMEM((len(arrays) * rows // 2, width), BF16),
        in_specs=[VMEM] * len(arrays) + [ANY],
        out_specs=VMEM,
        compiler_params=params(),
        name="pass_on",
        cost_estimate=SHORT,
    )(*map(in_vmem, arrays), in_vmem(after))


def load_kernel(parts, weight, after, out, sems):
    rows = weight.shape[0] // parts
    spans = [pl.ds(part * rows, rows) for part in range(parts)]
    copy_all([(weight.at[span, :], out.at[span, :]) for span in spans], sems)


def load(weight, after):
    parts = 4
    return pl.pallas_call(
        functools.partial(load_kernel, parts),
        out_shape=pltpu.VMEM(weight.shape, BF16),
        in_specs=[HBM, ANY],
        out_specs=VMEM,
        scratch_shapes=[pltpu.SemaphoreType.DMA((parts,))],
        compiler_params=params(),
        name="load",
        cost_estimate=pl.CostEstimate(flops=0, bytes_accessed=2 * weight.size, transcendentals=0),
    )(in_hbm(weight), in_vmem(after))


def gate(array, after):
    return pl.pallas_call(
        lambda *refs: None,
        in_specs=[ANY, ANY],
        out_specs=ANY,
        out_shape=jax.ShapeDtypeStruct(array.shape, array.dtype),
        input_output_aliases={0: 0},
        compiler_params=params(),
        name="gate",
        cost_estimate=SHORT,
    )(in_vmem(array), in_vmem(after))


def copied_kernel(array, after, out):
    out[...] = array[...]


def copied(array, after):
    return pl.pallas_call(
        copied_kernel,
        in_specs=[VMEM, ANY],
        out_specs=VMEM,
        out_shape=pltpu.VMEM(array.shape, array.dtype),
        compiler_params=params(),
        name="copied",
        cost_estimate=SHORT,
    )(in_vmem(array), in_vmem(after))


def dot_t(left, right):
    return lax.dot_general(left, right, (((1,), (1,)), ((), ())), preferred_element_type=F32)


def wide(column, count):
    return jnp.concatenate([column] * count, axis=1)


def with_ones(values):
    return jnp.concatenate([values, jnp.ones_like(values)], axis=1)


def current_kernel(step, queries, own_keys, own_values, sibling, out, lse, q, own_k, own_v, sems):
    heads, rows, _ = out.shape
    count = own_k.shape[0]
    half = pl.ds(pl.multiple_of(lax.axis_index("sub") * q.shape[1], 128), q.shape[1])
    copy_all(
        [(queries.at[:, half], q), (own_keys.at[:, half], own_k), (own_values.at[:, half], own_v)],
        sems,
    )

    @pl.loop(0, heads)
    def _(head):
        columns = pl.ds(pl.multiple_of(head * HD, HD), HD)
        keys = jnp.concatenate([own_k[:, columns], sibling[pl.ds(0, count), columns]], axis=0)
        values = with_ones(jnp.concatenate([own_v[:, columns], sibling[pl.ds(count, count), columns]], axis=0))
        for low in range(0, rows, step):
            span = pl.ds(low, step)
            scores = dot_t(q[span, columns], keys)
            row_max = jnp.broadcast_to(jnp.max(scores, axis=1, keepdims=True), (step, HD))
            weights = jnp.exp2((scores - wide(row_max, 2 * count // HD)) * EXP2_SCALE).astype(BF16)
            product = jnp.dot(weights, values, preferred_element_type=F32)
            total = product[:, HD:]
            out[head, span, :] = product[:, :HD] / total
            lse[head, span, :] = row_max * EXP2_SCALE + jnp.log2(total)


def attend_current(queries, cur_keys, cur_values, sibling, heads):
    rows = queries.shape[0]
    keys = cur_keys.shape[0]
    return pl.pallas_call(
        functools.partial(current_kernel, 512),
        in_specs=[HBM] * 3 + [VMEM],
        out_specs=[VMEM] * 3,
        out_shape=[pltpu.VMEM((heads, rows, HD), F32)] * 2 + [pltpu.VMEM((rows, heads * HD), BF16)],
        scratch_shapes=[pltpu.VMEM((keys, heads * HD), BF16)] * 2 + [pltpu.SemaphoreType.DMA((3,))],
        compiler_params=params(),
        name="attend_current",
        cost_estimate=pl.CostEstimate(
            flops=6 * heads * rows * 2 * keys * HD, bytes_accessed=heads * rows * HD * 12, transcendentals=heads * rows * 2 * keys
        ),
    )(in_hbm(queries), in_hbm(cur_keys), in_hbm(cur_values), in_vmem(sibling))


def frames_kernel(heads, far, starts, bias, q, held, lse, *rest):
    frames = rest[: len(starts)]
    out = rest[-1]
    count, rows = len(starts), out.shape[0]
    head_index = lax.axis_index("head")
    half = 1 - head_index if far else head_index
    span = pl.ds(pl.multiple_of(half * rows, rows), rows)
    mask = jnp.concatenate([bias[pl.ds(index, 1), :] for index in range(count)], axis=1)

    def gathered(head, part):
        columns = pl.ds(head * HD, HD)
        return jnp.concatenate(
            [frame[pl.ds(start + part * FT, FT), columns] for frame, start in zip(frames, starts)], axis=0
        )

    def scores_of(head):
        return dot_t(q[span, pl.ds(head * HD, HD)], gathered(head, 0))

    def finish(head, scores):
        scores = scores * EXP2_SCALE + mask
        old = lse[head, span, :]
        new_max = jnp.maximum(old, jnp.max(scores, axis=1, keepdims=True))
        weights = jnp.exp2(scores - wide(new_max, count * FT // HD)).astype(BF16)
        product = jnp.dot(weights, with_ones(gathered(head, 1)), preferred_element_type=F32)
        scale = jnp.exp2(old - new_max)
        top = held[head, span, :] * scale + product[:, :HD]
        out[:, pl.ds(head * HD, HD)] = (top / (scale + product[:, HD:])).astype(BF16)

    scores = scores_of(0)
    for head in range(heads):
        following = scores_of(head + 1) if head + 1 < heads else None
        finish(head, scores)
        scores = following


def attend_frames(far, bias, q, held, lse, frames, starts, after=()):
    heads, rows, _ = held.shape
    operands = [bias, q, held, lse, *frames]
    return pl.pallas_call(
        functools.partial(frames_kernel, heads, far, tuple(starts)),
        in_specs=[VMEM] * len(operands) + [ANY] * len(after),
        out_specs=VMEM,
        out_shape=pltpu.VMEM((rows // 2, heads * HD), BF16),
        compiler_params=params(),
        name="attend_far" if far else "attend_near",
        cost_estimate=SHORT,
    )(*map(in_vmem, operands), *map(in_vmem, after))


def both(mine, other):
    first, second = mine[...], other[...]
    return jnp.where(
        lax.axis_index("sub") == 0,
        jnp.concatenate([first, second], axis=1),
        jnp.concatenate([second, first], axis=1),
    )


def project_kernel(step, mine, other, weight, *rest):
    out = rest[-1]
    rows = both(mine, other)

    @pl.loop(0, out.shape[1] // step)
    def _(index):
        columns = pl.ds(pl.multiple_of(index * step, step), step)
        out[:, columns] = jnp.dot(rows, weight[:, columns], preferred_element_type=F32).astype(BF16)


def unshared_kernel(low, mine, other, weight, *rest):
    out = rest[-1]
    rows = both(mine, other)
    share = out.shape[1] - low
    start = pl.multiple_of(low + quarter(True, True) * share, 128)
    for columns, span in ((pl.ds(0, low), pl.ds(0, low)), (pl.ds(start, share), pl.ds(low, share))):
        out[:, span] = jnp.dot(rows, weight[:, columns], preferred_element_type=F32).astype(BF16)


def project_call(kernel, name, mine, other, weight, width, after):
    return pl.pallas_call(
        kernel,
        in_specs=[VMEM] * 3 + [ANY] * len(after),
        out_specs=VMEM,
        out_shape=pltpu.VMEM((mine.shape[0], width), BF16),
        compiler_params=params(),
        name=name,
        cost_estimate=SHORT,
    )(*map(in_vmem, (mine, other, weight, *after)))


def project(mine, other, weight, after):
    return project_call(functools.partial(project_kernel, 512), "project", mine, other, weight, weight.shape[1], after)


def project_unshared(mine, other, weight, low, share, after):
    kernel = functools.partial(unshared_kernel, low)
    return project_call(kernel, "project_unshared", mine, other, weight, low + share, after)


def write_blocks(blocks, out, scratch, sems):
    copies, start = [], 0
    for index, (block, low) in enumerate(blocks):
        span = pl.ds(start, block.shape[1])
        scratch[:, span] = block.astype(BF16)
        copy = pltpu.make_async_copy(scratch.at[:, span], out.at[:, pl.ds(low, block.shape[1])], sems.at[index])
        copy.start()
        copies.append(copy)
        start += block.shape[1]
    for copy in copies:
        copy.wait()


def remote_kernel(first, other_seq, other_group, terms, mine, other, weight, total, out, scratch, sems):
    block = weight.shape[1]
    low = pl.multiple_of(first + quarter(other_seq, other_group) * block, 128)
    product = jnp.dot(both(mine, other), weight[...], preferred_element_type=F32)
    write_blocks([(terms[:, pl.ds(low, block)].astype(F32) + product, low)], out, scratch, sems)


def add_kernel(low, terms, came, total, out, scratch, sems):
    share = came.shape[1] - low
    start = pl.multiple_of(low + quarter(True, True) * share, 128)
    blocks = []
    for columns, span in ((pl.ds(0, low), pl.ds(0, low)), (pl.ds(start, share), pl.ds(low, share))):
        blocks.append((terms[:, columns].astype(F32) + came[:, span].astype(F32), columns.start))
    write_blocks(blocks, out, scratch, sems)


def finish_block(kernel, name, operands, total, rows, width, block):
    count = len(operands)
    if total is None:
        body = lambda *refs: kernel(*refs[:count], None, *refs[count:])
        totals, aliases = [], {}
    else:
        body, totals, aliases = kernel, [in_hbm(total)], {count: 0}
    return pl.pallas_call(
        body,
        in_specs=[VMEM] * count + [HBM] * len(totals),
        out_specs=HBM,
        out_shape=pltpu.HBM((rows, width), BF16),
        input_output_aliases=aliases,
        scratch_shapes=[pltpu.VMEM((rows, block), BF16), pltpu.SemaphoreType.DMA((2,))],
        compiler_params=params(),
        name=name,
        cost_estimate=SHORT,
    )(*map(in_vmem, operands), *totals)


def add_remote(terms, mine, other, weight, first, other_seq, other_group, total):
    kernel = functools.partial(remote_kernel, first, other_seq, other_group)
    return finish_block(kernel, "add_remote", (terms, mine, other, weight), total, *terms.shape, weight.shape[1])


def add_unshared(terms, came, low, total):
    kernel = functools.partial(add_kernel, low)
    return finish_block(kernel, "add_unshared", (terms, came), total, *terms.shape, came.shape[1])


def local(queries, cur_keys, cur_values, mem_keys, mem_values, frame_ids, frame_counts, out_weight):
    seq_count = lax.axis_size("seq")
    heads = queries.shape[1] // HD // 2
    keys = cur_keys.shape[0]
    out_cols = out_weight.shape[1]
    share = out_cols // 5 // 128 * 128
    low = out_cols - 4 * share

    *sends, to_sibling, columns, bias = pack(
        frame_ids, frame_counts, mem_keys, mem_values, cur_keys, cur_values, out_weight, low, share, seq_count
    )
    columns = lax.ppermute(columns, "head", SWAP)
    mine = [sends[0]]
    for shift in range(1, seq_count):
        pairs = [(index, (index + shift) % seq_count) for index in range(seq_count)]
        mine.append(lax.ppermute(sends[shift], "seq", pairs))
    sibling = lax.ppermute(to_sibling, "sub", SWAP)

    held, lse, q = attend_current(queries, cur_keys, cur_values, sibling, heads)
    weight = load(out_weight, lse)
    columns = gate(columns, weight)
    group_columns = lax.ppermute(columns, "groups", SWAP)
    passed = pass_on(mine[1:], columns)
    theirs = lax.ppermute(passed, "sub", SWAP)
    columns_copy = copied(columns, passed)
    seq_columns = lax.ppermute(columns_copy, "seq", [(index, index ^ 1) for index in range(seq_count)])
    frames = [*mine, sibling] + [theirs] * (seq_count - 1)
    starts = [0] * seq_count + [2 * keys] + [2 * FT * index for index in range(seq_count - 1)]

    far = attend_frames(True, bias, q, held, lse, frames, starts, (columns_copy,))
    came_mine = lax.ppermute(far, "head", SWAP)
    far_sibling = lax.ppermute(far, "sub", SWAP)
    near = attend_frames(False, bias, q, held, lse, frames, starts, (far,))
    near_sibling = lax.ppermute(near, "sub", SWAP)

    term = project_unshared(far, far_sibling, weight, low, share, (near,))
    came = lax.ppermute(term, "head", SWAP)
    came_mine = gate(came_mine, term)
    came_other = lax.ppermute(came_mine, "sub", SWAP)
    terms = project(near, near_sibling, weight, (came_mine,))

    arrived = (terms, came_mine, came_other)
    total = add_remote(*arrived, columns, low, False, False, None)
    total = add_remote(*arrived, group_columns, low, False, True, total)
    total = add_remote(*arrived, seq_columns, low, True, False, total)
    return add_unshared(terms, came, low, total)


def local_any(queries, cur_keys, cur_values, mem_keys, mem_values, frame_ids, frame_counts, out_weight):
    seq_count = lax.axis_size("seq")
    sub_count = lax.axis_size("sub")
    seq_index = lax.axis_index("seq")
    owner_self = seq_index * sub_count + lax.axis_index("sub")
    row_count, col_count = queries.shape
    heads = col_count // HD
    mine = row_count // sub_count
    wanted = jnp.sum(jnp.where(frame_ids // FR_DEV == owner_self, frame_ids, 0), axis=1) - owner_self * FR_DEV
    own_list = lax.dynamic_index_in_dim(frame_ids, seq_index, 0, keepdims=False)
    owners = jnp.arange(seq_count * sub_count, dtype=jnp.int32)
    hit = (own_list // FR_DEV)[None, :] == owners[:, None]
    got_ids = jnp.sum(jnp.where(hit, own_list[None, :], 0), axis=1).reshape(seq_count, sub_count).T.reshape(-1)
    live = jnp.arange(FT, dtype=jnp.int32)[None, :] < jnp.take(frame_counts, got_ids)[:, None]

    def spread(cached, current):
        sent = lax.all_to_all(jnp.take(cached, wanted, axis=0), "seq", split_axis=0, concat_axis=0, tiled=True)
        far = lax.all_gather(sent, "sub").reshape(-1, heads, HD)
        return jnp.concatenate([lax.all_gather(current, "sub").reshape(-1, heads, HD), far], axis=0)

    keys, values = spread(mem_keys, cur_keys), spread(mem_values, cur_values)
    key_live = jnp.concatenate([jnp.ones((keys.shape[0] - live.size,), bool), live.reshape(-1)])
    start = lax.axis_index("sub") * mine
    query_heads = lax.dynamic_slice_in_dim(queries, start, mine, 0).reshape(mine, heads, HD)
    scores = jnp.einsum("qhd,khd->hqk", query_heads, keys, preferred_element_type=F32) / math.sqrt(HD)
    scores = jnp.where(key_live[None, None, :], scores, -jnp.inf)
    expo = jnp.exp(scores - jnp.max(scores, axis=-1, keepdims=True))
    total = jnp.sum(expo, axis=-1)
    weighted = jnp.einsum("hqk,khd->qhd", expo.astype(BF16), values, preferred_element_type=F32)
    attended = (weighted / total.T[:, :, None]).reshape(mine, col_count).astype(BF16)
    attended = lax.all_gather(attended, "sub", axis=0, tiled=True)
    term = jnp.dot(attended, out_weight, preferred_element_type=F32).astype(BF16)
    return lax.psum_scatter(term, "head", scatter_dimension=0, tiled=True)


def solution(mesh):
    in_specs = (
        P(("groups", "seq"), "head"),
        P(("groups", "seq", "sub"), "head"),
        P(("groups", "seq", "sub"), "head"),
        P(("groups", "seq", "sub"), None, "head"),
        P(("groups", "seq", "sub"), None, "head"),
        P("groups", None),
        P("groups"),
        P("head", "sub"),
    )
    out_specs = P(("groups", "seq", "head"), "sub")

    def apply(queries, *rest):
        heads = queries.shape[1] // mesh.shape["head"] // HD
        paired = heads % 2 == 0 and mesh.shape["seq"] % 2 == 0
        paired = paired and all(mesh.shape[axis] == 2 for axis in ("groups", "head", "sub"))
        body = local if paired else local_any
        return jax.shard_map(body, mesh=mesh, in_specs=in_specs, out_specs=out_specs, check_vma=False)(queries, *rest)

    return apply
```

```python
import functools
import math

import jax
import jax.numpy as jnp
from jax import lax
from jax.experimental import pallas as pl
from jax.experimental.pallas import tpu as pltpu
from jax.sharding import PartitionSpec as P

HD = 128
FT = 64
FR_DEV = 16
F32 = jnp.float32
BF16 = jnp.bfloat16
EXP2_SCALE = math.log2(math.e) / math.sqrt(HD)
MASKED = -1e30
VMEM_LIMIT = 24 * 1024 * 1024
SWAP = [(0, 1), (1, 0)]
SHORT = pl.CostEstimate(flops=1024, bytes_accessed=1024, transcendentals=0)
ANY = pl.BlockSpec(memory_space=pl.ANY)
HBM = pl.BlockSpec(memory_space=pltpu.HBM)
VMEM = pl.BlockSpec(memory_space=pltpu.VMEM)


def params():
    return pltpu.CompilerParams(vmem_limit_bytes=VMEM_LIMIT)


def in_hbm(array):
    return pltpu.with_memory_space_constraint(array, pltpu.HBM)


def in_vmem(array):
    return pltpu.with_memory_space_constraint(array, pltpu.VMEM)


def quarter(other_seq, other_group):
    seq_part = lax.rem(lax.axis_index("seq"), 2)
    group = lax.axis_index("groups")
    return 2 * (1 - seq_part if other_seq else seq_part) + (1 - group if other_group else group)


def copy_all(pairs, sems):
    copies = [pltpu.make_async_copy(*pair, sems.at[index]) for index, pair in enumerate(pairs)]
    for copy in copies:
        copy.start()
    for copy in copies:
        copy.wait()


def pack_kernel(seq_count, low, parts, ids, counts, keys, values, cur_keys, cur_values, weight, *rest):
    outs = rest[:seq_count]
    sibling, columns_out, mask, sems = rest[seq_count:]
    seq_index = lax.axis_index("seq")
    sub_index = lax.axis_index("sub")
    width = sibling.shape[1]
    block = columns_out.shape[1]
    count = cur_keys.shape[0]
    frame_count = 2 * seq_count

    def columns_of(half):
        return pl.ds(pl.multiple_of(half * width, 128), width)

    def held_by(stretch, owner):
        found = jnp.int32(0)
        for entry in range(frame_count):
            frame = ids[stretch, entry]
            slot = frame - owner * FR_DEV
            found = jnp.where((slot >= 0) & (slot < FR_DEV), frame, found)
        return found

    pairs = []
    for shift, out in enumerate(outs):
        owner = seq_index * 2 + sub_index
        wanted = held_by(lax.rem(seq_index + shift, seq_count), owner) - owner * FR_DEV
        for turn in range(2):
            half = sub_index if turn == 0 else 1 - sub_index
            for part, source in enumerate((keys, values)):
                if shift == 0 and turn == 1:
                    target = sibling.at[pl.ds(2 * count + part * FT, FT), :]
                else:
                    target = out.at[pl.ds((2 * turn + part) * FT, FT), :]
                pairs.append((source.at[wanted, :, columns_of(half)], target))
    rows = count // parts
    for part, source in enumerate((cur_keys, cur_values)):
        for low_row in range(0, count, rows):
            target = sibling.at[pl.ds(part * count + low_row, rows), :]
            pairs.append((source.at[pl.ds(low_row, rows), columns_of(1 - sub_index)], target))
    first = pl.multiple_of(low + quarter(False, False) * block, 128)
    rows = weight.shape[0] // parts
    for part in range(parts):
        span = pl.ds(part * rows, rows)
        pairs.append((weight.at[span, pl.ds(first, block)], columns_out.at[span, :]))
    copies = [pltpu.make_async_copy(*pair, sems.at[index]) for index, pair in enumerate(pairs)]
    for copy in copies:
        copy.start()
    slot = lax.broadcasted_iota(jnp.int32, (1, FT), 1)
    for index in range(frame_count):
        turn, shift = divmod(index, seq_count)
        source = lax.rem(seq_index + seq_count - shift, seq_count) * 2
        owner = source + (sub_index if turn == 0 else 1 - sub_index)
        live = slot < counts[held_by(seq_index, owner)]
        mask[pl.ds(index, 1), :] = jnp.where(live, 0.0, MASKED).astype(F32)
    for copy in copies:
        copy.wait()


def pack(frame_ids, frame_counts, mem_keys, mem_values, cur_keys, cur_values, weight, low, block, seq_count):
    parts = 4
    width = mem_keys.shape[2] // 2
    rows = [2 * FT] + [4 * FT] * (seq_count - 1) + [2 * cur_keys.shape[0] + 2 * FT]
    shapes = [(count, width) for count in rows] + [(weight.shape[0], block)]
    return pl.pallas_call(
        functools.partial(pack_kernel, seq_count, low, parts),
        out_shape=[pltpu.VMEM(shape, BF16) for shape in shapes] + [pltpu.VMEM((2 * seq_count, FT), F32)],
        in_specs=[pl.BlockSpec(memory_space=pltpu.SMEM)] * 2 + [HBM] * 5,
        out_specs=[VMEM] * (len(shapes) + 1),
        scratch_shapes=[pltpu.SemaphoreType.DMA((4 * seq_count + 3 * parts,))],
        compiler_params=params(),
        name="pack",
        cost_estimate=pl.CostEstimate(flops=0, bytes_accessed=12 * 2**20, transcendentals=0),
    )(*map(in_hbm, (frame_ids, frame_counts, mem_keys, mem_values, cur_keys, cur_values, weight)))


def pass_on_kernel(*refs):
    arrays, out = refs[:-2], refs[-1]
    rows = out.shape[0] // len(arrays)
    for index, array in enumerate(arrays):
        out[pl.ds(index * rows, rows), :] = array[pl.ds(rows, rows), :]


def pass_on(arrays, after):
    rows, width = arrays[0].shape
    return pl.pallas_call(
        pass_on_kernel,
        out_shape=pltpu.VMEM((len(arrays) * rows // 2, width), BF16),
        in_specs=[VMEM] * len(arrays) + [ANY],
        out_specs=VMEM,
        compiler_params=params(),
        name="pass_on",
        cost_estimate=SHORT,
    )(*map(in_vmem, arrays), in_vmem(after))


def load_kernel(parts, weight, after, out, sems):
    rows = weight.shape[0] // parts
    spans = [pl.ds(part * rows, rows) for part in range(parts)]
    copy_all([(weight.at[span, :], out.at[span, :]) for span in spans], sems)


def load(weight, after):
    parts = 8
    return pl.pallas_call(
        functools.partial(load_kernel, parts),
        out_shape=pltpu.VMEM(weight.shape, BF16),
        in_specs=[HBM, ANY],
        out_specs=VMEM,
        scratch_shapes=[pltpu.SemaphoreType.DMA((parts,))],
        compiler_params=params(),
        name="load",
        cost_estimate=pl.CostEstimate(flops=0, bytes_accessed=2 * weight.size, transcendentals=0),
    )(in_hbm(weight), in_vmem(after))


def gate(array, after):
    return pl.pallas_call(
        lambda *refs: None,
        in_specs=[ANY, ANY],
        out_specs=ANY,
        out_shape=jax.ShapeDtypeStruct(array.shape, array.dtype),
        input_output_aliases={0: 0},
        compiler_params=params(),
        name="gate",
        cost_estimate=SHORT,
    )(in_vmem(array), in_vmem(after))


def copied_kernel(array, after, out):
    out[...] = array[...]


def copied(array, after):
    return pl.pallas_call(
        copied_kernel,
        in_specs=[VMEM, ANY],
        out_specs=VMEM,
        out_shape=pltpu.VMEM(array.shape, array.dtype),
        compiler_params=params(),
        name="copied",
        cost_estimate=SHORT,
    )(in_vmem(array), in_vmem(after))


def dot_t(left, right):
    return lax.dot_general(left, right, (((1,), (1,)), ((), ())), preferred_element_type=F32)


def wide(column, count):
    return jnp.concatenate([column] * count, axis=1)


def with_ones(values):
    return jnp.concatenate([values, jnp.ones_like(values)], axis=1)


def current_kernel(step, queries, own_keys, own_values, sibling, out, lse, q, own_k, own_v, sems):
    heads, rows, _ = out.shape
    count = own_k.shape[0]
    half = pl.ds(pl.multiple_of(lax.axis_index("sub") * q.shape[1], 128), q.shape[1])
    copy_all(
        [(queries.at[:, half], q), (own_keys.at[:, half], own_k), (own_values.at[:, half], own_v)],
        sems,
    )

    @pl.loop(0, heads)
    def _(head):
        columns = pl.ds(pl.multiple_of(head * HD, HD), HD)
        keys = jnp.concatenate([own_k[:, columns], sibling[pl.ds(0, count), columns]], axis=0)
        values = with_ones(jnp.concatenate([own_v[:, columns], sibling[pl.ds(count, count), columns]], axis=0))
        for low in range(0, rows, step):
            span = pl.ds(low, step)
            scores = dot_t(q[span, columns], keys)
            row_max = jnp.broadcast_to(jnp.max(scores, axis=1, keepdims=True), (step, HD))
            weights = jnp.exp2((scores - wide(row_max, 2 * count // HD)) * EXP2_SCALE).astype(BF16)
            product = jnp.dot(weights, values, preferred_element_type=F32)
            total = product[:, HD:]
            out[head, span, :] = product[:, :HD] / total
            lse[head, span, :] = row_max * EXP2_SCALE + jnp.log2(total)


def attend_current(queries, cur_keys, cur_values, sibling, heads):
    rows = queries.shape[0]
    keys = cur_keys.shape[0]
    return pl.pallas_call(
        functools.partial(current_kernel, 512),
        in_specs=[HBM] * 3 + [VMEM],
        out_specs=[VMEM] * 3,
        out_shape=[pltpu.VMEM((heads, rows, HD), F32)] * 2 + [pltpu.VMEM((rows, heads * HD), BF16)],
        scratch_shapes=[pltpu.VMEM((keys, heads * HD), BF16)] * 2 + [pltpu.SemaphoreType.DMA((3,))],
        compiler_params=params(),
        name="attend_current",
        cost_estimate=pl.CostEstimate(
            flops=60 * heads * rows * 2 * keys * HD, bytes_accessed=heads * rows * HD * 12, transcendentals=heads * rows * 2 * keys
        ),
    )(in_hbm(queries), in_hbm(cur_keys), in_hbm(cur_values), in_vmem(sibling))


def frames_kernel(heads, far, starts, bias, q, held, lse, *rest):
    frames = rest[: len(starts)]
    out = rest[-1]
    count, rows = len(starts), out.shape[0]
    head_index = lax.axis_index("head")
    half = 1 - head_index if far else head_index
    span = pl.ds(pl.multiple_of(half * rows, rows), rows)
    mask = jnp.concatenate([bias[pl.ds(index, 1), :] for index in range(count)], axis=1)

    def gathered(head, part):
        columns = pl.ds(head * HD, HD)
        return jnp.concatenate(
            [frame[pl.ds(start + part * FT, FT), columns] for frame, start in zip(frames, starts)], axis=0
        )

    def scores_of(head):
        return dot_t(q[span, pl.ds(head * HD, HD)], gathered(head, 0))

    def finish(head, scores):
        scores = scores * EXP2_SCALE + mask
        old = lse[head, span, :]
        new_max = jnp.maximum(old, jnp.max(scores, axis=1, keepdims=True))
        weights = jnp.exp2(scores - wide(new_max, count * FT // HD)).astype(BF16)
        product = jnp.dot(weights, with_ones(gathered(head, 1)), preferred_element_type=F32)
        scale = jnp.exp2(old - new_max)
        top = held[head, span, :] * scale + product[:, :HD]
        out[:, pl.ds(head * HD, HD)] = (top / (scale + product[:, HD:])).astype(BF16)

    scores = scores_of(0)
    for head in range(heads):
        following = scores_of(head + 1) if head + 1 < heads else None
        finish(head, scores)
        scores = following


def attend_frames(far, bias, q, held, lse, frames, starts, after=()):
    heads, rows, _ = held.shape
    operands = [bias, q, held, lse, *frames]
    return pl.pallas_call(
        functools.partial(frames_kernel, heads, far, tuple(starts)),
        in_specs=[VMEM] * len(operands) + [ANY] * len(after),
        out_specs=VMEM,
        out_shape=pltpu.VMEM((rows // 2, heads * HD), BF16),
        compiler_params=params(),
        name="attend_far" if far else "attend_near",
        cost_estimate=SHORT,
    )(*map(in_vmem, operands), *map(in_vmem, after))


def both(mine, other):
    first, second = mine[...], other[...]
    return jnp.where(
        lax.axis_index("sub") == 0,
        jnp.concatenate([first, second], axis=1),
        jnp.concatenate([second, first], axis=1),
    )


def project_kernel(step, mine, other, weight, *rest):
    out = rest[-1]
    rows = both(mine, other)

    @pl.loop(0, out.shape[1] // step)
    def _(index):
        columns = pl.ds(pl.multiple_of(index * step, step), step)
        out[:, columns] = jnp.dot(rows, weight[:, columns], preferred_element_type=F32).astype(BF16)


def unshared_kernel(low, mine, other, weight, *rest):
    out = rest[-1]
    rows = both(mine, other)
    share = out.shape[1] - low
    start = pl.multiple_of(low + quarter(True, True) * share, 128)
    for columns, span in ((pl.ds(0, low), pl.ds(0, low)), (pl.ds(start, share), pl.ds(low, share))):
        out[:, span] = jnp.dot(rows, weight[:, columns], preferred_element_type=F32).astype(BF16)


def project_call(kernel, name, mine, other, weight, width, after):
    return pl.pallas_call(
        kernel,
        in_specs=[VMEM] * 3 + [ANY] * len(after),
        out_specs=VMEM,
        out_shape=pltpu.VMEM((mine.shape[0], width), BF16),
        compiler_params=params(),
        name=name,
        cost_estimate=SHORT,
    )(*map(in_vmem, (mine, other, weight, *after)))


def project(mine, other, weight, after):
    return project_call(functools.partial(project_kernel, 512), "project", mine, other, weight, weight.shape[1], after)


def project_unshared(mine, other, weight, low, share, after):
    kernel = functools.partial(unshared_kernel, low)
    return project_call(kernel, "project_unshared", mine, other, weight, low + share, after)


def write_blocks(blocks, out, scratch, sems):
    copies, start = [], 0
    for index, (block, low) in enumerate(blocks):
        span = pl.ds(start, block.shape[1])
        scratch[:, span] = block.astype(BF16)
        copy = pltpu.make_async_copy(scratch.at[:, span], out.at[:, pl.ds(low, block.shape[1])], sems.at[index])
        copy.start()
        copies.append(copy)
        start += block.shape[1]
    for copy in copies:
        copy.wait()


def remote_kernel(first, other_seq, other_group, terms, mine, other, weight, total, out, scratch, sems):
    block = weight.shape[1]
    low = pl.multiple_of(first + quarter(other_seq, other_group) * block, 128)
    product = jnp.dot(both(mine, other), weight[...], preferred_element_type=F32)
    write_blocks([(terms[:, pl.ds(low, block)].astype(F32) + product, low)], out, scratch, sems)


def add_kernel(low, terms, came, total, out, scratch, sems):
    share = came.shape[1] - low
    start = pl.multiple_of(low + quarter(True, True) * share, 128)
    blocks = []
    for columns, span in ((pl.ds(0, low), pl.ds(0, low)), (pl.ds(start, share), pl.ds(low, share))):
        blocks.append((terms[:, columns].astype(F32) + came[:, span].astype(F32), columns.start))
    write_blocks(blocks, out, scratch, sems)


def finish_block(kernel, name, operands, total, rows, width, block):
    count = len(operands)
    if total is None:
        body = lambda *refs: kernel(*refs[:count], None, *refs[count:])
        totals, aliases = [], {}
    else:
        body, totals, aliases = kernel, [in_hbm(total)], {count: 0}
    return pl.pallas_call(
        body,
        in_specs=[VMEM] * count + [HBM] * len(totals),
        out_specs=HBM,
        out_shape=pltpu.HBM((rows, width), BF16),
        input_output_aliases=aliases,
        scratch_shapes=[pltpu.VMEM((rows, block), BF16), pltpu.SemaphoreType.DMA((2,))],
        compiler_params=params(),
        name=name,
        cost_estimate=SHORT,
    )(*map(in_vmem, operands), *totals)


def add_remote(terms, mine, other, weight, first, other_seq, other_group, total):
    kernel = functools.partial(remote_kernel, first, other_seq, other_group)
    return finish_block(kernel, "add_remote", (terms, mine, other, weight), total, *terms.shape, weight.shape[1])


def add_unshared(terms, came, low, total):
    kernel = functools.partial(add_kernel, low)
    return finish_block(kernel, "add_unshared", (terms, came), total, *terms.shape, came.shape[1])


def local(queries, cur_keys, cur_values, mem_keys, mem_values, frame_ids, frame_counts, out_weight):
    seq_count = lax.axis_size("seq")
    heads = queries.shape[1] // HD // 2
    keys = cur_keys.shape[0]
    out_cols = out_weight.shape[1]
    share = out_cols // 5 // 128 * 128
    low = out_cols - 4 * share

    *sends, to_sibling, columns, bias = pack(
        frame_ids, frame_counts, mem_keys, mem_values, cur_keys, cur_values, out_weight, low, share, seq_count
    )
    got = {0: sends[0]}
    order = sorted(range(1, seq_count), key=lambda shift: -min(shift, seq_count - shift))
    for shift in order:
        if shift == order[-1]:
            columns = lax.ppermute(columns, "head", SWAP)
        pairs = [(index, (index + shift) % seq_count) for index in range(seq_count)]
        got[shift] = lax.ppermute(sends[shift], "seq", pairs)
    mine = [got[shift] for shift in range(seq_count)]
    sibling = lax.ppermute(to_sibling, "sub", SWAP)

    held, lse, q = attend_current(queries, cur_keys, cur_values, sibling, heads)
    weight = load(out_weight, lse)
    passed = pass_on(mine[1:], weight)
    theirs = lax.ppermute(passed, "sub", SWAP)
    frames = [*mine, sibling] + [theirs] * (seq_count - 1)
    starts = [0] * seq_count + [2 * keys] + [2 * FT * index for index in range(seq_count - 1)]

    far = attend_frames(True, bias, q, held, lse, frames, starts)
    came_mine = lax.ppermute(far, "head", SWAP)
    far_sibling = lax.ppermute(far, "sub", SWAP)
    group_columns = lax.ppermute(columns, "groups", SWAP)
    columns_copy = copied(columns, far)
    seq_columns = lax.ppermute(columns_copy, "seq", [(index, index ^ 1) for index in range(seq_count)])
    near = attend_frames(False, bias, q, held, lse, frames, starts, (columns_copy,))
    near_sibling = lax.ppermute(near, "sub", SWAP)

    term = project_unshared(far, far_sibling, weight, low, share, (near,))
    came = lax.ppermute(term, "head", SWAP)
    came_mine = gate(came_mine, term)
    came_other = lax.ppermute(came_mine, "sub", SWAP)
    terms = project(near, near_sibling, weight, (came_mine,))

    arrived = (terms, came_mine, came_other)
    total = add_remote(*arrived, columns, low, False, False, None)
    total = add_remote(*arrived, group_columns, low, False, True, total)
    total = add_remote(*arrived, seq_columns, low, True, False, total)
    return add_unshared(terms, came, low, total)


def local_any(queries, cur_keys, cur_values, mem_keys, mem_values, frame_ids, frame_counts, out_weight):
    seq_count = lax.axis_size("seq")
    sub_count = lax.axis_size("sub")
    seq_index = lax.axis_index("seq")
    owner_self = seq_index * sub_count + lax.axis_index("sub")
    row_count, col_count = queries.shape
    heads = col_count // HD
    mine = row_count // sub_count
    wanted = jnp.sum(jnp.where(frame_ids // FR_DEV == owner_self, frame_ids, 0), axis=1) - owner_self * FR_DEV
    own_list = lax.dynamic_index_in_dim(frame_ids, seq_index, 0, keepdims=False)
    owners = jnp.arange(seq_count * sub_count, dtype=jnp.int32)
    hit = (own_list // FR_DEV)[None, :] == owners[:, None]
    got_ids = jnp.sum(jnp.where(hit, own_list[None, :], 0), axis=1).reshape(seq_count, sub_count).T.reshape(-1)
    live = jnp.arange(FT, dtype=jnp.int32)[None, :] < jnp.take(frame_counts, got_ids)[:, None]

    def spread(cached, current):
        sent = lax.all_to_all(jnp.take(cached, wanted, axis=0), "seq", split_axis=0, concat_axis=0, tiled=True)
        far = lax.all_gather(sent, "sub").reshape(-1, heads, HD)
        return jnp.concatenate([lax.all_gather(current, "sub").reshape(-1, heads, HD), far], axis=0)

    keys, values = spread(mem_keys, cur_keys), spread(mem_values, cur_values)
    key_live = jnp.concatenate([jnp.ones((keys.shape[0] - live.size,), bool), live.reshape(-1)])
    start = lax.axis_index("sub") * mine
    query_heads = lax.dynamic_slice_in_dim(queries, start, mine, 0).reshape(mine, heads, HD)
    scores = jnp.einsum("qhd,khd->hqk", query_heads, keys, preferred_element_type=F32) / math.sqrt(HD)
    scores = jnp.where(key_live[None, None, :], scores, -jnp.inf)
    expo = jnp.exp(scores - jnp.max(scores, axis=-1, keepdims=True))
    total = jnp.sum(expo, axis=-1)
    weighted = jnp.einsum("hqk,khd->qhd", expo.astype(BF16), values, preferred_element_type=F32)
    attended = (weighted / total.T[:, :, None]).reshape(mine, col_count).astype(BF16)
    attended = lax.all_gather(attended, "sub", axis=0, tiled=True)
    term = jnp.dot(attended, out_weight, preferred_element_type=F32).astype(BF16)
    return lax.psum_scatter(term, "head", scatter_dimension=0, tiled=True)


def solution(mesh):
    in_specs = (
        P(("groups", "seq"), "head"),
        P(("groups", "seq", "sub"), "head"),
        P(("groups", "seq", "sub"), "head"),
        P(("groups", "seq", "sub"), None, "head"),
        P(("groups", "seq", "sub"), None, "head"),
        P("groups", None),
        P("groups"),
        P("head", "sub"),
    )
    out_specs = P(("groups", "seq", "head"), "sub")

    def apply(queries, *rest):
        heads = queries.shape[1] // mesh.shape["head"] // HD
        paired = heads % 2 == 0 and mesh.shape["seq"] % 2 == 0
        paired = paired and all(mesh.shape[axis] == 2 for axis in ("groups", "head", "sub"))
        body = local if paired else local_any
        return jax.shard_map(body, mesh=mesh, in_specs=in_specs, out_specs=out_specs, check_vma=False)(queries, *rest)

    return apply
```

```python
import functools
import math

import jax
import jax.numpy as jnp
from jax import lax
from jax.experimental import pallas as pl
from jax.experimental.pallas import tpu as pltpu
from jax.sharding import PartitionSpec as P

HD = 128
FT = 64
FR_DEV = 16
F32 = jnp.float32
BF16 = jnp.bfloat16
EXP2_SCALE = math.log2(math.e) / math.sqrt(HD)
MASKED = -1e30
VMEM_LIMIT = 24 * 1024 * 1024
SWAP = [(0, 1), (1, 0)]
SHORT = pl.CostEstimate(flops=1024, bytes_accessed=1024, transcendentals=0)
ANY = pl.BlockSpec(memory_space=pl.ANY)
HBM = pl.BlockSpec(memory_space=pltpu.HBM)
VMEM = pl.BlockSpec(memory_space=pltpu.VMEM)


def params():
    return pltpu.CompilerParams(vmem_limit_bytes=VMEM_LIMIT)


def in_hbm(array):
    return pltpu.with_memory_space_constraint(array, pltpu.HBM)


def in_vmem(array):
    return pltpu.with_memory_space_constraint(array, pltpu.VMEM)


def quarter(other_seq, other_group):
    seq_part = lax.rem(lax.axis_index("seq"), 2)
    group = lax.axis_index("groups")
    return 2 * (1 - seq_part if other_seq else seq_part) + (1 - group if other_group else group)


def copy_all(pairs, sems):
    copies = [pltpu.make_async_copy(*pair, sems.at[index]) for index, pair in enumerate(pairs)]
    for copy in copies:
        copy.start()
    for copy in copies:
        copy.wait()


def held_by(ids, stretch, owner, count):
    found = jnp.int32(0)
    for entry in range(count):
        frame = ids[stretch, entry]
        slot = frame - owner * FR_DEV
        found = jnp.where((slot >= 0) & (slot < FR_DEV), frame, found)
    return found


def pack_kernel(seq_count, low, parts, ids, keys, values, cur_keys, cur_values, weight, *rest):
    outs = rest[:seq_count]
    sibling, *columns_out, sems = rest[seq_count:]
    seq_index = lax.axis_index("seq")
    sub_index = lax.axis_index("sub")
    width = sibling.shape[1]
    block = columns_out[0].shape[1]
    count = cur_keys.shape[0]
    frame_count = 2 * seq_count

    def columns_of(half):
        return pl.ds(pl.multiple_of(half * width, 128), width)

    pairs = []
    for shift, out in enumerate(outs):
        owner = seq_index * 2 + sub_index
        wanted = held_by(ids, lax.rem(seq_index + shift, seq_count), owner, frame_count) - owner * FR_DEV
        for turn in range(2):
            half = sub_index if turn == 0 else 1 - sub_index
            for part, source in enumerate((keys, values)):
                if shift == 0 and turn == 1:
                    target = sibling.at[pl.ds(2 * count + part * FT, FT), :]
                else:
                    target = out.at[pl.ds((2 * turn + part) * FT, FT), :]
                pairs.append((source.at[wanted, :, columns_of(half)], target))
    rows = count // parts
    for part, source in enumerate((cur_keys, cur_values)):
        for low_row in range(0, count, rows):
            target = sibling.at[pl.ds(part * count + low_row, rows), :]
            pairs.append((source.at[pl.ds(low_row, rows), columns_of(1 - sub_index)], target))
    first = pl.multiple_of(low + quarter(False, False) * block, 128)
    rows = weight.shape[0] // parts
    for part in range(parts):
        place, index = divmod(part, parts // 2)
        target = columns_out[place].at[pl.ds(index * rows, rows), :]
        pairs.append((weight.at[pl.ds(part * rows, rows), pl.ds(first, block)], target))
    copy_all(pairs, sems)


def pack(frame_ids, mem_keys, mem_values, cur_keys, cur_values, weight, low, block, seq_count):
    parts = 4
    width = mem_keys.shape[2] // 2
    rows = [2 * FT] + [4 * FT] * (seq_count - 1) + [2 * cur_keys.shape[0] + 2 * FT]
    shapes = [(count, width) for count in rows] + [(weight.shape[0] // 2, block)] * 2
    return pl.pallas_call(
        functools.partial(pack_kernel, seq_count, low, parts),
        out_shape=[pltpu.VMEM(shape, BF16) for shape in shapes],
        in_specs=[pl.BlockSpec(memory_space=pltpu.SMEM)] + [HBM] * 5,
        out_specs=[VMEM] * len(shapes),
        scratch_shapes=[pltpu.SemaphoreType.DMA((4 * seq_count + 3 * parts,))],
        compiler_params=params(),
        name="pack",
        cost_estimate=pl.CostEstimate(flops=0, bytes_accessed=12 * 2**20, transcendentals=0),
    )(*map(in_hbm, (frame_ids, mem_keys, mem_values, cur_keys, cur_values, weight)))


def pass_on_kernel(*refs):
    arrays, out = refs[:-2], refs[-1]
    rows = out.shape[0] // len(arrays)
    for index, array in enumerate(arrays):
        out[pl.ds(index * rows, rows), :] = array[pl.ds(rows, rows), :]


def pass_on(arrays, after):
    rows, width = arrays[0].shape
    return pl.pallas_call(
        pass_on_kernel,
        out_shape=pltpu.VMEM((len(arrays) * rows // 2, width), BF16),
        in_specs=[VMEM] * len(arrays) + [ANY],
        out_specs=VMEM,
        compiler_params=params(),
        name="pass_on",
        cost_estimate=SHORT,
    )(*map(in_vmem, arrays), in_vmem(after))


def load_kernel(parts, seq_count, ids, counts, weight, after, out, mask, sems):
    rows = weight.shape[0] // parts
    spans = [pl.ds(part * rows, rows) for part in range(parts)]
    copies = [pltpu.make_async_copy(weight.at[span, :], out.at[span, :], sems.at[index]) for index, span in enumerate(spans)]
    for copy in copies:
        copy.start()
    seq_index = lax.axis_index("seq")
    sub_index = lax.axis_index("sub")
    slot = lax.broadcasted_iota(jnp.int32, (1, FT), 1)
    for index in range(2 * seq_count):
        turn, shift = divmod(index, seq_count)
        source = lax.rem(seq_index + seq_count - shift, seq_count) * 2
        owner = source + (sub_index if turn == 0 else 1 - sub_index)
        live = slot < counts[held_by(ids, seq_index, owner, 2 * seq_count)]
        mask[pl.ds(index, 1), :] = jnp.where(live, 0.0, MASKED).astype(F32)
    for copy in copies:
        copy.wait()


def load(frame_ids, frame_counts, weight, seq_count, after):
    parts = 8
    return pl.pallas_call(
        functools.partial(load_kernel, parts, seq_count),
        out_shape=[pltpu.VMEM(weight.shape, BF16), pltpu.VMEM((2 * seq_count, FT), F32)],
        in_specs=[pl.BlockSpec(memory_space=pltpu.SMEM)] * 2 + [HBM, ANY],
        out_specs=[VMEM, VMEM],
        scratch_shapes=[pltpu.SemaphoreType.DMA((parts,))],
        compiler_params=params(),
        name="load",
        cost_estimate=pl.CostEstimate(flops=0, bytes_accessed=2 * weight.size, transcendentals=0),
    )(*map(in_hbm, (frame_ids, frame_counts, weight)), in_vmem(after))


def gate(array, after):
    return pl.pallas_call(
        lambda *refs: None,
        in_specs=[ANY, ANY],
        out_specs=ANY,
        out_shape=jax.ShapeDtypeStruct(array.shape, array.dtype),
        input_output_aliases={0: 0},
        compiler_params=params(),
        name="gate",
        cost_estimate=SHORT,
    )(in_vmem(array), in_vmem(after))


def joined_kernel(upper, lower, after, out):
    rows = upper.shape[0]
    out[pl.ds(0, rows), :] = upper[...]
    out[pl.ds(rows, rows), :] = lower[...]


def joined(upper, lower, after):
    rows, width = upper.shape
    return pl.pallas_call(
        joined_kernel,
        in_specs=[VMEM, VMEM, ANY],
        out_specs=VMEM,
        out_shape=pltpu.VMEM((2 * rows, width), upper.dtype),
        compiler_params=params(),
        name="joined",
        cost_estimate=SHORT,
    )(*map(in_vmem, (upper, lower, after)))


def dot_t(left, right):
    return lax.dot_general(left, right, (((1,), (1,)), ((), ())), preferred_element_type=F32)


def wide(column, count):
    return jnp.concatenate([column] * count, axis=1)


def with_ones(values):
    return jnp.concatenate([values, jnp.ones_like(values)], axis=1)


def current_kernel(step, queries, own_keys, own_values, sibling, out, lse, q, own_k, own_v, sems):
    heads, rows, _ = out.shape
    count = own_k.shape[0]
    half = pl.ds(pl.multiple_of(lax.axis_index("sub") * q.shape[1], 128), q.shape[1])
    copy_all(
        [(queries.at[:, half], q), (own_keys.at[:, half], own_k), (own_values.at[:, half], own_v)],
        sems,
    )

    @pl.loop(0, heads)
    def _(head):
        columns = pl.ds(pl.multiple_of(head * HD, HD), HD)
        keys = jnp.concatenate([own_k[:, columns], sibling[pl.ds(0, count), columns]], axis=0)
        values = with_ones(jnp.concatenate([own_v[:, columns], sibling[pl.ds(count, count), columns]], axis=0))
        for low in range(0, rows, step):
            span = pl.ds(low, step)
            scores = dot_t(q[span, columns], keys)
            row_max = jnp.broadcast_to(jnp.max(scores, axis=1, keepdims=True), (step, HD))
            weights = jnp.exp2((scores - wide(row_max, 2 * count // HD)) * EXP2_SCALE).astype(BF16)
            product = jnp.dot(weights, values, preferred_element_type=F32)
            total = product[:, HD:]
            out[head, span, :] = product[:, :HD] / total
            lse[head, span, :] = row_max * EXP2_SCALE + jnp.log2(total)


def attend_current(queries, cur_keys, cur_values, sibling, heads):
    rows = queries.shape[0]
    keys = cur_keys.shape[0]
    return pl.pallas_call(
        functools.partial(current_kernel, 512),
        in_specs=[HBM] * 3 + [VMEM],
        out_specs=[VMEM] * 3,
        out_shape=[pltpu.VMEM((heads, rows, HD), F32)] * 2 + [pltpu.VMEM((rows, heads * HD), BF16)],
        scratch_shapes=[pltpu.VMEM((keys, heads * HD), BF16)] * 2 + [pltpu.SemaphoreType.DMA((3,))],
        compiler_params=params(),
        name="attend_current",
        cost_estimate=pl.CostEstimate(
            flops=60 * heads * rows * 2 * keys * HD, bytes_accessed=heads * rows * HD * 12, transcendentals=heads * rows * 2 * keys
        ),
    )(in_hbm(queries), in_hbm(cur_keys), in_hbm(cur_values), in_vmem(sibling))


def frames_kernel(heads, far, starts, bias, q, held, lse, *rest):
    frames = rest[: len(starts)]
    out = rest[-1]
    count, rows = len(starts), out.shape[0]
    head_index = lax.axis_index("head")
    half = 1 - head_index if far else head_index
    span = pl.ds(pl.multiple_of(half * rows, rows), rows)
    mask = jnp.concatenate([bias[pl.ds(index, 1), :] for index in range(count)], axis=1)

    def gathered(head, part):
        columns = pl.ds(head * HD, HD)
        return jnp.concatenate(
            [frame[pl.ds(start + part * FT, FT), columns] for frame, start in zip(frames, starts)], axis=0
        )

    def scores_of(head):
        return dot_t(q[span, pl.ds(head * HD, HD)], gathered(head, 0))

    def finish(head, scores):
        scores = scores * EXP2_SCALE + mask
        old = lse[head, span, :]
        new_max = jnp.maximum(old, jnp.max(scores, axis=1, keepdims=True))
        weights = jnp.exp2(scores - wide(new_max, count * FT // HD)).astype(BF16)
        product = jnp.dot(weights, with_ones(gathered(head, 1)), preferred_element_type=F32)
        scale = jnp.exp2(old - new_max)
        top = held[head, span, :] * scale + product[:, :HD]
        out[:, pl.ds(head * HD, HD)] = (top / (scale + product[:, HD:])).astype(BF16)

    scores = scores_of(0)
    for head in range(heads):
        following = scores_of(head + 1) if head + 1 < heads else None
        finish(head, scores)
        scores = following


def attend_frames(far, bias, q, held, lse, frames, starts, after=()):
    heads, rows, _ = held.shape
    operands = [bias, q, held, lse, *frames]
    return pl.pallas_call(
        functools.partial(frames_kernel, heads, far, tuple(starts)),
        in_specs=[VMEM] * len(operands) + [ANY] * len(after),
        out_specs=VMEM,
        out_shape=pltpu.VMEM((rows // 2, heads * HD), BF16),
        compiler_params=params(),
        name="attend_far" if far else "attend_near",
        cost_estimate=SHORT,
    )(*map(in_vmem, operands), *map(in_vmem, after))


def both(mine, other):
    first, second = mine[...], other[...]
    return jnp.where(
        lax.axis_index("sub") == 0,
        jnp.concatenate([first, second], axis=1),
        jnp.concatenate([second, first], axis=1),
    )


def project_kernel(step, mine, other, weight, *rest):
    out = rest[-1]
    rows = both(mine, other)

    @pl.loop(0, out.shape[1] // step)
    def _(index):
        columns = pl.ds(pl.multiple_of(index * step, step), step)
        out[:, columns] = jnp.dot(rows, weight[:, columns], preferred_element_type=F32).astype(BF16)


def unshared_columns(low, share):
    return pl.ds(0, low), pl.ds(pl.multiple_of(low + quarter(True, True) * share, 128), share)


def unshared_kernel(low, mine, other, weight, *rest):
    out = rest[-1]
    rows = both(mine, other)
    start = 0
    for columns in unshared_columns(low, out.shape[1] - low):
        out[:, pl.ds(start, columns.size)] = jnp.dot(rows, weight[:, columns], preferred_element_type=F32).astype(BF16)
        start += columns.size


def project_call(kernel, name, mine, other, weight, width, after):
    return pl.pallas_call(
        kernel,
        in_specs=[VMEM] * 3 + [ANY] * len(after),
        out_specs=VMEM,
        out_shape=pltpu.VMEM((mine.shape[0], width), BF16),
        compiler_params=params(),
        name=name,
        cost_estimate=SHORT,
    )(*map(in_vmem, (mine, other, weight, *after)))


def project(mine, other, weight, after):
    return project_call(functools.partial(project_kernel, 512), "project", mine, other, weight, weight.shape[1], after)


def project_unshared(mine, other, weight, low, share, after):
    kernel = functools.partial(unshared_kernel, low)
    return project_call(kernel, "project_unshared", mine, other, weight, low + share, after)


def write_blocks(blocks, out, scratch, sems):
    copies, start = [], 0
    for index, (block, low) in enumerate(blocks):
        span = pl.ds(start, block.shape[1])
        scratch[:, span] = block.astype(BF16)
        copy = pltpu.make_async_copy(scratch.at[:, span], out.at[:, pl.ds(low, block.shape[1])], sems.at[index])
        copy.start()
        copies.append(copy)
        start += block.shape[1]
    for copy in copies:
        copy.wait()


def remote_kernel(first, other_seq, other_group, terms, mine, other, weight, total, out, scratch, sems):
    block = weight.shape[1]
    low = pl.multiple_of(first + quarter(other_seq, other_group) * block, 128)
    product = jnp.dot(both(mine, other), weight[...], preferred_element_type=F32)
    write_blocks([(terms[:, pl.ds(low, block)].astype(F32) + product, low)], out, scratch, sems)


def add_kernel(low, terms, came, total, out, scratch, sems):
    blocks, start = [], 0
    for columns in unshared_columns(low, came.shape[1] - low):
        block = terms[:, columns].astype(F32) + came[:, pl.ds(start, columns.size)].astype(F32)
        blocks.append((block, columns.start))
        start += columns.size
    write_blocks(blocks, out, scratch, sems)


def finish_block(kernel, name, operands, total, rows, width, block):
    count = len(operands)
    if total is None:
        body = lambda *refs: kernel(*refs[:count], None, *refs[count:])
        totals, aliases = [], {}
    else:
        body, totals, aliases = kernel, [in_hbm(total)], {count: 0}
    return pl.pallas_call(
        body,
        in_specs=[VMEM] * count + [HBM] * len(totals),
        out_specs=HBM,
        out_shape=pltpu.HBM((rows, width), BF16),
        input_output_aliases=aliases,
        scratch_shapes=[pltpu.VMEM((rows, block), BF16), pltpu.SemaphoreType.DMA((2,))],
        compiler_params=params(),
        name=name,
        cost_estimate=SHORT,
    )(*map(in_vmem, operands), *totals)


def add_remote(terms, mine, other, weight, first, other_seq, other_group, total):
    kernel = functools.partial(remote_kernel, first, other_seq, other_group)
    return finish_block(kernel, "add_remote", (terms, mine, other, weight), total, *terms.shape, weight.shape[1])


def add_unshared(terms, came, low, total):
    kernel = functools.partial(add_kernel, low)
    return finish_block(kernel, "add_unshared", (terms, came), total, *terms.shape, came.shape[1])


def local(queries, cur_keys, cur_values, mem_keys, mem_values, frame_ids, frame_counts, out_weight):
    seq_count = lax.axis_size("seq")
    heads = queries.shape[1] // HD // 2
    keys = cur_keys.shape[0]
    out_cols = out_weight.shape[1]
    share = out_cols // 5 // 128 * 128
    low = out_cols - 4 * share

    *sends, to_sibling, upper, lower = pack(
        frame_ids, mem_keys, mem_values, cur_keys, cur_values, out_weight, low, share, seq_count
    )
    mine = [sends[0]]
    for shift in range(1, seq_count):
        pairs = [(index, (index + shift) % seq_count) for index in range(seq_count)]
        mine.append(lax.ppermute(sends[shift], "seq", pairs))
    upper, lower = lax.ppermute(upper, "head", SWAP), lax.ppermute(lower, "head", SWAP)
    sibling = lax.ppermute(to_sibling, "sub", SWAP)

    held, lse, q = attend_current(queries, cur_keys, cur_values, sibling, heads)
    weight, bias = load(frame_ids, frame_counts, out_weight, seq_count, lse)
    passed = pass_on(mine[1:], weight)
    theirs = lax.ppermute(passed, "sub", SWAP)
    frames = [*mine, sibling] + [theirs] * (seq_count - 1)
    starts = [0] * seq_count + [2 * keys] + [2 * FT * index for index in range(seq_count - 1)]

    far = attend_frames(True, bias, q, held, lse, frames, starts)
    came_mine = lax.ppermute(far, "head", SWAP)
    far_sibling = lax.ppermute(far, "sub", SWAP)
    columns = joined(upper, lower, far)
    group_columns = lax.ppermute(columns, "groups", SWAP)
    seq_columns = lax.ppermute(columns, "seq", [(index, index ^ 1) for index in range(seq_count)])
    near = attend_frames(False, bias, q, held, lse, frames, starts, (columns,))
    near_sibling = lax.ppermute(near, "sub", SWAP)

    term = project_unshared(far, far_sibling, weight, low, share, (near,))
    came = lax.ppermute(term, "head", SWAP)
    came_mine = gate(came_mine, term)
    came_other = lax.ppermute(came_mine, "sub", SWAP)
    terms = project(near, near_sibling, weight, (came_mine,))

    arrived = (terms, came_mine, came_other)
    total = add_remote(*arrived, columns, low, False, False, None)
    total = add_remote(*arrived, group_columns, low, False, True, total)
    total = add_remote(*arrived, seq_columns, low, True, False, total)
    return add_unshared(terms, came, low, total)


def local_any(queries, cur_keys, cur_values, mem_keys, mem_values, frame_ids, frame_counts, out_weight):
    seq_count = lax.axis_size("seq")
    sub_count = lax.axis_size("sub")
    seq_index = lax.axis_index("seq")
    owner_self = seq_index * sub_count + lax.axis_index("sub")
    row_count, col_count = queries.shape
    heads = col_count // HD
    mine = row_count // sub_count
    wanted = jnp.sum(jnp.where(frame_ids // FR_DEV == owner_self, frame_ids, 0), axis=1) - owner_self * FR_DEV
    own_list = lax.dynamic_index_in_dim(frame_ids, seq_index, 0, keepdims=False)
    owners = jnp.arange(seq_count * sub_count, dtype=jnp.int32)
    hit = (own_list // FR_DEV)[None, :] == owners[:, None]
    got_ids = jnp.sum(jnp.where(hit, own_list[None, :], 0), axis=1).reshape(seq_count, sub_count).T.reshape(-1)
    live = jnp.arange(FT, dtype=jnp.int32)[None, :] < jnp.take(frame_counts, got_ids)[:, None]

    def spread(cached, current):
        sent = lax.all_to_all(jnp.take(cached, wanted, axis=0), "seq", split_axis=0, concat_axis=0, tiled=True)
        far = lax.all_gather(sent, "sub").reshape(-1, heads, HD)
        return jnp.concatenate([lax.all_gather(current, "sub").reshape(-1, heads, HD), far], axis=0)

    keys, values = spread(mem_keys, cur_keys), spread(mem_values, cur_values)
    key_live = jnp.concatenate([jnp.ones((keys.shape[0] - live.size,), bool), live.reshape(-1)])
    start = lax.axis_index("sub") * mine
    query_heads = lax.dynamic_slice_in_dim(queries, start, mine, 0).reshape(mine, heads, HD)
    scores = jnp.einsum("qhd,khd->hqk", query_heads, keys, preferred_element_type=F32) / math.sqrt(HD)
    scores = jnp.where(key_live[None, None, :], scores, -jnp.inf)
    expo = jnp.exp(scores - jnp.max(scores, axis=-1, keepdims=True))
    total = jnp.sum(expo, axis=-1)
    weighted = jnp.einsum("hqk,khd->qhd", expo.astype(BF16), values, preferred_element_type=F32)
    attended = (weighted / total.T[:, :, None]).reshape(mine, col_count).astype(BF16)
    attended = lax.all_gather(attended, "sub", axis=0, tiled=True)
    term = jnp.dot(attended, out_weight, preferred_element_type=F32).astype(BF16)
    return lax.psum_scatter(term, "head", scatter_dimension=0, tiled=True)


def solution(mesh):
    in_specs = (
        P(("groups", "seq"), "head"),
        P(("groups", "seq", "sub"), "head"),
        P(("groups", "seq", "sub"), "head"),
        P(("groups", "seq", "sub"), None, "head"),
        P(("groups", "seq", "sub"), None, "head"),
        P("groups", None),
        P("groups"),
        P("head", "sub"),
    )
    out_specs = P(("groups", "seq", "head"), "sub")

    def apply(queries, *rest):
        heads = queries.shape[1] // mesh.shape["head"] // HD
        paired = heads % 2 == 0 and mesh.shape["seq"] % 2 == 0
        paired = paired and all(mesh.shape[axis] == 2 for axis in ("groups", "head", "sub"))
        body = local if paired else local_any
        return jax.shard_map(body, mesh=mesh, in_specs=in_specs, out_specs=out_specs, check_vma=False)(queries, *rest)

    return apply
```

```python
import functools
import math

import jax
import jax.numpy as jnp
from jax import lax
from jax.experimental import pallas as pl
from jax.experimental.pallas import tpu as pltpu
from jax.sharding import PartitionSpec as P

HD = 128
FT = 64
FR_DEV = 16
F32 = jnp.float32
BF16 = jnp.bfloat16
EXP2_SCALE = math.log2(math.e) / math.sqrt(HD)
MASKED = -1e30
VMEM_LIMIT = 24 * 1024 * 1024
SWAP = [(0, 1), (1, 0)]
SHORT = pl.CostEstimate(flops=1024, bytes_accessed=1024, transcendentals=0)
ANY = pl.BlockSpec(memory_space=pl.ANY)
HBM = pl.BlockSpec(memory_space=pltpu.HBM)
VMEM = pl.BlockSpec(memory_space=pltpu.VMEM)


def params():
    return pltpu.CompilerParams(vmem_limit_bytes=VMEM_LIMIT)


def in_hbm(array):
    return pltpu.with_memory_space_constraint(array, pltpu.HBM)


def in_vmem(array):
    return pltpu.with_memory_space_constraint(array, pltpu.VMEM)


def quarter(other_seq, other_group):
    seq_part = lax.rem(lax.axis_index("seq"), 2)
    group = lax.axis_index("groups")
    return 2 * (1 - seq_part if other_seq else seq_part) + (1 - group if other_group else group)


def copy_all(pairs, sems):
    copies = [pltpu.make_async_copy(*pair, sems.at[index]) for index, pair in enumerate(pairs)]
    for copy in copies:
        copy.start()
    for copy in copies:
        copy.wait()


def held_by(ids, stretch, owner, count):
    found = jnp.int32(0)
    for entry in range(count):
        frame = ids[stretch, entry]
        slot = frame - owner * FR_DEV
        found = jnp.where((slot >= 0) & (slot < FR_DEV), frame, found)
    return found


def pack_kernel(seq_count, low, parts, ids, keys, values, cur_keys, cur_values, weight, *rest):
    outs = rest[:seq_count]
    sibling, *columns_out, sems = rest[seq_count:]
    seq_index = lax.axis_index("seq")
    sub_index = lax.axis_index("sub")
    width = sibling.shape[1]
    block = columns_out[0].shape[1]
    count = cur_keys.shape[0]
    frame_count = 2 * seq_count

    def columns_of(half):
        return pl.ds(pl.multiple_of(half * width, 128), width)

    pairs = []
    for shift, out in enumerate(outs):
        owner = seq_index * 2 + sub_index
        wanted = held_by(ids, lax.rem(seq_index + shift, seq_count), owner, frame_count) - owner * FR_DEV
        for turn in range(2):
            half = sub_index if turn == 0 else 1 - sub_index
            for part, source in enumerate((keys, values)):
                if shift == 0 and turn == 1:
                    target = sibling.at[pl.ds(2 * count + part * FT, FT), :]
                else:
                    target = out.at[pl.ds((2 * turn + part) * FT, FT), :]
                pairs.append((source.at[wanted, :, columns_of(half)], target))
    rows = count // parts
    for part, source in enumerate((cur_keys, cur_values)):
        for low_row in range(0, count, rows):
            target = sibling.at[pl.ds(part * count + low_row, rows), :]
            pairs.append((source.at[pl.ds(low_row, rows), columns_of(1 - sub_index)], target))
    first = pl.multiple_of(low + quarter(False, False) * block, 128)
    rows = weight.shape[0] // parts
    for part in range(parts):
        place, index = divmod(part, parts // 2)
        target = columns_out[place].at[pl.ds(index * rows, rows), :]
        pairs.append((weight.at[pl.ds(part * rows, rows), pl.ds(first, block)], target))
    copy_all(pairs, sems)


def pack(frame_ids, mem_keys, mem_values, cur_keys, cur_values, weight, low, block, seq_count):
    parts = 4
    width = mem_keys.shape[2] // 2
    rows = [2 * FT] + [4 * FT] * (seq_count - 1) + [2 * cur_keys.shape[0] + 2 * FT]
    shapes = [(count, width) for count in rows] + [(weight.shape[0] // 2, block)] * 2
    return pl.pallas_call(
        functools.partial(pack_kernel, seq_count, low, parts),
        out_shape=[pltpu.VMEM(shape, BF16) for shape in shapes],
        in_specs=[pl.BlockSpec(memory_space=pltpu.SMEM)] + [HBM] * 5,
        out_specs=[VMEM] * len(shapes),
        scratch_shapes=[pltpu.SemaphoreType.DMA((4 * seq_count + 3 * parts,))],
        compiler_params=params(),
        name="pack",
        cost_estimate=pl.CostEstimate(flops=0, bytes_accessed=12 * 2**20, transcendentals=0),
    )(*map(in_hbm, (frame_ids, mem_keys, mem_values, cur_keys, cur_values, weight)))


def pass_on_kernel(*refs):
    arrays, out = refs[:-2], refs[-1]
    rows = out.shape[0] // len(arrays)
    for index, array in enumerate(arrays):
        out[pl.ds(index * rows, rows), :] = array[pl.ds(rows, rows), :]


def pass_on(arrays, after):
    rows, width = arrays[0].shape
    return pl.pallas_call(
        pass_on_kernel,
        out_shape=pltpu.VMEM((len(arrays) * rows // 2, width), BF16),
        in_specs=[VMEM] * len(arrays) + [ANY],
        out_specs=VMEM,
        compiler_params=params(),
        name="pass_on",
        cost_estimate=SHORT,
    )(*map(in_vmem, arrays), in_vmem(after))


def load_kernel(parts, seq_count, ids, counts, weight, after, out, mask, sems):
    rows = weight.shape[0] // parts
    spans = [pl.ds(part * rows, rows) for part in range(parts)]
    copies = [pltpu.make_async_copy(weight.at[span, :], out.at[span, :], sems.at[index]) for index, span in enumerate(spans)]
    for copy in copies:
        copy.start()
    seq_index = lax.axis_index("seq")
    sub_index = lax.axis_index("sub")
    slot = lax.broadcasted_iota(jnp.int32, (1, FT), 1)
    for index in range(2 * seq_count):
        turn, shift = divmod(index, seq_count)
        source = lax.rem(seq_index + seq_count - shift, seq_count) * 2
        owner = source + (sub_index if turn == 0 else 1 - sub_index)
        live = slot < counts[held_by(ids, seq_index, owner, 2 * seq_count)]
        mask[pl.ds(index, 1), :] = jnp.where(live, 0.0, MASKED).astype(F32)
    for copy in copies:
        copy.wait()


def load(frame_ids, frame_counts, weight, seq_count, after):
    parts = 8
    return pl.pallas_call(
        functools.partial(load_kernel, parts, seq_count),
        out_shape=[pltpu.VMEM(weight.shape, BF16), pltpu.VMEM((2 * seq_count, FT), F32)],
        in_specs=[pl.BlockSpec(memory_space=pltpu.SMEM)] * 2 + [HBM, ANY],
        out_specs=[VMEM, VMEM],
        scratch_shapes=[pltpu.SemaphoreType.DMA((parts,))],
        compiler_params=params(),
        name="load",
        cost_estimate=pl.CostEstimate(flops=0, bytes_accessed=2 * weight.size, transcendentals=0),
    )(*map(in_hbm, (frame_ids, frame_counts, weight)), in_vmem(after))


def gate(array, after):
    return pl.pallas_call(
        lambda *refs: None,
        in_specs=[ANY, ANY],
        out_specs=ANY,
        out_shape=jax.ShapeDtypeStruct(array.shape, array.dtype),
        input_output_aliases={0: 0},
        compiler_params=params(),
        name="gate",
        cost_estimate=SHORT,
    )(in_vmem(array), in_vmem(after))


def joined_kernel(upper, lower, after, out):
    rows = upper.shape[0]
    out[pl.ds(0, rows), :] = upper[...]
    out[pl.ds(rows, rows), :] = lower[...]


def joined(upper, lower, after):
    rows, width = upper.shape
    return pl.pallas_call(
        joined_kernel,
        in_specs=[VMEM, VMEM, ANY],
        out_specs=VMEM,
        out_shape=pltpu.VMEM((2 * rows, width), upper.dtype),
        compiler_params=params(),
        name="joined",
        cost_estimate=SHORT,
    )(*map(in_vmem, (upper, lower, after)))


def dot_t(left, right):
    return lax.dot_general(left, right, (((1,), (1,)), ((), ())), preferred_element_type=F32)


def wide(column, count):
    return jnp.concatenate([column] * count, axis=1)


def with_ones(values):
    return jnp.concatenate([values, jnp.ones_like(values)], axis=1)


def current_kernel(step, queries, own_keys, own_values, sibling, out, lse, q, own_k, own_v, sems):
    heads, rows, _ = out.shape
    count = own_k.shape[0]
    half = pl.ds(pl.multiple_of(lax.axis_index("sub") * q.shape[1], 128), q.shape[1])
    copy_all(
        [(queries.at[:, half], q), (own_keys.at[:, half], own_k), (own_values.at[:, half], own_v)],
        sems,
    )

    @pl.loop(0, heads)
    def _(head):
        columns = pl.ds(pl.multiple_of(head * HD, HD), HD)
        keys = jnp.concatenate([own_k[:, columns], sibling[pl.ds(0, count), columns]], axis=0)
        values = with_ones(jnp.concatenate([own_v[:, columns], sibling[pl.ds(count, count), columns]], axis=0))
        for low in range(0, rows, step):
            span = pl.ds(low, step)
            scores = dot_t(q[span, columns], keys)
            row_max = jnp.broadcast_to(jnp.max(scores, axis=1, keepdims=True), (step, HD))
            weights = jnp.exp2((scores - wide(row_max, 2 * count // HD)) * EXP2_SCALE).astype(BF16)
            product = jnp.dot(weights, values, preferred_element_type=F32)
            total = product[:, HD:]
            out[head, span, :] = product[:, :HD] / total
            lse[head, span, :] = row_max * EXP2_SCALE + jnp.log2(total)


def attend_current(queries, cur_keys, cur_values, sibling, heads):
    rows = queries.shape[0]
    keys = cur_keys.shape[0]
    return pl.pallas_call(
        functools.partial(current_kernel, 512),
        in_specs=[HBM] * 3 + [VMEM],
        out_specs=[VMEM] * 3,
        out_shape=[pltpu.VMEM((heads, rows, HD), F32)] * 2 + [pltpu.VMEM((rows, heads * HD), BF16)],
        scratch_shapes=[pltpu.VMEM((keys, heads * HD), BF16)] * 2 + [pltpu.SemaphoreType.DMA((3,))],
        compiler_params=params(),
        name="attend_current",
        cost_estimate=pl.CostEstimate(
            flops=60 * heads * rows * 2 * keys * HD, bytes_accessed=heads * rows * HD * 12, transcendentals=heads * rows * 2 * keys
        ),
    )(in_hbm(queries), in_hbm(cur_keys), in_hbm(cur_values), in_vmem(sibling))


def frames_kernel(heads, far, starts, bias, q, held, lse, *rest):
    frames = rest[: len(starts)]
    out = rest[-1]
    count, rows = len(starts), out.shape[0]
    head_index = lax.axis_index("head")
    half = 1 - head_index if far else head_index
    span = pl.ds(pl.multiple_of(half * rows, rows), rows)
    mask = jnp.concatenate([bias[pl.ds(index, 1), :] for index in range(count)], axis=1)

    def gathered(head, part):
        columns = pl.ds(head * HD, HD)
        return jnp.concatenate(
            [frame[pl.ds(start + part * FT, FT), columns] for frame, start in zip(frames, starts)], axis=0
        )

    def scores_of(head):
        return dot_t(q[span, pl.ds(head * HD, HD)], gathered(head, 0))

    def finish(head, scores):
        scores = scores * EXP2_SCALE + mask
        old = lse[head, span, :]
        new_max = jnp.maximum(old, jnp.max(scores, axis=1, keepdims=True))
        weights = jnp.exp2(scores - wide(new_max, count * FT // HD)).astype(BF16)
        product = jnp.dot(weights, with_ones(gathered(head, 1)), preferred_element_type=F32)
        scale = jnp.exp2(old - new_max)
        top = held[head, span, :] * scale + product[:, :HD]
        out[:, pl.ds(head * HD, HD)] = (top / (scale + product[:, HD:])).astype(BF16)

    scores = scores_of(0)
    for head in range(heads):
        following = scores_of(head + 1) if head + 1 < heads else None
        finish(head, scores)
        scores = following


def attend_frames(far, bias, q, held, lse, frames, starts, after=()):
    heads, rows, _ = held.shape
    operands = [bias, q, held, lse, *frames]
    return pl.pallas_call(
        functools.partial(frames_kernel, heads, far, tuple(starts)),
        in_specs=[VMEM] * len(operands) + [ANY] * len(after),
        out_specs=VMEM,
        out_shape=pltpu.VMEM((rows // 2, heads * HD), BF16),
        compiler_params=params(),
        name="attend_far" if far else "attend_near",
        cost_estimate=SHORT,
    )(*map(in_vmem, operands), *map(in_vmem, after))


def both(mine, other):
    first, second = mine[...], other[...]
    return jnp.where(
        lax.axis_index("sub") == 0,
        jnp.concatenate([first, second], axis=1),
        jnp.concatenate([second, first], axis=1),
    )


def project_kernel(step, mine, other, weight, *rest):
    out = rest[-1]
    rows = both(mine, other)

    @pl.loop(0, out.shape[1] // step)
    def _(index):
        columns = pl.ds(pl.multiple_of(index * step, step), step)
        out[:, columns] = jnp.dot(rows, weight[:, columns], preferred_element_type=F32).astype(BF16)


def unshared_columns(low, share):
    return pl.ds(0, low), pl.ds(pl.multiple_of(low + quarter(True, True) * share, 128), share)


def unshared_kernel(low, mine, other, weight, *rest):
    out = rest[-1]
    rows = both(mine, other)
    start = 0
    for columns in unshared_columns(low, out.shape[1] - low):
        out[:, pl.ds(start, columns.size)] = jnp.dot(rows, weight[:, columns], preferred_element_type=F32).astype(BF16)
        start += columns.size


def project_call(kernel, name, mine, other, weight, width, after):
    return pl.pallas_call(
        kernel,
        in_specs=[VMEM] * 3 + [ANY] * len(after),
        out_specs=VMEM,
        out_shape=pltpu.VMEM((mine.shape[0], width), BF16),
        compiler_params=params(),
        name=name,
        cost_estimate=SHORT,
    )(*map(in_vmem, (mine, other, weight, *after)))


def project(mine, other, weight, after):
    return project_call(functools.partial(project_kernel, 512), "project", mine, other, weight, weight.shape[1], after)


def project_unshared(mine, other, weight, low, share, after):
    kernel = functools.partial(unshared_kernel, low)
    return project_call(kernel, "project_unshared", mine, other, weight, low + share, after)


def write_blocks(blocks, out, scratch, sems):
    copies, start = [], 0
    for index, (block, low) in enumerate(blocks):
        span = pl.ds(start, block.shape[1])
        scratch[:, span] = block.astype(BF16)
        copy = pltpu.make_async_copy(scratch.at[:, span], out.at[:, pl.ds(low, block.shape[1])], sems.at[index])
        copy.start()
        copies.append(copy)
        start += block.shape[1]
    for copy in copies:
        copy.wait()


def remote_kernel(first, other_seq, other_group, terms, mine, other, weight, total, out, scratch, sems):
    block = weight.shape[1]
    low = pl.multiple_of(first + quarter(other_seq, other_group) * block, 128)
    product = jnp.dot(both(mine, other), weight[...], preferred_element_type=F32)
    write_blocks([(terms[:, pl.ds(low, block)].astype(F32) + product, low)], out, scratch, sems)


def add_kernel(low, terms, came, total, out, scratch, sems):
    blocks, start = [], 0
    for columns in unshared_columns(low, came.shape[1] - low):
        block = terms[:, columns].astype(F32) + came[:, pl.ds(start, columns.size)].astype(F32)
        blocks.append((block, columns.start))
        start += columns.size
    write_blocks(blocks, out, scratch, sems)


def finish_block(kernel, name, operands, total, rows, width, block):
    count = len(operands)
    if total is None:
        body = lambda *refs: kernel(*refs[:count], None, *refs[count:])
        totals, aliases = [], {}
    else:
        body, totals, aliases = kernel, [in_hbm(total)], {count: 0}
    return pl.pallas_call(
        body,
        in_specs=[VMEM] * count + [HBM] * len(totals),
        out_specs=HBM,
        out_shape=pltpu.HBM((rows, width), BF16),
        input_output_aliases=aliases,
        scratch_shapes=[pltpu.VMEM((rows, block), BF16), pltpu.SemaphoreType.DMA((2,))],
        compiler_params=params(),
        name=name,
        cost_estimate=SHORT,
    )(*map(in_vmem, operands), *totals)


def add_remote(terms, mine, other, weight, first, other_seq, other_group, total):
    kernel = functools.partial(remote_kernel, first, other_seq, other_group)
    return finish_block(kernel, "add_remote", (terms, mine, other, weight), total, *terms.shape, weight.shape[1])


def add_unshared(terms, came, low, total):
    kernel = functools.partial(add_kernel, low)
    return finish_block(kernel, "add_unshared", (terms, came), total, *terms.shape, came.shape[1])


def local(queries, cur_keys, cur_values, mem_keys, mem_values, frame_ids, frame_counts, out_weight):
    seq_count = lax.axis_size("seq")
    heads = queries.shape[1] // HD // 2
    keys = cur_keys.shape[0]
    out_cols = out_weight.shape[1]
    share = out_cols // 5 // 128 * 128
    low = out_cols - 4 * share

    *sends, to_sibling, upper, lower = pack(
        frame_ids, mem_keys, mem_values, cur_keys, cur_values, out_weight, low, share, seq_count
    )
    mine = [sends[0]]
    for shift in range(1, seq_count):
        pairs = [(index, (index + shift) % seq_count) for index in range(seq_count)]
        mine.append(lax.ppermute(sends[shift], "seq", pairs))
    upper, lower = lax.ppermute(upper, "head", SWAP), lax.ppermute(lower, "head", SWAP)
    sibling = lax.ppermute(to_sibling, "sub", SWAP)

    held, lse, q = attend_current(queries, cur_keys, cur_values, sibling, heads)
    weight, bias = load(frame_ids, frame_counts, out_weight, seq_count, lse)
    passed = pass_on(mine[1:], weight)
    theirs = lax.ppermute(passed, "sub", SWAP)
    frames = [*mine, sibling] + [theirs] * (seq_count - 1)
    starts = [0] * seq_count + [2 * keys] + [2 * FT * index for index in range(seq_count - 1)]

    columns = joined(upper, lower, passed)
    far = attend_frames(True, bias, q, held, lse, frames, starts, (columns,))
    came_mine = lax.ppermute(far, "head", SWAP)
    far_sibling = lax.ppermute(far, "sub", SWAP)
    group_columns = lax.ppermute(columns, "groups", SWAP)
    seq_columns = lax.ppermute(columns, "seq", [(index, index ^ 1) for index in range(seq_count)])
    near = attend_frames(False, bias, q, held, lse, frames, starts, (far,))
    near_sibling = lax.ppermute(near, "sub", SWAP)

    term = project_unshared(far, far_sibling, weight, low, share, (near,))
    came = lax.ppermute(term, "head", SWAP)
    came_mine = gate(came_mine, term)
    came_other = lax.ppermute(came_mine, "sub", SWAP)
    terms = project(near, near_sibling, weight, (came_mine,))

    arrived = (terms, came_mine, came_other)
    total = add_remote(*arrived, columns, low, False, False, None)
    total = add_remote(*arrived, group_columns, low, False, True, total)
    total = add_remote(*arrived, seq_columns, low, True, False, total)
    return add_unshared(terms, came, low, total)


def local_any(queries, cur_keys, cur_values, mem_keys, mem_values, frame_ids, frame_counts, out_weight):
    seq_count = lax.axis_size("seq")
    sub_count = lax.axis_size("sub")
    seq_index = lax.axis_index("seq")
    owner_self = seq_index * sub_count + lax.axis_index("sub")
    row_count, col_count = queries.shape
    heads = col_count // HD
    mine = row_count // sub_count
    wanted = jnp.sum(jnp.where(frame_ids // FR_DEV == owner_self, frame_ids, 0), axis=1) - owner_self * FR_DEV
    own_list = lax.dynamic_index_in_dim(frame_ids, seq_index, 0, keepdims=False)
    owners = jnp.arange(seq_count * sub_count, dtype=jnp.int32)
    hit = (own_list // FR_DEV)[None, :] == owners[:, None]
    got_ids = jnp.sum(jnp.where(hit, own_list[None, :], 0), axis=1).reshape(seq_count, sub_count).T.reshape(-1)
    live = jnp.arange(FT, dtype=jnp.int32)[None, :] < jnp.take(frame_counts, got_ids)[:, None]

    def spread(cached, current):
        sent = lax.all_to_all(jnp.take(cached, wanted, axis=0), "seq", split_axis=0, concat_axis=0, tiled=True)
        far = lax.all_gather(sent, "sub").reshape(-1, heads, HD)
        return jnp.concatenate([lax.all_gather(current, "sub").reshape(-1, heads, HD), far], axis=0)

    keys, values = spread(mem_keys, cur_keys), spread(mem_values, cur_values)
    key_live = jnp.concatenate([jnp.ones((keys.shape[0] - live.size,), bool), live.reshape(-1)])
    start = lax.axis_index("sub") * mine
    query_heads = lax.dynamic_slice_in_dim(queries, start, mine, 0).reshape(mine, heads, HD)
    scores = jnp.einsum("qhd,khd->hqk", query_heads, keys, preferred_element_type=F32) / math.sqrt(HD)
    scores = jnp.where(key_live[None, None, :], scores, -jnp.inf)
    expo = jnp.exp(scores - jnp.max(scores, axis=-1, keepdims=True))
    total = jnp.sum(expo, axis=-1)
    weighted = jnp.einsum("hqk,khd->qhd", expo.astype(BF16), values, preferred_element_type=F32)
    attended = (weighted / total.T[:, :, None]).reshape(mine, col_count).astype(BF16)
    attended = lax.all_gather(attended, "sub", axis=0, tiled=True)
    term = jnp.dot(attended, out_weight, preferred_element_type=F32).astype(BF16)
    return lax.psum_scatter(term, "head", scatter_dimension=0, tiled=True)


def solution(mesh):
    in_specs = (
        P(("groups", "seq"), "head"),
        P(("groups", "seq", "sub"), "head"),
        P(("groups", "seq", "sub"), "head"),
        P(("groups", "seq", "sub"), None, "head"),
        P(("groups", "seq", "sub"), None, "head"),
        P("groups", None),
        P("groups"),
        P("head", "sub"),
    )
    out_specs = P(("groups", "seq", "head"), "sub")

    def apply(queries, *rest):
        heads = queries.shape[1] // mesh.shape["head"] // HD
        paired = heads % 2 == 0 and mesh.shape["seq"] % 2 == 0
        paired = paired and all(mesh.shape[axis] == 2 for axis in ("groups", "head", "sub"))
        body = local if paired else local_any
        return jax.shard_map(body, mesh=mesh, in_specs=in_specs, out_specs=out_specs, check_vma=False)(queries, *rest)

    return apply
```

```python
import functools
import math

import jax
import jax.numpy as jnp
from jax import lax
from jax.experimental import pallas as pl
from jax.experimental.pallas import tpu as pltpu
from jax.sharding import PartitionSpec as P

HD = 128
FT = 64
FR_DEV = 16
F32 = jnp.float32
BF16 = jnp.bfloat16
EXP2_SCALE = math.log2(math.e) / math.sqrt(HD)
MASKED = -1e30
VMEM_LIMIT = 24 * 1024 * 1024
SWAP = [(0, 1), (1, 0)]
SHORT = pl.CostEstimate(flops=1024, bytes_accessed=1024, transcendentals=0)
ANY = pl.BlockSpec(memory_space=pl.ANY)
HBM = pl.BlockSpec(memory_space=pltpu.HBM)
VMEM = pl.BlockSpec(memory_space=pltpu.VMEM)


def params():
    return pltpu.CompilerParams(vmem_limit_bytes=VMEM_LIMIT)


def in_hbm(array):
    return pltpu.with_memory_space_constraint(array, pltpu.HBM)


def in_vmem(array):
    return pltpu.with_memory_space_constraint(array, pltpu.VMEM)


def quarter(other_seq, other_group):
    seq_part = lax.rem(lax.axis_index("seq"), 2)
    group = lax.axis_index("groups")
    return 2 * (1 - seq_part if other_seq else seq_part) + (1 - group if other_group else group)


def copy_all(pairs, sems):
    copies = [pltpu.make_async_copy(*pair, sems.at[index]) for index, pair in enumerate(pairs)]
    for copy in copies:
        copy.start()
    for copy in copies:
        copy.wait()


def held_by(ids, stretch, owner, count):
    found = jnp.int32(0)
    for entry in range(count):
        frame = ids[stretch, entry]
        slot = frame - owner * FR_DEV
        found = jnp.where((slot >= 0) & (slot < FR_DEV), frame, found)
    return found


def pack_kernel(seq_count, parts, ids, keys, values, cur_keys, cur_values, *rest):
    outs = rest[:seq_count]
    sibling, sems = rest[seq_count:]
    seq_index = lax.axis_index("seq")
    sub_index = lax.axis_index("sub")
    width = sibling.shape[1]
    count = cur_keys.shape[0]
    frame_count = 2 * seq_count

    def columns_of(half):
        return pl.ds(pl.multiple_of(half * width, 128), width)

    pairs = []
    for shift, out in enumerate(outs):
        owner = seq_index * 2 + sub_index
        wanted = held_by(ids, lax.rem(seq_index + shift, seq_count), owner, frame_count) - owner * FR_DEV
        for turn in range(2):
            half = sub_index if turn == 0 else 1 - sub_index
            for part, source in enumerate((keys, values)):
                if shift == 0 and turn == 1:
                    target = sibling.at[pl.ds(2 * count + part * FT, FT), :]
                else:
                    target = out.at[pl.ds((2 * turn + part) * FT, FT), :]
                pairs.append((source.at[wanted, :, columns_of(half)], target))
    rows = count // parts
    for part, source in enumerate((cur_keys, cur_values)):
        for low_row in range(0, count, rows):
            target = sibling.at[pl.ds(part * count + low_row, rows), :]
            pairs.append((source.at[pl.ds(low_row, rows), columns_of(1 - sub_index)], target))
    copy_all(pairs, sems)


def pack(frame_ids, mem_keys, mem_values, cur_keys, cur_values, seq_count):
    parts = 4
    width = mem_keys.shape[2] // 2
    rows = [2 * FT] + [4 * FT] * (seq_count - 1) + [2 * cur_keys.shape[0] + 2 * FT]
    shapes = [(count, width) for count in rows]
    return pl.pallas_call(
        functools.partial(pack_kernel, seq_count, parts),
        out_shape=[pltpu.VMEM(shape, BF16) for shape in shapes],
        in_specs=[pl.BlockSpec(memory_space=pltpu.SMEM)] + [HBM] * 4,
        out_specs=[VMEM] * len(shapes),
        scratch_shapes=[pltpu.SemaphoreType.DMA((4 * seq_count + 2 * parts,))],
        compiler_params=params(),
        name="pack",
        cost_estimate=pl.CostEstimate(flops=0, bytes_accessed=12 * 2**20, transcendentals=0),
    )(*map(in_hbm, (frame_ids, mem_keys, mem_values, cur_keys, cur_values)))


def pack_columns_kernel(low, parts, weight, after, out, sems):
    first = pl.multiple_of(low + quarter(False, False) * out.shape[1], 128)
    rows = weight.shape[0] // parts
    spans = [pl.ds(part * rows, rows) for part in range(parts)]
    copy_all([(weight.at[span, pl.ds(first, out.shape[1])], out.at[span, :]) for span in spans], sems)


def pack_columns(weight, low, share, after):
    parts = 8
    return pl.pallas_call(
        functools.partial(pack_columns_kernel, low, parts),
        out_shape=pltpu.VMEM((weight.shape[0], share), BF16),
        in_specs=[HBM, ANY],
        out_specs=VMEM,
        scratch_shapes=[pltpu.SemaphoreType.DMA((parts,))],
        compiler_params=params(),
        name="pack_columns",
        cost_estimate=SHORT,
    )(in_hbm(weight), in_vmem(after))


def pass_on_kernel(*refs):
    arrays, out = refs[:-2], refs[-1]
    rows = out.shape[0] // len(arrays)
    for index, array in enumerate(arrays):
        out[pl.ds(index * rows, rows), :] = array[pl.ds(rows, rows), :]


def pass_on(arrays, after):
    rows, width = arrays[0].shape
    return pl.pallas_call(
        pass_on_kernel,
        out_shape=pltpu.VMEM((len(arrays) * rows // 2, width), BF16),
        in_specs=[VMEM] * len(arrays) + [ANY],
        out_specs=VMEM,
        compiler_params=params(),
        name="pass_on",
        cost_estimate=SHORT,
    )(*map(in_vmem, arrays), in_vmem(after))


def load_kernel(parts, seq_count, ids, counts, weight, after, out, mask, sems):
    rows = weight.shape[0] // parts
    spans = [pl.ds(part * rows, rows) for part in range(parts)]
    copies = [pltpu.make_async_copy(weight.at[span, :], out.at[span, :], sems.at[index]) for index, span in enumerate(spans)]
    for copy in copies:
        copy.start()
    seq_index = lax.axis_index("seq")
    sub_index = lax.axis_index("sub")
    slot = lax.broadcasted_iota(jnp.int32, (1, FT), 1)
    for index in range(2 * seq_count):
        turn, shift = divmod(index, seq_count)
        source = lax.rem(seq_index + seq_count - shift, seq_count) * 2
        owner = source + (sub_index if turn == 0 else 1 - sub_index)
        live = slot < counts[held_by(ids, seq_index, owner, 2 * seq_count)]
        mask[pl.ds(index, 1), :] = jnp.where(live, 0.0, MASKED).astype(F32)
    for copy in copies:
        copy.wait()


def load(frame_ids, frame_counts, weight, seq_count, after):
    parts = 8
    return pl.pallas_call(
        functools.partial(load_kernel, parts, seq_count),
        out_shape=[pltpu.VMEM(weight.shape, BF16), pltpu.VMEM((2 * seq_count, FT), F32)],
        in_specs=[pl.BlockSpec(memory_space=pltpu.SMEM)] * 2 + [HBM, ANY],
        out_specs=[VMEM, VMEM],
        scratch_shapes=[pltpu.SemaphoreType.DMA((parts,))],
        compiler_params=params(),
        name="load",
        cost_estimate=pl.CostEstimate(flops=0, bytes_accessed=2 * weight.size, transcendentals=0),
    )(*map(in_hbm, (frame_ids, frame_counts, weight)), in_vmem(after))


def gate(array, after):
    return pl.pallas_call(
        lambda *refs: None,
        in_specs=[ANY, ANY],
        out_specs=ANY,
        out_shape=jax.ShapeDtypeStruct(array.shape, array.dtype),
        input_output_aliases={0: 0},
        compiler_params=params(),
        name="gate",
        cost_estimate=SHORT,
    )(in_vmem(array), in_vmem(after))


def copied_kernel(array, after, out):
    out[...] = array[...]


def copied(array, after):
    return pl.pallas_call(
        copied_kernel,
        in_specs=[VMEM, ANY],
        out_specs=VMEM,
        out_shape=pltpu.VMEM(array.shape, array.dtype),
        compiler_params=params(),
        name="copied",
        cost_estimate=SHORT,
    )(in_vmem(array), in_vmem(after))


def dot_t(left, right):
    return lax.dot_general(left, right, (((1,), (1,)), ((), ())), preferred_element_type=F32)


def wide(column, count):
    return jnp.concatenate([column] * count, axis=1)


def with_ones(values):
    return jnp.concatenate([values, jnp.ones_like(values)], axis=1)


def current_kernel(step, queries, own_keys, own_values, sibling, out, lse, q, own_k, own_v, sems):
    heads, rows, _ = out.shape
    count = own_k.shape[0]
    half = pl.ds(pl.multiple_of(lax.axis_index("sub") * q.shape[1], 128), q.shape[1])
    copy_all(
        [(queries.at[:, half], q), (own_keys.at[:, half], own_k), (own_values.at[:, half], own_v)],
        sems,
    )

    @pl.loop(0, heads)
    def _(head):
        columns = pl.ds(pl.multiple_of(head * HD, HD), HD)
        keys = jnp.concatenate([own_k[:, columns], sibling[pl.ds(0, count), columns]], axis=0)
        values = with_ones(jnp.concatenate([own_v[:, columns], sibling[pl.ds(count, count), columns]], axis=0))
        for low in range(0, rows, step):
            span = pl.ds(low, step)
            scores = dot_t(q[span, columns], keys)
            row_max = jnp.broadcast_to(jnp.max(scores, axis=1, keepdims=True), (step, HD))
            weights = jnp.exp2((scores - wide(row_max, 2 * count // HD)) * EXP2_SCALE).astype(BF16)
            product = jnp.dot(weights, values, preferred_element_type=F32)
            total = product[:, HD:]
            out[head, span, :] = product[:, :HD] / total
            lse[head, span, :] = row_max * EXP2_SCALE + jnp.log2(total)


def attend_current(queries, cur_keys, cur_values, sibling, heads):
    rows = queries.shape[0]
    keys = cur_keys.shape[0]
    return pl.pallas_call(
        functools.partial(current_kernel, 512),
        in_specs=[HBM] * 3 + [VMEM],
        out_specs=[VMEM] * 3,
        out_shape=[pltpu.VMEM((heads, rows, HD), F32)] * 2 + [pltpu.VMEM((rows, heads * HD), BF16)],
        scratch_shapes=[pltpu.VMEM((keys, heads * HD), BF16)] * 2 + [pltpu.SemaphoreType.DMA((3,))],
        compiler_params=params(),
        name="attend_current",
        cost_estimate=pl.CostEstimate(
            flops=60 * heads * rows * 2 * keys * HD, bytes_accessed=heads * rows * HD * 12, transcendentals=heads * rows * 2 * keys
        ),
    )(in_hbm(queries), in_hbm(cur_keys), in_hbm(cur_values), in_vmem(sibling))


def frames_kernel(heads, half_of, state_half_of, first, starts, final, bias, q, held, lse, *rest):
    frames = rest[: len(starts)]
    outs = rest[-1:] if final else rest[-2:]
    count, rows = len(starts), outs[0].shape[-2]

    def rows_of(half):
        return pl.ds(pl.multiple_of(half() * rows, rows), rows)

    span, state_span = rows_of(half_of), rows_of(state_half_of)
    mask = jnp.concatenate([bias[pl.ds(first + index, 1), :] for index in range(count)], axis=1)

    def gathered(head, part):
        columns = pl.ds(head * HD, HD)
        return jnp.concatenate(
            [frame[pl.ds(start + part * FT, FT), columns] for frame, start in zip(frames, starts)], axis=0
        )

    def scores_of(head):
        return dot_t(q[span, pl.ds(head * HD, HD)], gathered(head, 0))

    def finish(head, scores):
        scores = scores * EXP2_SCALE + mask
        old = lse[head, state_span, :]
        new_max = jnp.maximum(old, jnp.max(scores, axis=1, keepdims=True))
        weights = jnp.exp2(scores - wide(new_max, count * FT // HD)).astype(BF16)
        product = jnp.dot(weights, with_ones(gathered(head, 1)), preferred_element_type=F32)
        scale = jnp.exp2(old - new_max)
        total = scale + product[:, HD:]
        top = (held[head, state_span, :] * scale + product[:, :HD]) / total
        if final:
            outs[0][:, pl.ds(head * HD, HD)] = top.astype(BF16)
        else:
            outs[0][head] = top
            outs[1][head] = new_max + jnp.log2(total)

    scores = scores_of(0)
    for head in range(heads):
        following = scores_of(head + 1) if head + 1 < heads else None
        finish(head, scores)
        scores = following


def far_half():
    return 1 - lax.axis_index("head")


def near_half():
    return lax.axis_index("head")


def attend_frames(name, half, bias, first, q, held, lse, frames, starts, final, after=()):
    heads, state_rows, _ = held.shape
    rows = q.shape[0] // 2
    state_half = half if state_rows > rows else lambda: jnp.int32(0)
    operands = [bias, q, held, lse, *frames]
    if final:
        out_shape = [pltpu.VMEM((rows, heads * HD), BF16)]
    else:
        out_shape = [pltpu.VMEM((heads, rows, HD), F32)] * 2
    outs = pl.pallas_call(
        functools.partial(frames_kernel, heads, half, state_half, first, tuple(starts), final),
        in_specs=[VMEM] * len(operands) + [ANY] * len(after),
        out_specs=[VMEM] * len(out_shape),
        out_shape=out_shape,
        compiler_params=params(),
        name=name,
        cost_estimate=SHORT,
    )(*map(in_vmem, operands), *map(in_vmem, after))
    return outs[0] if final else outs


def both(mine, other):
    first, second = mine[...], other[...]
    return jnp.where(
        lax.axis_index("sub") == 0,
        jnp.concatenate([first, second], axis=1),
        jnp.concatenate([second, first], axis=1),
    )


def project_kernel(step, mine, other, weight, *rest):
    out = rest[-1]
    rows = both(mine, other)

    @pl.loop(0, out.shape[1] // step)
    def _(index):
        columns = pl.ds(pl.multiple_of(index * step, step), step)
        out[:, columns] = jnp.dot(rows, weight[:, columns], preferred_element_type=F32).astype(BF16)


def unshared_columns(low, share):
    return pl.ds(0, low), pl.ds(pl.multiple_of(low + quarter(True, True) * share, 128), share)


def unshared_kernel(low, mine, other, weight, *rest):
    out = rest[-1]
    rows = both(mine, other)
    start = 0
    for columns in unshared_columns(low, out.shape[1] - low):
        out[:, pl.ds(start, columns.size)] = jnp.dot(rows, weight[:, columns], preferred_element_type=F32).astype(BF16)
        start += columns.size


def project_call(kernel, name, mine, other, weight, width, after):
    return pl.pallas_call(
        kernel,
        in_specs=[VMEM] * 3 + [ANY] * len(after),
        out_specs=VMEM,
        out_shape=pltpu.VMEM((mine.shape[0], width), BF16),
        compiler_params=params(),
        name=name,
        cost_estimate=SHORT,
    )(*map(in_vmem, (mine, other, weight, *after)))


def project(mine, other, weight, after):
    return project_call(functools.partial(project_kernel, 512), "project", mine, other, weight, weight.shape[1], after)


def project_unshared(mine, other, weight, low, share, after):
    kernel = functools.partial(unshared_kernel, low)
    return project_call(kernel, "project_unshared", mine, other, weight, low + share, after)


def write_blocks(blocks, out, scratch, sems):
    copies, start = [], 0
    for index, (block, low) in enumerate(blocks):
        span = pl.ds(start, block.shape[1])
        scratch[:, span] = block.astype(BF16)
        copy = pltpu.make_async_copy(scratch.at[:, span], out.at[:, pl.ds(low, block.shape[1])], sems.at[index])
        copy.start()
        copies.append(copy)
        start += block.shape[1]
    for copy in copies:
        copy.wait()


def remote_kernel(first, other_seq, other_group, terms, mine, other, weight, total, out, scratch, sems):
    block = weight.shape[1]
    low = pl.multiple_of(first + quarter(other_seq, other_group) * block, 128)
    product = jnp.dot(both(mine, other), weight[...], preferred_element_type=F32)
    write_blocks([(terms[:, pl.ds(low, block)].astype(F32) + product, low)], out, scratch, sems)


def add_kernel(low, terms, came, total, out, scratch, sems):
    blocks, start = [], 0
    for columns in unshared_columns(low, came.shape[1] - low):
        block = terms[:, columns].astype(F32) + came[:, pl.ds(start, columns.size)].astype(F32)
        blocks.append((block, columns.start))
        start += columns.size
    write_blocks(blocks, out, scratch, sems)


def finish_block(kernel, name, operands, total, rows, width, block):
    count = len(operands)
    if total is None:
        body = lambda *refs: kernel(*refs[:count], None, *refs[count:])
        totals, aliases = [], {}
    else:
        body, totals, aliases = kernel, [in_hbm(total)], {count: 0}
    return pl.pallas_call(
        body,
        in_specs=[VMEM] * count + [HBM] * len(totals),
        out_specs=HBM,
        out_shape=pltpu.HBM((rows, width), BF16),
        input_output_aliases=aliases,
        scratch_shapes=[pltpu.VMEM((rows, block), BF16), pltpu.SemaphoreType.DMA((2,))],
        compiler_params=params(),
        name=name,
        cost_estimate=SHORT,
    )(*map(in_vmem, operands), *totals)


def add_remote(terms, mine, other, weight, first, other_seq, other_group, total):
    kernel = functools.partial(remote_kernel, first, other_seq, other_group)
    return finish_block(kernel, "add_remote", (terms, mine, other, weight), total, *terms.shape, weight.shape[1])


def add_unshared(terms, came, low, total):
    kernel = functools.partial(add_kernel, low)
    return finish_block(kernel, "add_unshared", (terms, came), total, *terms.shape, came.shape[1])


def local(queries, cur_keys, cur_values, mem_keys, mem_values, frame_ids, frame_counts, out_weight):
    seq_count = lax.axis_size("seq")
    heads = queries.shape[1] // HD // 2
    keys = cur_keys.shape[0]
    out_cols = out_weight.shape[1]
    share = out_cols // 5 // 128 * 128
    low = out_cols - 4 * share

    *sends, to_sibling = pack(frame_ids, mem_keys, mem_values, cur_keys, cur_values, seq_count)
    columns = pack_columns(out_weight, low, share, to_sibling)
    mine = [sends[0]]
    for shift in range(1, seq_count):
        pairs = [(index, (index + shift) % seq_count) for index in range(seq_count)]
        mine.append(lax.ppermute(sends[shift], "seq", pairs))
    columns = lax.ppermute(columns, "head", SWAP)
    sibling = lax.ppermute(to_sibling, "sub", SWAP)

    held, lse, q = attend_current(queries, cur_keys, cur_values, sibling, heads)
    weight, bias = load(frame_ids, frame_counts, out_weight, seq_count, lse)
    passed = pass_on(mine[1:], weight)
    theirs = lax.ppermute(passed, "sub", SWAP)
    others = [sibling] + [theirs] * (seq_count - 1)
    starts = [2 * keys] + [2 * FT * index for index in range(seq_count - 1)]

    state = attend_frames("far_first", far_half, bias, 0, q, held, lse, mine, [0] * seq_count, False, (passed,))
    far = attend_frames("far_last", far_half, bias, seq_count, q, *state, others, starts, True)
    came_mine = lax.ppermute(far, "head", SWAP)
    far_sibling = lax.ppermute(far, "sub", SWAP)
    group_columns = lax.ppermute(columns, "groups", SWAP)
    columns_copy = copied(columns, far)
    seq_columns = lax.ppermute(columns_copy, "seq", [(index, index ^ 1) for index in range(seq_count)])
    starts = [0] * seq_count + starts
    near = attend_frames("near", near_half, bias, 0, q, held, lse, mine + others, starts, True, (columns_copy,))
    near_sibling = lax.ppermute(near, "sub", SWAP)

    term = project_unshared(far, far_sibling, weight, low, share, (near,))
    came = lax.ppermute(term, "head", SWAP)
    came_mine = gate(came_mine, term)
    came_other = lax.ppermute(came_mine, "sub", SWAP)
    terms = project(near, near_sibling, weight, (came_mine,))

    arrived = (terms, came_mine, came_other)
    total = add_remote(*arrived, columns, low, False, False, None)
    total = add_remote(*arrived, group_columns, low, False, True, total)
    total = add_remote(*arrived, seq_columns, low, True, False, total)
    return add_unshared(terms, came, low, total)


def local_any(queries, cur_keys, cur_values, mem_keys, mem_values, frame_ids, frame_counts, out_weight):
    seq_count = lax.axis_size("seq")
    sub_count = lax.axis_size("sub")
    seq_index = lax.axis_index("seq")
    owner_self = seq_index * sub_count + lax.axis_index("sub")
    row_count, col_count = queries.shape
    heads = col_count // HD
    mine = row_count // sub_count
    wanted = jnp.sum(jnp.where(frame_ids // FR_DEV == owner_self, frame_ids, 0), axis=1) - owner_self * FR_DEV
    own_list = lax.dynamic_index_in_dim(frame_ids, seq_index, 0, keepdims=False)
    owners = jnp.arange(seq_count * sub_count, dtype=jnp.int32)
    hit = (own_list // FR_DEV)[None, :] == owners[:, None]
    got_ids = jnp.sum(jnp.where(hit, own_list[None, :], 0), axis=1).reshape(seq_count, sub_count).T.reshape(-1)
    live = jnp.arange(FT, dtype=jnp.int32)[None, :] < jnp.take(frame_counts, got_ids)[:, None]

    def spread(cached, current):
        sent = lax.all_to_all(jnp.take(cached, wanted, axis=0), "seq", split_axis=0, concat_axis=0, tiled=True)
        far = lax.all_gather(sent, "sub").reshape(-1, heads, HD)
        return jnp.concatenate([lax.all_gather(current, "sub").reshape(-1, heads, HD), far], axis=0)

    keys, values = spread(mem_keys, cur_keys), spread(mem_values, cur_values)
    key_live = jnp.concatenate([jnp.ones((keys.shape[0] - live.size,), bool), live.reshape(-1)])
    start = lax.axis_index("sub") * mine
    query_heads = lax.dynamic_slice_in_dim(queries, start, mine, 0).reshape(mine, heads, HD)
    scores = jnp.einsum("qhd,khd->hqk", query_heads, keys, preferred_element_type=F32) / math.sqrt(HD)
    scores = jnp.where(key_live[None, None, :], scores, -jnp.inf)
    expo = jnp.exp(scores - jnp.max(scores, axis=-1, keepdims=True))
    total = jnp.sum(expo, axis=-1)
    weighted = jnp.einsum("hqk,khd->qhd", expo.astype(BF16), values, preferred_element_type=F32)
    attended = (weighted / total.T[:, :, None]).reshape(mine, col_count).astype(BF16)
    attended = lax.all_gather(attended, "sub", axis=0, tiled=True)
    term = jnp.dot(attended, out_weight, preferred_element_type=F32).astype(BF16)
    return lax.psum_scatter(term, "head", scatter_dimension=0, tiled=True)


def solution(mesh):
    in_specs = (
        P(("groups", "seq"), "head"),
        P(("groups", "seq", "sub"), "head"),
        P(("groups", "seq", "sub"), "head"),
        P(("groups", "seq", "sub"), None, "head"),
        P(("groups", "seq", "sub"), None, "head"),
        P("groups", None),
        P("groups"),
        P("head", "sub"),
    )
    out_specs = P(("groups", "seq", "head"), "sub")

    def apply(queries, *rest):
        heads = queries.shape[1] // mesh.shape["head"] // HD
        paired = heads % 2 == 0 and mesh.shape["seq"] % 2 == 0
        paired = paired and all(mesh.shape[axis] == 2 for axis in ("groups", "head", "sub"))
        body = local if paired else local_any
        return jax.shard_map(body, mesh=mesh, in_specs=in_specs, out_specs=out_specs, check_vma=False)(queries, *rest)

    return apply
```

```python
import functools
import math

import jax
import jax.numpy as jnp
from jax import lax
from jax.experimental import pallas as pl
from jax.experimental.pallas import tpu as pltpu
from jax.sharding import PartitionSpec as P

HD = 128
FT = 64
FR_DEV = 16
F32 = jnp.float32
BF16 = jnp.bfloat16
EXP2_SCALE = math.log2(math.e) / math.sqrt(HD)
MASKED = -1e30
VMEM_LIMIT = 24 * 1024 * 1024
SWAP = [(0, 1), (1, 0)]
SHORT = pl.CostEstimate(flops=1024, bytes_accessed=1024, transcendentals=0)
ANY = pl.BlockSpec(memory_space=pl.ANY)
HBM = pl.BlockSpec(memory_space=pltpu.HBM)
VMEM = pl.BlockSpec(memory_space=pltpu.VMEM)


def params():
    return pltpu.CompilerParams(vmem_limit_bytes=VMEM_LIMIT)


def in_hbm(array):
    return pltpu.with_memory_space_constraint(array, pltpu.HBM)


def in_vmem(array):
    return pltpu.with_memory_space_constraint(array, pltpu.VMEM)


def quarter(other_seq, other_group):
    seq_part = lax.rem(lax.axis_index("seq"), 2)
    group = lax.axis_index("groups")
    return 2 * (1 - seq_part if other_seq else seq_part) + (1 - group if other_group else group)


def copy_all(pairs, sems):
    copies = [pltpu.make_async_copy(*pair, sems.at[index]) for index, pair in enumerate(pairs)]
    for copy in copies:
        copy.start()
    for copy in copies:
        copy.wait()


def held_by(ids, stretch, owner, count):
    found = jnp.int32(0)
    for entry in range(count):
        frame = ids[stretch, entry]
        slot = frame - owner * FR_DEV
        found = jnp.where((slot >= 0) & (slot < FR_DEV), frame, found)
    return found


def pack_kernel(seq_count, low, parts, ids_in, keys, values, cur_keys, cur_values, weight, *rest):
    outs = rest[:seq_count]
    sibling, columns_out, ids, sems = rest[seq_count:]
    seq_index = lax.axis_index("seq")
    sub_index = lax.axis_index("sub")
    width = sibling.shape[1]
    block = columns_out.shape[1]
    count = cur_keys.shape[0]
    frame_count = 2 * seq_count
    copies = []

    def start(source, target):
        copy = pltpu.make_async_copy(source, target, sems.at[len(copies)])
        copy.start()
        copies.append(copy)
        return copy

    def columns_of(half):
        return pl.ds(pl.multiple_of(half * width, 128), width)

    listed = start(ids_in, ids)
    rows = count // parts
    for part, source in enumerate((cur_keys, cur_values)):
        for low_row in range(0, count, rows):
            target = sibling.at[pl.ds(part * count + low_row, rows), :]
            start(source.at[pl.ds(low_row, rows), columns_of(1 - sub_index)], target)
    first = pl.multiple_of(low + quarter(False, False) * block, 128)
    rows = weight.shape[0] // parts
    for part in range(parts):
        span = pl.ds(part * rows, rows)
        start(weight.at[span, pl.ds(first, block)], columns_out.at[span, :])
    listed.wait()
    for shift, out in enumerate(outs):
        owner = seq_index * 2 + sub_index
        wanted = held_by(ids, lax.rem(seq_index + shift, seq_count), owner, frame_count) - owner * FR_DEV
        wanted = jnp.clip(wanted, 0, FR_DEV - 1)
        for turn in range(2):
            half = sub_index if turn == 0 else 1 - sub_index
            for part, source in enumerate((keys, values)):
                if shift == 0 and turn == 1:
                    target = sibling.at[pl.ds(2 * count + part * FT, FT), :]
                else:
                    target = out.at[pl.ds((2 * turn + part) * FT, FT), :]
                start(source.at[wanted, :, columns_of(half)], target)
    for copy in copies[1:]:
        copy.wait()


def pack(frame_ids, mem_keys, mem_values, cur_keys, cur_values, weight, low, share, seq_count):
    parts = 4
    width = mem_keys.shape[2] // 2
    rows = [2 * FT] + [4 * FT] * (seq_count - 1) + [2 * cur_keys.shape[0] + 2 * FT]
    shapes = [(count, width) for count in rows] + [(weight.shape[0], share)]
    return pl.pallas_call(
        functools.partial(pack_kernel, seq_count, low, parts),
        out_shape=[pltpu.VMEM(shape, BF16) for shape in shapes],
        in_specs=[HBM] * 6,
        out_specs=[VMEM] * len(shapes),
        scratch_shapes=[
            pltpu.SMEM(frame_ids.shape, jnp.int32),
            pltpu.SemaphoreType.DMA((1 + 4 * seq_count + 3 * parts,)),
        ],
        compiler_params=params(),
        name="pack",
        cost_estimate=pl.CostEstimate(flops=0, bytes_accessed=12 * 2**20, transcendentals=0),
    )(*map(in_hbm, (frame_ids, mem_keys, mem_values, cur_keys, cur_values, weight)))


def pass_on_kernel(*refs):
    arrays, out = refs[:-2], refs[-1]
    rows = out.shape[0] // len(arrays)
    for index, array in enumerate(arrays):
        out[pl.ds(index * rows, rows), :] = array[pl.ds(rows, rows), :]


def pass_on(arrays, after):
    rows, width = arrays[0].shape
    return pl.pallas_call(
        pass_on_kernel,
        out_shape=pltpu.VMEM((len(arrays) * rows // 2, width), BF16),
        in_specs=[VMEM] * len(arrays) + [ANY],
        out_specs=VMEM,
        compiler_params=params(),
        name="pass_on",
        cost_estimate=SHORT,
    )(*map(in_vmem, arrays), in_vmem(after))


def load_kernel(parts, seq_count, ids, counts, weight, after, out, mask, sems):
    rows = weight.shape[0] // parts
    spans = [pl.ds(part * rows, rows) for part in range(parts)]
    copies = [pltpu.make_async_copy(weight.at[span, :], out.at[span, :], sems.at[index]) for index, span in enumerate(spans)]
    for copy in copies:
        copy.start()
    seq_index = lax.axis_index("seq")
    sub_index = lax.axis_index("sub")
    slot = lax.broadcasted_iota(jnp.int32, (1, FT), 1)
    for index in range(2 * seq_count):
        turn, shift = divmod(index, seq_count)
        source = lax.rem(seq_index + seq_count - shift, seq_count) * 2
        owner = source + (sub_index if turn == 0 else 1 - sub_index)
        live = slot < counts[held_by(ids, seq_index, owner, 2 * seq_count)]
        mask[pl.ds(index, 1), :] = jnp.where(live, 0.0, MASKED).astype(F32)
    for copy in copies:
        copy.wait()


def load(frame_ids, frame_counts, weight, seq_count, after):
    parts = 8
    return pl.pallas_call(
        functools.partial(load_kernel, parts, seq_count),
        out_shape=[pltpu.VMEM(weight.shape, BF16), pltpu.VMEM((2 * seq_count, FT), F32)],
        in_specs=[pl.BlockSpec(memory_space=pltpu.SMEM)] * 2 + [HBM, ANY],
        out_specs=[VMEM, VMEM],
        scratch_shapes=[pltpu.SemaphoreType.DMA((parts,))],
        compiler_params=params(),
        name="load",
        cost_estimate=pl.CostEstimate(flops=0, bytes_accessed=2 * weight.size, transcendentals=0),
    )(*map(in_hbm, (frame_ids, frame_counts, weight)), in_vmem(after))


def gate(array, after):
    return pl.pallas_call(
        lambda *refs: None,
        in_specs=[ANY, ANY],
        out_specs=ANY,
        out_shape=jax.ShapeDtypeStruct(array.shape, array.dtype),
        input_output_aliases={0: 0},
        compiler_params=params(),
        name="gate",
        cost_estimate=SHORT,
    )(in_vmem(array), in_vmem(after))


def copied_kernel(array, after, out):
    out[...] = array[...]


def copied(array, after):
    return pl.pallas_call(
        copied_kernel,
        in_specs=[VMEM, ANY],
        out_specs=VMEM,
        out_shape=pltpu.VMEM(array.shape, array.dtype),
        compiler_params=params(),
        name="copied",
        cost_estimate=SHORT,
    )(in_vmem(array), in_vmem(after))


def dot_t(left, right):
    return lax.dot_general(left, right, (((1,), (1,)), ((), ())), preferred_element_type=F32)


def wide(column, count):
    return jnp.concatenate([column] * count, axis=1)


def with_ones(values):
    return jnp.concatenate([values, jnp.ones_like(values)], axis=1)


def current_kernel(step, queries, own_keys, own_values, sibling, out, lse, q, own_k, own_v, sems):
    heads, rows, _ = out.shape
    count = own_k.shape[0]
    half = pl.ds(pl.multiple_of(lax.axis_index("sub") * q.shape[1], 128), q.shape[1])
    copy_all(
        [(queries.at[:, half], q), (own_keys.at[:, half], own_k), (own_values.at[:, half], own_v)],
        sems,
    )

    @pl.loop(0, heads)
    def _(head):
        columns = pl.ds(pl.multiple_of(head * HD, HD), HD)
        keys = jnp.concatenate([own_k[:, columns], sibling[pl.ds(0, count), columns]], axis=0)
        values = with_ones(jnp.concatenate([own_v[:, columns], sibling[pl.ds(count, count), columns]], axis=0))
        for low in range(0, rows, step):
            span = pl.ds(low, step)
            scores = dot_t(q[span, columns], keys)
            row_max = jnp.broadcast_to(jnp.max(scores, axis=1, keepdims=True), (step, HD))
            weights = jnp.exp2((scores - wide(row_max, 2 * count // HD)) * EXP2_SCALE).astype(BF16)
            product = jnp.dot(weights, values, preferred_element_type=F32)
            total = product[:, HD:]
            out[head, span, :] = product[:, :HD] / total
            lse[head, span, :] = row_max * EXP2_SCALE + jnp.log2(total)


def attend_current(queries, cur_keys, cur_values, sibling, heads):
    rows = queries.shape[0]
    keys = cur_keys.shape[0]
    return pl.pallas_call(
        functools.partial(current_kernel, 512),
        in_specs=[HBM] * 3 + [VMEM],
        out_specs=[VMEM] * 3,
        out_shape=[pltpu.VMEM((heads, rows, HD), F32)] * 2 + [pltpu.VMEM((rows, heads * HD), BF16)],
        scratch_shapes=[pltpu.VMEM((keys, heads * HD), BF16)] * 2 + [pltpu.SemaphoreType.DMA((3,))],
        compiler_params=params(),
        name="attend_current",
        cost_estimate=pl.CostEstimate(
            flops=60 * heads * rows * 2 * keys * HD, bytes_accessed=heads * rows * HD * 12, transcendentals=heads * rows * 2 * keys
        ),
    )(in_hbm(queries), in_hbm(cur_keys), in_hbm(cur_values), in_vmem(sibling))


def frames_kernel(heads, half_of, state_half_of, first, starts, final, bias, q, held, lse, *rest):
    frames = rest[: len(starts)]
    outs = rest[-1:] if final else rest[-2:]
    count, rows = len(starts), outs[0].shape[-2]

    def rows_of(half):
        return pl.ds(pl.multiple_of(half() * rows, rows), rows)

    span, state_span = rows_of(half_of), rows_of(state_half_of)
    mask = jnp.concatenate([bias[pl.ds(first + index, 1), :] for index in range(count)], axis=1)

    def gathered(head, part):
        columns = pl.ds(head * HD, HD)
        return jnp.concatenate(
            [frame[pl.ds(start + part * FT, FT), columns] for frame, start in zip(frames, starts)], axis=0
        )

    def scores_of(head):
        return dot_t(q[span, pl.ds(head * HD, HD)], gathered(head, 0))

    def finish(head, scores):
        scores = scores * EXP2_SCALE + mask
        old = lse[head, state_span, :]
        new_max = jnp.maximum(old, jnp.max(scores, axis=1, keepdims=True))
        weights = jnp.exp2(scores - wide(new_max, count * FT // HD)).astype(BF16)
        product = jnp.dot(weights, with_ones(gathered(head, 1)), preferred_element_type=F32)
        scale = jnp.exp2(old - new_max)
        total = scale + product[:, HD:]
        top = (held[head, state_span, :] * scale + product[:, :HD]) / total
        if final:
            outs[0][:, pl.ds(head * HD, HD)] = top.astype(BF16)
        else:
            outs[0][head] = top
            outs[1][head] = new_max + jnp.log2(total)

    scores = scores_of(0)
    for head in range(heads):
        following = scores_of(head + 1) if head + 1 < heads else None
        finish(head, scores)
        scores = following


def far_half():
    return 1 - lax.axis_index("head")


def near_half():
    return lax.axis_index("head")


def attend_frames(name, half, bias, first, q, held, lse, frames, starts, final, after=()):
    heads, state_rows, _ = held.shape
    rows = q.shape[0] // 2
    state_half = half if state_rows > rows else lambda: jnp.int32(0)
    operands = [bias, q, held, lse, *frames]
    if final:
        out_shape = [pltpu.VMEM((rows, heads * HD), BF16)]
    else:
        out_shape = [pltpu.VMEM((heads, rows, HD), F32)] * 2
    outs = pl.pallas_call(
        functools.partial(frames_kernel, heads, half, state_half, first, tuple(starts), final),
        in_specs=[VMEM] * len(operands) + [ANY] * len(after),
        out_specs=[VMEM] * len(out_shape),
        out_shape=out_shape,
        compiler_params=params(),
        name=name,
        cost_estimate=SHORT,
    )(*map(in_vmem, operands), *map(in_vmem, after))
    return outs[0] if final else outs


def both(mine, other):
    first, second = mine[...], other[...]
    return jnp.where(
        lax.axis_index("sub") == 0,
        jnp.concatenate([first, second], axis=1),
        jnp.concatenate([second, first], axis=1),
    )


def project_kernel(step, mine, other, weight, *rest):
    out = rest[-1]
    rows = both(mine, other)

    @pl.loop(0, out.shape[1] // step)
    def _(index):
        columns = pl.ds(pl.multiple_of(index * step, step), step)
        out[:, columns] = jnp.dot(rows, weight[:, columns], preferred_element_type=F32).astype(BF16)


def unshared_columns(low, share):
    return pl.ds(0, low), pl.ds(pl.multiple_of(low + quarter(True, True) * share, 128), share)


def unshared_kernel(low, mine, other, weight, *rest):
    out = rest[-1]
    rows = both(mine, other)
    start = 0
    for columns in unshared_columns(low, out.shape[1] - low):
        out[:, pl.ds(start, columns.size)] = jnp.dot(rows, weight[:, columns], preferred_element_type=F32).astype(BF16)
        start += columns.size


def project_call(kernel, name, mine, other, weight, width, after):
    return pl.pallas_call(
        kernel,
        in_specs=[VMEM] * 3 + [ANY] * len(after),
        out_specs=VMEM,
        out_shape=pltpu.VMEM((mine.shape[0], width), BF16),
        compiler_params=params(),
        name=name,
        cost_estimate=SHORT,
    )(*map(in_vmem, (mine, other, weight, *after)))


def project(mine, other, weight, after):
    return project_call(functools.partial(project_kernel, 512), "project", mine, other, weight, weight.shape[1], after)


def project_unshared(mine, other, weight, low, share, after):
    kernel = functools.partial(unshared_kernel, low)
    return project_call(kernel, "project_unshared", mine, other, weight, low + share, after)


def write_blocks(blocks, out, scratch, sems):
    copies, start = [], 0
    for index, (block, low) in enumerate(blocks):
        span = pl.ds(start, block.shape[1])
        scratch[:, span] = block.astype(BF16)
        copy = pltpu.make_async_copy(scratch.at[:, span], out.at[:, pl.ds(low, block.shape[1])], sems.at[index])
        copy.start()
        copies.append(copy)
        start += block.shape[1]
    for copy in copies:
        copy.wait()


def remote_kernel(first, other_seq, other_group, terms, mine, other, weight, total, out, scratch, sems):
    block = weight.shape[1]
    low = pl.multiple_of(first + quarter(other_seq, other_group) * block, 128)
    product = jnp.dot(both(mine, other), weight[...], preferred_element_type=F32)
    write_blocks([(terms[:, pl.ds(low, block)].astype(F32) + product, low)], out, scratch, sems)


def add_kernel(low, terms, came, total, out, scratch, sems):
    blocks, start = [], 0
    for columns in unshared_columns(low, came.shape[1] - low):
        block = terms[:, columns].astype(F32) + came[:, pl.ds(start, columns.size)].astype(F32)
        blocks.append((block, columns.start))
        start += columns.size
    write_blocks(blocks, out, scratch, sems)


def finish_block(kernel, name, operands, total, rows, width, block):
    count = len(operands)
    if total is None:
        body = lambda *refs: kernel(*refs[:count], None, *refs[count:])
        totals, aliases = [], {}
    else:
        body, totals, aliases = kernel, [in_hbm(total)], {count: 0}
    return pl.pallas_call(
        body,
        in_specs=[VMEM] * count + [HBM] * len(totals),
        out_specs=HBM,
        out_shape=pltpu.HBM((rows, width), BF16),
        input_output_aliases=aliases,
        scratch_shapes=[pltpu.VMEM((rows, block), BF16), pltpu.SemaphoreType.DMA((2,))],
        compiler_params=params(),
        name=name,
        cost_estimate=SHORT,
    )(*map(in_vmem, operands), *totals)


def add_remote(terms, mine, other, weight, first, other_seq, other_group, total):
    kernel = functools.partial(remote_kernel, first, other_seq, other_group)
    return finish_block(kernel, "add_remote", (terms, mine, other, weight), total, *terms.shape, weight.shape[1])


def add_unshared(terms, came, low, total):
    kernel = functools.partial(add_kernel, low)
    return finish_block(kernel, "add_unshared", (terms, came), total, *terms.shape, came.shape[1])


def local(queries, cur_keys, cur_values, mem_keys, mem_values, frame_ids, frame_counts, out_weight):
    seq_count = lax.axis_size("seq")
    heads = queries.shape[1] // HD // 2
    keys = cur_keys.shape[0]
    out_cols = out_weight.shape[1]
    share = out_cols // 5 // 128 * 128
    low = out_cols - 4 * share

    *sends, to_sibling, columns = pack(
        frame_ids, mem_keys, mem_values, cur_keys, cur_values, out_weight, low, share, seq_count
    )
    mine = [sends[0]]
    for shift in range(1, seq_count):
        pairs = [(index, (index + shift) % seq_count) for index in range(seq_count)]
        mine.append(lax.ppermute(sends[shift], "seq", pairs))
    columns = lax.ppermute(columns, "head", SWAP)
    sibling = lax.ppermute(to_sibling, "sub", SWAP)

    held, lse, q = attend_current(queries, cur_keys, cur_values, sibling, heads)
    weight, bias = load(frame_ids, frame_counts, out_weight, seq_count, lse)
    passed = pass_on(mine[1:], weight)
    theirs = lax.ppermute(passed, "sub", SWAP)
    others = [sibling] + [theirs] * (seq_count - 1)
    starts = [2 * keys] + [2 * FT * index for index in range(seq_count - 1)]

    state = attend_frames("far_first", far_half, bias, 0, q, held, lse, mine, [0] * seq_count, False, (passed,))
    far = attend_frames("far_last", far_half, bias, seq_count, q, *state, others, starts, True)
    came_mine = lax.ppermute(far, "head", SWAP)
    far_sibling = lax.ppermute(far, "sub", SWAP)
    group_columns = lax.ppermute(columns, "groups", SWAP)
    columns_copy = copied(columns, far)
    seq_columns = lax.ppermute(columns_copy, "seq", [(index, index ^ 1) for index in range(seq_count)])
    starts = [0] * seq_count + starts
    near = attend_frames("near", near_half, bias, 0, q, held, lse, mine + others, starts, True, (columns_copy,))
    near_sibling = lax.ppermute(near, "sub", SWAP)

    term = project_unshared(far, far_sibling, weight, low, share, (near,))
    came = lax.ppermute(term, "head", SWAP)
    came_mine = gate(came_mine, term)
    came_other = lax.ppermute(came_mine, "sub", SWAP)
    terms = project(near, near_sibling, weight, (came_mine,))

    arrived = (terms, came_mine, came_other)
    total = add_remote(*arrived, columns, low, False, False, None)
    total = add_remote(*arrived, group_columns, low, False, True, total)
    total = add_remote(*arrived, seq_columns, low, True, False, total)
    return add_unshared(terms, came, low, total)


def local_any(queries, cur_keys, cur_values, mem_keys, mem_values, frame_ids, frame_counts, out_weight):
    seq_count = lax.axis_size("seq")
    sub_count = lax.axis_size("sub")
    seq_index = lax.axis_index("seq")
    owner_self = seq_index * sub_count + lax.axis_index("sub")
    row_count, col_count = queries.shape
    heads = col_count // HD
    mine = row_count // sub_count
    wanted = jnp.sum(jnp.where(frame_ids // FR_DEV == owner_self, frame_ids, 0), axis=1) - owner_self * FR_DEV
    own_list = lax.dynamic_index_in_dim(frame_ids, seq_index, 0, keepdims=False)
    owners = jnp.arange(seq_count * sub_count, dtype=jnp.int32)
    hit = (own_list // FR_DEV)[None, :] == owners[:, None]
    got_ids = jnp.sum(jnp.where(hit, own_list[None, :], 0), axis=1).reshape(seq_count, sub_count).T.reshape(-1)
    live = jnp.arange(FT, dtype=jnp.int32)[None, :] < jnp.take(frame_counts, got_ids)[:, None]

    def spread(cached, current):
        sent = lax.all_to_all(jnp.take(cached, wanted, axis=0), "seq", split_axis=0, concat_axis=0, tiled=True)
        far = lax.all_gather(sent, "sub").reshape(-1, heads, HD)
        return jnp.concatenate([lax.all_gather(current, "sub").reshape(-1, heads, HD), far], axis=0)

    keys, values = spread(mem_keys, cur_keys), spread(mem_values, cur_values)
    key_live = jnp.concatenate([jnp.ones((keys.shape[0] - live.size,), bool), live.reshape(-1)])
    start = lax.axis_index("sub") * mine
    query_heads = lax.dynamic_slice_in_dim(queries, start, mine, 0).reshape(mine, heads, HD)
    scores = jnp.einsum("qhd,khd->hqk", query_heads, keys, preferred_element_type=F32) / math.sqrt(HD)
    scores = jnp.where(key_live[None, None, :], scores, -jnp.inf)
    expo = jnp.exp(scores - jnp.max(scores, axis=-1, keepdims=True))
    total = jnp.sum(expo, axis=-1)
    weighted = jnp.einsum("hqk,khd->qhd", expo.astype(BF16), values, preferred_element_type=F32)
    attended = (weighted / total.T[:, :, None]).reshape(mine, col_count).astype(BF16)
    attended = lax.all_gather(attended, "sub", axis=0, tiled=True)
    term = jnp.dot(attended, out_weight, preferred_element_type=F32).astype(BF16)
    return lax.psum_scatter(term, "head", scatter_dimension=0, tiled=True)


def solution(mesh):
    in_specs = (
        P(("groups", "seq"), "head"),
        P(("groups", "seq", "sub"), "head"),
        P(("groups", "seq", "sub"), "head"),
        P(("groups", "seq", "sub"), None, "head"),
        P(("groups", "seq", "sub"), None, "head"),
        P("groups", None),
        P("groups"),
        P("head", "sub"),
    )
    out_specs = P(("groups", "seq", "head"), "sub")

    def apply(queries, *rest):
        heads = queries.shape[1] // mesh.shape["head"] // HD
        paired = heads % 2 == 0 and mesh.shape["seq"] % 2 == 0
        paired = paired and all(mesh.shape[axis] == 2 for axis in ("groups", "head", "sub"))
        body = local if paired else local_any
        return jax.shard_map(body, mesh=mesh, in_specs=in_specs, out_specs=out_specs, check_vma=False)(queries, *rest)

    return apply
```

```python
import functools
import math

import jax
import jax.numpy as jnp
from jax import lax
from jax.experimental import pallas as pl
from jax.experimental.pallas import tpu as pltpu
from jax.sharding import PartitionSpec as P

HD = 128
FT = 64
FR_DEV = 16
F32 = jnp.float32
BF16 = jnp.bfloat16
EXP2_SCALE = math.log2(math.e) / math.sqrt(HD)
MASKED = -1e30
VMEM_LIMIT = 24 * 1024 * 1024
SWAP = [(0, 1), (1, 0)]
SHORT = pl.CostEstimate(flops=1024, bytes_accessed=1024, transcendentals=0)
ANY = pl.BlockSpec(memory_space=pl.ANY)
HBM = pl.BlockSpec(memory_space=pltpu.HBM)
VMEM = pl.BlockSpec(memory_space=pltpu.VMEM)


def params():
    return pltpu.CompilerParams(vmem_limit_bytes=VMEM_LIMIT)


def in_hbm(array):
    return pltpu.with_memory_space_constraint(array, pltpu.HBM)


def in_vmem(array):
    return pltpu.with_memory_space_constraint(array, pltpu.VMEM)


def quarter(other_seq, other_group):
    seq_part = lax.rem(lax.axis_index("seq"), 2)
    group = lax.axis_index("groups")
    return 2 * (1 - seq_part if other_seq else seq_part) + (1 - group if other_group else group)


def copy_all(pairs, sems):
    copies = [pltpu.make_async_copy(*pair, sems.at[index]) for index, pair in enumerate(pairs)]
    for copy in copies:
        copy.start()
    for copy in copies:
        copy.wait()


def exchange_order(seq_count):
    return [0, *range(seq_count - 1, 0, -1)]


def held_by(ids, stretch, owner, count):
    found = jnp.int32(0)
    for entry in range(count):
        frame = ids[stretch, entry]
        slot = frame - owner * FR_DEV
        found = jnp.where((slot >= 0) & (slot < FR_DEV), frame, found)
    return found


def pack_kernel(seq_count, low, parts, ids_in, keys, values, cur_keys, cur_values, weight, *rest):
    outs = rest[:seq_count]
    sibling, columns_out, ids, sems = rest[seq_count:]
    seq_index = lax.axis_index("seq")
    sub_index = lax.axis_index("sub")
    width = sibling.shape[1]
    block = columns_out.shape[1]
    count = cur_keys.shape[0]
    frame_count = 2 * seq_count
    copies = []

    def start(source, target):
        copy = pltpu.make_async_copy(source, target, sems.at[len(copies)])
        copy.start()
        copies.append(copy)
        return copy

    def columns_of(half):
        return pl.ds(pl.multiple_of(half * width, 128), width)

    listed = start(ids_in, ids)
    rows = count // parts
    for part, source in enumerate((cur_keys, cur_values)):
        for low_row in range(0, count, rows):
            target = sibling.at[pl.ds(part * count + low_row, rows), :]
            start(source.at[pl.ds(low_row, rows), columns_of(1 - sub_index)], target)
    first = pl.multiple_of(low + quarter(False, False) * block, 128)
    rows = weight.shape[0] // parts
    for part in range(parts):
        span = pl.ds(part * rows, rows)
        start(weight.at[span, pl.ds(first, block)], columns_out.at[span, :])
    listed.wait()
    for flip, out in zip(exchange_order(seq_count), outs):
        owner = seq_index * 2 + sub_index
        wanted = held_by(ids, lax.bitwise_xor(seq_index, flip), owner, frame_count) - owner * FR_DEV
        wanted = jnp.clip(wanted, 0, FR_DEV - 1)
        for turn in range(2):
            half = sub_index if turn == 0 else 1 - sub_index
            for part, source in enumerate((keys, values)):
                if flip == 0 and turn == 1:
                    target = sibling.at[pl.ds(2 * count + part * FT, FT), :]
                else:
                    target = out.at[pl.ds((2 * turn + part) * FT, FT), :]
                start(source.at[wanted, :, columns_of(half)], target)
    for copy in copies[1:]:
        copy.wait()


def pack(frame_ids, mem_keys, mem_values, cur_keys, cur_values, weight, low, share, seq_count):
    parts = 4
    width = mem_keys.shape[2] // 2
    rows = [2 * FT] + [4 * FT] * (seq_count - 1) + [2 * cur_keys.shape[0] + 2 * FT]
    shapes = [(count, width) for count in rows] + [(weight.shape[0], share)]
    return pl.pallas_call(
        functools.partial(pack_kernel, seq_count, low, parts),
        out_shape=[pltpu.VMEM(shape, BF16) for shape in shapes],
        in_specs=[HBM] * 6,
        out_specs=[VMEM] * len(shapes),
        scratch_shapes=[
            pltpu.SMEM(frame_ids.shape, jnp.int32),
            pltpu.SemaphoreType.DMA((1 + 4 * seq_count + 3 * parts,)),
        ],
        compiler_params=params(),
        name="pack",
        cost_estimate=pl.CostEstimate(flops=0, bytes_accessed=12 * 2**20, transcendentals=0),
    )(*map(in_hbm, (frame_ids, mem_keys, mem_values, cur_keys, cur_values, weight)))


def pass_on_kernel(*refs):
    arrays, out = refs[:-2], refs[-1]
    rows = out.shape[0] // len(arrays)
    for index, array in enumerate(arrays):
        out[pl.ds(index * rows, rows), :] = array[pl.ds(rows, rows), :]


def pass_on(arrays, after):
    rows, width = arrays[0].shape
    return pl.pallas_call(
        pass_on_kernel,
        out_shape=pltpu.VMEM((len(arrays) * rows // 2, width), BF16),
        in_specs=[VMEM] * len(arrays) + [ANY],
        out_specs=VMEM,
        compiler_params=params(),
        name="pass_on",
        cost_estimate=SHORT,
    )(*map(in_vmem, arrays), in_vmem(after))


def load_kernel(parts, seq_count, ids, counts, weight, after, out, mask, sems):
    rows = weight.shape[0] // parts
    spans = [pl.ds(part * rows, rows) for part in range(parts)]
    copies = [pltpu.make_async_copy(weight.at[span, :], out.at[span, :], sems.at[index]) for index, span in enumerate(spans)]
    for copy in copies:
        copy.start()
    seq_index = lax.axis_index("seq")
    sub_index = lax.axis_index("sub")
    slot = lax.broadcasted_iota(jnp.int32, (1, FT), 1)
    for index in range(2 * seq_count):
        turn, place = divmod(index, seq_count)
        source = lax.bitwise_xor(seq_index, exchange_order(seq_count)[place]) * 2
        owner = source + (sub_index if turn == 0 else 1 - sub_index)
        live = slot < counts[held_by(ids, seq_index, owner, 2 * seq_count)]
        mask[pl.ds(index, 1), :] = jnp.where(live, 0.0, MASKED).astype(F32)
    for copy in copies:
        copy.wait()


def load(frame_ids, frame_counts, weight, seq_count, after):
    parts = 8
    return pl.pallas_call(
        functools.partial(load_kernel, parts, seq_count),
        out_shape=[pltpu.VMEM(weight.shape, BF16), pltpu.VMEM((2 * seq_count, FT), F32)],
        in_specs=[pl.BlockSpec(memory_space=pltpu.SMEM)] * 2 + [HBM, ANY],
        out_specs=[VMEM, VMEM],
        scratch_shapes=[pltpu.SemaphoreType.DMA((parts,))],
        compiler_params=params(),
        name="load",
        cost_estimate=pl.CostEstimate(flops=0, bytes_accessed=2 * weight.size, transcendentals=0),
    )(*map(in_hbm, (frame_ids, frame_counts, weight)), in_vmem(after))


def gate(array, after):
    return pl.pallas_call(
        lambda *refs: None,
        in_specs=[ANY, ANY],
        out_specs=ANY,
        out_shape=jax.ShapeDtypeStruct(array.shape, array.dtype),
        input_output_aliases={0: 0},
        compiler_params=params(),
        name="gate",
        cost_estimate=SHORT,
    )(in_vmem(array), in_vmem(after))


def copied_kernel(array, after, out):
    out[...] = array[...]


def copied(array, after):
    return pl.pallas_call(
        copied_kernel,
        in_specs=[VMEM, ANY],
        out_specs=VMEM,
        out_shape=pltpu.VMEM(array.shape, array.dtype),
        compiler_params=params(),
        name="copied",
        cost_estimate=SHORT,
    )(in_vmem(array), in_vmem(after))


def dot_t(left, right):
    return lax.dot_general(left, right, (((1,), (1,)), ((), ())), preferred_element_type=F32)


def wide(column, count):
    return jnp.concatenate([column] * count, axis=1)


def with_ones(values):
    return jnp.concatenate([values, jnp.ones_like(values)], axis=1)


def current_kernel(step, queries, own_keys, own_values, sibling, out, lse, q, own_k, own_v, sems):
    heads, rows, _ = out.shape
    count = own_k.shape[0]
    half = pl.ds(pl.multiple_of(lax.axis_index("sub") * q.shape[1], 128), q.shape[1])
    copy_all(
        [(queries.at[:, half], q), (own_keys.at[:, half], own_k), (own_values.at[:, half], own_v)],
        sems,
    )

    @pl.loop(0, heads)
    def _(head):
        columns = pl.ds(pl.multiple_of(head * HD, HD), HD)
        keys = jnp.concatenate([own_k[:, columns], sibling[pl.ds(0, count), columns]], axis=0)
        values = with_ones(jnp.concatenate([own_v[:, columns], sibling[pl.ds(count, count), columns]], axis=0))
        for low in range(0, rows, step):
            span = pl.ds(low, step)
            scores = dot_t(q[span, columns], keys)
            row_max = jnp.broadcast_to(jnp.max(scores, axis=1, keepdims=True), (step, HD))
            weights = jnp.exp2((scores - wide(row_max, 2 * count // HD)) * EXP2_SCALE).astype(BF16)
            product = jnp.dot(weights, values, preferred_element_type=F32)
            total = product[:, HD:]
            out[head, span, :] = product[:, :HD] / total
            lse[head, span, :] = row_max * EXP2_SCALE + jnp.log2(total)


def attend_current(queries, cur_keys, cur_values, sibling, heads):
    rows = queries.shape[0]
    keys = cur_keys.shape[0]
    return pl.pallas_call(
        functools.partial(current_kernel, 512),
        in_specs=[HBM] * 3 + [VMEM],
        out_specs=[VMEM] * 3,
        out_shape=[pltpu.VMEM((heads, rows, HD), F32)] * 2 + [pltpu.VMEM((rows, heads * HD), BF16)],
        scratch_shapes=[pltpu.VMEM((keys, heads * HD), BF16)] * 2 + [pltpu.SemaphoreType.DMA((3,))],
        compiler_params=params(),
        name="attend_current",
        cost_estimate=pl.CostEstimate(
            flops=60 * heads * rows * 2 * keys * HD, bytes_accessed=heads * rows * HD * 12, transcendentals=heads * rows * 2 * keys
        ),
    )(in_hbm(queries), in_hbm(cur_keys), in_hbm(cur_values), in_vmem(sibling))


def frames_kernel(heads, half_of, state_half_of, first, starts, final, bias, q, held, lse, *rest):
    frames = rest[: len(starts)]
    outs = rest[-1:] if final else rest[-2:]
    count, rows = len(starts), outs[0].shape[-2]

    def rows_of(half):
        return pl.ds(pl.multiple_of(half() * rows, rows), rows)

    span, state_span = rows_of(half_of), rows_of(state_half_of)
    mask = jnp.concatenate([bias[pl.ds(first + index, 1), :] for index in range(count)], axis=1)

    def gathered(head, part):
        columns = pl.ds(head * HD, HD)
        return jnp.concatenate(
            [frame[pl.ds(start + part * FT, FT), columns] for frame, start in zip(frames, starts)], axis=0
        )

    def scores_of(head):
        return dot_t(q[span, pl.ds(head * HD, HD)], gathered(head, 0))

    def finish(head, scores):
        scores = scores * EXP2_SCALE + mask
        old = lse[head, state_span, :]
        new_max = jnp.maximum(old, jnp.max(scores, axis=1, keepdims=True))
        weights = jnp.exp2(scores - wide(new_max, count * FT // HD)).astype(BF16)
        product = jnp.dot(weights, with_ones(gathered(head, 1)), preferred_element_type=F32)
        scale = jnp.exp2(old - new_max)
        total = scale + product[:, HD:]
        top = (held[head, state_span, :] * scale + product[:, :HD]) / total
        if final:
            outs[0][:, pl.ds(head * HD, HD)] = top.astype(BF16)
        else:
            outs[0][head] = top
            outs[1][head] = new_max + jnp.log2(total)

    scores = scores_of(0)
    for head in range(heads):
        following = scores_of(head + 1) if head + 1 < heads else None
        finish(head, scores)
        scores = following


def far_half():
    return 1 - lax.axis_index("head")


def near_half():
    return lax.axis_index("head")


def attend_frames(name, half, bias, first, q, held, lse, frames, starts, final, after=()):
    heads, state_rows, _ = held.shape
    rows = q.shape[0] // 2
    state_half = half if state_rows > rows else lambda: jnp.int32(0)
    operands = [bias, q, held, lse, *frames]
    if final:
        out_shape = [pltpu.VMEM((rows, heads * HD), BF16)]
    else:
        out_shape = [pltpu.VMEM((heads, rows, HD), F32)] * 2
    outs = pl.pallas_call(
        functools.partial(frames_kernel, heads, half, state_half, first, tuple(starts), final),
        in_specs=[VMEM] * len(operands) + [ANY] * len(after),
        out_specs=[VMEM] * len(out_shape),
        out_shape=out_shape,
        compiler_params=params(),
        name=name,
        cost_estimate=SHORT,
    )(*map(in_vmem, operands), *map(in_vmem, after))
    return outs[0] if final else outs


def both(mine, other):
    first, second = mine[...], other[...]
    return jnp.where(
        lax.axis_index("sub") == 0,
        jnp.concatenate([first, second], axis=1),
        jnp.concatenate([second, first], axis=1),
    )


def project_kernel(step, mine, other, weight, *rest):
    out = rest[-1]
    rows = both(mine, other)

    @pl.loop(0, out.shape[1] // step)
    def _(index):
        columns = pl.ds(pl.multiple_of(index * step, step), step)
        out[:, columns] = jnp.dot(rows, weight[:, columns], preferred_element_type=F32).astype(BF16)


def unshared_columns(low, share):
    return pl.ds(0, low), pl.ds(pl.multiple_of(low + quarter(True, True) * share, 128), share)


def unshared_kernel(low, mine, other, weight, *rest):
    out = rest[-1]
    rows = both(mine, other)
    start = 0
    for columns in unshared_columns(low, out.shape[1] - low):
        out[:, pl.ds(start, columns.size)] = jnp.dot(rows, weight[:, columns], preferred_element_type=F32).astype(BF16)
        start += columns.size


def project_call(kernel, name, mine, other, weight, width, after):
    return pl.pallas_call(
        kernel,
        in_specs=[VMEM] * 3 + [ANY] * len(after),
        out_specs=VMEM,
        out_shape=pltpu.VMEM((mine.shape[0], width), BF16),
        compiler_params=params(),
        name=name,
        cost_estimate=SHORT,
    )(*map(in_vmem, (mine, other, weight, *after)))


def project(mine, other, weight, after):
    return project_call(functools.partial(project_kernel, 512), "project", mine, other, weight, weight.shape[1], after)


def project_unshared(mine, other, weight, low, share, after):
    kernel = functools.partial(unshared_kernel, low)
    return project_call(kernel, "project_unshared", mine, other, weight, low + share, after)


def write_blocks(blocks, out, scratch, sems):
    copies, start = [], 0
    for index, (block, low) in enumerate(blocks):
        span = pl.ds(start, block.shape[1])
        scratch[:, span] = block.astype(BF16)
        copy = pltpu.make_async_copy(scratch.at[:, span], out.at[:, pl.ds(low, block.shape[1])], sems.at[index])
        copy.start()
        copies.append(copy)
        start += block.shape[1]
    for copy in copies:
        copy.wait()


def remote_kernel(first, other_seq, other_group, terms, mine, other, weight, total, out, scratch, sems):
    block = weight.shape[1]
    low = pl.multiple_of(first + quarter(other_seq, other_group) * block, 128)
    product = jnp.dot(both(mine, other), weight[...], preferred_element_type=F32)
    write_blocks([(terms[:, pl.ds(low, block)].astype(F32) + product, low)], out, scratch, sems)


def add_kernel(low, terms, came, total, out, scratch, sems):
    blocks, start = [], 0
    for columns in unshared_columns(low, came.shape[1] - low):
        block = terms[:, columns].astype(F32) + came[:, pl.ds(start, columns.size)].astype(F32)
        blocks.append((block, columns.start))
        start += columns.size
    write_blocks(blocks, out, scratch, sems)


def finish_block(kernel, name, operands, total, rows, width, block):
    count = len(operands)
    if total is None:
        body = lambda *refs: kernel(*refs[:count], None, *refs[count:])
        totals, aliases = [], {}
    else:
        body, totals, aliases = kernel, [in_hbm(total)], {count: 0}
    return pl.pallas_call(
        body,
        in_specs=[VMEM] * count + [HBM] * len(totals),
        out_specs=HBM,
        out_shape=pltpu.HBM((rows, width), BF16),
        input_output_aliases=aliases,
        scratch_shapes=[pltpu.VMEM((rows, block), BF16), pltpu.SemaphoreType.DMA((2,))],
        compiler_params=params(),
        name=name,
        cost_estimate=SHORT,
    )(*map(in_vmem, operands), *totals)


def add_remote(terms, mine, other, weight, first, other_seq, other_group, total):
    kernel = functools.partial(remote_kernel, first, other_seq, other_group)
    return finish_block(kernel, "add_remote", (terms, mine, other, weight), total, *terms.shape, weight.shape[1])


def add_unshared(terms, came, low, total):
    kernel = functools.partial(add_kernel, low)
    return finish_block(kernel, "add_unshared", (terms, came), total, *terms.shape, came.shape[1])


def local(queries, cur_keys, cur_values, mem_keys, mem_values, frame_ids, frame_counts, out_weight):
    seq_count = lax.axis_size("seq")
    heads = queries.shape[1] // HD // 2
    keys = cur_keys.shape[0]
    out_cols = out_weight.shape[1]
    share = out_cols // 5 // 128 * 128
    low = out_cols - 4 * share

    *sends, to_sibling, columns = pack(
        frame_ids, mem_keys, mem_values, cur_keys, cur_values, out_weight, low, share, seq_count
    )
    mine = [sends[0]]
    for flip, sent in list(zip(exchange_order(seq_count), sends))[1:]:
        mine.append(lax.ppermute(sent, "seq", [(index, index ^ flip) for index in range(seq_count)]))
    columns = lax.ppermute(columns, "head", SWAP)
    sibling = lax.ppermute(to_sibling, "sub", SWAP)

    held, lse, q = attend_current(queries, cur_keys, cur_values, sibling, heads)
    weight, bias = load(frame_ids, frame_counts, out_weight, seq_count, lse)
    passed = pass_on(mine[1:], weight)
    theirs = lax.ppermute(passed, "sub", SWAP)
    others = [sibling] + [theirs] * (seq_count - 1)
    starts = [2 * keys] + [2 * FT * index for index in range(seq_count - 1)]

    state = attend_frames("far_first", far_half, bias, 0, q, held, lse, mine, [0] * seq_count, False, (passed,))
    far = attend_frames("far_last", far_half, bias, seq_count, q, *state, others, starts, True)
    came_mine = lax.ppermute(far, "head", SWAP)
    far_sibling = lax.ppermute(far, "sub", SWAP)
    group_columns = lax.ppermute(columns, "groups", SWAP)
    columns_copy = copied(columns, far)
    seq_columns = lax.ppermute(columns_copy, "seq", [(index, index ^ 1) for index in range(seq_count)])
    starts = [0] * seq_count + starts
    near = attend_frames("near", near_half, bias, 0, q, held, lse, mine + others, starts, True, (columns_copy,))
    near_sibling = lax.ppermute(near, "sub", SWAP)

    term = project_unshared(far, far_sibling, weight, low, share, (near,))
    came = lax.ppermute(term, "head", SWAP)
    came_mine = gate(came_mine, term)
    came_other = lax.ppermute(came_mine, "sub", SWAP)
    terms = project(near, near_sibling, weight, (came_mine,))

    arrived = (terms, came_mine, came_other)
    total = add_remote(*arrived, columns, low, False, False, None)
    total = add_remote(*arrived, group_columns, low, False, True, total)
    total = add_remote(*arrived, seq_columns, low, True, False, total)
    return add_unshared(terms, came, low, total)


def local_any(queries, cur_keys, cur_values, mem_keys, mem_values, frame_ids, frame_counts, out_weight):
    seq_count = lax.axis_size("seq")
    sub_count = lax.axis_size("sub")
    seq_index = lax.axis_index("seq")
    owner_self = seq_index * sub_count + lax.axis_index("sub")
    row_count, col_count = queries.shape
    heads = col_count // HD
    mine = row_count // sub_count
    wanted = jnp.sum(jnp.where(frame_ids // FR_DEV == owner_self, frame_ids, 0), axis=1) - owner_self * FR_DEV
    own_list = lax.dynamic_index_in_dim(frame_ids, seq_index, 0, keepdims=False)
    owners = jnp.arange(seq_count * sub_count, dtype=jnp.int32)
    hit = (own_list // FR_DEV)[None, :] == owners[:, None]
    got_ids = jnp.sum(jnp.where(hit, own_list[None, :], 0), axis=1).reshape(seq_count, sub_count).T.reshape(-1)
    live = jnp.arange(FT, dtype=jnp.int32)[None, :] < jnp.take(frame_counts, got_ids)[:, None]

    def spread(cached, current):
        sent = lax.all_to_all(jnp.take(cached, wanted, axis=0), "seq", split_axis=0, concat_axis=0, tiled=True)
        far = lax.all_gather(sent, "sub").reshape(-1, heads, HD)
        return jnp.concatenate([lax.all_gather(current, "sub").reshape(-1, heads, HD), far], axis=0)

    keys, values = spread(mem_keys, cur_keys), spread(mem_values, cur_values)
    key_live = jnp.concatenate([jnp.ones((keys.shape[0] - live.size,), bool), live.reshape(-1)])
    start = lax.axis_index("sub") * mine
    query_heads = lax.dynamic_slice_in_dim(queries, start, mine, 0).reshape(mine, heads, HD)
    scores = jnp.einsum("qhd,khd->hqk", query_heads, keys, preferred_element_type=F32) / math.sqrt(HD)
    scores = jnp.where(key_live[None, None, :], scores, -jnp.inf)
    expo = jnp.exp(scores - jnp.max(scores, axis=-1, keepdims=True))
    total = jnp.sum(expo, axis=-1)
    weighted = jnp.einsum("hqk,khd->qhd", expo.astype(BF16), values, preferred_element_type=F32)
    attended = (weighted / total.T[:, :, None]).reshape(mine, col_count).astype(BF16)
    attended = lax.all_gather(attended, "sub", axis=0, tiled=True)
    term = jnp.dot(attended, out_weight, preferred_element_type=F32).astype(BF16)
    return lax.psum_scatter(term, "head", scatter_dimension=0, tiled=True)


def solution(mesh):
    in_specs = (
        P(("groups", "seq"), "head"),
        P(("groups", "seq", "sub"), "head"),
        P(("groups", "seq", "sub"), "head"),
        P(("groups", "seq", "sub"), None, "head"),
        P(("groups", "seq", "sub"), None, "head"),
        P("groups", None),
        P("groups"),
        P("head", "sub"),
    )
    out_specs = P(("groups", "seq", "head"), "sub")

    def apply(queries, *rest):
        heads = queries.shape[1] // mesh.shape["head"] // HD
        paired = heads % 2 == 0 and mesh.shape["seq"] in (2, 4, 8)
        paired = paired and all(mesh.shape[axis] == 2 for axis in ("groups", "head", "sub"))
        body = local if paired else local_any
        return jax.shard_map(body, mesh=mesh, in_specs=in_specs, out_specs=out_specs, check_vma=False)(queries, *rest)

    return apply
```

```python
import functools
import math

import jax
import jax.numpy as jnp
from jax import lax
from jax.experimental import pallas as pl
from jax.experimental.pallas import tpu as pltpu
from jax.sharding import PartitionSpec as P

HD = 128
FT = 64
FR_DEV = 16
F32 = jnp.float32
BF16 = jnp.bfloat16
EXP2_SCALE = math.log2(math.e) / math.sqrt(HD)
MASKED = -1e30
VMEM_LIMIT = 24 * 1024 * 1024
SWAP = [(0, 1), (1, 0)]
SHORT = pl.CostEstimate(flops=1024, bytes_accessed=1024, transcendentals=0)
ANY = pl.BlockSpec(memory_space=pl.ANY)
HBM = pl.BlockSpec(memory_space=pltpu.HBM)
VMEM = pl.BlockSpec(memory_space=pltpu.VMEM)


def params():
    return pltpu.CompilerParams(vmem_limit_bytes=VMEM_LIMIT)


def in_hbm(array):
    return pltpu.with_memory_space_constraint(array, pltpu.HBM)


def in_vmem(array):
    return pltpu.with_memory_space_constraint(array, pltpu.VMEM)


def quarter(other_seq, other_group):
    seq_part = lax.rem(lax.axis_index("seq"), 2)
    group = lax.axis_index("groups")
    return 2 * (1 - seq_part if other_seq else seq_part) + (1 - group if other_group else group)


def copy_all(pairs, sems):
    copies = [pltpu.make_async_copy(*pair, sems.at[index]) for index, pair in enumerate(pairs)]
    for copy in copies:
        copy.start()
    for copy in copies:
        copy.wait()


def exchange_order(seq_count):
    return [0, *range(seq_count // 2, seq_count), *range(1, seq_count // 2)]


def held_by(ids, stretch, owner, count):
    found = jnp.int32(0)
    for entry in range(count):
        frame = ids[stretch, entry]
        slot = frame - owner * FR_DEV
        found = jnp.where((slot >= 0) & (slot < FR_DEV), frame, found)
    return found


def pack_kernel(seq_count, low, parts, ids_in, keys, values, cur_keys, cur_values, weight, *rest):
    outs = rest[:seq_count]
    sibling, columns_out, ids, sems = rest[seq_count:]
    seq_index = lax.axis_index("seq")
    sub_index = lax.axis_index("sub")
    width = sibling.shape[1]
    block = columns_out.shape[1]
    count = cur_keys.shape[0]
    frame_count = 2 * seq_count
    copies = []

    def start(source, target):
        copy = pltpu.make_async_copy(source, target, sems.at[len(copies)])
        copy.start()
        copies.append(copy)
        return copy

    def columns_of(half):
        return pl.ds(pl.multiple_of(half * width, 128), width)

    listed = start(ids_in, ids)
    rows = count // parts
    for part, source in enumerate((cur_keys, cur_values)):
        for low_row in range(0, count, rows):
            target = sibling.at[pl.ds(part * count + low_row, rows), :]
            start(source.at[pl.ds(low_row, rows), columns_of(1 - sub_index)], target)
    first = pl.multiple_of(low + quarter(False, False) * block, 128)
    rows = weight.shape[0] // parts
    for part in range(parts):
        span = pl.ds(part * rows, rows)
        start(weight.at[span, pl.ds(first, block)], columns_out.at[span, :])
    listed.wait()
    for flip, out in zip(exchange_order(seq_count), outs):
        owner = seq_index * 2 + sub_index
        wanted = held_by(ids, lax.bitwise_xor(seq_index, flip), owner, frame_count) - owner * FR_DEV
        wanted = jnp.clip(wanted, 0, FR_DEV - 1)
        for turn in range(2):
            half = sub_index if turn == 0 else 1 - sub_index
            for part, source in enumerate((keys, values)):
                if flip == 0 and turn == 1:
                    target = sibling.at[pl.ds(2 * count + part * FT, FT), :]
                else:
                    target = out.at[pl.ds((2 * turn + part) * FT, FT), :]
                start(source.at[wanted, :, columns_of(half)], target)
    for copy in copies[1:]:
        copy.wait()


def pack(frame_ids, mem_keys, mem_values, cur_keys, cur_values, weight, low, share, seq_count):
    parts = 4
    width = mem_keys.shape[2] // 2
    rows = [2 * FT] + [4 * FT] * (seq_count - 1) + [2 * cur_keys.shape[0] + 2 * FT]
    shapes = [(count, width) for count in rows] + [(weight.shape[0], share)]
    return pl.pallas_call(
        functools.partial(pack_kernel, seq_count, low, parts),
        out_shape=[pltpu.VMEM(shape, BF16) for shape in shapes],
        in_specs=[HBM] * 6,
        out_specs=[VMEM] * len(shapes),
        scratch_shapes=[
            pltpu.SMEM(frame_ids.shape, jnp.int32),
            pltpu.SemaphoreType.DMA((1 + 4 * seq_count + 3 * parts,)),
        ],
        compiler_params=params(),
        name="pack",
        cost_estimate=pl.CostEstimate(flops=0, bytes_accessed=12 * 2**20, transcendentals=0),
    )(*map(in_hbm, (frame_ids, mem_keys, mem_values, cur_keys, cur_values, weight)))


def pass_on_kernel(*refs):
    arrays, out = refs[:-2], refs[-1]
    rows = out.shape[0] // len(arrays)
    for index, array in enumerate(arrays):
        out[pl.ds(index * rows, rows), :] = array[pl.ds(rows, rows), :]


def pass_on(arrays, after):
    rows, width = arrays[0].shape
    return pl.pallas_call(
        pass_on_kernel,
        out_shape=pltpu.VMEM((len(arrays) * rows // 2, width), BF16),
        in_specs=[VMEM] * len(arrays) + [ANY],
        out_specs=VMEM,
        compiler_params=params(),
        name="pass_on",
        cost_estimate=SHORT,
    )(*map(in_vmem, arrays), in_vmem(after))


def load_kernel(parts, seq_count, ids, counts, weight, after, out, mask, sems):
    rows = weight.shape[0] // parts
    spans = [pl.ds(part * rows, rows) for part in range(parts)]
    copies = [pltpu.make_async_copy(weight.at[span, :], out.at[span, :], sems.at[index]) for index, span in enumerate(spans)]
    for copy in copies:
        copy.start()
    seq_index = lax.axis_index("seq")
    sub_index = lax.axis_index("sub")
    slot = lax.broadcasted_iota(jnp.int32, (1, FT), 1)
    for index in range(2 * seq_count):
        turn, place = divmod(index, seq_count)
        source = lax.bitwise_xor(seq_index, exchange_order(seq_count)[place]) * 2
        owner = source + (sub_index if turn == 0 else 1 - sub_index)
        live = slot < counts[held_by(ids, seq_index, owner, 2 * seq_count)]
        mask[pl.ds(index, 1), :] = jnp.where(live, 0.0, MASKED).astype(F32)
    for copy in copies:
        copy.wait()


def load(frame_ids, frame_counts, weight, seq_count, after):
    parts = 8
    return pl.pallas_call(
        functools.partial(load_kernel, parts, seq_count),
        out_shape=[pltpu.VMEM(weight.shape, BF16), pltpu.VMEM((2 * seq_count, FT), F32)],
        in_specs=[pl.BlockSpec(memory_space=pltpu.SMEM)] * 2 + [HBM, ANY],
        out_specs=[VMEM, VMEM],
        scratch_shapes=[pltpu.SemaphoreType.DMA((parts,))],
        compiler_params=params(),
        name="load",
        cost_estimate=pl.CostEstimate(flops=0, bytes_accessed=2 * weight.size, transcendentals=0),
    )(*map(in_hbm, (frame_ids, frame_counts, weight)), in_vmem(after))


def gate(array, after):
    return pl.pallas_call(
        lambda *refs: None,
        in_specs=[ANY, ANY],
        out_specs=ANY,
        out_shape=jax.ShapeDtypeStruct(array.shape, array.dtype),
        input_output_aliases={0: 0},
        compiler_params=params(),
        name="gate",
        cost_estimate=SHORT,
    )(in_vmem(array), in_vmem(after))


def copied_kernel(array, after, out):
    out[...] = array[...]


def copied(array, after):
    return pl.pallas_call(
        copied_kernel,
        in_specs=[VMEM, ANY],
        out_specs=VMEM,
        out_shape=pltpu.VMEM(array.shape, array.dtype),
        compiler_params=params(),
        name="copied",
        cost_estimate=SHORT,
    )(in_vmem(array), in_vmem(after))


def dot_t(left, right):
    return lax.dot_general(left, right, (((1,), (1,)), ((), ())), preferred_element_type=F32)


def wide(column, count):
    return jnp.concatenate([column] * count, axis=1)


def with_ones(values):
    return jnp.concatenate([values, jnp.ones_like(values)], axis=1)


def current_kernel(step, queries, own_keys, own_values, sibling, out, lse, q, own_k, own_v, sems):
    heads, rows, _ = out.shape
    count = own_k.shape[0]
    half = pl.ds(pl.multiple_of(lax.axis_index("sub") * q.shape[1], 128), q.shape[1])
    copy_all(
        [(queries.at[:, half], q), (own_keys.at[:, half], own_k), (own_values.at[:, half], own_v)],
        sems,
    )

    @pl.loop(0, heads)
    def _(head):
        columns = pl.ds(pl.multiple_of(head * HD, HD), HD)
        keys = jnp.concatenate([own_k[:, columns], sibling[pl.ds(0, count), columns]], axis=0)
        values = with_ones(jnp.concatenate([own_v[:, columns], sibling[pl.ds(count, count), columns]], axis=0))
        for low in range(0, rows, step):
            span = pl.ds(low, step)
            scores = dot_t(q[span, columns], keys)
            row_max = jnp.broadcast_to(jnp.max(scores, axis=1, keepdims=True), (step, HD))
            weights = jnp.exp2((scores - wide(row_max, 2 * count // HD)) * EXP2_SCALE).astype(BF16)
            product = jnp.dot(weights, values, preferred_element_type=F32)
            total = product[:, HD:]
            out[head, span, :] = product[:, :HD] / total
            lse[head, span, :] = row_max * EXP2_SCALE + jnp.log2(total)


def attend_current(queries, cur_keys, cur_values, sibling, heads):
    rows = queries.shape[0]
    keys = cur_keys.shape[0]
    return pl.pallas_call(
        functools.partial(current_kernel, 512),
        in_specs=[HBM] * 3 + [VMEM],
        out_specs=[VMEM] * 3,
        out_shape=[pltpu.VMEM((heads, rows, HD), F32)] * 2 + [pltpu.VMEM((rows, heads * HD), BF16)],
        scratch_shapes=[pltpu.VMEM((keys, heads * HD), BF16)] * 2 + [pltpu.SemaphoreType.DMA((3,))],
        compiler_params=params(),
        name="attend_current",
        cost_estimate=pl.CostEstimate(
            flops=60 * heads * rows * 2 * keys * HD, bytes_accessed=heads * rows * HD * 12, transcendentals=heads * rows * 2 * keys
        ),
    )(in_hbm(queries), in_hbm(cur_keys), in_hbm(cur_values), in_vmem(sibling))


def frames_kernel(heads, half_of, state_half_of, first, starts, final, bias, q, held, lse, *rest):
    frames = rest[: len(starts)]
    outs = rest[-1:] if final else rest[-2:]
    count, rows = len(starts), outs[0].shape[-2]

    def rows_of(half):
        return pl.ds(pl.multiple_of(half() * rows, rows), rows)

    span, state_span = rows_of(half_of), rows_of(state_half_of)
    mask = jnp.concatenate([bias[pl.ds(first + index, 1), :] for index in range(count)], axis=1)

    def gathered(head, part):
        columns = pl.ds(head * HD, HD)
        return jnp.concatenate(
            [frame[pl.ds(start + part * FT, FT), columns] for frame, start in zip(frames, starts)], axis=0
        )

    def scores_of(head):
        return dot_t(q[span, pl.ds(head * HD, HD)], gathered(head, 0))

    def finish(head, scores):
        scores = scores * EXP2_SCALE + mask
        old = lse[head, state_span, :]
        new_max = jnp.maximum(old, jnp.max(scores, axis=1, keepdims=True))
        weights = jnp.exp2(scores - wide(new_max, count * FT // HD)).astype(BF16)
        product = jnp.dot(weights, with_ones(gathered(head, 1)), preferred_element_type=F32)
        scale = jnp.exp2(old - new_max)
        total = scale + product[:, HD:]
        top = (held[head, state_span, :] * scale + product[:, :HD]) / total
        if final:
            outs[0][:, pl.ds(head * HD, HD)] = top.astype(BF16)
        else:
            outs[0][head] = top
            outs[1][head] = new_max + jnp.log2(total)

    scores = scores_of(0)
    for head in range(heads):
        following = scores_of(head + 1) if head + 1 < heads else None
        finish(head, scores)
        scores = following


def far_half():
    return 1 - lax.axis_index("head")


def near_half():
    return lax.axis_index("head")


def attend_frames(name, half, bias, first, q, held, lse, frames, starts, final, after=()):
    heads, state_rows, _ = held.shape
    rows = q.shape[0] // 2
    state_half = half if state_rows > rows else lambda: jnp.int32(0)
    operands = [bias, q, held, lse, *frames]
    if final:
        out_shape = [pltpu.VMEM((rows, heads * HD), BF16)]
    else:
        out_shape = [pltpu.VMEM((heads, rows, HD), F32)] * 2
    outs = pl.pallas_call(
        functools.partial(frames_kernel, heads, half, state_half, first, tuple(starts), final),
        in_specs=[VMEM] * len(operands) + [ANY] * len(after),
        out_specs=[VMEM] * len(out_shape),
        out_shape=out_shape,
        compiler_params=params(),
        name=name,
        cost_estimate=SHORT,
    )(*map(in_vmem, operands), *map(in_vmem, after))
    return outs[0] if final else outs


def both(mine, other):
    first, second = mine[...], other[...]
    return jnp.where(
        lax.axis_index("sub") == 0,
        jnp.concatenate([first, second], axis=1),
        jnp.concatenate([second, first], axis=1),
    )


def project_kernel(step, mine, other, weight, *rest):
    out = rest[-1]
    rows = both(mine, other)

    @pl.loop(0, out.shape[1] // step)
    def _(index):
        columns = pl.ds(pl.multiple_of(index * step, step), step)
        out[:, columns] = jnp.dot(rows, weight[:, columns], preferred_element_type=F32).astype(BF16)


def unshared_columns(low, share):
    return pl.ds(0, low), pl.ds(pl.multiple_of(low + quarter(True, True) * share, 128), share)


def unshared_kernel(low, mine, other, weight, *rest):
    out = rest[-1]
    rows = both(mine, other)
    start = 0
    for columns in unshared_columns(low, out.shape[1] - low):
        out[:, pl.ds(start, columns.size)] = jnp.dot(rows, weight[:, columns], preferred_element_type=F32).astype(BF16)
        start += columns.size


def project_call(kernel, name, mine, other, weight, width, after):
    return pl.pallas_call(
        kernel,
        in_specs=[VMEM] * 3 + [ANY] * len(after),
        out_specs=VMEM,
        out_shape=pltpu.VMEM((mine.shape[0], width), BF16),
        compiler_params=params(),
        name=name,
        cost_estimate=SHORT,
    )(*map(in_vmem, (mine, other, weight, *after)))


def project(mine, other, weight, after):
    return project_call(functools.partial(project_kernel, 512), "project", mine, other, weight, weight.shape[1], after)


def project_unshared(mine, other, weight, low, share, after):
    kernel = functools.partial(unshared_kernel, low)
    return project_call(kernel, "project_unshared", mine, other, weight, low + share, after)


def write_blocks(blocks, out, scratch, sems):
    copies, start = [], 0
    for index, (block, low) in enumerate(blocks):
        span = pl.ds(start, block.shape[1])
        scratch[:, span] = block.astype(BF16)
        copy = pltpu.make_async_copy(scratch.at[:, span], out.at[:, pl.ds(low, block.shape[1])], sems.at[index])
        copy.start()
        copies.append(copy)
        start += block.shape[1]
    for copy in copies:
        copy.wait()


def remote_kernel(first, other_seq, other_group, terms, mine, other, weight, total, out, scratch, sems):
    block = weight.shape[1]
    low = pl.multiple_of(first + quarter(other_seq, other_group) * block, 128)
    product = jnp.dot(both(mine, other), weight[...], preferred_element_type=F32)
    write_blocks([(terms[:, pl.ds(low, block)].astype(F32) + product, low)], out, scratch, sems)


def add_kernel(low, terms, came, total, out, scratch, sems):
    blocks, start = [], 0
    for columns in unshared_columns(low, came.shape[1] - low):
        block = terms[:, columns].astype(F32) + came[:, pl.ds(start, columns.size)].astype(F32)
        blocks.append((block, columns.start))
        start += columns.size
    write_blocks(blocks, out, scratch, sems)


def finish_block(kernel, name, operands, total, rows, width, block):
    count = len(operands)
    if total is None:
        body = lambda *refs: kernel(*refs[:count], None, *refs[count:])
        totals, aliases = [], {}
    else:
        body, totals, aliases = kernel, [in_hbm(total)], {count: 0}
    return pl.pallas_call(
        body,
        in_specs=[VMEM] * count + [HBM] * len(totals),
        out_specs=HBM,
        out_shape=pltpu.HBM((rows, width), BF16),
        input_output_aliases=aliases,
        scratch_shapes=[pltpu.VMEM((rows, block), BF16), pltpu.SemaphoreType.DMA((2,))],
        compiler_params=params(),
        name=name,
        cost_estimate=SHORT,
    )(*map(in_vmem, operands), *totals)


def add_remote(terms, mine, other, weight, first, other_seq, other_group, total):
    kernel = functools.partial(remote_kernel, first, other_seq, other_group)
    return finish_block(kernel, "add_remote", (terms, mine, other, weight), total, *terms.shape, weight.shape[1])


def add_unshared(terms, came, low, total):
    kernel = functools.partial(add_kernel, low)
    return finish_block(kernel, "add_unshared", (terms, came), total, *terms.shape, came.shape[1])


def local(queries, cur_keys, cur_values, mem_keys, mem_values, frame_ids, frame_counts, out_weight):
    seq_count = lax.axis_size("seq")
    heads = queries.shape[1] // HD // 2
    keys = cur_keys.shape[0]
    out_cols = out_weight.shape[1]
    share = out_cols // 5 // 128 * 128
    low = out_cols - 4 * share

    *sends, to_sibling, columns = pack(
        frame_ids, mem_keys, mem_values, cur_keys, cur_values, out_weight, low, share, seq_count
    )
    mine = [sends[0]]
    for flip, sent in list(zip(exchange_order(seq_count), sends))[1:]:
        mine.append(lax.ppermute(sent, "seq", [(index, index ^ flip) for index in range(seq_count)]))
    columns = lax.ppermute(columns, "head", SWAP)
    sibling = lax.ppermute(to_sibling, "sub", SWAP)

    held, lse, q = attend_current(queries, cur_keys, cur_values, sibling, heads)
    weight, bias = load(frame_ids, frame_counts, out_weight, seq_count, lse)
    passed = pass_on(mine[1:], weight)
    theirs = lax.ppermute(passed, "sub", SWAP)
    others = [sibling] + [theirs] * (seq_count - 1)
    starts = [2 * keys] + [2 * FT * index for index in range(seq_count - 1)]

    state = attend_frames("far_first", far_half, bias, 0, q, held, lse, mine, [0] * seq_count, False, (passed,))
    far = attend_frames("far_last", far_half, bias, seq_count, q, *state, others, starts, True)
    came_mine = lax.ppermute(far, "head", SWAP)
    far_sibling = lax.ppermute(far, "sub", SWAP)
    group_columns = lax.ppermute(columns, "groups", SWAP)
    columns_copy = copied(columns, far)
    seq_columns = lax.ppermute(columns_copy, "seq", [(index, index ^ 1) for index in range(seq_count)])
    starts = [0] * seq_count + starts
    near = attend_frames("near", near_half, bias, 0, q, held, lse, mine + others, starts, True, (columns_copy,))
    near_sibling = lax.ppermute(near, "sub", SWAP)

    term = project_unshared(far, far_sibling, weight, low, share, (near,))
    came = lax.ppermute(term, "head", SWAP)
    came_mine = gate(came_mine, term)
    came_other = lax.ppermute(came_mine, "sub", SWAP)
    terms = project(near, near_sibling, weight, (came_mine,))

    arrived = (terms, came_mine, came_other)
    total = add_remote(*arrived, columns, low, False, False, None)
    total = add_remote(*arrived, group_columns, low, False, True, total)
    total = add_remote(*arrived, seq_columns, low, True, False, total)
    return add_unshared(terms, came, low, total)


def local_any(queries, cur_keys, cur_values, mem_keys, mem_values, frame_ids, frame_counts, out_weight):
    seq_count = lax.axis_size("seq")
    sub_count = lax.axis_size("sub")
    seq_index = lax.axis_index("seq")
    owner_self = seq_index * sub_count + lax.axis_index("sub")
    row_count, col_count = queries.shape
    heads = col_count // HD
    mine = row_count // sub_count
    wanted = jnp.sum(jnp.where(frame_ids // FR_DEV == owner_self, frame_ids, 0), axis=1) - owner_self * FR_DEV
    own_list = lax.dynamic_index_in_dim(frame_ids, seq_index, 0, keepdims=False)
    owners = jnp.arange(seq_count * sub_count, dtype=jnp.int32)
    hit = (own_list // FR_DEV)[None, :] == owners[:, None]
    got_ids = jnp.sum(jnp.where(hit, own_list[None, :], 0), axis=1).reshape(seq_count, sub_count).T.reshape(-1)
    live = jnp.arange(FT, dtype=jnp.int32)[None, :] < jnp.take(frame_counts, got_ids)[:, None]

    def spread(cached, current):
        sent = lax.all_to_all(jnp.take(cached, wanted, axis=0), "seq", split_axis=0, concat_axis=0, tiled=True)
        far = lax.all_gather(sent, "sub").reshape(-1, heads, HD)
        return jnp.concatenate([lax.all_gather(current, "sub").reshape(-1, heads, HD), far], axis=0)

    keys, values = spread(mem_keys, cur_keys), spread(mem_values, cur_values)
    key_live = jnp.concatenate([jnp.ones((keys.shape[0] - live.size,), bool), live.reshape(-1)])
    start = lax.axis_index("sub") * mine
    query_heads = lax.dynamic_slice_in_dim(queries, start, mine, 0).reshape(mine, heads, HD)
    scores = jnp.einsum("qhd,khd->hqk", query_heads, keys, preferred_element_type=F32) / math.sqrt(HD)
    scores = jnp.where(key_live[None, None, :], scores, -jnp.inf)
    expo = jnp.exp(scores - jnp.max(scores, axis=-1, keepdims=True))
    total = jnp.sum(expo, axis=-1)
    weighted = jnp.einsum("hqk,khd->qhd", expo.astype(BF16), values, preferred_element_type=F32)
    attended = (weighted / total.T[:, :, None]).reshape(mine, col_count).astype(BF16)
    attended = lax.all_gather(attended, "sub", axis=0, tiled=True)
    term = jnp.dot(attended, out_weight, preferred_element_type=F32).astype(BF16)
    return lax.psum_scatter(term, "head", scatter_dimension=0, tiled=True)


def solution(mesh):
    in_specs = (
        P(("groups", "seq"), "head"),
        P(("groups", "seq", "sub"), "head"),
        P(("groups", "seq", "sub"), "head"),
        P(("groups", "seq", "sub"), None, "head"),
        P(("groups", "seq", "sub"), None, "head"),
        P("groups", None),
        P("groups"),
        P("head", "sub"),
    )
    out_specs = P(("groups", "seq", "head"), "sub")

    def apply(queries, *rest):
        heads = queries.shape[1] // mesh.shape["head"] // HD
        paired = heads % 2 == 0 and mesh.shape["seq"] in (2, 4, 8)
        paired = paired and all(mesh.shape[axis] == 2 for axis in ("groups", "head", "sub"))
        body = local if paired else local_any
        return jax.shard_map(body, mesh=mesh, in_specs=in_specs, out_specs=out_specs, check_vma=False)(queries, *rest)

    return apply
```

```python
import functools
import math

import jax
import jax.numpy as jnp
from jax import lax
from jax.experimental import pallas as pl
from jax.experimental.pallas import tpu as pltpu
from jax.sharding import PartitionSpec as P

HD = 128
FT = 64
FR_DEV = 16
F32 = jnp.float32
BF16 = jnp.bfloat16
EXP2_SCALE = math.log2(math.e) / math.sqrt(HD)
MASKED = -1e30
VMEM_LIMIT = 24 * 1024 * 1024
SWAP = [(0, 1), (1, 0)]
SHORT = pl.CostEstimate(flops=1024, bytes_accessed=1024, transcendentals=0)
ANY = pl.BlockSpec(memory_space=pl.ANY)
HBM = pl.BlockSpec(memory_space=pltpu.HBM)
VMEM = pl.BlockSpec(memory_space=pltpu.VMEM)


def params():
    return pltpu.CompilerParams(vmem_limit_bytes=VMEM_LIMIT)


def in_hbm(array):
    return pltpu.with_memory_space_constraint(array, pltpu.HBM)


def in_vmem(array):
    return pltpu.with_memory_space_constraint(array, pltpu.VMEM)


def quarter(other_seq, other_group):
    seq_part = lax.rem(lax.axis_index("seq"), 2)
    group = lax.axis_index("groups")
    return 2 * (1 - seq_part if other_seq else seq_part) + (1 - group if other_group else group)


def copy_all(pairs, sems):
    copies = [pltpu.make_async_copy(*pair, sems.at[index]) for index, pair in enumerate(pairs)]
    for copy in copies:
        copy.start()
    for copy in copies:
        copy.wait()


def exchange_order(seq_count):
    return [0, *range(seq_count // 2, seq_count), *range(1, seq_count // 2)]


def held_by(ids, stretch, owner, count):
    found = jnp.int32(0)
    for entry in range(count):
        frame = ids[stretch, entry]
        slot = frame - owner * FR_DEV
        found = jnp.where((slot >= 0) & (slot < FR_DEV), frame, found)
    return found


def pack_kernel(seq_count, low, parts, ids_in, keys, values, cur_keys, cur_values, weight, *rest):
    outs = rest[:seq_count]
    sibling, columns_out, ids, sems = rest[seq_count:]
    seq_index = lax.axis_index("seq")
    sub_index = lax.axis_index("sub")
    width = sibling.shape[1]
    block = columns_out.shape[1]
    count = cur_keys.shape[0]
    frame_count = 2 * seq_count
    copies = []

    def start(source, target):
        copy = pltpu.make_async_copy(source, target, sems.at[len(copies)])
        copy.start()
        copies.append(copy)
        return copy

    def columns_of(half):
        return pl.ds(pl.multiple_of(half * width, 128), width)

    listed = start(ids_in, ids)
    rows = count // parts
    for part, source in enumerate((cur_keys, cur_values)):
        for low_row in range(0, count, rows):
            target = sibling.at[pl.ds(part * count + low_row, rows), :]
            start(source.at[pl.ds(low_row, rows), columns_of(1 - sub_index)], target)
    first = pl.multiple_of(low + quarter(False, False) * block, 128)
    rows = weight.shape[0] // parts
    for part in range(parts):
        span = pl.ds(part * rows, rows)
        start(weight.at[span, pl.ds(first, block)], columns_out.at[span, :])
    listed.wait()
    for flip, out in zip(exchange_order(seq_count), outs):
        owner = seq_index * 2 + sub_index
        wanted = held_by(ids, lax.bitwise_xor(seq_index, flip), owner, frame_count) - owner * FR_DEV
        wanted = jnp.clip(wanted, 0, FR_DEV - 1)
        for turn in range(2):
            half = sub_index if turn == 0 else 1 - sub_index
            for part, source in enumerate((keys, values)):
                if flip == 0 and turn == 1:
                    target = sibling.at[pl.ds(2 * count + part * FT, FT), :]
                else:
                    target = out.at[pl.ds((2 * turn + part) * FT, FT), :]
                start(source.at[wanted, :, columns_of(half)], target)
    for copy in copies[1:]:
        copy.wait()


def pack(frame_ids, mem_keys, mem_values, cur_keys, cur_values, weight, low, share, seq_count):
    parts = 4
    width = mem_keys.shape[2] // 2
    rows = [2 * FT] + [4 * FT] * (seq_count - 1) + [2 * cur_keys.shape[0] + 2 * FT]
    shapes = [(count, width) for count in rows] + [(weight.shape[0], share)]
    return pl.pallas_call(
        functools.partial(pack_kernel, seq_count, low, parts),
        out_shape=[pltpu.VMEM(shape, BF16) for shape in shapes],
        in_specs=[HBM] * 6,
        out_specs=[VMEM] * len(shapes),
        scratch_shapes=[
            pltpu.SMEM(frame_ids.shape, jnp.int32),
            pltpu.SemaphoreType.DMA((1 + 4 * seq_count + 3 * parts,)),
        ],
        compiler_params=params(),
        name="pack",
        cost_estimate=pl.CostEstimate(flops=0, bytes_accessed=12 * 2**20, transcendentals=0),
    )(*map(in_hbm, (frame_ids, mem_keys, mem_values, cur_keys, cur_values, weight)))


def pass_on_kernel(*refs):
    arrays, out = refs[:-2], refs[-1]
    rows = out.shape[0] // len(arrays)
    for index, array in enumerate(arrays):
        out[pl.ds(index * rows, rows), :] = array[pl.ds(rows, rows), :]


def pass_on(arrays, after):
    rows, width = arrays[0].shape
    return pl.pallas_call(
        pass_on_kernel,
        out_shape=pltpu.VMEM((len(arrays) * rows // 2, width), BF16),
        in_specs=[VMEM] * len(arrays) + [ANY],
        out_specs=VMEM,
        compiler_params=params(),
        name="pass_on",
        cost_estimate=SHORT,
    )(*map(in_vmem, arrays), in_vmem(after))


def load_kernel(parts, seq_count, ids, counts, weight, after, out, mask, sems):
    rows = weight.shape[0] // parts
    spans = [pl.ds(part * rows, rows) for part in range(parts)]
    copies = [pltpu.make_async_copy(weight.at[span, :], out.at[span, :], sems.at[index]) for index, span in enumerate(spans)]
    for copy in copies:
        copy.start()
    seq_index = lax.axis_index("seq")
    sub_index = lax.axis_index("sub")
    slot = lax.broadcasted_iota(jnp.int32, (1, FT), 1)
    for index in range(2 * seq_count):
        turn, place = divmod(index, seq_count)
        source = lax.bitwise_xor(seq_index, exchange_order(seq_count)[place]) * 2
        owner = source + (sub_index if turn == 0 else 1 - sub_index)
        live = slot < counts[held_by(ids, seq_index, owner, 2 * seq_count)]
        mask[pl.ds(index, 1), :] = jnp.where(live, 0.0, MASKED).astype(F32)
    for copy in copies:
        copy.wait()


def load(frame_ids, frame_counts, weight, seq_count, after):
    parts = 8
    return pl.pallas_call(
        functools.partial(load_kernel, parts, seq_count),
        out_shape=[pltpu.VMEM(weight.shape, BF16), pltpu.VMEM((2 * seq_count, FT), F32)],
        in_specs=[pl.BlockSpec(memory_space=pltpu.SMEM)] * 2 + [HBM, ANY],
        out_specs=[VMEM, VMEM],
        scratch_shapes=[pltpu.SemaphoreType.DMA((parts,))],
        compiler_params=params(),
        name="load",
        cost_estimate=pl.CostEstimate(flops=0, bytes_accessed=2 * weight.size, transcendentals=0),
    )(*map(in_hbm, (frame_ids, frame_counts, weight)), in_vmem(after))


def gate(array, after):
    return pl.pallas_call(
        lambda *refs: None,
        in_specs=[ANY, ANY],
        out_specs=ANY,
        out_shape=jax.ShapeDtypeStruct(array.shape, array.dtype),
        input_output_aliases={0: 0},
        compiler_params=params(),
        name="gate",
        cost_estimate=SHORT,
    )(in_vmem(array), in_vmem(after))


def leading_kernel(array, after, out):
    out[...] = array[:, pl.ds(0, out.shape[1])]


def leading(array, width, after):
    return pl.pallas_call(
        leading_kernel,
        in_specs=[VMEM, ANY],
        out_specs=VMEM,
        out_shape=pltpu.VMEM((array.shape[0], width), array.dtype),
        compiler_params=params(),
        name="leading",
        cost_estimate=SHORT,
    )(in_vmem(array), in_vmem(after))


def dot_t(left, right):
    return lax.dot_general(left, right, (((1,), (1,)), ((), ())), preferred_element_type=F32)


def wide(column, count):
    return jnp.concatenate([column] * count, axis=1)


def with_ones(values):
    return jnp.concatenate([values, jnp.ones_like(values)], axis=1)


def current_kernel(step, queries, own_keys, own_values, sibling, out, lse, q, own_k, own_v, sems):
    heads, rows, _ = out.shape
    count = own_k.shape[0]
    half = pl.ds(pl.multiple_of(lax.axis_index("sub") * q.shape[1], 128), q.shape[1])
    copy_all(
        [(queries.at[:, half], q), (own_keys.at[:, half], own_k), (own_values.at[:, half], own_v)],
        sems,
    )

    @pl.loop(0, heads)
    def _(head):
        columns = pl.ds(pl.multiple_of(head * HD, HD), HD)
        keys = jnp.concatenate([own_k[:, columns], sibling[pl.ds(0, count), columns]], axis=0)
        values = with_ones(jnp.concatenate([own_v[:, columns], sibling[pl.ds(count, count), columns]], axis=0))
        for low in range(0, rows, step):
            span = pl.ds(low, step)
            scores = dot_t(q[span, columns], keys)
            row_max = jnp.broadcast_to(jnp.max(scores, axis=1, keepdims=True), (step, HD))
            weights = jnp.exp2((scores - wide(row_max, 2 * count // HD)) * EXP2_SCALE).astype(BF16)
            product = jnp.dot(weights, values, preferred_element_type=F32)
            total = product[:, HD:]
            out[head, span, :] = product[:, :HD] / total
            lse[head, span, :] = row_max * EXP2_SCALE + jnp.log2(total)


def attend_current(queries, cur_keys, cur_values, sibling, heads):
    rows = queries.shape[0]
    keys = cur_keys.shape[0]
    return pl.pallas_call(
        functools.partial(current_kernel, 512),
        in_specs=[HBM] * 3 + [VMEM],
        out_specs=[VMEM] * 3,
        out_shape=[pltpu.VMEM((heads, rows, HD), F32)] * 2 + [pltpu.VMEM((rows, heads * HD), BF16)],
        scratch_shapes=[pltpu.VMEM((keys, heads * HD), BF16)] * 2 + [pltpu.SemaphoreType.DMA((3,))],
        compiler_params=params(),
        name="attend_current",
        cost_estimate=pl.CostEstimate(
            flops=6 * heads * rows * 2 * keys * HD, bytes_accessed=heads * rows * HD * 12, transcendentals=heads * rows * 2 * keys
        ),
    )(in_hbm(queries), in_hbm(cur_keys), in_hbm(cur_values), in_vmem(sibling))


def frames_kernel(heads, half_of, state_half_of, first, starts, final, bias, q, held, lse, *rest):
    frames = rest[: len(starts)]
    outs = rest[-1:] if final else rest[-2:]
    count, rows = len(starts), outs[0].shape[-2]

    def rows_of(half):
        return pl.ds(pl.multiple_of(half() * rows, rows), rows)

    span, state_span = rows_of(half_of), rows_of(state_half_of)
    mask = jnp.concatenate([bias[pl.ds(first + index, 1), :] for index in range(count)], axis=1)

    def gathered(head, part):
        columns = pl.ds(head * HD, HD)
        return jnp.concatenate(
            [frame[pl.ds(start + part * FT, FT), columns] for frame, start in zip(frames, starts)], axis=0
        )

    def scores_of(head):
        return dot_t(q[span, pl.ds(head * HD, HD)], gathered(head, 0))

    def finish(head, scores):
        scores = scores * EXP2_SCALE + mask
        old = lse[head, state_span, :]
        new_max = jnp.maximum(old, jnp.max(scores, axis=1, keepdims=True))
        weights = jnp.exp2(scores - wide(new_max, count * FT // HD)).astype(BF16)
        product = jnp.dot(weights, with_ones(gathered(head, 1)), preferred_element_type=F32)
        scale = jnp.exp2(old - new_max)
        total = scale + product[:, HD:]
        top = (held[head, state_span, :] * scale + product[:, :HD]) / total
        if final:
            outs[0][:, pl.ds(head * HD, HD)] = top.astype(BF16)
        else:
            outs[0][head] = top
            outs[1][head] = new_max + jnp.log2(total)

    scores = scores_of(0)
    for head in range(heads):
        following = scores_of(head + 1) if head + 1 < heads else None
        finish(head, scores)
        scores = following


def far_half():
    return 1 - lax.axis_index("head")


def near_half():
    return lax.axis_index("head")


def attend_frames(name, half, bias, first, q, held, lse, frames, starts, final, after=()):
    heads, state_rows, _ = held.shape
    rows = q.shape[0] // 2
    state_half = half if state_rows > rows else lambda: jnp.int32(0)
    operands = [bias, q, held, lse, *frames]
    if final:
        out_shape = [pltpu.VMEM((rows, heads * HD), BF16)]
    else:
        out_shape = [pltpu.VMEM((heads, rows, HD), F32)] * 2
    outs = pl.pallas_call(
        functools.partial(frames_kernel, heads, half, state_half, first, tuple(starts), final),
        in_specs=[VMEM] * len(operands) + [ANY] * len(after),
        out_specs=[VMEM] * len(out_shape),
        out_shape=out_shape,
        compiler_params=params(),
        name=name,
        cost_estimate=SHORT,
    )(*map(in_vmem, operands), *map(in_vmem, after))
    return outs[0] if final else outs


def both(mine, other):
    first, second = mine[...], other[...]
    return jnp.where(
        lax.axis_index("sub") == 0,
        jnp.concatenate([first, second], axis=1),
        jnp.concatenate([second, first], axis=1),
    )


def project_kernel(step, mine, other, weight, *rest):
    out = rest[-1]
    rows = both(mine, other)

    @pl.loop(0, out.shape[1] // step)
    def _(index):
        columns = pl.ds(pl.multiple_of(index * step, step), step)
        out[:, columns] = jnp.dot(rows, weight[:, columns], preferred_element_type=F32).astype(BF16)


def unshared_columns(low, share, passed):
    found = [pl.ds(0, low)] if low else []
    for other_seq, other_group, skipped in ((True, True, 0), (False, True, passed), (True, False, passed)):
        if skipped < share:
            start = low + quarter(other_seq, other_group) * share + skipped
            found.append(pl.ds(pl.multiple_of(start, 128), share - skipped))
    return found


def unshared_kernel(low, share, passed, mine, other, weight, *rest):
    out = rest[-1]
    rows = both(mine, other)
    start = 0
    for columns in unshared_columns(low, share, passed):
        out[:, pl.ds(start, columns.size)] = jnp.dot(rows, weight[:, columns], preferred_element_type=F32).astype(BF16)
        start += columns.size


def project_call(kernel, name, mine, other, weight, width, after):
    return pl.pallas_call(
        kernel,
        in_specs=[VMEM] * 3 + [ANY] * len(after),
        out_specs=VMEM,
        out_shape=pltpu.VMEM((mine.shape[0], width), BF16),
        compiler_params=params(),
        name=name,
        cost_estimate=SHORT,
    )(*map(in_vmem, (mine, other, weight, *after)))


def project(mine, other, weight, after):
    return project_call(functools.partial(project_kernel, 512), "project", mine, other, weight, weight.shape[1], after)


def project_unshared(mine, other, weight, low, share, passed, after):
    kernel = functools.partial(unshared_kernel, low, share, passed)
    width = low + share + 2 * (share - passed)
    return project_call(kernel, "project_unshared", mine, other, weight, width, after)


def write_blocks(blocks, out, scratch, sems):
    copies, start = [], 0
    for index, (block, low) in enumerate(blocks):
        span = pl.ds(start, block.shape[1])
        scratch[:, span] = block.astype(BF16)
        copy = pltpu.make_async_copy(scratch.at[:, span], out.at[:, pl.ds(low, block.shape[1])], sems.at[index])
        copy.start()
        copies.append(copy)
        start += block.shape[1]
    for copy in copies:
        copy.wait()


def remote_kernel(first, share, other_seq, other_group, terms, mine, other, weight, total, out, scratch, sems):
    block = weight.shape[1]
    low = pl.multiple_of(first + quarter(other_seq, other_group) * share, 128)
    product = jnp.dot(both(mine, other), weight[...], preferred_element_type=F32)
    write_blocks([(terms[:, pl.ds(low, block)].astype(F32) + product, low)], out, scratch, sems)


def add_kernel(low, share, passed, terms, came, total, out, scratch, sems):
    blocks, start = [], 0
    for columns in unshared_columns(low, share, passed):
        block = terms[:, columns].astype(F32) + came[:, pl.ds(start, columns.size)].astype(F32)
        blocks.append((block, columns.start))
        start += columns.size
    write_blocks(blocks, out, scratch, sems)


def finish_block(kernel, name, operands, total, rows, width, block):
    count = len(operands)
    if total is None:
        body = lambda *refs: kernel(*refs[:count], None, *refs[count:])
        totals, aliases = [], {}
    else:
        body, totals, aliases = kernel, [in_hbm(total)], {count: 0}
    return pl.pallas_call(
        body,
        in_specs=[VMEM] * count + [HBM] * len(totals),
        out_specs=HBM,
        out_shape=pltpu.HBM((rows, width), BF16),
        input_output_aliases=aliases,
        scratch_shapes=[pltpu.VMEM((rows, block), BF16), pltpu.SemaphoreType.DMA((4,))],
        compiler_params=params(),
        name=name,
        cost_estimate=SHORT,
    )(*map(in_vmem, operands), *totals)


def add_remote(terms, mine, other, weight, first, share, other_seq, other_group, total):
    kernel = functools.partial(remote_kernel, first, share, other_seq, other_group)
    return finish_block(kernel, "add_remote", (terms, mine, other, weight), total, *terms.shape, weight.shape[1])


def add_unshared(terms, came, low, share, passed, total):
    kernel = functools.partial(add_kernel, low, share, passed)
    return finish_block(kernel, "add_unshared", (terms, came), total, *terms.shape, came.shape[1])


def local(queries, cur_keys, cur_values, mem_keys, mem_values, frame_ids, frame_counts, out_weight):
    seq_count = lax.axis_size("seq")
    heads = queries.shape[1] // HD // 2
    keys = cur_keys.shape[0]
    out_cols = out_weight.shape[1]
    share = out_cols // 4 // 128 * 128
    passed_on = share * 4 // 5 // 128 * 128
    low = out_cols - 4 * share

    *sends, to_sibling, columns = pack(
        frame_ids, mem_keys, mem_values, cur_keys, cur_values, out_weight, low, share, seq_count
    )
    mine = [sends[0]]
    for flip, sent in list(zip(exchange_order(seq_count), sends))[1:]:
        mine.append(lax.ppermute(sent, "seq", [(index, index ^ flip) for index in range(seq_count)]))
    columns = lax.ppermute(columns, "head", SWAP)
    sibling = lax.ppermute(to_sibling, "sub", SWAP)

    held, lse, q = attend_current(queries, cur_keys, cur_values, sibling, heads)
    weight, bias = load(frame_ids, frame_counts, out_weight, seq_count, lse)
    passed = pass_on(mine[1:], weight)
    theirs = lax.ppermute(passed, "sub", SWAP)
    others = [sibling] + [theirs] * (seq_count - 1)
    starts = [2 * keys] + [2 * FT * index for index in range(seq_count - 1)]

    state = attend_frames("far_first", far_half, bias, 0, q, held, lse, mine, [0] * seq_count, False, (passed,))
    far = attend_frames("far_last", far_half, bias, seq_count, q, *state, others, starts, True)
    came_mine = lax.ppermute(far, "head", SWAP)
    far_sibling = lax.ppermute(far, "sub", SWAP)
    columns_copy = leading(columns, passed_on, far)
    group_columns = lax.ppermute(columns_copy, "groups", SWAP)
    seq_columns = lax.ppermute(columns_copy, "seq", [(index, index ^ 1) for index in range(seq_count)])
    starts = [0] * seq_count + starts
    near = attend_frames("near", near_half, bias, 0, q, held, lse, mine + others, starts, True, (columns_copy,))
    near_sibling = lax.ppermute(near, "sub", SWAP)

    term = project_unshared(far, far_sibling, weight, low, share, passed_on, (near,))
    came = lax.ppermute(term, "head", SWAP)
    came_mine = gate(came_mine, term)
    came_other = lax.ppermute(came_mine, "sub", SWAP)
    terms = project(near, near_sibling, weight, (came_mine,))

    arrived = (terms, came_mine, came_other)
    total = add_remote(*arrived, columns, low, share, False, False, None)
    total = add_remote(*arrived, group_columns, low, share, False, True, total)
    total = add_remote(*arrived, seq_columns, low, share, True, False, total)
    return add_unshared(terms, came, low, share, passed_on, total)


def local_any(queries, cur_keys, cur_values, mem_keys, mem_values, frame_ids, frame_counts, out_weight):
    seq_count = lax.axis_size("seq")
    sub_count = lax.axis_size("sub")
    seq_index = lax.axis_index("seq")
    owner_self = seq_index * sub_count + lax.axis_index("sub")
    row_count, col_count = queries.shape
    heads = col_count // HD
    mine = row_count // sub_count
    wanted = jnp.sum(jnp.where(frame_ids // FR_DEV == owner_self, frame_ids, 0), axis=1) - owner_self * FR_DEV
    own_list = lax.dynamic_index_in_dim(frame_ids, seq_index, 0, keepdims=False)
    owners = jnp.arange(seq_count * sub_count, dtype=jnp.int32)
    hit = (own_list // FR_DEV)[None, :] == owners[:, None]
    got_ids = jnp.sum(jnp.where(hit, own_list[None, :], 0), axis=1).reshape(seq_count, sub_count).T.reshape(-1)
    live = jnp.arange(FT, dtype=jnp.int32)[None, :] < jnp.take(frame_counts, got_ids)[:, None]

    def spread(cached, current):
        sent = lax.all_to_all(jnp.take(cached, wanted, axis=0), "seq", split_axis=0, concat_axis=0, tiled=True)
        far = lax.all_gather(sent, "sub").reshape(-1, heads, HD)
        return jnp.concatenate([lax.all_gather(current, "sub").reshape(-1, heads, HD), far], axis=0)

    keys, values = spread(mem_keys, cur_keys), spread(mem_values, cur_values)
    key_live = jnp.concatenate([jnp.ones((keys.shape[0] - live.size,), bool), live.reshape(-1)])
    start = lax.axis_index("sub") * mine
    query_heads = lax.dynamic_slice_in_dim(queries, start, mine, 0).reshape(mine, heads, HD)
    scores = jnp.einsum("qhd,khd->hqk", query_heads, keys, preferred_element_type=F32) / math.sqrt(HD)
    scores = jnp.where(key_live[None, None, :], scores, -jnp.inf)
    expo = jnp.exp(scores - jnp.max(scores, axis=-1, keepdims=True))
    total = jnp.sum(expo, axis=-1)
    weighted = jnp.einsum("hqk,khd->qhd", expo.astype(BF16), values, preferred_element_type=F32)
    attended = (weighted / total.T[:, :, None]).reshape(mine, col_count).astype(BF16)
    attended = lax.all_gather(attended, "sub", axis=0, tiled=True)
    term = jnp.dot(attended, out_weight, preferred_element_type=F32).astype(BF16)
    return lax.psum_scatter(term, "head", scatter_dimension=0, tiled=True)


def solution(mesh):
    in_specs = (
        P(("groups", "seq"), "head"),
        P(("groups", "seq", "sub"), "head"),
        P(("groups", "seq", "sub"), "head"),
        P(("groups", "seq", "sub"), None, "head"),
        P(("groups", "seq", "sub"), None, "head"),
        P("groups", None),
        P("groups"),
        P("head", "sub"),
    )
    out_specs = P(("groups", "seq", "head"), "sub")

    def apply(queries, *rest):
        heads = queries.shape[1] // mesh.shape["head"] // HD
        paired = heads % 2 == 0 and mesh.shape["seq"] in (2, 4, 8)
        paired = paired and all(mesh.shape[axis] == 2 for axis in ("groups", "head", "sub"))
        body = local if paired else local_any
        return jax.shard_map(body, mesh=mesh, in_specs=in_specs, out_specs=out_specs, check_vma=False)(queries, *rest)

    return apply
```

```python
import functools
import math

import jax
import jax.numpy as jnp
from jax import lax
from jax.experimental import pallas as pl
from jax.experimental.pallas import tpu as pltpu
from jax.sharding import PartitionSpec as P

HD = 128
FT = 64
FR_DEV = 16
F32 = jnp.float32
BF16 = jnp.bfloat16
EXP2_SCALE = math.log2(math.e) / math.sqrt(HD)
MASKED = -1e30
VMEM_LIMIT = 24 * 1024 * 1024
SWAP = [(0, 1), (1, 0)]
SHORT = pl.CostEstimate(flops=1024, bytes_accessed=1024, transcendentals=0)
ANY = pl.BlockSpec(memory_space=pl.ANY)
HBM = pl.BlockSpec(memory_space=pltpu.HBM)
VMEM = pl.BlockSpec(memory_space=pltpu.VMEM)


def params():
    return pltpu.CompilerParams(vmem_limit_bytes=VMEM_LIMIT)


def in_hbm(array):
    return pltpu.with_memory_space_constraint(array, pltpu.HBM)


def in_vmem(array):
    return pltpu.with_memory_space_constraint(array, pltpu.VMEM)


def quarter(other_seq, other_group):
    seq_part = lax.rem(lax.axis_index("seq"), 2)
    group = lax.axis_index("groups")
    return 2 * (1 - seq_part if other_seq else seq_part) + (1 - group if other_group else group)


def copy_all(pairs, sems):
    copies = [pltpu.make_async_copy(*pair, sems.at[index]) for index, pair in enumerate(pairs)]
    for copy in copies:
        copy.start()
    for copy in copies:
        copy.wait()


def exchange_order(seq_count):
    return [0, *range(seq_count // 2, seq_count), *range(1, seq_count // 2)]


def held_by(ids, stretch, owner, count):
    found = jnp.int32(0)
    for entry in range(count):
        frame = ids[stretch, entry]
        slot = frame - owner * FR_DEV
        found = jnp.where((slot >= 0) & (slot < FR_DEV), frame, found)
    return found


def pack_kernel(seq_count, ids_in, keys, values, after, *rest):
    outs, ids, listed, sems = rest[:-3], *rest[-3:]
    copy_all([(ids_in, ids)], listed)
    seq_index = lax.axis_index("seq")
    sub_index = lax.axis_index("sub")
    owner = seq_index * 2 + sub_index
    width = outs[0].shape[1]
    pairs = []
    for flip, out in zip(exchange_order(seq_count), outs):
        wanted = held_by(ids, lax.bitwise_xor(seq_index, flip), owner, 2 * seq_count) - owner * FR_DEV
        wanted = jnp.clip(wanted, 0, FR_DEV - 1)
        for turn in range(2):
            half = sub_index if turn == 0 else 1 - sub_index
            columns = pl.ds(pl.multiple_of(half * width, 128), width)
            for part, source in enumerate((keys, values)):
                pairs.append((source.at[wanted, :, columns], out.at[pl.ds((2 * turn + part) * FT, FT), :]))
    copy_all(pairs, sems)


def pack(frame_ids, mem_keys, mem_values, seq_count, after):
    return pl.pallas_call(
        functools.partial(pack_kernel, seq_count),
        out_shape=[pltpu.VMEM((4 * FT, mem_keys.shape[2] // 2), BF16)] * seq_count,
        in_specs=[HBM] * 3 + [ANY],
        out_specs=[VMEM] * seq_count,
        scratch_shapes=[
            pltpu.SMEM(frame_ids.shape, jnp.int32),
            pltpu.SemaphoreType.DMA((1,)),
            pltpu.SemaphoreType.DMA((4 * seq_count,)),
        ],
        compiler_params=params(),
        name="pack",
        cost_estimate=SHORT,
    )(*map(in_hbm, (frame_ids, mem_keys, mem_values)), in_vmem(after))


def pack_first_kernel(low, parts, cur_keys, cur_values, weight, sibling, columns_out, sems):
    first = pl.multiple_of(low + quarter(False, False) * columns_out.shape[1], 128)
    rows = weight.shape[0] // (2 * parts)
    pairs = []
    for part in range(2 * parts):
        span = pl.ds(part * rows, rows)
        pairs.append((weight.at[span, pl.ds(first, columns_out.shape[1])], columns_out.at[span, :]))
    count, width = cur_keys.shape[0], sibling.shape[1]
    half = pl.ds(pl.multiple_of((1 - lax.axis_index("sub")) * width, 128), width)
    rows = count // parts
    for part, source in enumerate((cur_keys, cur_values)):
        for row in range(0, count, rows):
            pairs.append((source.at[pl.ds(row, rows), half], sibling.at[pl.ds(part * count + row, rows), :]))
    copy_all(pairs, sems)


def pack_first(cur_keys, cur_values, weight, low, share):
    parts = 4
    count, width = cur_keys.shape
    return pl.pallas_call(
        functools.partial(pack_first_kernel, low, parts),
        out_shape=[pltpu.VMEM((2 * count, width // 2), BF16), pltpu.VMEM((weight.shape[0], share), BF16)],
        in_specs=[HBM] * 3,
        out_specs=[VMEM, VMEM],
        scratch_shapes=[pltpu.SemaphoreType.DMA((4 * parts,))],
        compiler_params=params(),
        name="pack_first",
        cost_estimate=SHORT,
    )(*map(in_hbm, (cur_keys, cur_values, weight)))


def pass_on_kernel(*refs):
    arrays, out = refs[:-2], refs[-1]
    rows = out.shape[0] // len(arrays)
    for index, array in enumerate(arrays):
        out[pl.ds(index * rows, rows), :] = array[pl.ds(rows, rows), :]


def pass_on(arrays, after):
    rows, width = arrays[0].shape
    return pl.pallas_call(
        pass_on_kernel,
        out_shape=pltpu.VMEM((len(arrays) * rows // 2, width), BF16),
        in_specs=[VMEM] * len(arrays) + [ANY],
        out_specs=VMEM,
        compiler_params=params(),
        name="pass_on",
        cost_estimate=SHORT,
    )(*map(in_vmem, arrays), in_vmem(after))


def load_kernel(parts, seq_count, ids, counts, weight, after, out, mask, sems):
    rows = weight.shape[0] // parts
    spans = [pl.ds(part * rows, rows) for part in range(parts)]
    copies = [pltpu.make_async_copy(weight.at[span, :], out.at[span, :], sems.at[index]) for index, span in enumerate(spans)]
    for copy in copies:
        copy.start()
    seq_index = lax.axis_index("seq")
    sub_index = lax.axis_index("sub")
    slot = lax.broadcasted_iota(jnp.int32, (1, FT), 1)
    for index in range(2 * seq_count):
        turn, place = divmod(index, seq_count)
        source = lax.bitwise_xor(seq_index, exchange_order(seq_count)[place]) * 2
        owner = source + (sub_index if turn == 0 else 1 - sub_index)
        live = slot < counts[held_by(ids, seq_index, owner, 2 * seq_count)]
        mask[pl.ds(index, 1), :] = jnp.where(live, 0.0, MASKED).astype(F32)
    for copy in copies:
        copy.wait()


def load(frame_ids, frame_counts, weight, seq_count, after):
    parts = 8
    return pl.pallas_call(
        functools.partial(load_kernel, parts, seq_count),
        out_shape=[pltpu.VMEM(weight.shape, BF16), pltpu.VMEM((2 * seq_count, FT), F32)],
        in_specs=[pl.BlockSpec(memory_space=pltpu.SMEM)] * 2 + [HBM, ANY],
        out_specs=[VMEM, VMEM],
        scratch_shapes=[pltpu.SemaphoreType.DMA((parts,))],
        compiler_params=params(),
        name="load",
        cost_estimate=pl.CostEstimate(flops=0, bytes_accessed=2 * weight.size, transcendentals=0),
    )(*map(in_hbm, (frame_ids, frame_counts, weight)), in_vmem(after))


def gate(array, after):
    return pl.pallas_call(
        lambda *refs: None,
        in_specs=[ANY, ANY],
        out_specs=ANY,
        out_shape=jax.ShapeDtypeStruct(array.shape, array.dtype),
        input_output_aliases={0: 0},
        compiler_params=params(),
        name="gate",
        cost_estimate=SHORT,
    )(in_vmem(array), in_vmem(after))


def leading_kernel(array, after, out):
    out[...] = array[:, pl.ds(0, out.shape[1])]


def leading(array, width, after):
    return pl.pallas_call(
        leading_kernel,
        in_specs=[VMEM, ANY],
        out_specs=VMEM,
        out_shape=pltpu.VMEM((array.shape[0], width), array.dtype),
        compiler_params=params(),
        name="leading",
        cost_estimate=SHORT,
    )(in_vmem(array), in_vmem(after))


def dot_t(left, right):
    return lax.dot_general(left, right, (((1,), (1,)), ((), ())), preferred_element_type=F32)


def wide(column, count):
    return jnp.concatenate([column] * count, axis=1)


def with_ones(values):
    return jnp.concatenate([values, jnp.ones_like(values)], axis=1)


def current_kernel(step, queries, own_keys, own_values, sibling, out, lse, q, own_k, own_v, sems):
    heads, rows, _ = out.shape
    count = own_k.shape[0]
    half = pl.ds(pl.multiple_of(lax.axis_index("sub") * q.shape[1], 128), q.shape[1])
    copy_all(
        [(queries.at[:, half], q), (own_keys.at[:, half], own_k), (own_values.at[:, half], own_v)],
        sems,
    )

    @pl.loop(0, heads)
    def _(head):
        columns = pl.ds(pl.multiple_of(head * HD, HD), HD)
        keys = jnp.concatenate([own_k[:, columns], sibling[pl.ds(0, count), columns]], axis=0)
        values = with_ones(jnp.concatenate([own_v[:, columns], sibling[pl.ds(count, count), columns]], axis=0))
        for low in range(0, rows, step):
            span = pl.ds(low, step)
            scores = dot_t(q[span, columns], keys)
            row_max = jnp.broadcast_to(jnp.max(scores, axis=1, keepdims=True), (step, HD))
            weights = jnp.exp2((scores - wide(row_max, 2 * count // HD)) * EXP2_SCALE).astype(BF16)
            product = jnp.dot(weights, values, preferred_element_type=F32)
            total = product[:, HD:]
            out[head, span, :] = product[:, :HD] / total
            lse[head, span, :] = row_max * EXP2_SCALE + jnp.log2(total)


def attend_current(queries, cur_keys, cur_values, sibling, heads):
    rows = queries.shape[0]
    keys = cur_keys.shape[0]
    return pl.pallas_call(
        functools.partial(current_kernel, 512),
        in_specs=[HBM] * 3 + [VMEM],
        out_specs=[VMEM] * 3,
        out_shape=[pltpu.VMEM((heads, rows, HD), F32)] * 2 + [pltpu.VMEM((rows, heads * HD), BF16)],
        scratch_shapes=[pltpu.VMEM((keys, heads * HD), BF16)] * 2 + [pltpu.SemaphoreType.DMA((3,))],
        compiler_params=params(),
        name="attend_current",
        cost_estimate=SHORT,
    )(in_hbm(queries), in_hbm(cur_keys), in_hbm(cur_values), in_vmem(sibling))


def frames_kernel(heads, half_of, state_half_of, first, starts, final, bias, q, held, lse, *rest):
    frames = rest[: len(starts)]
    outs = rest[-1:] if final else rest[-2:]
    count, rows = len(starts), outs[0].shape[-2]

    def rows_of(half):
        return pl.ds(pl.multiple_of(half() * rows, rows), rows)

    span, state_span = rows_of(half_of), rows_of(state_half_of)
    mask = jnp.concatenate([bias[pl.ds(first + index, 1), :] for index in range(count)], axis=1)

    def gathered(head, part):
        columns = pl.ds(head * HD, HD)
        return jnp.concatenate(
            [frame[pl.ds(start + part * FT, FT), columns] for frame, start in zip(frames, starts)], axis=0
        )

    def scores_of(head):
        return dot_t(q[span, pl.ds(head * HD, HD)], gathered(head, 0))

    def finish(head, scores):
        scores = scores * EXP2_SCALE + mask
        old = lse[head, state_span, :]
        new_max = jnp.maximum(old, jnp.max(scores, axis=1, keepdims=True))
        weights = jnp.exp2(scores - wide(new_max, count * FT // HD)).astype(BF16)
        product = jnp.dot(weights, with_ones(gathered(head, 1)), preferred_element_type=F32)
        scale = jnp.exp2(old - new_max)
        total = scale + product[:, HD:]
        top = (held[head, state_span, :] * scale + product[:, :HD]) / total
        if final:
            outs[0][:, pl.ds(head * HD, HD)] = top.astype(BF16)
        else:
            outs[0][head] = top
            outs[1][head] = new_max + jnp.log2(total)

    scores = scores_of(0)
    for head in range(heads):
        following = scores_of(head + 1) if head + 1 < heads else None
        finish(head, scores)
        scores = following


def far_half():
    return 1 - lax.axis_index("head")


def near_half():
    return lax.axis_index("head")


def attend_frames(name, half, bias, first, q, held, lse, frames, starts, final, after=()):
    heads, state_rows, _ = held.shape
    rows = q.shape[0] // 2
    state_half = half if state_rows > rows else lambda: jnp.int32(0)
    operands = [bias, q, held, lse, *frames]
    if final:
        out_shape = [pltpu.VMEM((rows, heads * HD), BF16)]
    else:
        out_shape = [pltpu.VMEM((heads, rows, HD), F32)] * 2
    outs = pl.pallas_call(
        functools.partial(frames_kernel, heads, half, state_half, first, tuple(starts), final),
        in_specs=[VMEM] * len(operands) + [ANY] * len(after),
        out_specs=[VMEM] * len(out_shape),
        out_shape=out_shape,
        compiler_params=params(),
        name=name,
        cost_estimate=SHORT,
    )(*map(in_vmem, operands), *map(in_vmem, after))
    return outs[0] if final else outs


def both(mine, other):
    first, second = mine[...], other[...]
    return jnp.where(
        lax.axis_index("sub") == 0,
        jnp.concatenate([first, second], axis=1),
        jnp.concatenate([second, first], axis=1),
    )


def project_kernel(step, mine, other, weight, *rest):
    out = rest[-1]
    rows = both(mine, other)

    @pl.loop(0, out.shape[1] // step)
    def _(index):
        columns = pl.ds(pl.multiple_of(index * step, step), step)
        out[:, columns] = jnp.dot(rows, weight[:, columns], preferred_element_type=F32).astype(BF16)


def unshared_columns(low, share, passed):
    found = [pl.ds(0, low)] if low else []
    for other_seq, other_group, skipped in ((True, True, 0), (False, True, passed), (True, False, passed)):
        if skipped < share:
            start = low + quarter(other_seq, other_group) * share + skipped
            found.append(pl.ds(pl.multiple_of(start, 128), share - skipped))
    return found


def unshared_kernel(low, share, passed, mine, other, weight, *rest):
    out = rest[-1]
    rows = both(mine, other)
    start = 0
    for columns in unshared_columns(low, share, passed):
        out[:, pl.ds(start, columns.size)] = jnp.dot(rows, weight[:, columns], preferred_element_type=F32).astype(BF16)
        start += columns.size


def project_call(kernel, name, mine, other, weight, width, after):
    return pl.pallas_call(
        kernel,
        in_specs=[VMEM] * 3 + [ANY] * len(after),
        out_specs=VMEM,
        out_shape=pltpu.VMEM((mine.shape[0], width), BF16),
        compiler_params=params(),
        name=name,
        cost_estimate=SHORT,
    )(*map(in_vmem, (mine, other, weight, *after)))


def project(mine, other, weight, after):
    return project_call(functools.partial(project_kernel, 512), "project", mine, other, weight, weight.shape[1], after)


def project_unshared(mine, other, weight, low, share, passed, after):
    kernel = functools.partial(unshared_kernel, low, share, passed)
    width = low + share + 2 * (share - passed)
    return project_call(kernel, "project_unshared", mine, other, weight, width, after)


def write_blocks(blocks, out, scratch, sems):
    copies, start = [], 0
    for index, (block, low) in enumerate(blocks):
        span = pl.ds(start, block.shape[1])
        scratch[:, span] = block.astype(BF16)
        copy = pltpu.make_async_copy(scratch.at[:, span], out.at[:, pl.ds(low, block.shape[1])], sems.at[index])
        copy.start()
        copies.append(copy)
        start += block.shape[1]
    for copy in copies:
        copy.wait()


def remote_kernel(first, share, other_seq, other_group, terms, mine, other, weight, total, out, scratch, sems):
    block = weight.shape[1]
    rows = both(mine, other)

    def blocks():
        step = 256 if block % 256 == 0 else 128
        for start in range(0, block, step):
            low = pl.multiple_of(first + quarter(other_seq, other_group) * share + start, 128)
            product = jnp.dot(rows, weight[:, pl.ds(start, step)], preferred_element_type=F32)
            yield terms[:, pl.ds(low, step)].astype(F32) + product, low

    write_blocks(blocks(), out, scratch, sems)


def add_kernel(low, share, passed, terms, came, total, out, scratch, sems):
    blocks, start = [], 0
    for columns in unshared_columns(low, share, passed):
        block = terms[:, columns].astype(F32) + came[:, pl.ds(start, columns.size)].astype(F32)
        blocks.append((block, columns.start))
        start += columns.size
    write_blocks(blocks, out, scratch, sems)


def finish_block(kernel, name, operands, total, rows, width, block):
    count = len(operands)
    if total is None:
        body = lambda *refs: kernel(*refs[:count], None, *refs[count:])
        totals, aliases = [], {}
    else:
        body, totals, aliases = kernel, [in_hbm(total)], {count: 0}
    return pl.pallas_call(
        body,
        in_specs=[VMEM] * count + [HBM] * len(totals),
        out_specs=HBM,
        out_shape=pltpu.HBM((rows, width), BF16),
        input_output_aliases=aliases,
        scratch_shapes=[pltpu.VMEM((rows, block), BF16), pltpu.SemaphoreType.DMA((8,))],
        compiler_params=params(),
        name=name,
        cost_estimate=SHORT,
    )(*map(in_vmem, operands), *totals)


def add_remote(terms, mine, other, weight, first, share, other_seq, other_group, total):
    kernel = functools.partial(remote_kernel, first, share, other_seq, other_group)
    return finish_block(kernel, "add_remote", (terms, mine, other, weight), total, *terms.shape, weight.shape[1])


def add_unshared(terms, came, low, share, passed, total):
    kernel = functools.partial(add_kernel, low, share, passed)
    return finish_block(kernel, "add_unshared", (terms, came), total, *terms.shape, came.shape[1])


def local(queries, cur_keys, cur_values, mem_keys, mem_values, frame_ids, frame_counts, out_weight):
    seq_count = lax.axis_size("seq")
    heads = queries.shape[1] // HD // 2
    out_cols = out_weight.shape[1]
    share = out_cols // 4 // 128 * 128
    passed_on = share * 4 // 5 // 128 * 128
    low = out_cols - 4 * share

    to_sibling, columns = pack_first(cur_keys, cur_values, out_weight, low, share)
    sends = pack(frame_ids, mem_keys, mem_values, seq_count, columns)
    mine = [sends[0]]
    for flip, sent in list(zip(exchange_order(seq_count), sends))[1:]:
        mine.append(lax.ppermute(sent, "seq", [(index, index ^ flip) for index in range(seq_count)]))
    columns = lax.ppermute(columns, "head", SWAP)
    sibling = lax.ppermute(to_sibling, "sub", SWAP)

    held, lse, q = attend_current(queries, cur_keys, cur_values, sibling, heads)
    weight, bias = load(frame_ids, frame_counts, out_weight, seq_count, lse)
    passed = pass_on(mine, weight)
    theirs = lax.ppermute(passed, "sub", SWAP)
    others = [theirs] * seq_count
    starts = [2 * FT * index for index in range(seq_count)]

    state = attend_frames("far_first", far_half, bias, 0, q, held, lse, mine, [0] * seq_count, False, (passed,))
    far = attend_frames("far_last", far_half, bias, seq_count, q, *state, others, starts, True)
    came_mine = lax.ppermute(far, "head", SWAP)
    far_sibling = lax.ppermute(far, "sub", SWAP)
    columns_copy = leading(columns, passed_on, far)
    group_columns = lax.ppermute(columns_copy, "groups", SWAP)
    seq_columns = lax.ppermute(columns_copy, "seq", [(index, index ^ 1) for index in range(seq_count)])
    starts = [0] * seq_count + starts
    near = attend_frames("near", near_half, bias, 0, q, held, lse, mine + others, starts, True, (columns_copy,))
    near_sibling = lax.ppermute(near, "sub", SWAP)

    term = project_unshared(far, far_sibling, weight, low, share, passed_on, (near,))
    came = lax.ppermute(term, "head", SWAP)
    came_mine = gate(came_mine, term)
    came_other = lax.ppermute(came_mine, "sub", SWAP)
    terms = project(near, near_sibling, weight, (came_mine,))

    arrived = (terms, came_mine, came_other)
    total = add_remote(*arrived, columns, low, share, False, False, None)
    total = add_remote(*arrived, group_columns, low, share, False, True, total)
    total = add_remote(*arrived, seq_columns, low, share, True, False, total)
    return add_unshared(terms, came, low, share, passed_on, total)


def local_any(queries, cur_keys, cur_values, mem_keys, mem_values, frame_ids, frame_counts, out_weight):
    seq_count = lax.axis_size("seq")
    sub_count = lax.axis_size("sub")
    seq_index = lax.axis_index("seq")
    owner_self = seq_index * sub_count + lax.axis_index("sub")
    row_count, col_count = queries.shape
    heads = col_count // HD
    mine = row_count // sub_count
    wanted = jnp.sum(jnp.where(frame_ids // FR_DEV == owner_self, frame_ids, 0), axis=1) - owner_self * FR_DEV
    own_list = lax.dynamic_index_in_dim(frame_ids, seq_index, 0, keepdims=False)
    owners = jnp.arange(seq_count * sub_count, dtype=jnp.int32)
    hit = (own_list // FR_DEV)[None, :] == owners[:, None]
    got_ids = jnp.sum(jnp.where(hit, own_list[None, :], 0), axis=1).reshape(seq_count, sub_count).T.reshape(-1)
    live = jnp.arange(FT, dtype=jnp.int32)[None, :] < jnp.take(frame_counts, got_ids)[:, None]

    def spread(cached, current):
        sent = lax.all_to_all(jnp.take(cached, wanted, axis=0), "seq", split_axis=0, concat_axis=0, tiled=True)
        far = lax.all_gather(sent, "sub").reshape(-1, heads, HD)
        return jnp.concatenate([lax.all_gather(current, "sub").reshape(-1, heads, HD), far], axis=0)

    keys, values = spread(mem_keys, cur_keys), spread(mem_values, cur_values)
    key_live = jnp.concatenate([jnp.ones((keys.shape[0] - live.size,), bool), live.reshape(-1)])
    start = lax.axis_index("sub") * mine
    query_heads = lax.dynamic_slice_in_dim(queries, start, mine, 0).reshape(mine, heads, HD)
    scores = jnp.einsum("qhd,khd->hqk", query_heads, keys, preferred_element_type=F32) / math.sqrt(HD)
    scores = jnp.where(key_live[None, None, :], scores, -jnp.inf)
    expo = jnp.exp(scores - jnp.max(scores, axis=-1, keepdims=True))
    total = jnp.sum(expo, axis=-1)
    weighted = jnp.einsum("hqk,khd->qhd", expo.astype(BF16), values, preferred_element_type=F32)
    attended = (weighted / total.T[:, :, None]).reshape(mine, col_count).astype(BF16)
    attended = lax.all_gather(attended, "sub", axis=0, tiled=True)
    term = jnp.dot(attended, out_weight, preferred_element_type=F32).astype(BF16)
    return lax.psum_scatter(term, "head", scatter_dimension=0, tiled=True)


def solution(mesh):
    in_specs = (
        P(("groups", "seq"), "head"),
        P(("groups", "seq", "sub"), "head"),
        P(("groups", "seq", "sub"), "head"),
        P(("groups", "seq", "sub"), None, "head"),
        P(("groups", "seq", "sub"), None, "head"),
        P("groups", None),
        P("groups"),
        P("head", "sub"),
    )
    out_specs = P(("groups", "seq", "head"), "sub")

    def apply(queries, *rest):
        heads = queries.shape[1] // mesh.shape["head"] // HD
        paired = heads % 2 == 0 and mesh.shape["seq"] in (2, 4, 8)
        paired = paired and all(mesh.shape[axis] == 2 for axis in ("groups", "head", "sub"))
        body = local if paired else local_any
        return jax.shard_map(body, mesh=mesh, in_specs=in_specs, out_specs=out_specs, check_vma=False)(queries, *rest)

    return apply
```

```python
import functools
import math

import jax
import jax.numpy as jnp
from jax import lax
from jax.experimental import pallas as pl
from jax.experimental.pallas import tpu as pltpu
from jax.sharding import PartitionSpec as P

HD = 128
FT = 64
FR_DEV = 16
F32 = jnp.float32
BF16 = jnp.bfloat16
EXP2_SCALE = math.log2(math.e) / math.sqrt(HD)
MASKED = -1e30
VMEM_LIMIT = 24 * 1024 * 1024
SWAP = [(0, 1), (1, 0)]
SHORT = pl.CostEstimate(flops=1024, bytes_accessed=1024, transcendentals=0)
ANY = pl.BlockSpec(memory_space=pl.ANY)
HBM = pl.BlockSpec(memory_space=pltpu.HBM)
VMEM = pl.BlockSpec(memory_space=pltpu.VMEM)


def params():
    return pltpu.CompilerParams(vmem_limit_bytes=VMEM_LIMIT)


def in_hbm(array):
    return pltpu.with_memory_space_constraint(array, pltpu.HBM)


def in_vmem(array):
    return pltpu.with_memory_space_constraint(array, pltpu.VMEM)


def quarter(other_seq, other_group):
    seq_part = lax.rem(lax.axis_index("seq"), 2)
    group = lax.axis_index("groups")
    return 2 * (1 - seq_part if other_seq else seq_part) + (1 - group if other_group else group)


def copy_all(pairs, sems):
    copies = [pltpu.make_async_copy(*pair, sems.at[index]) for index, pair in enumerate(pairs)]
    for copy in copies:
        copy.start()
    for copy in copies:
        copy.wait()


def exchange_order(seq_count):
    return [0, *range(seq_count - 1, 0, -1)]


def held_by(ids, stretch, owner, count):
    found = jnp.int32(0)
    for entry in range(count):
        frame = ids[stretch, entry]
        slot = frame - owner * FR_DEV
        found = jnp.where((slot >= 0) & (slot < FR_DEV), frame, found)
    return found


def pack_kernel(seq_count, low, parts, ids_in, keys, values, cur_keys, cur_values, weight, *rest):
    outs = rest[:seq_count]
    sibling, columns_out, ids, sems = rest[seq_count:]
    seq_index = lax.axis_index("seq")
    sub_index = lax.axis_index("sub")
    width = sibling.shape[1]
    block = columns_out.shape[1]
    count = cur_keys.shape[0]
    frame_count = 2 * seq_count
    copies = []

    def start(source, target):
        copy = pltpu.make_async_copy(source, target, sems.at[len(copies)])
        copy.start()
        copies.append(copy)
        return copy

    def columns_of(half):
        return pl.ds(pl.multiple_of(half * width, 128), width)

    listed = start(ids_in, ids)
    rows = count // parts
    for part, source in enumerate((cur_keys, cur_values)):
        for low_row in range(0, count, rows):
            target = sibling.at[pl.ds(part * count + low_row, rows), :]
            start(source.at[pl.ds(low_row, rows), columns_of(1 - sub_index)], target)
    first = pl.multiple_of(low + quarter(False, False) * block, 128)
    rows = weight.shape[0] // parts
    for part in range(parts):
        span = pl.ds(part * rows, rows)
        start(weight.at[span, pl.ds(first, block)], columns_out.at[span, :])
    listed.wait()
    for flip, out in zip(exchange_order(seq_count), outs):
        owner = seq_index * 2 + sub_index
        wanted = held_by(ids, lax.bitwise_xor(seq_index, flip), owner, frame_count) - owner * FR_DEV
        wanted = jnp.clip(wanted, 0, FR_DEV - 1)
        for turn in range(2):
            half = sub_index if turn == 0 else 1 - sub_index
            for part, source in enumerate((keys, values)):
                if flip == 0 and turn == 1:
                    target = sibling.at[pl.ds(2 * count + part * FT, FT), :]
                else:
                    target = out.at[pl.ds((2 * turn + part) * FT, FT), :]
                start(source.at[wanted, :, columns_of(half)], target)
    for copy in copies[1:]:
        copy.wait()


def pack(frame_ids, mem_keys, mem_values, cur_keys, cur_values, weight, low, share, seq_count):
    parts = 4
    width = mem_keys.shape[2] // 2
    rows = [2 * FT] + [4 * FT] * (seq_count - 1) + [2 * cur_keys.shape[0] + 2 * FT]
    shapes = [(count, width) for count in rows] + [(weight.shape[0], share)]
    return pl.pallas_call(
        functools.partial(pack_kernel, seq_count, low, parts),
        out_shape=[pltpu.VMEM(shape, BF16) for shape in shapes],
        in_specs=[HBM] * 6,
        out_specs=[VMEM] * len(shapes),
        scratch_shapes=[
            pltpu.SMEM(frame_ids.shape, jnp.int32),
            pltpu.SemaphoreType.DMA((1 + 4 * seq_count + 3 * parts,)),
        ],
        compiler_params=params(),
        name="pack",
        cost_estimate=pl.CostEstimate(flops=0, bytes_accessed=12 * 2**20, transcendentals=0),
    )(*map(in_hbm, (frame_ids, mem_keys, mem_values, cur_keys, cur_values, weight)))


def pass_on_kernel(*refs):
    arrays, out = refs[:-2], refs[-1]
    rows = out.shape[0] // len(arrays)
    for index, array in enumerate(arrays):
        out[pl.ds(index * rows, rows), :] = array[pl.ds(rows, rows), :]


def pass_on(arrays, after):
    rows, width = arrays[0].shape
    return pl.pallas_call(
        pass_on_kernel,
        out_shape=pltpu.VMEM((len(arrays) * rows // 2, width), BF16),
        in_specs=[VMEM] * len(arrays) + [ANY],
        out_specs=VMEM,
        compiler_params=params(),
        name="pass_on",
        cost_estimate=SHORT,
    )(*map(in_vmem, arrays), in_vmem(after))


def load_kernel(parts, seq_count, ids, counts, weight, after, out, mask, sems):
    rows = weight.shape[0] // parts
    spans = [pl.ds(part * rows, rows) for part in range(parts)]
    copies = [pltpu.make_async_copy(weight.at[span, :], out.at[span, :], sems.at[index]) for index, span in enumerate(spans)]
    for copy in copies:
        copy.start()
    seq_index = lax.axis_index("seq")
    sub_index = lax.axis_index("sub")
    slot = lax.broadcasted_iota(jnp.int32, (1, FT), 1)
    for index in range(2 * seq_count):
        turn, place = divmod(index, seq_count)
        source = lax.bitwise_xor(seq_index, exchange_order(seq_count)[place]) * 2
        owner = source + (sub_index if turn == 0 else 1 - sub_index)
        live = slot < counts[held_by(ids, seq_index, owner, 2 * seq_count)]
        mask[pl.ds(index, 1), :] = jnp.where(live, 0.0, MASKED).astype(F32)
    for copy in copies:
        copy.wait()


def load(frame_ids, frame_counts, weight, seq_count, after):
    parts = 8
    return pl.pallas_call(
        functools.partial(load_kernel, parts, seq_count),
        out_shape=[pltpu.VMEM(weight.shape, BF16), pltpu.VMEM((2 * seq_count, FT), F32)],
        in_specs=[pl.BlockSpec(memory_space=pltpu.SMEM)] * 2 + [HBM, ANY],
        out_specs=[VMEM, VMEM],
        scratch_shapes=[pltpu.SemaphoreType.DMA((parts,))],
        compiler_params=params(),
        name="load",
        cost_estimate=pl.CostEstimate(flops=0, bytes_accessed=2 * weight.size, transcendentals=0),
    )(*map(in_hbm, (frame_ids, frame_counts, weight)), in_vmem(after))


def gate(array, after):
    return pl.pallas_call(
        lambda *refs: None,
        in_specs=[ANY, ANY],
        out_specs=ANY,
        out_shape=jax.ShapeDtypeStruct(array.shape, array.dtype),
        input_output_aliases={0: 0},
        compiler_params=params(),
        name="gate",
        cost_estimate=SHORT,
    )(in_vmem(array), in_vmem(after))


def leading_kernel(array, after, out):
    out[...] = array[:, pl.ds(0, out.shape[1])]


def leading(array, width, after):
    return pl.pallas_call(
        leading_kernel,
        in_specs=[VMEM, ANY],
        out_specs=VMEM,
        out_shape=pltpu.VMEM((array.shape[0], width), array.dtype),
        compiler_params=params(),
        name="leading",
        cost_estimate=SHORT,
    )(in_vmem(array), in_vmem(after))


def dot_t(left, right):
    return lax.dot_general(left, right, (((1,), (1,)), ((), ())), preferred_element_type=F32)


def wide(column, count):
    return jnp.concatenate([column] * count, axis=1)


def with_ones(values):
    return jnp.concatenate([values, jnp.ones_like(values)], axis=1)


def current_kernel(step, queries, own_keys, own_values, sibling, out, lse, q, own_k, own_v, sems):
    heads, rows, _ = out.shape
    count = own_k.shape[0]
    half = pl.ds(pl.multiple_of(lax.axis_index("sub") * q.shape[1], 128), q.shape[1])
    copy_all(
        [(queries.at[:, half], q), (own_keys.at[:, half], own_k), (own_values.at[:, half], own_v)],
        sems,
    )

    @pl.loop(0, heads)
    def _(head):
        columns = pl.ds(pl.multiple_of(head * HD, HD), HD)
        keys = jnp.concatenate([own_k[:, columns], sibling[pl.ds(0, count), columns]], axis=0)
        values = with_ones(jnp.concatenate([own_v[:, columns], sibling[pl.ds(count, count), columns]], axis=0))
        for low in range(0, rows, step):
            span = pl.ds(low, step)
            scores = dot_t(q[span, columns], keys)
            row_max = jnp.broadcast_to(jnp.max(scores, axis=1, keepdims=True), (step, HD))
            weights = jnp.exp2((scores - wide(row_max, 2 * count // HD)) * EXP2_SCALE).astype(BF16)
            product = jnp.dot(weights, values, preferred_element_type=F32)
            total = product[:, HD:]
            out[head, span, :] = product[:, :HD] / total
            lse[head, span, :] = row_max * EXP2_SCALE + jnp.log2(total)


def attend_current(queries, cur_keys, cur_values, sibling, heads):
    rows = queries.shape[0]
    keys = cur_keys.shape[0]
    return pl.pallas_call(
        functools.partial(current_kernel, 512),
        in_specs=[HBM] * 3 + [VMEM],
        out_specs=[VMEM] * 3,
        out_shape=[pltpu.VMEM((heads, rows, HD), F32)] * 2 + [pltpu.VMEM((rows, heads * HD), BF16)],
        scratch_shapes=[pltpu.VMEM((keys, heads * HD), BF16)] * 2 + [pltpu.SemaphoreType.DMA((3,))],
        compiler_params=params(),
        name="attend_current",
        cost_estimate=pl.CostEstimate(
            flops=6 * heads * rows * 2 * keys * HD, bytes_accessed=heads * rows * HD * 12, transcendentals=heads * rows * 2 * keys
        ),
    )(in_hbm(queries), in_hbm(cur_keys), in_hbm(cur_values), in_vmem(sibling))


def frames_kernel(heads, half_of, state_half_of, first, starts, final, bias, q, held, lse, *rest):
    frames = rest[: len(starts)]
    outs = rest[-1:] if final else rest[-2:]
    count, rows = len(starts), outs[0].shape[-2]

    def rows_of(half):
        return pl.ds(pl.multiple_of(half() * rows, rows), rows)

    span, state_span = rows_of(half_of), rows_of(state_half_of)
    mask = jnp.concatenate([bias[pl.ds(first + index, 1), :] for index in range(count)], axis=1)

    def gathered(head, part):
        columns = pl.ds(head * HD, HD)
        return jnp.concatenate(
            [frame[pl.ds(start + part * FT, FT), columns] for frame, start in zip(frames, starts)], axis=0
        )

    def scores_of(head):
        return dot_t(q[span, pl.ds(head * HD, HD)], gathered(head, 0))

    def finish(head, scores):
        scores = scores * EXP2_SCALE + mask
        old = lse[head, state_span, :]
        new_max = jnp.maximum(old, jnp.max(scores, axis=1, keepdims=True))
        weights = jnp.exp2(scores - wide(new_max, count * FT // HD)).astype(BF16)
        product = jnp.dot(weights, with_ones(gathered(head, 1)), preferred_element_type=F32)
        scale = jnp.exp2(old - new_max)
        total = scale + product[:, HD:]
        top = (held[head, state_span, :] * scale + product[:, :HD]) / total
        if final:
            outs[0][:, pl.ds(head * HD, HD)] = top.astype(BF16)
        else:
            outs[0][head] = top
            outs[1][head] = new_max + jnp.log2(total)

    scores = scores_of(0)
    for head in range(heads):
        following = scores_of(head + 1) if head + 1 < heads else None
        finish(head, scores)
        scores = following


def far_half():
    return 1 - lax.axis_index("head")


def near_half():
    return lax.axis_index("head")


def attend_frames(name, half, bias, first, q, held, lse, frames, starts, final, after=()):
    heads, state_rows, _ = held.shape
    rows = q.shape[0] // 2
    state_half = half if state_rows > rows else lambda: jnp.int32(0)
    operands = [bias, q, held, lse, *frames]
    if final:
        out_shape = [pltpu.VMEM((rows, heads * HD), BF16)]
    else:
        out_shape = [pltpu.VMEM((heads, rows, HD), F32)] * 2
    outs = pl.pallas_call(
        functools.partial(frames_kernel, heads, half, state_half, first, tuple(starts), final),
        in_specs=[VMEM] * len(operands) + [ANY] * len(after),
        out_specs=[VMEM] * len(out_shape),
        out_shape=out_shape,
        compiler_params=params(),
        name=name,
        cost_estimate=SHORT,
    )(*map(in_vmem, operands), *map(in_vmem, after))
    return outs[0] if final else outs


def both(mine, other):
    first, second = mine[...], other[...]
    return jnp.where(
        lax.axis_index("sub") == 0,
        jnp.concatenate([first, second], axis=1),
        jnp.concatenate([second, first], axis=1),
    )


def project_kernel(step, mine, other, weight, *rest):
    out = rest[-1]
    rows = both(mine, other)

    @pl.loop(0, out.shape[1] // step)
    def _(index):
        columns = pl.ds(pl.multiple_of(index * step, step), step)
        out[:, columns] = jnp.dot(rows, weight[:, columns], preferred_element_type=F32).astype(BF16)


def unshared_columns(low, share, passed):
    found = [pl.ds(0, low)] if low else []
    for other_seq, other_group, skipped in ((True, True, 0), (False, True, passed), (True, False, passed)):
        if skipped < share:
            start = low + quarter(other_seq, other_group) * share + skipped
            found.append(pl.ds(pl.multiple_of(start, 128), share - skipped))
    return found


def unshared_kernel(low, share, passed, mine, other, weight, *rest):
    out = rest[-1]
    rows = both(mine, other)
    start = 0
    for columns in unshared_columns(low, share, passed):
        out[:, pl.ds(start, columns.size)] = jnp.dot(rows, weight[:, columns], preferred_element_type=F32).astype(BF16)
        start += columns.size


def project_call(kernel, name, mine, other, weight, width, after):
    return pl.pallas_call(
        kernel,
        in_specs=[VMEM] * 3 + [ANY] * len(after),
        out_specs=VMEM,
        out_shape=pltpu.VMEM((mine.shape[0], width), BF16),
        compiler_params=params(),
        name=name,
        cost_estimate=SHORT,
    )(*map(in_vmem, (mine, other, weight, *after)))


def project(mine, other, weight, after):
    return project_call(functools.partial(project_kernel, 512), "project", mine, other, weight, weight.shape[1], after)


def project_unshared(mine, other, weight, low, share, passed, after):
    kernel = functools.partial(unshared_kernel, low, share, passed)
    width = low + share + 2 * (share - passed)
    return project_call(kernel, "project_unshared", mine, other, weight, width, after)


def write_blocks(blocks, out, scratch, sems):
    copies, start = [], 0
    for index, (block, low) in enumerate(blocks):
        span = pl.ds(start, block.shape[1])
        scratch[:, span] = block.astype(BF16)
        copy = pltpu.make_async_copy(scratch.at[:, span], out.at[:, pl.ds(low, block.shape[1])], sems.at[index])
        copy.start()
        copies.append(copy)
        start += block.shape[1]
    for copy in copies:
        copy.wait()


def remote_kernel(first, share, other_seq, other_group, terms, mine, other, weight, total, out, scratch, sems):
    block = weight.shape[1]
    low = pl.multiple_of(first + quarter(other_seq, other_group) * share, 128)
    product = jnp.dot(both(mine, other), weight[...], preferred_element_type=F32)
    write_blocks([(terms[:, pl.ds(low, block)].astype(F32) + product, low)], out, scratch, sems)


def add_kernel(low, share, passed, terms, came, total, out, scratch, sems):
    blocks, start = [], 0
    for columns in unshared_columns(low, share, passed):
        block = terms[:, columns].astype(F32) + came[:, pl.ds(start, columns.size)].astype(F32)
        blocks.append((block, columns.start))
        start += columns.size
    write_blocks(blocks, out, scratch, sems)


def finish_block(kernel, name, operands, total, rows, width, block):
    count = len(operands)
    if total is None:
        body = lambda *refs: kernel(*refs[:count], None, *refs[count:])
        totals, aliases = [], {}
    else:
        body, totals, aliases = kernel, [in_hbm(total)], {count: 0}
    return pl.pallas_call(
        body,
        in_specs=[VMEM] * count + [HBM] * len(totals),
        out_specs=HBM,
        out_shape=pltpu.HBM((rows, width), BF16),
        input_output_aliases=aliases,
        scratch_shapes=[pltpu.VMEM((rows, block), BF16), pltpu.SemaphoreType.DMA((4,))],
        compiler_params=params(),
        name=name,
        cost_estimate=SHORT,
    )(*map(in_vmem, operands), *totals)


def add_remote(terms, mine, other, weight, first, share, other_seq, other_group, total):
    kernel = functools.partial(remote_kernel, first, share, other_seq, other_group)
    return finish_block(kernel, "add_remote", (terms, mine, other, weight), total, *terms.shape, weight.shape[1])


def add_unshared(terms, came, low, share, passed, total):
    kernel = functools.partial(add_kernel, low, share, passed)
    return finish_block(kernel, "add_unshared", (terms, came), total, *terms.shape, came.shape[1])


def local(queries, cur_keys, cur_values, mem_keys, mem_values, frame_ids, frame_counts, out_weight):
    seq_count = lax.axis_size("seq")
    heads = queries.shape[1] // HD // 2
    keys = cur_keys.shape[0]
    out_cols = out_weight.shape[1]
    share = out_cols // 4 // 128 * 128
    passed_on = share * 4 // 5 // 128 * 128
    low = out_cols - 4 * share

    *sends, to_sibling, columns = pack(
        frame_ids, mem_keys, mem_values, cur_keys, cur_values, out_weight, low, share, seq_count
    )
    mine = [sends[0]]
    for flip, sent in list(zip(exchange_order(seq_count), sends))[1:]:
        mine.append(lax.ppermute(sent, "seq", [(index, index ^ flip) for index in range(seq_count)]))
    columns = lax.ppermute(columns, "head", SWAP)
    sibling = lax.ppermute(to_sibling, "sub", SWAP)

    held, lse, q = attend_current(queries, cur_keys, cur_values, sibling, heads)
    weight, bias = load(frame_ids, frame_counts, out_weight, seq_count, lse)
    passed = pass_on(mine[1:], weight)
    theirs = lax.ppermute(passed, "sub", SWAP)
    others = [sibling] + [theirs] * (seq_count - 1)
    starts = [2 * keys] + [2 * FT * index for index in range(seq_count - 1)]

    state = attend_frames("far_first", far_half, bias, 0, q, held, lse, mine, [0] * seq_count, False, (passed,))
    far = attend_frames("far_last", far_half, bias, seq_count, q, *state, others, starts, True)
    came_mine = lax.ppermute(far, "head", SWAP)
    far_sibling = lax.ppermute(far, "sub", SWAP)
    columns_copy = leading(columns, passed_on, far)
    group_columns = lax.ppermute(columns_copy, "groups", SWAP)
    seq_columns = lax.ppermute(columns_copy, "seq", [(index, index ^ 1) for index in range(seq_count)])
    starts = [0] * seq_count + starts
    near = attend_frames("near", near_half, bias, 0, q, held, lse, mine + others, starts, True, (columns_copy,))
    near_sibling = lax.ppermute(near, "sub", SWAP)

    term = project_unshared(far, far_sibling, weight, low, share, passed_on, (near,))
    came = lax.ppermute(term, "head", SWAP)
    came_mine = gate(came_mine, term)
    came_other = lax.ppermute(came_mine, "sub", SWAP)
    terms = project(near, near_sibling, weight, (came_mine,))

    arrived = (terms, came_mine, came_other)
    total = add_remote(*arrived, columns, low, share, False, False, None)
    total = add_remote(*arrived, group_columns, low, share, False, True, total)
    total = add_remote(*arrived, seq_columns, low, share, True, False, total)
    return add_unshared(terms, came, low, share, passed_on, total)


def local_any(queries, cur_keys, cur_values, mem_keys, mem_values, frame_ids, frame_counts, out_weight):
    seq_count = lax.axis_size("seq")
    sub_count = lax.axis_size("sub")
    seq_index = lax.axis_index("seq")
    owner_self = seq_index * sub_count + lax.axis_index("sub")
    row_count, col_count = queries.shape
    heads = col_count // HD
    mine = row_count // sub_count
    wanted = jnp.sum(jnp.where(frame_ids // FR_DEV == owner_self, frame_ids, 0), axis=1) - owner_self * FR_DEV
    own_list = lax.dynamic_index_in_dim(frame_ids, seq_index, 0, keepdims=False)
    owners = jnp.arange(seq_count * sub_count, dtype=jnp.int32)
    hit = (own_list // FR_DEV)[None, :] == owners[:, None]
    got_ids = jnp.sum(jnp.where(hit, own_list[None, :], 0), axis=1).reshape(seq_count, sub_count).T.reshape(-1)
    live = jnp.arange(FT, dtype=jnp.int32)[None, :] < jnp.take(frame_counts, got_ids)[:, None]

    def spread(cached, current):
        sent = lax.all_to_all(jnp.take(cached, wanted, axis=0), "seq", split_axis=0, concat_axis=0, tiled=True)
        far = lax.all_gather(sent, "sub").reshape(-1, heads, HD)
        return jnp.concatenate([lax.all_gather(current, "sub").reshape(-1, heads, HD), far], axis=0)

    keys, values = spread(mem_keys, cur_keys), spread(mem_values, cur_values)
    key_live = jnp.concatenate([jnp.ones((keys.shape[0] - live.size,), bool), live.reshape(-1)])
    start = lax.axis_index("sub") * mine
    query_heads = lax.dynamic_slice_in_dim(queries, start, mine, 0).reshape(mine, heads, HD)
    scores = jnp.einsum("qhd,khd->hqk", query_heads, keys, preferred_element_type=F32) / math.sqrt(HD)
    scores = jnp.where(key_live[None, None, :], scores, -jnp.inf)
    expo = jnp.exp(scores - jnp.max(scores, axis=-1, keepdims=True))
    total = jnp.sum(expo, axis=-1)
    weighted = jnp.einsum("hqk,khd->qhd", expo.astype(BF16), values, preferred_element_type=F32)
    attended = (weighted / total.T[:, :, None]).reshape(mine, col_count).astype(BF16)
    attended = lax.all_gather(attended, "sub", axis=0, tiled=True)
    term = jnp.dot(attended, out_weight, preferred_element_type=F32).astype(BF16)
    return lax.psum_scatter(term, "head", scatter_dimension=0, tiled=True)


def solution(mesh):
    in_specs = (
        P(("groups", "seq"), "head"),
        P(("groups", "seq", "sub"), "head"),
        P(("groups", "seq", "sub"), "head"),
        P(("groups", "seq", "sub"), None, "head"),
        P(("groups", "seq", "sub"), None, "head"),
        P("groups", None),
        P("groups"),
        P("head", "sub"),
    )
    out_specs = P(("groups", "seq", "head"), "sub")

    def apply(queries, *rest):
        heads = queries.shape[1] // mesh.shape["head"] // HD
        paired = heads % 2 == 0 and mesh.shape["seq"] in (2, 4, 8)
        paired = paired and all(mesh.shape[axis] == 2 for axis in ("groups", "head", "sub"))
        body = local if paired else local_any
        return jax.shard_map(body, mesh=mesh, in_specs=in_specs, out_specs=out_specs, check_vma=False)(queries, *rest)

    return apply
```

```python
import functools
import math

import jax
import jax.numpy as jnp
from jax import lax
from jax.experimental import pallas as pl
from jax.experimental.pallas import tpu as pltpu
from jax.sharding import PartitionSpec as P

HD = 128
FT = 64
FR_DEV = 16
F32 = jnp.float32
BF16 = jnp.bfloat16
EXP2_SCALE = math.log2(math.e) / math.sqrt(HD)
MASKED = -1e30
VMEM_LIMIT = 24 * 1024 * 1024
SWAP = [(0, 1), (1, 0)]
SHORT = pl.CostEstimate(flops=1024, bytes_accessed=1024, transcendentals=0)
ANY = pl.BlockSpec(memory_space=pl.ANY)
HBM = pl.BlockSpec(memory_space=pltpu.HBM)
VMEM = pl.BlockSpec(memory_space=pltpu.VMEM)


def params():
    return pltpu.CompilerParams(vmem_limit_bytes=VMEM_LIMIT)


def in_hbm(array):
    return pltpu.with_memory_space_constraint(array, pltpu.HBM)


def in_vmem(array):
    return pltpu.with_memory_space_constraint(array, pltpu.VMEM)


def quarter(other_seq, other_group):
    seq_part = lax.rem(lax.axis_index("seq"), 2)
    group = lax.axis_index("groups")
    return 2 * (1 - seq_part if other_seq else seq_part) + (1 - group if other_group else group)


def copy_all(pairs, sems):
    copies = [pltpu.make_async_copy(*pair, sems.at[index]) for index, pair in enumerate(pairs)]
    for copy in copies:
        copy.start()
    for copy in copies:
        copy.wait()


def exchange_orders(seq_count):
    across, beside = list(range(seq_count // 2, seq_count)), list(range(1, seq_count // 2))
    return [0, *across, *beside], [0, *reversed(across), *beside]


def exchange_flip(place, sub, seq_count):
    first, second = exchange_orders(seq_count)
    return jnp.where(sub == 0, jnp.int32(first[place]), jnp.int32(second[place]))


def held_by(ids, stretch, owner, count):
    found = jnp.int32(0)
    for entry in range(count):
        frame = ids[stretch, entry]
        slot = frame - owner * FR_DEV
        found = jnp.where((slot >= 0) & (slot < FR_DEV), frame, found)
    return found


def pack_kernel(seq_count, low, parts, ids_in, keys, values, cur_keys, cur_values, weight, *rest):
    outs = rest[:seq_count]
    sibling, columns_out, ids, sems = rest[seq_count:]
    seq_index = lax.axis_index("seq")
    sub_index = lax.axis_index("sub")
    width = sibling.shape[1]
    block = columns_out.shape[1]
    count = cur_keys.shape[0]
    frame_count = 2 * seq_count
    copies = []

    def start(source, target):
        copy = pltpu.make_async_copy(source, target, sems.at[len(copies)])
        copy.start()
        copies.append(copy)
        return copy

    def columns_of(half):
        return pl.ds(pl.multiple_of(half * width, 128), width)

    listed = start(ids_in, ids)
    rows = count // parts
    for part, source in enumerate((cur_keys, cur_values)):
        for low_row in range(0, count, rows):
            target = sibling.at[pl.ds(part * count + low_row, rows), :]
            start(source.at[pl.ds(low_row, rows), columns_of(1 - sub_index)], target)
    first = pl.multiple_of(low + quarter(False, False) * block, 128)
    rows = weight.shape[0] // parts
    for part in range(parts):
        span = pl.ds(part * rows, rows)
        start(weight.at[span, pl.ds(first, block)], columns_out.at[span, :])
    listed.wait()
    for place, out in enumerate(outs):
        flip = exchange_flip(place, sub_index, seq_count)
        owner = seq_index * 2 + sub_index
        wanted = held_by(ids, lax.bitwise_xor(seq_index, flip), owner, frame_count) - owner * FR_DEV
        wanted = jnp.clip(wanted, 0, FR_DEV - 1)
        for turn in range(2):
            half = sub_index if turn == 0 else 1 - sub_index
            for part, source in enumerate((keys, values)):
                if place == 0 and turn == 1:
                    target = sibling.at[pl.ds(2 * count + part * FT, FT), :]
                else:
                    target = out.at[pl.ds((2 * turn + part) * FT, FT), :]
                start(source.at[wanted, :, columns_of(half)], target)
    for copy in copies[1:]:
        copy.wait()


def pack(frame_ids, mem_keys, mem_values, cur_keys, cur_values, weight, low, share, seq_count):
    parts = 4
    width = mem_keys.shape[2] // 2
    rows = [2 * FT] + [4 * FT] * (seq_count - 1) + [2 * cur_keys.shape[0] + 2 * FT]
    shapes = [(count, width) for count in rows] + [(weight.shape[0], share)]
    return pl.pallas_call(
        functools.partial(pack_kernel, seq_count, low, parts),
        out_shape=[pltpu.VMEM(shape, BF16) for shape in shapes],
        in_specs=[HBM] * 6,
        out_specs=[VMEM] * len(shapes),
        scratch_shapes=[
            pltpu.SMEM(frame_ids.shape, jnp.int32),
            pltpu.SemaphoreType.DMA((1 + 4 * seq_count + 3 * parts,)),
        ],
        compiler_params=params(),
        name="pack",
        cost_estimate=pl.CostEstimate(flops=0, bytes_accessed=12 * 2**20, transcendentals=0),
    )(*map(in_hbm, (frame_ids, mem_keys, mem_values, cur_keys, cur_values, weight)))


def pass_on_kernel(*refs):
    arrays, out = refs[:-2], refs[-1]
    rows = out.shape[0] // len(arrays)
    for index, array in enumerate(arrays):
        out[pl.ds(index * rows, rows), :] = array[pl.ds(rows, rows), :]


def pass_on(arrays, after):
    rows, width = arrays[0].shape
    return pl.pallas_call(
        pass_on_kernel,
        out_shape=pltpu.VMEM((len(arrays) * rows // 2, width), BF16),
        in_specs=[VMEM] * len(arrays) + [ANY],
        out_specs=VMEM,
        compiler_params=params(),
        name="pass_on",
        cost_estimate=SHORT,
    )(*map(in_vmem, arrays), in_vmem(after))


def load_kernel(parts, seq_count, ids, counts, weight, after, out, mask, sems):
    rows = weight.shape[0] // parts
    spans = [pl.ds(part * rows, rows) for part in range(parts)]
    copies = [pltpu.make_async_copy(weight.at[span, :], out.at[span, :], sems.at[index]) for index, span in enumerate(spans)]
    for copy in copies:
        copy.start()
    seq_index = lax.axis_index("seq")
    sub_index = lax.axis_index("sub")
    slot = lax.broadcasted_iota(jnp.int32, (1, FT), 1)
    for index in range(2 * seq_count):
        turn, place = divmod(index, seq_count)
        source_sub = sub_index if turn == 0 else 1 - sub_index
        owner = lax.bitwise_xor(seq_index, exchange_flip(place, source_sub, seq_count)) * 2 + source_sub
        live = slot < counts[held_by(ids, seq_index, owner, 2 * seq_count)]
        mask[pl.ds(index, 1), :] = jnp.where(live, 0.0, MASKED).astype(F32)
    for copy in copies:
        copy.wait()


def load(frame_ids, frame_counts, weight, seq_count, after):
    parts = 8
    return pl.pallas_call(
        functools.partial(load_kernel, parts, seq_count),
        out_shape=[pltpu.VMEM(weight.shape, BF16), pltpu.VMEM((2 * seq_count, FT), F32)],
        in_specs=[pl.BlockSpec(memory_space=pltpu.SMEM)] * 2 + [HBM, ANY],
        out_specs=[VMEM, VMEM],
        scratch_shapes=[pltpu.SemaphoreType.DMA((parts,))],
        compiler_params=params(),
        name="load",
        cost_estimate=pl.CostEstimate(flops=0, bytes_accessed=2 * weight.size, transcendentals=0),
    )(*map(in_hbm, (frame_ids, frame_counts, weight)), in_vmem(after))


def gate(array, after):
    return pl.pallas_call(
        lambda *refs: None,
        in_specs=[ANY, ANY],
        out_specs=ANY,
        out_shape=jax.ShapeDtypeStruct(array.shape, array.dtype),
        input_output_aliases={0: 0},
        compiler_params=params(),
        name="gate",
        cost_estimate=SHORT,
    )(in_vmem(array), in_vmem(after))


def leading_kernel(array, after, out):
    out[...] = array[:, pl.ds(0, out.shape[1])]


def leading(array, width, after):
    return pl.pallas_call(
        leading_kernel,
        in_specs=[VMEM, ANY],
        out_specs=VMEM,
        out_shape=pltpu.VMEM((array.shape[0], width), array.dtype),
        compiler_params=params(),
        name="leading",
        cost_estimate=SHORT,
    )(in_vmem(array), in_vmem(after))


def dot_t(left, right):
    return lax.dot_general(left, right, (((1,), (1,)), ((), ())), preferred_element_type=F32)


def wide(column, count):
    return jnp.concatenate([column] * count, axis=1)


def with_ones(values):
    return jnp.concatenate([values, jnp.ones_like(values)], axis=1)


def current_kernel(step, queries, own_keys, own_values, sibling, out, lse, q, own_k, own_v, sems):
    heads, rows, _ = out.shape
    count = own_k.shape[0]
    half = pl.ds(pl.multiple_of(lax.axis_index("sub") * q.shape[1], 128), q.shape[1])
    copy_all(
        [(queries.at[:, half], q), (own_keys.at[:, half], own_k), (own_values.at[:, half], own_v)],
        sems,
    )

    @pl.loop(0, heads)
    def _(head):
        columns = pl.ds(pl.multiple_of(head * HD, HD), HD)
        keys = jnp.concatenate([own_k[:, columns], sibling[pl.ds(0, count), columns]], axis=0)
        values = with_ones(jnp.concatenate([own_v[:, columns], sibling[pl.ds(count, count), columns]], axis=0))
        for low in range(0, rows, step):
            span = pl.ds(low, step)
            scores = dot_t(q[span, columns], keys)
            row_max = jnp.broadcast_to(jnp.max(scores, axis=1, keepdims=True), (step, HD))
            weights = jnp.exp2((scores - wide(row_max, 2 * count // HD)) * EXP2_SCALE).astype(BF16)
            product = jnp.dot(weights, values, preferred_element_type=F32)
            total = product[:, HD:]
            out[head, span, :] = product[:, :HD] / total
            lse[head, span, :] = row_max * EXP2_SCALE + jnp.log2(total)


def attend_current(queries, cur_keys, cur_values, sibling, heads):
    rows = queries.shape[0]
    keys = cur_keys.shape[0]
    return pl.pallas_call(
        functools.partial(current_kernel, 512),
        in_specs=[HBM] * 3 + [VMEM],
        out_specs=[VMEM] * 3,
        out_shape=[pltpu.VMEM((heads, rows, HD), F32)] * 2 + [pltpu.VMEM((rows, heads * HD), BF16)],
        scratch_shapes=[pltpu.VMEM((keys, heads * HD), BF16)] * 2 + [pltpu.SemaphoreType.DMA((3,))],
        compiler_params=params(),
        name="attend_current",
        cost_estimate=pl.CostEstimate(
            flops=6 * heads * rows * 2 * keys * HD, bytes_accessed=heads * rows * HD * 12, transcendentals=heads * rows * 2 * keys
        ),
    )(in_hbm(queries), in_hbm(cur_keys), in_hbm(cur_values), in_vmem(sibling))


def frames_kernel(heads, half_of, state_half_of, first, starts, final, bias, q, held, lse, *rest):
    frames = rest[: len(starts)]
    outs = rest[-1:] if final else rest[-2:]
    count, rows = len(starts), outs[0].shape[-2]

    def rows_of(half):
        return pl.ds(pl.multiple_of(half() * rows, rows), rows)

    span, state_span = rows_of(half_of), rows_of(state_half_of)
    mask = jnp.concatenate([bias[pl.ds(first + index, 1), :] for index in range(count)], axis=1)

    def gathered(head, part):
        columns = pl.ds(head * HD, HD)
        return jnp.concatenate(
            [frame[pl.ds(start + part * FT, FT), columns] for frame, start in zip(frames, starts)], axis=0
        )

    def scores_of(head):
        return dot_t(q[span, pl.ds(head * HD, HD)], gathered(head, 0))

    def finish(head, scores):
        scores = scores * EXP2_SCALE + mask
        old = lse[head, state_span, :]
        new_max = jnp.maximum(old, jnp.max(scores, axis=1, keepdims=True))
        weights = jnp.exp2(scores - wide(new_max, count * FT // HD)).astype(BF16)
        product = jnp.dot(weights, with_ones(gathered(head, 1)), preferred_element_type=F32)
        scale = jnp.exp2(old - new_max)
        total = scale + product[:, HD:]
        top = (held[head, state_span, :] * scale + product[:, :HD]) / total
        if final:
            outs[0][:, pl.ds(head * HD, HD)] = top.astype(BF16)
        else:
            outs[0][head] = top
            outs[1][head] = new_max + jnp.log2(total)

    scores = scores_of(0)
    for head in range(heads):
        following = scores_of(head + 1) if head + 1 < heads else None
        finish(head, scores)
        scores = following


def far_half():
    return 1 - lax.axis_index("head")


def near_half():
    return lax.axis_index("head")


def attend_frames(name, half, bias, first, q, held, lse, frames, starts, final, after=()):
    heads, state_rows, _ = held.shape
    rows = q.shape[0] // 2
    state_half = half if state_rows > rows else lambda: jnp.int32(0)
    operands = [bias, q, held, lse, *frames]
    if final:
        out_shape = [pltpu.VMEM((rows, heads * HD), BF16)]
    else:
        out_shape = [pltpu.VMEM((heads, rows, HD), F32)] * 2
    outs = pl.pallas_call(
        functools.partial(frames_kernel, heads, half, state_half, first, tuple(starts), final),
        in_specs=[VMEM] * len(operands) + [ANY] * len(after),
        out_specs=[VMEM] * len(out_shape),
        out_shape=out_shape,
        compiler_params=params(),
        name=name,
        cost_estimate=SHORT,
    )(*map(in_vmem, operands), *map(in_vmem, after))
    return outs[0] if final else outs


def both(mine, other):
    first, second = mine[...], other[...]
    return jnp.where(
        lax.axis_index("sub") == 0,
        jnp.concatenate([first, second], axis=1),
        jnp.concatenate([second, first], axis=1),
    )


def project_kernel(step, mine, other, weight, *rest):
    out = rest[-1]
    rows = both(mine, other)

    @pl.loop(0, out.shape[1] // step)
    def _(index):
        columns = pl.ds(pl.multiple_of(index * step, step), step)
        out[:, columns] = jnp.dot(rows, weight[:, columns], preferred_element_type=F32).astype(BF16)


def unshared_columns(low, share, passed):
    found = [pl.ds(0, low)] if low else []
    for other_seq, other_group, skipped in ((True, True, 0), (False, True, passed), (True, False, passed)):
        if skipped < share:
            start = low + quarter(other_seq, other_group) * share + skipped
            found.append(pl.ds(pl.multiple_of(start, 128), share - skipped))
    return found


def unshared_kernel(low, share, passed, mine, other, weight, *rest):
    out = rest[-1]
    rows = both(mine, other)
    start = 0
    for columns in unshared_columns(low, share, passed):
        out[:, pl.ds(start, columns.size)] = jnp.dot(rows, weight[:, columns], preferred_element_type=F32).astype(BF16)
        start += columns.size


def project_call(kernel, name, mine, other, weight, width, after):
    return pl.pallas_call(
        kernel,
        in_specs=[VMEM] * 3 + [ANY] * len(after),
        out_specs=VMEM,
        out_shape=pltpu.VMEM((mine.shape[0], width), BF16),
        compiler_params=params(),
        name=name,
        cost_estimate=SHORT,
    )(*map(in_vmem, (mine, other, weight, *after)))


def project(mine, other, weight, after):
    return project_call(functools.partial(project_kernel, 512), "project", mine, other, weight, weight.shape[1], after)


def project_unshared(mine, other, weight, low, share, passed, after):
    kernel = functools.partial(unshared_kernel, low, share, passed)
    width = low + share + 2 * (share - passed)
    return project_call(kernel, "project_unshared", mine, other, weight, width, after)


def write_blocks(blocks, out, scratch, sems):
    copies, start = [], 0
    for index, (block, low) in enumerate(blocks):
        span = pl.ds(start, block.shape[1])
        scratch[:, span] = block.astype(BF16)
        copy = pltpu.make_async_copy(scratch.at[:, span], out.at[:, pl.ds(low, block.shape[1])], sems.at[index])
        copy.start()
        copies.append(copy)
        start += block.shape[1]
    for copy in copies:
        copy.wait()


def remote_kernel(first, share, other_seq, other_group, terms, mine, other, weight, total, out, scratch, sems):
    block = weight.shape[1]
    low = pl.multiple_of(first + quarter(other_seq, other_group) * share, 128)
    product = jnp.dot(both(mine, other), weight[...], preferred_element_type=F32)
    write_blocks([(terms[:, pl.ds(low, block)].astype(F32) + product, low)], out, scratch, sems)


def add_kernel(low, share, passed, terms, came, total, out, scratch, sems):
    blocks, start = [], 0
    for columns in unshared_columns(low, share, passed):
        block = terms[:, columns].astype(F32) + came[:, pl.ds(start, columns.size)].astype(F32)
        blocks.append((block, columns.start))
        start += columns.size
    write_blocks(blocks, out, scratch, sems)


def finish_block(kernel, name, operands, total, rows, width, block):
    count = len(operands)
    if total is None:
        body = lambda *refs: kernel(*refs[:count], None, *refs[count:])
        totals, aliases = [], {}
    else:
        body, totals, aliases = kernel, [in_hbm(total)], {count: 0}
    return pl.pallas_call(
        body,
        in_specs=[VMEM] * count + [HBM] * len(totals),
        out_specs=HBM,
        out_shape=pltpu.HBM((rows, width), BF16),
        input_output_aliases=aliases,
        scratch_shapes=[pltpu.VMEM((rows, block), BF16), pltpu.SemaphoreType.DMA((4,))],
        compiler_params=params(),
        name=name,
        cost_estimate=SHORT,
    )(*map(in_vmem, operands), *totals)


def add_remote(terms, mine, other, weight, first, share, other_seq, other_group, total):
    kernel = functools.partial(remote_kernel, first, share, other_seq, other_group)
    return finish_block(kernel, "add_remote", (terms, mine, other, weight), total, *terms.shape, weight.shape[1])


def add_unshared(terms, came, low, share, passed, total):
    kernel = functools.partial(add_kernel, low, share, passed)
    return finish_block(kernel, "add_unshared", (terms, came), total, *terms.shape, came.shape[1])


def local(queries, cur_keys, cur_values, mem_keys, mem_values, frame_ids, frame_counts, out_weight):
    seq_count = lax.axis_size("seq")
    heads = queries.shape[1] // HD // 2
    keys = cur_keys.shape[0]
    out_cols = out_weight.shape[1]
    share = out_cols // 4 // 128 * 128
    passed_on = share * 4 // 5 // 128 * 128
    low = out_cols - 4 * share

    *sends, to_sibling, columns = pack(
        frame_ids, mem_keys, mem_values, cur_keys, cur_values, out_weight, low, share, seq_count
    )
    mine = [sends[0]]
    for place in range(1, seq_count):
        flips = [order[place] for order in exchange_orders(seq_count)]
        pairs = [(2 * seq + sub, 2 * (seq ^ flip) + sub) for seq in range(seq_count) for sub, flip in enumerate(flips)]
        mine.append(lax.ppermute(sends[place], ("seq", "sub"), pairs))
    columns = lax.ppermute(columns, "head", SWAP)
    sibling = lax.ppermute(to_sibling, "sub", SWAP)

    held, lse, q = attend_current(queries, cur_keys, cur_values, sibling, heads)
    weight, bias = load(frame_ids, frame_counts, out_weight, seq_count, lse)
    passed = pass_on(mine[1:], weight)
    theirs = lax.ppermute(passed, "sub", SWAP)
    others = [sibling] + [theirs] * (seq_count - 1)
    starts = [2 * keys] + [2 * FT * index for index in range(seq_count - 1)]

    state = attend_frames("far_first", far_half, bias, 0, q, held, lse, mine, [0] * seq_count, False, (passed,))
    far = attend_frames("far_last", far_half, bias, seq_count, q, *state, others, starts, True)
    came_mine = lax.ppermute(far, "head", SWAP)
    far_sibling = lax.ppermute(far, "sub", SWAP)
    columns_copy = leading(columns, passed_on, far)
    group_columns = lax.ppermute(columns_copy, "groups", SWAP)
    seq_columns = lax.ppermute(columns_copy, "seq", [(index, index ^ 1) for index in range(seq_count)])
    starts = [0] * seq_count + starts
    near = attend_frames("near", near_half, bias, 0, q, held, lse, mine + others, starts, True, (columns_copy,))
    near_sibling = lax.ppermute(near, "sub", SWAP)

    term = project_unshared(far, far_sibling, weight, low, share, passed_on, (near,))
    came = lax.ppermute(term, "head", SWAP)
    came_mine = gate(came_mine, term)
    came_other = lax.ppermute(came_mine, "sub", SWAP)
    terms = project(near, near_sibling, weight, (came_mine,))

    arrived = (terms, came_mine, came_other)
    total = add_remote(*arrived, columns, low, share, False, False, None)
    total = add_remote(*arrived, group_columns, low, share, False, True, total)
    total = add_remote(*arrived, seq_columns, low, share, True, False, total)
    return add_unshared(terms, came, low, share, passed_on, total)


def local_any(queries, cur_keys, cur_values, mem_keys, mem_values, frame_ids, frame_counts, out_weight):
    seq_count = lax.axis_size("seq")
    sub_count = lax.axis_size("sub")
    seq_index = lax.axis_index("seq")
    owner_self = seq_index * sub_count + lax.axis_index("sub")
    row_count, col_count = queries.shape
    heads = col_count // HD
    mine = row_count // sub_count
    wanted = jnp.sum(jnp.where(frame_ids // FR_DEV == owner_self, frame_ids, 0), axis=1) - owner_self * FR_DEV
    own_list = lax.dynamic_index_in_dim(frame_ids, seq_index, 0, keepdims=False)
    owners = jnp.arange(seq_count * sub_count, dtype=jnp.int32)
    hit = (own_list // FR_DEV)[None, :] == owners[:, None]
    got_ids = jnp.sum(jnp.where(hit, own_list[None, :], 0), axis=1).reshape(seq_count, sub_count).T.reshape(-1)
    live = jnp.arange(FT, dtype=jnp.int32)[None, :] < jnp.take(frame_counts, got_ids)[:, None]

    def spread(cached, current):
        sent = lax.all_to_all(jnp.take(cached, wanted, axis=0), "seq", split_axis=0, concat_axis=0, tiled=True)
        far = lax.all_gather(sent, "sub").reshape(-1, heads, HD)
        return jnp.concatenate([lax.all_gather(current, "sub").reshape(-1, heads, HD), far], axis=0)

    keys, values = spread(mem_keys, cur_keys), spread(mem_values, cur_values)
    key_live = jnp.concatenate([jnp.ones((keys.shape[0] - live.size,), bool), live.reshape(-1)])
    start = lax.axis_index("sub") * mine
    query_heads = lax.dynamic_slice_in_dim(queries, start, mine, 0).reshape(mine, heads, HD)
    scores = jnp.einsum("qhd,khd->hqk", query_heads, keys, preferred_element_type=F32) / math.sqrt(HD)
    scores = jnp.where(key_live[None, None, :], scores, -jnp.inf)
    expo = jnp.exp(scores - jnp.max(scores, axis=-1, keepdims=True))
    total = jnp.sum(expo, axis=-1)
    weighted = jnp.einsum("hqk,khd->qhd", expo.astype(BF16), values, preferred_element_type=F32)
    attended = (weighted / total.T[:, :, None]).reshape(mine, col_count).astype(BF16)
    attended = lax.all_gather(attended, "sub", axis=0, tiled=True)
    term = jnp.dot(attended, out_weight, preferred_element_type=F32).astype(BF16)
    return lax.psum_scatter(term, "head", scatter_dimension=0, tiled=True)


def solution(mesh):
    in_specs = (
        P(("groups", "seq"), "head"),
        P(("groups", "seq", "sub"), "head"),
        P(("groups", "seq", "sub"), "head"),
        P(("groups", "seq", "sub"), None, "head"),
        P(("groups", "seq", "sub"), None, "head"),
        P("groups", None),
        P("groups"),
        P("head", "sub"),
    )
    out_specs = P(("groups", "seq", "head"), "sub")

    def apply(queries, *rest):
        heads = queries.shape[1] // mesh.shape["head"] // HD
        paired = heads % 2 == 0 and mesh.shape["seq"] in (2, 4, 8)
        paired = paired and all(mesh.shape[axis] == 2 for axis in ("groups", "head", "sub"))
        body = local if paired else local_any
        return jax.shard_map(body, mesh=mesh, in_specs=in_specs, out_specs=out_specs, check_vma=False)(queries, *rest)

    return apply
```

```python
import functools
import math

import jax
import jax.numpy as jnp
from jax import lax
from jax.experimental import pallas as pl
from jax.experimental.pallas import tpu as pltpu
from jax.sharding import PartitionSpec as P

HD = 128
FT = 64
FR_DEV = 16
F32 = jnp.float32
BF16 = jnp.bfloat16
EXP2_SCALE = math.log2(math.e) / math.sqrt(HD)
MASKED = -1e30
VMEM_LIMIT = 24 * 1024 * 1024
SWAP = [(0, 1), (1, 0)]
SHORT = pl.CostEstimate(flops=1024, bytes_accessed=1024, transcendentals=0)
ANY = pl.BlockSpec(memory_space=pl.ANY)
HBM = pl.BlockSpec(memory_space=pltpu.HBM)
VMEM = pl.BlockSpec(memory_space=pltpu.VMEM)


def params():
    return pltpu.CompilerParams(vmem_limit_bytes=VMEM_LIMIT)


def in_hbm(array):
    return pltpu.with_memory_space_constraint(array, pltpu.HBM)


def in_vmem(array):
    return pltpu.with_memory_space_constraint(array, pltpu.VMEM)


def quarter(other_seq, other_group):
    seq_part = lax.rem(lax.axis_index("seq"), 2)
    group = lax.axis_index("groups")
    return 2 * (1 - seq_part if other_seq else seq_part) + (1 - group if other_group else group)


def copy_all(pairs, sems):
    copies = [pltpu.make_async_copy(*pair, sems.at[index]) for index, pair in enumerate(pairs)]
    for copy in copies:
        copy.start()
    for copy in copies:
        copy.wait()


def exchange_orders(seq_count):
    across, beside = list(range(seq_count // 2, seq_count)), list(range(1, seq_count // 2))
    return [0, *across, *beside], [0, *reversed(across), *beside]


def exchange_flip(place, sub, seq_count):
    first, second = exchange_orders(seq_count)
    return jnp.where(sub == 0, jnp.int32(first[place]), jnp.int32(second[place]))


def held_by(ids, stretch, owner, count):
    found = jnp.int32(0)
    for entry in range(count):
        frame = ids[stretch, entry]
        slot = frame - owner * FR_DEV
        found = jnp.where((slot >= 0) & (slot < FR_DEV), frame, found)
    return found


def pack_kernel(seq_count, low, parts, ids_in, keys, values, cur_keys, cur_values, weight, *rest):
    outs = rest[:seq_count]
    sibling, columns_out, ids, sems = rest[seq_count:]
    seq_index = lax.axis_index("seq")
    sub_index = lax.axis_index("sub")
    width = sibling.shape[1]
    block = columns_out.shape[1]
    count = cur_keys.shape[0]
    frame_count = 2 * seq_count
    copies = []

    def start(source, target):
        copy = pltpu.make_async_copy(source, target, sems.at[len(copies)])
        copy.start()
        copies.append(copy)
        return copy

    def columns_of(half):
        return pl.ds(pl.multiple_of(half * width, 128), width)

    listed = start(ids_in, ids)
    rows = count // parts
    for part, source in enumerate((cur_keys, cur_values)):
        for low_row in range(0, count, rows):
            target = sibling.at[pl.ds(part * count + low_row, rows), :]
            start(source.at[pl.ds(low_row, rows), columns_of(1 - sub_index)], target)
    first = pl.multiple_of(low + quarter(False, False) * block, 128)
    rows = weight.shape[0] // parts
    for part in range(parts):
        span = pl.ds(part * rows, rows)
        start(weight.at[span, pl.ds(first, block)], columns_out.at[span, :])
    listed.wait()
    for place, out in enumerate(outs):
        flip = exchange_flip(place, sub_index, seq_count)
        owner = seq_index * 2 + sub_index
        wanted = held_by(ids, lax.bitwise_xor(seq_index, flip), owner, frame_count) - owner * FR_DEV
        wanted = jnp.clip(wanted, 0, FR_DEV - 1)
        for turn in range(2):
            half = sub_index if turn == 0 else 1 - sub_index
            for part, source in enumerate((keys, values)):
                if place == 0 and turn == 1:
                    target = sibling.at[pl.ds(2 * count + part * FT, FT), :]
                else:
                    target = out.at[pl.ds((2 * turn + part) * FT, FT), :]
                start(source.at[wanted, :, columns_of(half)], target)
    for copy in copies[1:]:
        copy.wait()


def pack(frame_ids, mem_keys, mem_values, cur_keys, cur_values, weight, low, share, seq_count):
    parts = 2
    width = mem_keys.shape[2] // 2
    rows = [2 * FT] + [4 * FT] * (seq_count - 1) + [2 * cur_keys.shape[0] + 2 * FT]
    shapes = [(count, width) for count in rows] + [(weight.shape[0], share)]
    return pl.pallas_call(
        functools.partial(pack_kernel, seq_count, low, parts),
        out_shape=[pltpu.VMEM(shape, BF16) for shape in shapes],
        in_specs=[HBM] * 6,
        out_specs=[VMEM] * len(shapes),
        scratch_shapes=[
            pltpu.SMEM(frame_ids.shape, jnp.int32),
            pltpu.SemaphoreType.DMA((1 + 4 * seq_count + 3 * parts,)),
        ],
        compiler_params=params(),
        name="pack",
        cost_estimate=pl.CostEstimate(flops=0, bytes_accessed=12 * 2**20, transcendentals=0),
    )(*map(in_hbm, (frame_ids, mem_keys, mem_values, cur_keys, cur_values, weight)))


def pass_on_kernel(*refs):
    arrays, out = refs[:-2], refs[-1]
    rows = out.shape[0] // len(arrays)
    for index, array in enumerate(arrays):
        out[pl.ds(index * rows, rows), :] = array[pl.ds(rows, rows), :]


def pass_on(arrays, after):
    rows, width = arrays[0].shape
    return pl.pallas_call(
        pass_on_kernel,
        out_shape=pltpu.VMEM((len(arrays) * rows // 2, width), BF16),
        in_specs=[VMEM] * len(arrays) + [ANY],
        out_specs=VMEM,
        compiler_params=params(),
        name="pass_on",
        cost_estimate=SHORT,
    )(*map(in_vmem, arrays), in_vmem(after))


def load_kernel(parts, seq_count, ids, counts, weight, after, out, mask, sems):
    rows = weight.shape[0] // parts
    spans = [pl.ds(part * rows, rows) for part in range(parts)]
    copies = [pltpu.make_async_copy(weight.at[span, :], out.at[span, :], sems.at[index]) for index, span in enumerate(spans)]
    for copy in copies:
        copy.start()
    seq_index = lax.axis_index("seq")
    sub_index = lax.axis_index("sub")
    slot = lax.broadcasted_iota(jnp.int32, (1, FT), 1)
    for index in range(2 * seq_count):
        turn, place = divmod(index, seq_count)
        source_sub = sub_index if turn == 0 else 1 - sub_index
        owner = lax.bitwise_xor(seq_index, exchange_flip(place, source_sub, seq_count)) * 2 + source_sub
        live = slot < counts[held_by(ids, seq_index, owner, 2 * seq_count)]
        mask[pl.ds(index, 1), :] = jnp.where(live, 0.0, MASKED).astype(F32)
    for copy in copies:
        copy.wait()


def load(frame_ids, frame_counts, weight, seq_count, after):
    parts = 8
    return pl.pallas_call(
        functools.partial(load_kernel, parts, seq_count),
        out_shape=[pltpu.VMEM(weight.shape, BF16), pltpu.VMEM((2 * seq_count, FT), F32)],
        in_specs=[pl.BlockSpec(memory_space=pltpu.SMEM)] * 2 + [HBM, ANY],
        out_specs=[VMEM, VMEM],
        scratch_shapes=[pltpu.SemaphoreType.DMA((parts,))],
        compiler_params=params(),
        name="load",
        cost_estimate=pl.CostEstimate(flops=0, bytes_accessed=2 * weight.size, transcendentals=0),
    )(*map(in_hbm, (frame_ids, frame_counts, weight)), in_vmem(after))


def gate(array, after):
    return pl.pallas_call(
        lambda *refs: None,
        in_specs=[ANY, ANY],
        out_specs=ANY,
        out_shape=jax.ShapeDtypeStruct(array.shape, array.dtype),
        input_output_aliases={0: 0},
        compiler_params=params(),
        name="gate",
        cost_estimate=SHORT,
    )(in_vmem(array), in_vmem(after))


def leading_kernel(array, after, out):
    out[...] = array[:, pl.ds(0, out.shape[1])]


def leading(array, width, after):
    return pl.pallas_call(
        leading_kernel,
        in_specs=[VMEM, ANY],
        out_specs=VMEM,
        out_shape=pltpu.VMEM((array.shape[0], width), array.dtype),
        compiler_params=params(),
        name="leading",
        cost_estimate=SHORT,
    )(in_vmem(array), in_vmem(after))


def dot_t(left, right):
    return lax.dot_general(left, right, (((1,), (1,)), ((), ())), preferred_element_type=F32)


def wide(column, count):
    return jnp.concatenate([column] * count, axis=1)


def with_ones(values):
    return jnp.concatenate([values, jnp.ones_like(values)], axis=1)


def current_kernel(step, queries, own_keys, own_values, sibling, out, lse, q, own_k, own_v, sems):
    heads, rows, _ = out.shape
    count = own_k.shape[0]
    half = pl.ds(pl.multiple_of(lax.axis_index("sub") * q.shape[1], 128), q.shape[1])
    copy_all(
        [(queries.at[:, half], q), (own_keys.at[:, half], own_k), (own_values.at[:, half], own_v)],
        sems,
    )

    @pl.loop(0, heads)
    def _(head):
        columns = pl.ds(pl.multiple_of(head * HD, HD), HD)
        keys = jnp.concatenate([own_k[:, columns], sibling[pl.ds(0, count), columns]], axis=0)
        values = with_ones(jnp.concatenate([own_v[:, columns], sibling[pl.ds(count, count), columns]], axis=0))
        for low in range(0, rows, step):
            span = pl.ds(low, step)
            scores = dot_t(q[span, columns], keys)
            row_max = jnp.broadcast_to(jnp.max(scores, axis=1, keepdims=True), (step, HD))
            weights = jnp.exp2((scores - wide(row_max, 2 * count // HD)) * EXP2_SCALE).astype(BF16)
            product = jnp.dot(weights, values, preferred_element_type=F32)
            total = product[:, HD:]
            out[head, span, :] = product[:, :HD] / total
            lse[head, span, :] = row_max * EXP2_SCALE + jnp.log2(total)


def attend_current(queries, cur_keys, cur_values, sibling, heads):
    rows = queries.shape[0]
    keys = cur_keys.shape[0]
    return pl.pallas_call(
        functools.partial(current_kernel, 512),
        in_specs=[HBM] * 3 + [VMEM],
        out_specs=[VMEM] * 3,
        out_shape=[pltpu.VMEM((heads, rows, HD), F32)] * 2 + [pltpu.VMEM((rows, heads * HD), BF16)],
        scratch_shapes=[pltpu.VMEM((keys, heads * HD), BF16)] * 2 + [pltpu.SemaphoreType.DMA((3,))],
        compiler_params=params(),
        name="attend_current",
        cost_estimate=pl.CostEstimate(
            flops=6 * heads * rows * 2 * keys * HD, bytes_accessed=heads * rows * HD * 12, transcendentals=heads * rows * 2 * keys
        ),
    )(in_hbm(queries), in_hbm(cur_keys), in_hbm(cur_values), in_vmem(sibling))


def frames_kernel(heads, half_of, state_half_of, first, starts, final, bias, q, held, lse, *rest):
    frames = rest[: len(starts)]
    outs = rest[-1:] if final else rest[-2:]
    count, rows = len(starts), outs[0].shape[-2]

    def rows_of(half):
        return pl.ds(pl.multiple_of(half() * rows, rows), rows)

    span, state_span = rows_of(half_of), rows_of(state_half_of)
    mask = jnp.concatenate([bias[pl.ds(first + index, 1), :] for index in range(count)], axis=1)

    def gathered(head, part):
        columns = pl.ds(head * HD, HD)
        return jnp.concatenate(
            [frame[pl.ds(start + part * FT, FT), columns] for frame, start in zip(frames, starts)], axis=0
        )

    def scores_of(head):
        return dot_t(q[span, pl.ds(head * HD, HD)], gathered(head, 0))

    def finish(head, scores):
        scores = scores * EXP2_SCALE + mask
        old = lse[head, state_span, :]
        new_max = jnp.maximum(old, jnp.max(scores, axis=1, keepdims=True))
        weights = jnp.exp2(scores - wide(new_max, count * FT // HD)).astype(BF16)
        product = jnp.dot(weights, with_ones(gathered(head, 1)), preferred_element_type=F32)
        scale = jnp.exp2(old - new_max)
        total = scale + product[:, HD:]
        top = (held[head, state_span, :] * scale + product[:, :HD]) / total
        if final:
            outs[0][:, pl.ds(head * HD, HD)] = top.astype(BF16)
        else:
            outs[0][head] = top
            outs[1][head] = new_max + jnp.log2(total)

    scores = scores_of(0)
    for head in range(heads):
        following = scores_of(head + 1) if head + 1 < heads else None
        finish(head, scores)
        scores = following


def far_half():
    return 1 - lax.axis_index("head")


def near_half():
    return lax.axis_index("head")


def attend_frames(name, half, bias, first, q, held, lse, frames, starts, final, after=()):
    heads, state_rows, _ = held.shape
    rows = q.shape[0] // 2
    state_half = half if state_rows > rows else lambda: jnp.int32(0)
    operands = [bias, q, held, lse, *frames]
    if final:
        out_shape = [pltpu.VMEM((rows, heads * HD), BF16)]
    else:
        out_shape = [pltpu.VMEM((heads, rows, HD), F32)] * 2
    outs = pl.pallas_call(
        functools.partial(frames_kernel, heads, half, state_half, first, tuple(starts), final),
        in_specs=[VMEM] * len(operands) + [ANY] * len(after),
        out_specs=[VMEM] * len(out_shape),
        out_shape=out_shape,
        compiler_params=params(),
        name=name,
        cost_estimate=SHORT,
    )(*map(in_vmem, operands), *map(in_vmem, after))
    return outs[0] if final else outs


def both(mine, other):
    first, second = mine[...], other[...]
    return jnp.where(
        lax.axis_index("sub") == 0,
        jnp.concatenate([first, second], axis=1),
        jnp.concatenate([second, first], axis=1),
    )


def side_by_side_kernel(mine, other, out):
    out[...] = both(mine, other)


def side_by_side(mine, other):
    return pl.pallas_call(
        side_by_side_kernel,
        in_specs=[VMEM] * 2,
        out_specs=VMEM,
        out_shape=pltpu.VMEM((mine.shape[0], 2 * mine.shape[1]), BF16),
        compiler_params=params(),
        name="side_by_side",
        cost_estimate=SHORT,
    )(in_vmem(mine), in_vmem(other))


def project_kernel(step, mine, other, weight, *rest):
    out = rest[-1]
    rows = both(mine, other)

    @pl.loop(0, out.shape[1] // step)
    def _(index):
        columns = pl.ds(pl.multiple_of(index * step, step), step)
        out[:, columns] = jnp.dot(rows, weight[:, columns], preferred_element_type=F32).astype(BF16)


def unshared_columns(low, share, passed):
    found = [pl.ds(0, low)] if low else []
    for other_seq, other_group, skipped in ((True, True, 0), (False, True, passed), (True, False, passed)):
        if skipped < share:
            start = low + quarter(other_seq, other_group) * share + skipped
            found.append(pl.ds(pl.multiple_of(start, 128), share - skipped))
    return found


def unshared_kernel(low, share, passed, mine, other, weight, *rest):
    out = rest[-1]
    rows = both(mine, other)
    start = 0
    for columns in unshared_columns(low, share, passed):
        out[:, pl.ds(start, columns.size)] = jnp.dot(rows, weight[:, columns], preferred_element_type=F32).astype(BF16)
        start += columns.size


def project_call(kernel, name, mine, other, weight, width, after):
    return pl.pallas_call(
        kernel,
        in_specs=[VMEM] * 3 + [ANY] * len(after),
        out_specs=VMEM,
        out_shape=pltpu.VMEM((mine.shape[0], width), BF16),
        compiler_params=params(),
        name=name,
        cost_estimate=SHORT,
    )(*map(in_vmem, (mine, other, weight, *after)))


def project(mine, other, weight, after):
    return project_call(functools.partial(project_kernel, 512), "project", mine, other, weight, weight.shape[1], after)


def project_unshared(mine, other, weight, low, share, passed, after):
    kernel = functools.partial(unshared_kernel, low, share, passed)
    width = low + share + 2 * (share - passed)
    return project_call(kernel, "project_unshared", mine, other, weight, width, after)


def write_blocks(blocks, out, scratch, sems):
    copies, start = [], 0
    for index, (block, low) in enumerate(blocks):
        span = pl.ds(start, block.shape[1])
        scratch[:, span] = block.astype(BF16)
        copy = pltpu.make_async_copy(scratch.at[:, span], out.at[:, pl.ds(low, block.shape[1])], sems.at[index])
        copy.start()
        copies.append(copy)
        start += block.shape[1]
    for copy in copies:
        copy.wait()


def remote_kernel(first, share, other_seq, other_group, terms, rows, weight, total, out, scratch, sems):
    block = weight.shape[1]
    low = pl.multiple_of(first + quarter(other_seq, other_group) * share, 128)
    product = jnp.dot(rows[...], weight[...], preferred_element_type=F32)
    write_blocks([(terms[:, pl.ds(low, block)].astype(F32) + product, low)], out, scratch, sems)


def add_kernel(low, share, passed, terms, came, total, out, scratch, sems):
    blocks, start = [], 0
    for columns in unshared_columns(low, share, passed):
        block = terms[:, columns].astype(F32) + came[:, pl.ds(start, columns.size)].astype(F32)
        blocks.append((block, columns.start))
        start += columns.size
    write_blocks(blocks, out, scratch, sems)


def finish_block(kernel, name, operands, total, rows, width, block):
    count = len(operands)
    if total is None:
        body = lambda *refs: kernel(*refs[:count], None, *refs[count:])
        totals, aliases = [], {}
    else:
        body, totals, aliases = kernel, [in_hbm(total)], {count: 0}
    return pl.pallas_call(
        body,
        in_specs=[VMEM] * count + [HBM] * len(totals),
        out_specs=HBM,
        out_shape=pltpu.HBM((rows, width), BF16),
        input_output_aliases=aliases,
        scratch_shapes=[pltpu.VMEM((rows, block), BF16), pltpu.SemaphoreType.DMA((4,))],
        compiler_params=params(),
        name=name,
        cost_estimate=SHORT,
    )(*map(in_vmem, operands), *totals)


def add_remote(terms, rows, weight, first, share, other_seq, other_group, total):
    kernel = functools.partial(remote_kernel, first, share, other_seq, other_group)
    return finish_block(kernel, "add_remote", (terms, rows, weight), total, *terms.shape, weight.shape[1])


def add_unshared(terms, came, low, share, passed, total):
    kernel = functools.partial(add_kernel, low, share, passed)
    return finish_block(kernel, "add_unshared", (terms, came), total, *terms.shape, came.shape[1])


def local(queries, cur_keys, cur_values, mem_keys, mem_values, frame_ids, frame_counts, out_weight):
    seq_count = lax.axis_size("seq")
    heads = queries.shape[1] // HD // 2
    keys = cur_keys.shape[0]
    out_cols = out_weight.shape[1]
    share = out_cols // 4 // 128 * 128
    passed_on = share * 4 // 5 // 128 * 128
    low = out_cols - 4 * share

    *sends, to_sibling, columns = pack(
        frame_ids, mem_keys, mem_values, cur_keys, cur_values, out_weight, low, share, seq_count
    )
    mine = [sends[0]]
    for place in range(1, seq_count):
        flips = [order[place] for order in exchange_orders(seq_count)]
        pairs = [(2 * seq + sub, 2 * (seq ^ flip) + sub) for seq in range(seq_count) for sub, flip in enumerate(flips)]
        mine.append(lax.ppermute(sends[place], ("seq", "sub"), pairs))
    columns = lax.ppermute(columns, "head", SWAP)
    sibling = lax.ppermute(to_sibling, "sub", SWAP)

    held, lse, q = attend_current(queries, cur_keys, cur_values, sibling, heads)
    weight, bias = load(frame_ids, frame_counts, out_weight, seq_count, lse)
    passed = pass_on(mine[1:], weight)
    theirs = lax.ppermute(passed, "sub", SWAP)
    others = [sibling] + [theirs] * (seq_count - 1)
    starts = [2 * keys] + [2 * FT * index for index in range(seq_count - 1)]

    state = attend_frames("far_first", far_half, bias, 0, q, held, lse, mine, [0] * seq_count, False, (passed,))
    far = attend_frames("far_last", far_half, bias, seq_count, q, *state, others, starts, True)
    came_mine = lax.ppermute(far, "head", SWAP)
    far_sibling = lax.ppermute(far, "sub", SWAP)
    columns_copy = leading(columns, passed_on, far)
    group_columns = lax.ppermute(columns_copy, "groups", SWAP)
    seq_columns = lax.ppermute(columns_copy, "seq", [(index, index ^ 1) for index in range(seq_count)])
    starts = [0] * seq_count + starts
    near = attend_frames("near", near_half, bias, 0, q, held, lse, mine + others, starts, True, (columns_copy,))
    near_sibling = lax.ppermute(near, "sub", SWAP)

    term = project_unshared(far, far_sibling, weight, low, share, passed_on, (near,))
    came = lax.ppermute(term, "head", SWAP)
    came_mine = gate(came_mine, term)
    came_other = lax.ppermute(came_mine, "sub", SWAP)
    terms = project(near, near_sibling, weight, (came_mine,))

    arrived = (terms, side_by_side(came_mine, came_other))
    total = add_remote(*arrived, columns, low, share, False, False, None)
    total = add_remote(*arrived, group_columns, low, share, False, True, total)
    total = add_remote(*arrived, seq_columns, low, share, True, False, total)
    return add_unshared(terms, came, low, share, passed_on, total)


def local_any(queries, cur_keys, cur_values, mem_keys, mem_values, frame_ids, frame_counts, out_weight):
    seq_count = lax.axis_size("seq")
    sub_count = lax.axis_size("sub")
    seq_index = lax.axis_index("seq")
    owner_self = seq_index * sub_count + lax.axis_index("sub")
    row_count, col_count = queries.shape
    heads = col_count // HD
    mine = row_count // sub_count
    wanted = jnp.sum(jnp.where(frame_ids // FR_DEV == owner_self, frame_ids, 0), axis=1) - owner_self * FR_DEV
    own_list = lax.dynamic_index_in_dim(frame_ids, seq_index, 0, keepdims=False)
    owners = jnp.arange(seq_count * sub_count, dtype=jnp.int32)
    hit = (own_list // FR_DEV)[None, :] == owners[:, None]
    got_ids = jnp.sum(jnp.where(hit, own_list[None, :], 0), axis=1).reshape(seq_count, sub_count).T.reshape(-1)
    live = jnp.arange(FT, dtype=jnp.int32)[None, :] < jnp.take(frame_counts, got_ids)[:, None]

    def spread(cached, current):
        sent = lax.all_to_all(jnp.take(cached, wanted, axis=0), "seq", split_axis=0, concat_axis=0, tiled=True)
        far = lax.all_gather(sent, "sub").reshape(-1, heads, HD)
        return jnp.concatenate([lax.all_gather(current, "sub").reshape(-1, heads, HD), far], axis=0)

    keys, values = spread(mem_keys, cur_keys), spread(mem_values, cur_values)
    key_live = jnp.concatenate([jnp.ones((keys.shape[0] - live.size,), bool), live.reshape(-1)])
    start = lax.axis_index("sub") * mine
    query_heads = lax.dynamic_slice_in_dim(queries, start, mine, 0).reshape(mine, heads, HD)
    scores = jnp.einsum("qhd,khd->hqk", query_heads, keys, preferred_element_type=F32) / math.sqrt(HD)
    scores = jnp.where(key_live[None, None, :], scores, -jnp.inf)
    expo = jnp.exp(scores - jnp.max(scores, axis=-1, keepdims=True))
    total = jnp.sum(expo, axis=-1)
    weighted = jnp.einsum("hqk,khd->qhd", expo.astype(BF16), values, preferred_element_type=F32)
    attended = (weighted / total.T[:, :, None]).reshape(mine, col_count).astype(BF16)
    attended = lax.all_gather(attended, "sub", axis=0, tiled=True)
    term = jnp.dot(attended, out_weight, preferred_element_type=F32).astype(BF16)
    return lax.psum_scatter(term, "head", scatter_dimension=0, tiled=True)


def solution(mesh):
    in_specs = (
        P(("groups", "seq"), "head"),
        P(("groups", "seq", "sub"), "head"),
        P(("groups", "seq", "sub"), "head"),
        P(("groups", "seq", "sub"), None, "head"),
        P(("groups", "seq", "sub"), None, "head"),
        P("groups", None),
        P("groups"),
        P("head", "sub"),
    )
    out_specs = P(("groups", "seq", "head"), "sub")

    def apply(queries, *rest):
        heads = queries.shape[1] // mesh.shape["head"] // HD
        paired = heads % 2 == 0 and mesh.shape["seq"] in (2, 4, 8)
        paired = paired and all(mesh.shape[axis] == 2 for axis in ("groups", "head", "sub"))
        body = local if paired else local_any
        return jax.shard_map(body, mesh=mesh, in_specs=in_specs, out_specs=out_specs, check_vma=False)(queries, *rest)

    return apply
```

```python
import functools
import math

import jax
import jax.numpy as jnp
from jax import lax
from jax.experimental import pallas as pl
from jax.experimental.pallas import tpu as pltpu
from jax.sharding import PartitionSpec as P

HD = 128
FT = 64
FR_DEV = 16
F32 = jnp.float32
BF16 = jnp.bfloat16
EXP2_SCALE = math.log2(math.e) / math.sqrt(HD)
MASKED = -1e30
VMEM_LIMIT = 24 * 1024 * 1024
SWAP = [(0, 1), (1, 0)]
SHORT = pl.CostEstimate(flops=1024, bytes_accessed=1024, transcendentals=0)
ANY = pl.BlockSpec(memory_space=pl.ANY)
HBM = pl.BlockSpec(memory_space=pltpu.HBM)
VMEM = pl.BlockSpec(memory_space=pltpu.VMEM)


def params():
    return pltpu.CompilerParams(vmem_limit_bytes=VMEM_LIMIT)


def in_hbm(array):
    return pltpu.with_memory_space_constraint(array, pltpu.HBM)


def in_vmem(array):
    return pltpu.with_memory_space_constraint(array, pltpu.VMEM)


def quarter(other_seq, other_group):
    seq_part = lax.rem(lax.axis_index("seq"), 2)
    group = lax.axis_index("groups")
    return 2 * (1 - seq_part if other_seq else seq_part) + (1 - group if other_group else group)


def copy_all(pairs, sems):
    copies = [pltpu.make_async_copy(*pair, sems.at[index]) for index, pair in enumerate(pairs)]
    for copy in copies:
        copy.start()
    for copy in copies:
        copy.wait()


def exchange_order(seq_count):
    return [0, *range(seq_count // 2, seq_count), *range(1, seq_count // 2)]


def held_by(ids, stretch, owner, count):
    found = jnp.int32(0)
    for entry in range(count):
        frame = ids[stretch, entry]
        slot = frame - owner * FR_DEV
        found = jnp.where((slot >= 0) & (slot < FR_DEV), frame, found)
    return found


def pack_kernel(seq_count, low, parts, ids_in, keys, values, cur_keys, cur_values, weight, *rest):
    outs = rest[:seq_count]
    sibling, columns_out, ids, sems = rest[seq_count:]
    seq_index = lax.axis_index("seq")
    sub_index = lax.axis_index("sub")
    width = sibling.shape[1]
    block = columns_out.shape[1]
    count = cur_keys.shape[0]
    frame_count = 2 * seq_count
    copies = []

    def start(source, target):
        copy = pltpu.make_async_copy(source, target, sems.at[len(copies)])
        copy.start()
        copies.append(copy)
        return copy

    def columns_of(half):
        return pl.ds(pl.multiple_of(half * width, 128), width)

    listed = start(ids_in, ids)
    rows = count // parts
    for part, source in enumerate((cur_keys, cur_values)):
        for low_row in range(0, count, rows):
            target = sibling.at[pl.ds(part * count + low_row, rows), :]
            start(source.at[pl.ds(low_row, rows), columns_of(1 - sub_index)], target)
    first = pl.multiple_of(low + quarter(False, False) * block, 128)
    rows = weight.shape[0] // parts
    for part in range(parts):
        span = pl.ds(part * rows, rows)
        start(weight.at[span, pl.ds(first, block)], columns_out.at[span, :])
    listed.wait()
    for flip, out in zip(exchange_order(seq_count), outs):
        owner = seq_index * 2 + sub_index
        wanted = held_by(ids, lax.bitwise_xor(seq_index, flip), owner, frame_count) - owner * FR_DEV
        wanted = jnp.clip(wanted, 0, FR_DEV - 1)
        for turn in range(2):
            half = sub_index if turn == 0 else 1 - sub_index
            for part, source in enumerate((keys, values)):
                if flip == 0 and turn == 1:
                    target = sibling.at[pl.ds(2 * count + part * FT, FT), :]
                else:
                    target = out.at[pl.ds((2 * turn + part) * FT, FT), :]
                start(source.at[wanted, :, columns_of(half)], target)
    for copy in copies[1:]:
        copy.wait()


def pack(frame_ids, mem_keys, mem_values, cur_keys, cur_values, weight, low, share, seq_count):
    parts = 4
    width = mem_keys.shape[2] // 2
    rows = [2 * FT] + [4 * FT] * (seq_count - 1) + [2 * cur_keys.shape[0] + 2 * FT]
    shapes = [(count, width) for count in rows] + [(weight.shape[0], share)]
    return pl.pallas_call(
        functools.partial(pack_kernel, seq_count, low, parts),
        out_shape=[pltpu.VMEM(shape, BF16) for shape in shapes],
        in_specs=[HBM] * 6,
        out_specs=[VMEM] * len(shapes),
        scratch_shapes=[
            pltpu.SMEM(frame_ids.shape, jnp.int32),
            pltpu.SemaphoreType.DMA((1 + 4 * seq_count + 3 * parts,)),
        ],
        compiler_params=params(),
        name="pack",
        cost_estimate=pl.CostEstimate(flops=0, bytes_accessed=12 * 2**20, transcendentals=0),
    )(*map(in_hbm, (frame_ids, mem_keys, mem_values, cur_keys, cur_values, weight)))


def pass_on_kernel(*refs):
    arrays, out = refs[:-2], refs[-1]
    rows = out.shape[0] // len(arrays)
    for index, array in enumerate(arrays):
        out[pl.ds(index * rows, rows), :] = array[pl.ds(rows, rows), :]


def pass_on(arrays, after):
    rows, width = arrays[0].shape
    return pl.pallas_call(
        pass_on_kernel,
        out_shape=pltpu.VMEM((len(arrays) * rows // 2, width), BF16),
        in_specs=[VMEM] * len(arrays) + [ANY],
        out_specs=VMEM,
        compiler_params=params(),
        name="pass_on",
        cost_estimate=SHORT,
    )(*map(in_vmem, arrays), in_vmem(after))


def load_kernel(parts, seq_count, ids, counts, weight, after, out, mask, sems):
    rows = weight.shape[0] // parts
    spans = [pl.ds(part * rows, rows) for part in range(parts)]
    copies = [pltpu.make_async_copy(weight.at[span, :], out.at[span, :], sems.at[index]) for index, span in enumerate(spans)]
    for copy in copies:
        copy.start()
    seq_index = lax.axis_index("seq")
    sub_index = lax.axis_index("sub")
    slot = lax.broadcasted_iota(jnp.int32, (1, FT), 1)
    for index in range(2 * seq_count):
        turn, place = divmod(index, seq_count)
        source = lax.bitwise_xor(seq_index, exchange_order(seq_count)[place]) * 2
        owner = source + (sub_index if turn == 0 else 1 - sub_index)
        live = slot < counts[held_by(ids, seq_index, owner, 2 * seq_count)]
        mask[pl.ds(index, 1), :] = jnp.where(live, 0.0, MASKED).astype(F32)
    for copy in copies:
        copy.wait()


def load(frame_ids, frame_counts, weight, seq_count, after):
    parts = 8
    return pl.pallas_call(
        functools.partial(load_kernel, parts, seq_count),
        out_shape=[pltpu.VMEM(weight.shape, BF16), pltpu.VMEM((2 * seq_count, FT), F32)],
        in_specs=[pl.BlockSpec(memory_space=pltpu.SMEM)] * 2 + [HBM, ANY],
        out_specs=[VMEM, VMEM],
        scratch_shapes=[pltpu.SemaphoreType.DMA((parts,))],
        compiler_params=params(),
        name="load",
        cost_estimate=pl.CostEstimate(flops=0, bytes_accessed=2 * weight.size, transcendentals=0),
    )(*map(in_hbm, (frame_ids, frame_counts, weight)), in_vmem(after))


def gate(array, after):
    return pl.pallas_call(
        lambda *refs: None,
        in_specs=[ANY, ANY],
        out_specs=ANY,
        out_shape=jax.ShapeDtypeStruct(array.shape, array.dtype),
        input_output_aliases={0: 0},
        compiler_params=params(),
        name="gate",
        cost_estimate=SHORT,
    )(in_vmem(array), in_vmem(after))


def leading_kernel(array, after, out):
    out[...] = array[:, pl.ds(0, out.shape[1])]


def leading(array, width, after):
    return pl.pallas_call(
        leading_kernel,
        in_specs=[VMEM, ANY],
        out_specs=VMEM,
        out_shape=pltpu.VMEM((array.shape[0], width), array.dtype),
        compiler_params=params(),
        name="leading",
        cost_estimate=SHORT,
    )(in_vmem(array), in_vmem(after))


def dot_t(left, right):
    return lax.dot_general(left, right, (((1,), (1,)), ((), ())), preferred_element_type=F32)


def wide(column, count):
    return jnp.concatenate([column] * count, axis=1)


def with_ones(values):
    return jnp.concatenate([values, jnp.ones_like(values)], axis=1)


def current_kernel(step, queries, own_keys, own_values, sibling, out, lse, q, own_k, own_v, sems):
    heads, rows, _ = out.shape
    count = own_k.shape[0]
    half = pl.ds(pl.multiple_of(lax.axis_index("sub") * q.shape[1], 128), q.shape[1])
    copy_all(
        [(queries.at[:, half], q), (own_keys.at[:, half], own_k), (own_values.at[:, half], own_v)],
        sems,
    )

    @pl.loop(0, heads)
    def _(head):
        columns = pl.ds(pl.multiple_of(head * HD, HD), HD)
        keys = jnp.concatenate([own_k[:, columns], sibling[pl.ds(0, count), columns]], axis=0)
        values = with_ones(jnp.concatenate([own_v[:, columns], sibling[pl.ds(count, count), columns]], axis=0))
        for low in range(0, rows, step):
            span = pl.ds(low, step)
            scores = dot_t(q[span, columns], keys)
            row_max = jnp.broadcast_to(jnp.max(scores, axis=1, keepdims=True), (step, HD))
            weights = jnp.exp2((scores - wide(row_max, 2 * count // HD)) * EXP2_SCALE).astype(BF16)
            product = jnp.dot(weights, values, preferred_element_type=F32)
            total = product[:, HD:]
            out[head, span, :] = product[:, :HD] / total
            lse[head, span, :] = row_max * EXP2_SCALE + jnp.log2(total)


def attend_current(queries, cur_keys, cur_values, sibling, heads):
    rows = queries.shape[0]
    keys = cur_keys.shape[0]
    return pl.pallas_call(
        functools.partial(current_kernel, 512),
        in_specs=[HBM] * 3 + [VMEM],
        out_specs=[VMEM] * 3,
        out_shape=[pltpu.VMEM((heads, rows, HD), F32)] * 2 + [pltpu.VMEM((rows, heads * HD), BF16)],
        scratch_shapes=[pltpu.VMEM((keys, heads * HD), BF16)] * 2 + [pltpu.SemaphoreType.DMA((3,))],
        compiler_params=params(),
        name="attend_current",
        cost_estimate=pl.CostEstimate(
            flops=6 * heads * rows * 2 * keys * HD, bytes_accessed=heads * rows * HD * 12, transcendentals=heads * rows * 2 * keys
        ),
    )(in_hbm(queries), in_hbm(cur_keys), in_hbm(cur_values), in_vmem(sibling))


def frames_kernel(heads, half_of, state_half_of, first, starts, final, bias, q, held, lse, *rest):
    frames = rest[: len(starts)]
    outs = rest[-1:] if final else rest[-2:]
    count, rows = len(starts), outs[0].shape[-2]

    def rows_of(half):
        return pl.ds(pl.multiple_of(half() * rows, rows), rows)

    span, state_span = rows_of(half_of), rows_of(state_half_of)
    mask = jnp.concatenate([bias[pl.ds(first + index, 1), :] for index in range(count)], axis=1)

    def gathered(head, part):
        columns = pl.ds(head * HD, HD)
        return jnp.concatenate(
            [frame[pl.ds(start + part * FT, FT), columns] for frame, start in zip(frames, starts)], axis=0
        )

    def scores_of(head):
        return dot_t(q[span, pl.ds(head * HD, HD)], gathered(head, 0))

    def finish(head, scores):
        scores = scores * EXP2_SCALE + mask
        old = lse[head, state_span, :]
        new_max = jnp.maximum(old, jnp.max(scores, axis=1, keepdims=True))
        weights = jnp.exp2(scores - wide(new_max, count * FT // HD)).astype(BF16)
        product = jnp.dot(weights, with_ones(gathered(head, 1)), preferred_element_type=F32)
        scale = jnp.exp2(old - new_max)
        total = scale + product[:, HD:]
        top = (held[head, state_span, :] * scale + product[:, :HD]) / total
        if final:
            outs[0][:, pl.ds(head * HD, HD)] = top.astype(BF16)
        else:
            outs[0][head] = top
            outs[1][head] = new_max + jnp.log2(total)

    scores = scores_of(0)
    for head in range(heads):
        following = scores_of(head + 1) if head + 1 < heads else None
        finish(head, scores)
        scores = following


def far_half():
    return 1 - lax.axis_index("head")


def near_half():
    return lax.axis_index("head")


def attend_frames(name, half, bias, first, q, held, lse, frames, starts, final, after=()):
    heads, state_rows, _ = held.shape
    rows = q.shape[0] // 2
    state_half = half if state_rows > rows else lambda: jnp.int32(0)
    operands = [bias, q, held, lse, *frames]
    if final:
        out_shape = [pltpu.VMEM((rows, heads * HD), BF16)]
    else:
        out_shape = [pltpu.VMEM((heads, rows, HD), F32)] * 2
    outs = pl.pallas_call(
        functools.partial(frames_kernel, heads, half, state_half, first, tuple(starts), final),
        in_specs=[VMEM] * len(operands) + [ANY] * len(after),
        out_specs=[VMEM] * len(out_shape),
        out_shape=out_shape,
        compiler_params=params(),
        name=name,
        cost_estimate=SHORT,
    )(*map(in_vmem, operands), *map(in_vmem, after))
    return outs[0] if final else outs


def both(mine, other):
    first, second = mine[...], other[...]
    return jnp.where(
        lax.axis_index("sub") == 0,
        jnp.concatenate([first, second], axis=1),
        jnp.concatenate([second, first], axis=1),
    )


def project_kernel(step, mine, other, weight, *rest):
    out = rest[-1]
    rows = both(mine, other)

    @pl.loop(0, out.shape[1] // step)
    def _(index):
        columns = pl.ds(pl.multiple_of(index * step, step), step)
        out[:, columns] = jnp.dot(rows, weight[:, columns], preferred_element_type=F32).astype(BF16)


def unshared_columns(low, share, passed):
    found = [pl.ds(0, low)] if low else []
    for other_seq, other_group, skipped in ((True, True, 0), (False, True, passed), (True, False, passed)):
        if skipped < share:
            start = low + quarter(other_seq, other_group) * share + skipped
            found.append(pl.ds(pl.multiple_of(start, 128), share - skipped))
    return found


def unshared_kernel(low, share, passed, mine, other, weight, *rest):
    out = rest[-1]
    rows = both(mine, other)
    start = 0
    for columns in unshared_columns(low, share, passed):
        out[:, pl.ds(start, columns.size)] = jnp.dot(rows, weight[:, columns], preferred_element_type=F32).astype(BF16)
        start += columns.size


def project_call(kernel, name, mine, other, weight, width, after):
    return pl.pallas_call(
        kernel,
        in_specs=[VMEM] * 3 + [ANY] * len(after),
        out_specs=VMEM,
        out_shape=pltpu.VMEM((mine.shape[0], width), BF16),
        compiler_params=params(),
        name=name,
        cost_estimate=SHORT,
    )(*map(in_vmem, (mine, other, weight, *after)))


def project(mine, other, weight, after):
    return project_call(functools.partial(project_kernel, 512), "project", mine, other, weight, weight.shape[1], after)


def project_unshared(mine, other, weight, low, share, passed, after):
    kernel = functools.partial(unshared_kernel, low, share, passed)
    width = low + share + 2 * (share - passed)
    return project_call(kernel, "project_unshared", mine, other, weight, width, after)


def write_blocks(blocks, out, scratch, sems):
    copies, start = [], 0
    for index, (block, low) in enumerate(blocks):
        span = pl.ds(start, block.shape[1])
        scratch[:, span] = block.astype(BF16)
        copy = pltpu.make_async_copy(scratch.at[:, span], out.at[:, pl.ds(low, block.shape[1])], sems.at[index])
        copy.start()
        copies.append(copy)
        start += block.shape[1]
    for copy in copies:
        copy.wait()


def remote_kernel(first, share, other_seq, other_group, terms, mine, other, weight, total, out, scratch, sems):
    block = weight.shape[1]
    low = pl.multiple_of(first + quarter(other_seq, other_group) * share, 128)
    product = jnp.dot(both(mine, other), weight[...], preferred_element_type=F32)
    write_blocks([(terms[:, pl.ds(low, block)].astype(F32) + product, low)], out, scratch, sems)


def add_kernel(low, share, passed, terms, came, total, out, scratch, sems):
    half = came.shape[0] // 2
    copies = []
    for row in (0, half):
        rows, start = pl.ds(row, half), 0
        for columns in unshared_columns(low, share, passed):
            span = pl.ds(start, columns.size)
            scratch[rows, span] = (terms[rows, columns].astype(F32) + came[rows, span].astype(F32)).astype(BF16)
            copy = pltpu.make_async_copy(scratch.at[rows, span], out.at[rows, columns], sems.at[len(copies)])
            copy.start()
            copies.append(copy)
            start += columns.size
    for copy in copies:
        copy.wait()


def finish_block(kernel, name, operands, total, rows, width, block):
    count = len(operands)
    if total is None:
        body = lambda *refs: kernel(*refs[:count], None, *refs[count:])
        totals, aliases = [], {}
    else:
        body, totals, aliases = kernel, [in_hbm(total)], {count: 0}
    return pl.pallas_call(
        body,
        in_specs=[VMEM] * count + [HBM] * len(totals),
        out_specs=HBM,
        out_shape=pltpu.HBM((rows, width), BF16),
        input_output_aliases=aliases,
        scratch_shapes=[pltpu.VMEM((rows, block), BF16), pltpu.SemaphoreType.DMA((8,))],
        compiler_params=params(),
        name=name,
        cost_estimate=SHORT,
    )(*map(in_vmem, operands), *totals)


def add_remote(terms, mine, other, weight, first, share, other_seq, other_group, total):
    kernel = functools.partial(remote_kernel, first, share, other_seq, other_group)
    return finish_block(kernel, "add_remote", (terms, mine, other, weight), total, *terms.shape, weight.shape[1])


def add_unshared(terms, came, low, share, passed, total):
    kernel = functools.partial(add_kernel, low, share, passed)
    return finish_block(kernel, "add_unshared", (terms, came), total, *terms.shape, came.shape[1])


def local(queries, cur_keys, cur_values, mem_keys, mem_values, frame_ids, frame_counts, out_weight):
    seq_count = lax.axis_size("seq")
    heads = queries.shape[1] // HD // 2
    keys = cur_keys.shape[0]
    out_cols = out_weight.shape[1]
    share = out_cols // 4 // 128 * 128
    passed_on = share * 4 // 5 // 128 * 128
    low = out_cols - 4 * share

    *sends, to_sibling, columns = pack(
        frame_ids, mem_keys, mem_values, cur_keys, cur_values, out_weight, low, share, seq_count
    )
    mine = [sends[0]]
    for flip, sent in list(zip(exchange_order(seq_count), sends))[1:]:
        mine.append(lax.ppermute(sent, "seq", [(index, index ^ flip) for index in range(seq_count)]))
    columns = lax.ppermute(columns, "head", SWAP)
    sibling = lax.ppermute(to_sibling, "sub", SWAP)

    held, lse, q = attend_current(queries, cur_keys, cur_values, sibling, heads)
    weight, bias = load(frame_ids, frame_counts, out_weight, seq_count, lse)
    passed = pass_on(mine[1:], weight)
    theirs = lax.ppermute(passed, "sub", SWAP)
    others = [sibling] + [theirs] * (seq_count - 1)
    starts = [2 * keys] + [2 * FT * index for index in range(seq_count - 1)]

    state = attend_frames("far_first", far_half, bias, 0, q, held, lse, mine, [0] * seq_count, False, (passed,))
    far = attend_frames("far_last", far_half, bias, seq_count, q, *state, others, starts, True)
    came_mine = lax.ppermute(far, "head", SWAP)
    far_sibling = lax.ppermute(far, "sub", SWAP)
    columns_copy = leading(columns, passed_on, far)
    group_columns = lax.ppermute(columns_copy, "groups", SWAP)
    seq_columns = lax.ppermute(columns_copy, "seq", [(index, index ^ 1) for index in range(seq_count)])
    starts = [0] * seq_count + starts
    near = attend_frames("near", near_half, bias, 0, q, held, lse, mine + others, starts, True, (columns_copy,))
    near_sibling = lax.ppermute(near, "sub", SWAP)

    term = project_unshared(far, far_sibling, weight, low, share, passed_on, (near,))
    came = lax.ppermute(term, "head", SWAP)
    came_mine = gate(came_mine, term)
    came_other = lax.ppermute(came_mine, "sub", SWAP)
    terms = project(near, near_sibling, weight, (came_mine,))

    arrived = (terms, came_mine, came_other)
    total = add_remote(*arrived, columns, low, share, False, False, None)
    total = add_remote(*arrived, group_columns, low, share, False, True, total)
    total = add_remote(*arrived, seq_columns, low, share, True, False, total)
    return add_unshared(terms, came, low, share, passed_on, total)


def local_any(queries, cur_keys, cur_values, mem_keys, mem_values, frame_ids, frame_counts, out_weight):
    seq_count = lax.axis_size("seq")
    sub_count = lax.axis_size("sub")
    seq_index = lax.axis_index("seq")
    owner_self = seq_index * sub_count + lax.axis_index("sub")
    row_count, col_count = queries.shape
    heads = col_count // HD
    mine = row_count // sub_count
    wanted = jnp.sum(jnp.where(frame_ids // FR_DEV == owner_self, frame_ids, 0), axis=1) - owner_self * FR_DEV
    own_list = lax.dynamic_index_in_dim(frame_ids, seq_index, 0, keepdims=False)
    owners = jnp.arange(seq_count * sub_count, dtype=jnp.int32)
    hit = (own_list // FR_DEV)[None, :] == owners[:, None]
    got_ids = jnp.sum(jnp.where(hit, own_list[None, :], 0), axis=1).reshape(seq_count, sub_count).T.reshape(-1)
    live = jnp.arange(FT, dtype=jnp.int32)[None, :] < jnp.take(frame_counts, got_ids)[:, None]

    def spread(cached, current):
        sent = lax.all_to_all(jnp.take(cached, wanted, axis=0), "seq", split_axis=0, concat_axis=0, tiled=True)
        far = lax.all_gather(sent, "sub").reshape(-1, heads, HD)
        return jnp.concatenate([lax.all_gather(current, "sub").reshape(-1, heads, HD), far], axis=0)

    keys, values = spread(mem_keys, cur_keys), spread(mem_values, cur_values)
    key_live = jnp.concatenate([jnp.ones((keys.shape[0] - live.size,), bool), live.reshape(-1)])
    start = lax.axis_index("sub") * mine
    query_heads = lax.dynamic_slice_in_dim(queries, start, mine, 0).reshape(mine, heads, HD)
    scores = jnp.einsum("qhd,khd->hqk", query_heads, keys, preferred_element_type=F32) / math.sqrt(HD)
    scores = jnp.where(key_live[None, None, :], scores, -jnp.inf)
    expo = jnp.exp(scores - jnp.max(scores, axis=-1, keepdims=True))
    total = jnp.sum(expo, axis=-1)
    weighted = jnp.einsum("hqk,khd->qhd", expo.astype(BF16), values, preferred_element_type=F32)
    attended = (weighted / total.T[:, :, None]).reshape(mine, col_count).astype(BF16)
    attended = lax.all_gather(attended, "sub", axis=0, tiled=True)
    term = jnp.dot(attended, out_weight, preferred_element_type=F32).astype(BF16)
    return lax.psum_scatter(term, "head", scatter_dimension=0, tiled=True)


def solution(mesh):
    in_specs = (
        P(("groups", "seq"), "head"),
        P(("groups", "seq", "sub"), "head"),
        P(("groups", "seq", "sub"), "head"),
        P(("groups", "seq", "sub"), None, "head"),
        P(("groups", "seq", "sub"), None, "head"),
        P("groups", None),
        P("groups"),
        P("head", "sub"),
    )
    out_specs = P(("groups", "seq", "head"), "sub")

    def apply(queries, *rest):
        heads = queries.shape[1] // mesh.shape["head"] // HD
        paired = heads % 2 == 0 and mesh.shape["seq"] in (2, 4, 8)
        paired = paired and all(mesh.shape[axis] == 2 for axis in ("groups", "head", "sub"))
        body = local if paired else local_any
        return jax.shard_map(body, mesh=mesh, in_specs=in_specs, out_specs=out_specs, check_vma=False)(queries, *rest)

    return apply
```
